32 devices in a mesh: grp: 8 (over z, core), tp: 4 (over y, x).
Axes of the slice: x: 2, y: 2, z: 4, core: 2. Of those that a mesh axis runs over, the one named last changes fastest.
Arguments:
- hidden: bfloat16 [512, 5120], P('grp', 'tp'), may hold values from -8 to 8
- query_key_value_weight: bfloat16 [5120, 10240], P(('grp', 'tp')), as said below
- w_out: bfloat16 [8192, 5120], P(None, ('grp', 'tp')), may hold values from -0.0625 to 0.0625
- k_cache: bfloat16 [64, 4096, 8, 128], P('grp', None, 'tp'), may hold values from -256 to 256
- value_cache: bfloat16 [64, 4096, 8, 128], P('grp', None, 'tp'), may hold values from -6 to 6
- lengths: int32 [512], P('grp'), may hold values from 1 to 4096, as said below
- assign: int32 [512], P('grp'), may hold values from 0 to 7, as said below
Outputs:
- attended: bfloat16 [512, 5120], P('grp', 'tp')
The draws below stay inside these ranges and needn't reach their ends.
Inputs may be any that keep to these rules, and one draw needn't show every extreme that they name: `lengths`: some row has length 4096. `assign`: within each rollout group's 64 rows every prompt is named by exactly 8 rows. `query_key_value_weight`: entries lie within 6 / sqrt(5120) of zero.
All inputs are finite; a program needn't handle non-finite values.
Results may differ from the reference program's by a relative error of at most 0.007.
Values may be sent and summed in bfloat16 or wider, within the bound.
No kernel may reach another device: no remote copies, remote signals or barrier semaphores. Data moves between devices by JAX's collectives and lax.ppermute only.
A program may use at most 192 MiB of HBM per device.

```python
import jax
import jax.numpy as jnp
from jax import lax

D = 5120
QUERY_HEADS = 64
KEY_VALUE_HEADS = 8
HEAD_SIZE = 128
CONTEXT_SLOTS = 4096
SAMPLE_COUNT = 8
PROMPTS = 8
QUERY_PER_KEY = 8
ROWS_GRP = 64
ROW_TOTAL = 512
PROMPT_TOTAL = 64
QKV = 10240


def draw_hidden(key, part):
    key = jax.random.fold_in(key, 5)
    noise_random_key = jax.random.fold_in(key, 0)
    entry_list = jnp.clip(jax.random.normal(noise_random_key, (ROW_TOTAL, D), jnp.float32), -6.0, 6.0)
    return entry_list.astype(jnp.bfloat16)


def draw_query_key_value_weight(key, part):
    key = jax.random.fold_in(key, 7)
    noise_random_key = jax.random.fold_in(key, 0)
    entry_list = jnp.clip(jax.random.normal(noise_random_key, (D, QKV), jnp.float32), -6.0, 6.0)
    return (entry_list * D ** (-0.5)).astype(jnp.bfloat16)


def draw_k_cache(key, part):
    key = jax.random.fold_in(key, 13)
    noise_random_key = jax.random.fold_in(key, 0)
    entry_list = jnp.clip(jax.random.normal(noise_random_key, (PROMPT_TOTAL, CONTEXT_SLOTS, KEY_VALUE_HEADS, HEAD_SIZE), jnp.float32), -6.0, 6.0)
    return entry_list.astype(jnp.bfloat16)


def draw_lengths(key, part):
    key = jax.random.fold_in(key, 11)
    lens = jax.random.randint(key, (ROW_TOTAL,), 1, CONTEXT_SLOTS + 1)
    return lens.at[0].set(CONTEXT_SLOTS).astype(jnp.int32)


def draw_assign(key, part):
    key = jax.random.fold_in(key, 23)
    keys = jax.random.split(key, ROW_TOTAL // ROWS_GRP)

    def shuffled(sub_key):
        return jax.random.permutation(sub_key, ROWS_GRP)
    perms = jax.vmap(shuffled)(keys)
    return (perms // SAMPLE_COUNT).reshape(ROW_TOTAL).astype(jnp.int32)


def level_of(key, extent, cuts, least, high):
    level, own = 1.0, jax.random.fold_in(key, 6)
    for position, parts in cuts:
        steps = jnp.exp(jax.random.uniform(jax.random.fold_in(own, position), (parts,), jnp.float32, least / len(cuts), high / len(cuts)))
        level = level * jnp.repeat(steps, extent[position] // parts).reshape([-1 if axis == position else 1 for axis in range(len(extent))])
    return level


def normal_values(stream_key, extent, scale, reach, cuts=(), kind=jnp.bfloat16):
    entries = jax.random.normal(stream_key, extent, jnp.float32) * scale
    if len(cuts) > 0:
        entries = level_of(stream_key, extent, cuts, -0.22, 0.18) * entries
    return jnp.clip(entries, min=-reach, max=reach).astype(kind)


def setup_inputs(seed: int = 0) -> dict:
    streams_of = jax.random.split(jax.random.key(seed), 8)
    return {
        "hidden": draw_hidden(jax.random.fold_in(streams_of[7], 71), 0),
        "query_key_value_weight": draw_query_key_value_weight(jax.random.fold_in(streams_of[7], 71), 0),
        "w_out": normal_values(streams_of[2], (QUERY_HEADS * HEAD_SIZE, D), (QUERY_HEADS * HEAD_SIZE) ** -0.5, 0.0625, ((1, 32),)),
        "k_cache": draw_k_cache(jax.random.fold_in(streams_of[7], 71), 0),
        "value_cache": normal_values(streams_of[4], (PROMPT_TOTAL, CONTEXT_SLOTS, KEY_VALUE_HEADS, HEAD_SIZE), 1.0, 6.0, ((0, 8), (2, 4))),
        "lengths": draw_lengths(jax.random.fold_in(streams_of[7], 71), 0),
        "assign": draw_assign(jax.random.fold_in(streams_of[7], 71), 0),
    }


EPS = 1e-06
ROPE_BASE = 1000000.0

def head_norm(vec):
    return vec * lax.rsqrt(lax.optimization_barrier(jnp.mean(vec * vec, axis=-1, keepdims=True)) + EPS)

def rotate(vec, positions):
    half = vec.shape[-1] // 2
    freq = ROPE_BASE ** (-jnp.arange(half, dtype=jnp.float32) * 2.0 / vec.shape[-1])
    angle = positions.astype(jnp.float32)[:, None] * freq[None, :]
    angle = angle.reshape((angle.shape[0],) + (1,) * (vec.ndim - 2) + (half,))
    cosine, sine = (jnp.cos(angle), jnp.sin(angle))
    first, second = (vec[..., :half], vec[..., half:])
    return jnp.concatenate([first * cosine - second * sine, second * cosine + first * sine], axis=-1)

def attend_prompt(inputs):
    query_rows, fresh_key_rows, fresh_value_rows, lens, keys, values = inputs
    scale = HEAD_SIZE ** (-0.5)
    qf = query_rows.astype(jnp.float32)
    scores = jnp.einsum('skjd,ckd->skjc', qf, keys.astype(jnp.float32)) * scale
    own = jnp.einsum('skjd,skd->skj', qf, fresh_key_rows.astype(jnp.float32)) * scale
    mask = (jnp.arange(CONTEXT_SLOTS, dtype=jnp.int32)[None, :] < lens[:, None])[:, None, None, :]
    scores = jnp.where(mask, scores, -jnp.inf)
    top = jnp.maximum(lax.optimization_barrier(jnp.max(scores, axis=-1)), own)
    expo = jnp.where(mask, jnp.exp(scores - top[..., None]), 0.0)
    own_expo = jnp.exp(own - top)
    total = lax.optimization_barrier(jnp.sum(expo, axis=-1)) + own_expo
    weights = (expo / total[..., None]).astype(jnp.bfloat16)
    own_weight = (own_expo / total).astype(jnp.bfloat16)
    mixed = jnp.einsum('skjc,ckd->skjd', weights.astype(jnp.float32), values.astype(jnp.float32))
    mixed = mixed + own_weight.astype(jnp.float32)[..., None] * fresh_value_rows.astype(jnp.float32)[:, :, None, :]
    return mixed.astype(jnp.bfloat16)

def reference(hidden, query_key_value_weight, w_out, k_cache, value_cache, lengths, assign):
    values32 = hidden.astype(jnp.float32)
    normed_rows = (values32 * lax.rsqrt(lax.optimization_barrier(jnp.mean(values32 * values32, axis=-1, keepdims=True)) + EPS)).astype(jnp.bfloat16)
    projected_rows = jnp.dot(normed_rows, query_key_value_weight, preferred_element_type=jnp.float32).reshape(ROW_TOTAL, KEY_VALUE_HEADS, QUERY_PER_KEY + 2, HEAD_SIZE)
    query_rows = rotate(head_norm(projected_rows[:, :, :QUERY_PER_KEY]), lengths).astype(jnp.bfloat16)
    fresh_key_rows = rotate(head_norm(projected_rows[:, :, QUERY_PER_KEY]), lengths).astype(jnp.bfloat16)
    fresh_value_rows = projected_rows[:, :, QUERY_PER_KEY + 1].astype(jnp.bfloat16)
    prompt_id = jnp.arange(ROW_TOTAL, dtype=jnp.int32) // ROWS_GRP * PROMPTS + assign
    sort_order = jnp.argsort(prompt_id, stable=True)
    back = jnp.argsort(sort_order, stable=True)
    ordered_query_rows = query_rows[sort_order].reshape(PROMPT_TOTAL, SAMPLE_COUNT, KEY_VALUE_HEADS, QUERY_PER_KEY, HEAD_SIZE)
    ordered_key_rows = fresh_key_rows[sort_order].reshape(PROMPT_TOTAL, SAMPLE_COUNT, KEY_VALUE_HEADS, HEAD_SIZE)
    ordered_value_rows = fresh_value_rows[sort_order].reshape(PROMPT_TOTAL, SAMPLE_COUNT, KEY_VALUE_HEADS, HEAD_SIZE)
    sorted_lens = lengths[sort_order].reshape(PROMPT_TOTAL, SAMPLE_COUNT)
    mixed = lax.map(attend_prompt, (ordered_query_rows, ordered_key_rows, ordered_value_rows, sorted_lens, k_cache, value_cache))
    mixed = mixed.reshape(ROW_TOTAL, QUERY_HEADS * HEAD_SIZE)[back]
    return jnp.dot(mixed, w_out, preferred_element_type=jnp.float32).astype(jnp.bfloat16)
```

```python
import jax
import jax.numpy as jnp
from jax import lax
from jax.sharding import PartitionSpec as P

QUERY_HEADS = 64
KEY_VALUE_HEADS = 8
HEAD_SIZE = 128


EPS = 1e-06
ROPE_BASE = 1000000.0


def head_norm(vec):
    return vec * lax.rsqrt(jnp.mean(vec * vec, axis=-1, keepdims=True) + EPS)


def rotate(vec, positions):
    half = vec.shape[-1] // 2
    freq = ROPE_BASE ** (-jnp.arange(half, dtype=jnp.float32) * 2.0 / vec.shape[-1])
    angle = positions.astype(jnp.float32)[:, None] * freq[None, :]
    angle = angle.reshape((angle.shape[0],) + (1,) * (vec.ndim - 2) + (half,))
    cosine, sine = (jnp.cos(angle), jnp.sin(angle))
    first, second = (vec[..., :half], vec[..., half:])
    return jnp.concatenate(
        [first * cosine - second * sine, second * cosine + first * sine], axis=-1
    )


def attention(projected_rows, k_cache, value_cache, lengths):
    row_count = projected_rows.shape[0]
    head_group = QUERY_HEADS // KEY_VALUE_HEADS
    kv_local = projected_rows.shape[1] // ((head_group + 2) * HEAD_SIZE)
    blocks = projected_rows.reshape(row_count, kv_local, head_group + 2, HEAD_SIZE)
    query_rows = rotate(head_norm(blocks[:, :, :head_group]), lengths).astype(jnp.bfloat16)
    fresh_key_rows = rotate(head_norm(blocks[:, :, head_group]), lengths).astype(jnp.bfloat16)
    fresh_value_rows = blocks[:, :, head_group + 1].astype(jnp.bfloat16)
    prompts, context = k_cache.shape[:2]
    samples = row_count // prompts
    query_rows = query_rows.reshape(prompts, samples, kv_local, head_group, HEAD_SIZE)
    fresh_key_rows = fresh_key_rows.reshape(prompts, samples, kv_local, HEAD_SIZE)
    fresh_value_rows = fresh_value_rows.reshape(prompts, samples, kv_local, HEAD_SIZE)
    lens = lengths.reshape(prompts, samples)
    scale = HEAD_SIZE ** (-0.5)
    scores = (
        jnp.einsum("pskjd,pckd->pskjc", query_rows, k_cache, preferred_element_type=jnp.float32)
        * scale
    )
    own = (
        jnp.einsum(
            "pskjd,pskd->pskj", query_rows, fresh_key_rows, preferred_element_type=jnp.float32
        )
        * scale
    )
    mask = (jnp.arange(context, dtype=jnp.int32)[None, None, :] < lens[:, :, None])[
        :, :, None, None, :
    ]
    scores = jnp.where(mask, scores, -jnp.inf)
    top = jnp.maximum(jnp.max(scores, axis=-1), own)
    expo = jnp.where(mask, jnp.exp(scores - top[..., None]), 0.0)
    own_expo = jnp.exp(own - top)
    total = jnp.sum(expo, axis=-1) + own_expo
    weights = (expo / total[..., None]).astype(jnp.bfloat16)
    own_weight = (own_expo / total).astype(jnp.bfloat16)
    mixed = jnp.einsum(
        "pskjc,pckd->pskjd", weights, value_cache, preferred_element_type=jnp.float32
    )
    mixed = (
        mixed
        + own_weight.astype(jnp.float32)[..., None]
        * fresh_value_rows.astype(jnp.float32)[:, :, :, None, :]
    )
    return mixed.astype(jnp.bfloat16).reshape(row_count, kv_local * head_group * HEAD_SIZE)


def local(hidden, query_key_value_weight, w_out, k_cache, value_cache, lengths, assign):
    tp_count = lax.axis_size("tp")
    grp_count = lax.axis_size("grp")
    ratio = grp_count // tp_count
    row_count = hidden.shape[0]

    index = jnp.arange(row_count, dtype=jnp.int32)
    key = assign * row_count + index
    place = jnp.sum((key[None, :] < key[:, None]).astype(jnp.int32), axis=1)
    sort_rows = (place[None, :] == index[:, None]).astype(jnp.bfloat16)
    sorted_lens = jnp.sum(
        jnp.where(place[None, :] == index[:, None], lengths[None, :], 0), axis=1
    )

    columns = lax.all_to_all(
        query_key_value_weight, "tp", split_axis=1, concat_axis=0, tiled=True
    )
    out_rows = lax.all_to_all(w_out, "tp", split_axis=0, concat_axis=1, tiled=True)

    hidden = jnp.dot(sort_rows, hidden, preferred_element_type=jnp.float32).astype(jnp.bfloat16)
    full = lax.all_gather(hidden, "tp", axis=1, tiled=True)
    values32 = full.astype(jnp.float32)
    normed = (
        values32 * lax.rsqrt(jnp.mean(values32 * values32, axis=-1, keepdims=True) + EPS)
    ).astype(jnp.bfloat16)
    features = lax.all_to_all(normed, "grp", split_axis=1, concat_axis=0, tiled=True)

    partial = jnp.dot(features, columns, preferred_element_type=jnp.float32).astype(jnp.bfloat16)
    pieces = lax.all_to_all(
        partial.reshape(grp_count, row_count, partial.shape[1]),
        "grp", split_axis=0, concat_axis=0, tiled=True,
    )
    projected = jnp.sum(pieces.astype(jnp.float32), axis=0)

    attn = attention(projected, k_cache, value_cache, sorted_lens)

    all_attn = lax.all_gather(attn, "grp", axis=0, tiled=True)
    partial_out = jnp.dot(all_attn, out_rows, preferred_element_type=jnp.float32)
    partial_out = partial_out.astype(jnp.bfloat16).reshape(
        tp_count, ratio * row_count, out_rows.shape[1]
    )
    out_pieces = lax.all_to_all(partial_out, "tp", split_axis=0, concat_axis=0, tiled=True)
    summed = jnp.sum(out_pieces.astype(jnp.float32), axis=0).astype(jnp.bfloat16)
    summed = summed.reshape(ratio, row_count, out_rows.shape[1])

    b = lax.axis_index("grp") % ratio
    received = []
    for shift in range(ratio):
        pairs = []
        for g in range(grp_count):
            for t in range(tp_count):
                target = ratio * t + (g % ratio + shift) % ratio
                pairs.append((g * tp_count + t, target * tp_count + g // ratio))
        mine = lax.dynamic_index_in_dim(summed, (b + shift) % ratio, 0, keepdims=False)
        received.append(lax.ppermute(mine, ("grp", "tp"), pairs))
    stacked = jnp.stack(received)
    ordered = [
        lax.dynamic_index_in_dim(stacked, (b - block) % ratio, 0, keepdims=False)
        for block in range(ratio)
    ]
    result = jnp.concatenate(ordered, axis=1)
    return lax.dot_general(
        sort_rows, result, (((0,), (0,)), ((), ())), preferred_element_type=jnp.float32
    ).astype(jnp.bfloat16)


def solution(mesh):
    return jax.shard_map(
        local,
        mesh=mesh,
        in_specs=(
            P("grp", "tp"),
            P(("grp", "tp"), None),
            P(None, ("grp", "tp")),
            P("grp", None, "tp", None),
            P("grp", None, "tp", None),
            P("grp"),
            P("grp"),
        ),
        out_specs=P("grp", "tp"),
        check_vma=False,
    )
```

```python
import functools

import jax
import jax.numpy as jnp
from jax import lax
from jax.experimental import pallas as pl
from jax.experimental.pallas import tpu as pltpu
from jax.sharding import PartitionSpec as P

QUERY_HEADS = 64
KEY_VALUE_HEADS = 8
HEAD_SIZE = 128
HEAD_GROUP = QUERY_HEADS // KEY_VALUE_HEADS


EPS = 1e-06
ROPE_BASE = 1000000.0
LOG2_E = 1.4426950408889634
MASKED = -1e30
VMEM_LIMIT = 48 * 1024 * 1024


def rotary_tables(positions):
    half = HEAD_SIZE // 2
    freq = ROPE_BASE ** (-jnp.arange(half, dtype=jnp.float32) * 2.0 / HEAD_SIZE)
    angle = positions.astype(jnp.float32)[:, None] * freq[None, :]
    cosine, sine = (jnp.cos(angle), jnp.sin(angle))
    return jnp.concatenate([cosine, cosine], axis=1), jnp.concatenate([-sine, sine], axis=1)


def column_tile(width):
    return next(tile for tile in (512, 640, 256, 128) if width % tile == 0)


def project_kernel(count, place_ref, x_ref, *refs):
    pieces, (out_ref, weight, sems) = refs[:count], refs[count:]
    rows, width = pieces[0].shape
    tile = column_tile(width)
    copies = []
    for c in range(width // tile):
        for n, piece in enumerate(pieces):
            start = pl.multiple_of(place_ref[n] * rows, 16)
            copy = pltpu.make_async_copy(
                piece.at[:, pl.ds(c * tile, tile)],
                weight.at[pl.ds(start, rows), pl.ds(c * tile, tile)],
                sems.at[c, n],
            )
            copy.start()
            copies.append(copy)
    for c in range(width // tile):
        for copy in copies[c * count : (c + 1) * count]:
            copy.wait()
        out_ref[:, c * tile : (c + 1) * tile] = jnp.dot(
            x_ref[...], weight[:, c * tile : (c + 1) * tile], preferred_element_type=jnp.float32
        ).astype(out_ref.dtype)


def project(x, pieces, places):
    rows, width = pieces[0].shape
    count = len(pieces)
    tile = column_tile(width)
    return pl.pallas_call(
        functools.partial(project_kernel, count),
        grid_spec=pltpu.PrefetchScalarGridSpec(
            num_scalar_prefetch=1,
            grid=(),
            in_specs=[pl.BlockSpec(memory_space=pltpu.VMEM)]
            + [pl.BlockSpec(memory_space=pl.ANY)] * count,
            out_specs=pl.BlockSpec(memory_space=pltpu.VMEM),
            scratch_shapes=[
                pltpu.VMEM((count * rows, width), jnp.bfloat16),
                pltpu.SemaphoreType.DMA((width // tile, count)),
            ],
        ),
        out_shape=jax.ShapeDtypeStruct((x.shape[0], width), jnp.bfloat16),
        compiler_params=pltpu.CompilerParams(vmem_limit_bytes=VMEM_LIMIT),
        cost_estimate=pl.CostEstimate(
            flops=2 * x.shape[0] * count * rows * width,
            bytes_accessed=2 * count * rows * width,
            transcendentals=0,
        ),
        name="project",
    )(places, x, *pieces)


def output_kernel(count, blocks, place_ref, *refs):
    mixed, pieces = refs[:blocks], refs[blocks : blocks + count]
    out_ref, weight, sems = refs[blocks + count :]
    rows = pieces[0].shape[0]
    copies = []
    for n, piece in enumerate(pieces):
        start = pl.multiple_of(place_ref[n] * rows, 16)
        copy = pltpu.make_async_copy(piece, weight.at[pl.ds(start, rows)], sems.at[n])
        copy.start()
        copies.append(copy)
    x = jnp.concatenate([ref[...] for ref in mixed], axis=0)
    for copy in copies:
        copy.wait()
    width = count * rows
    tile = next(size for size in (256, 320, 128) if width % size == 0)
    height = mixed[0].shape[0]
    for c in range(width // tile):
        result = lax.dot_general(
            x,
            weight[c * tile : (c + 1) * tile],
            (((1,), (1,)), ((), ())),
            preferred_element_type=jnp.float32,
        ).astype(out_ref.dtype)
        for n in range(blocks):
            out_ref[n, :, c * tile : (c + 1) * tile] = result[n * height : (n + 1) * height]


def output(mixed, pieces, places):
    rows, depth = pieces[0].shape
    count, blocks = len(pieces), len(mixed)
    height = mixed[0].shape[0]
    return pl.pallas_call(
        functools.partial(output_kernel, count, blocks),
        grid_spec=pltpu.PrefetchScalarGridSpec(
            num_scalar_prefetch=1,
            grid=(),
            in_specs=[pl.BlockSpec(memory_space=pltpu.VMEM)] * blocks
            + [pl.BlockSpec(memory_space=pl.ANY)] * count,
            out_specs=pl.BlockSpec(memory_space=pltpu.VMEM),
            scratch_shapes=[
                pltpu.VMEM((count * rows, depth), jnp.bfloat16),
                pltpu.SemaphoreType.DMA((count,)),
            ],
        ),
        out_shape=jax.ShapeDtypeStruct((blocks, height, count * rows), jnp.bfloat16),
        compiler_params=pltpu.CompilerParams(vmem_limit_bytes=VMEM_LIMIT),
        cost_estimate=pl.CostEstimate(
            flops=2 * blocks * height * count * rows * depth,
            bytes_accessed=2 * count * rows * depth,
            transcendentals=0,
        ),
        name="output",
    )(places, *mixed, *pieces)


def attention_kernel(parts, kv_local, samples, *refs):
    partials, (cos_ref, sin_ref, lens_ref, k_ref, v_ref, out_ref, scores) = refs[:parts], refs[parts:]
    together, context, depth = k_ref.shape
    scale = HEAD_SIZE ** (-0.5)
    tile = 1024
    proj = partials[0][...].astype(jnp.float32)
    for ref in partials[1:]:
        proj = proj + ref[...].astype(jnp.float32)
    cosine, sine = cos_ref[...], sin_ref[...]

    def head(index):
        vec = proj[:, index * HEAD_SIZE : (index + 1) * HEAD_SIZE]
        vec = vec * lax.rsqrt(jnp.mean(vec * vec, axis=-1, keepdims=True) + EPS)
        vec = vec * cosine + pltpu.roll(vec, HEAD_SIZE // 2, 1) * sine
        return vec.astype(jnp.bfloat16).astype(jnp.float32)

    queries, owns, fresh = [], [], []
    for h in range(kv_local):
        base = h * (HEAD_GROUP + 2)
        new_key = head(base + HEAD_GROUP)
        new_value = proj[:, (base + HEAD_GROUP + 1) * HEAD_SIZE : (base + HEAD_GROUP + 2) * HEAD_SIZE]
        fresh.append(new_value.astype(jnp.bfloat16).astype(jnp.float32))
        for j in range(HEAD_GROUP):
            query = head(base + j)
            queries.append(query)
            owns.append(jnp.sum(query * new_key, axis=-1, keepdims=True))

    results = []
    for u in range(together):
        rows = slice(u * samples, (u + 1) * samples)
        query = jnp.concatenate([q[rows] for q in queries], axis=0).astype(jnp.bfloat16)
        own = jnp.concatenate([o[rows] for o in owns], axis=0)
        group = HEAD_GROUP * samples
        if kv_local > 1:
            zeros = jnp.zeros((group, HEAD_SIZE), jnp.bfloat16)
            query = jnp.concatenate(
                [
                    jnp.concatenate(
                        [query[h * group : (h + 1) * group] if h == e else zeros for e in range(kv_local)],
                        axis=1,
                    )
                    for h in range(kv_local)
                ],
                axis=0,
            )
        height = kv_local * group
        lens = lens_ref[rows, 0:1]
        most = jnp.full((height, HEAD_SIZE), MASKED, jnp.float32)
        for c in range(0, context, tile):
            part = lax.dot_general(
                query,
                k_ref[u, c : c + tile],
                (((1,), (1,)), ((), ())),
                preferred_element_type=jnp.float32,
            )
            slots = lax.broadcasted_iota(jnp.int32, (samples, tile), 1) + c
            bias = jnp.where(slots < lens, 0.0, MASKED)
            part = (part.reshape(height // samples, samples, tile) + bias[None]).reshape(height, tile)
            scores[:, c : c + tile] = part
            for d in range(0, tile, HEAD_SIZE):
                most = jnp.maximum(most, part[:, d : d + HEAD_SIZE])
        top = jnp.maximum(jnp.max(most, axis=-1, keepdims=True), own)
        own_expo = jnp.exp2((own - top) * (scale * LOG2_E))
        sums = jnp.zeros((height, HEAD_SIZE), jnp.float32)
        mixed = jnp.zeros((height, depth), jnp.float32)
        for c in range(0, context, tile):
            expo = jnp.exp2((scores[:, c : c + tile] - top) * (scale * LOG2_E))
            for d in range(0, tile, HEAD_SIZE):
                sums = sums + expo[:, d : d + HEAD_SIZE]
            mixed = mixed + jnp.dot(
                expo.astype(jnp.bfloat16), v_ref[u, c : c + tile], preferred_element_type=jnp.float32
            )
        total = jnp.sum(sums, axis=-1, keepdims=True) + own_expo
        inverse = 1.0 / total
        own_weight = own_expo * inverse
        line = []
        for h in range(kv_local):
            value = fresh[h][rows]
            for j in range(HEAD_GROUP):
                at = slice(h * group + j * samples, h * group + (j + 1) * samples)
                lanes = slice(h * HEAD_SIZE, (h + 1) * HEAD_SIZE)
                line.append(mixed[at, lanes] * inverse[at] + own_weight[at] * value)
        results.append(jnp.concatenate(line, axis=1))
    out_ref[...] = jnp.concatenate(results, axis=0).astype(out_ref.dtype)


def attention(partials, cosine, sine, lens, k_cache, value_cache, kv_local):
    rows, width = partials[0].shape
    prompts, context, depth = k_cache.shape
    samples = rows // prompts
    together = 16 // samples
    height = together * samples
    heads = kv_local * HEAD_GROUP
    small = pl.BlockSpec((height, HEAD_SIZE), lambda i: (i, 0))
    cache = pl.BlockSpec((together, context, depth), lambda i: (i, 0, 0))
    return pl.pallas_call(
        functools.partial(attention_kernel, len(partials), kv_local, samples),
        grid=(prompts // together,),
        in_specs=[pl.BlockSpec((height, width), lambda i: (i, 0))] * len(partials)
        + [small] * 3
        + [cache] * 2,
        out_specs=pl.BlockSpec((height, heads * HEAD_SIZE), lambda i: (i, 0)),
        out_shape=jax.ShapeDtypeStruct((rows, heads * HEAD_SIZE), jnp.bfloat16),
        scratch_shapes=[pltpu.VMEM((heads * samples, context), jnp.float32)],
        compiler_params=pltpu.CompilerParams(vmem_limit_bytes=VMEM_LIMIT),
        cost_estimate=pl.CostEstimate(
            flops=4 * prompts * heads * samples * context * depth,
            bytes_accessed=4 * prompts * context * depth,
            transcendentals=prompts * heads * samples * context,
        ),
        name="attention",
    )(*partials, cosine, sine, lens, k_cache, value_cache)


def at_place(pieces, places):
    rows, width = pieces[0].shape
    if rows % 16 == 0:
        return pieces, places
    laid = jnp.zeros((len(pieces) * rows, width), pieces[0].dtype)
    for n, piece in enumerate(pieces):
        laid = lax.dynamic_update_slice_in_dim(laid, piece, places[n] * rows, 0)
    return [laid], jnp.zeros((1,), jnp.int32)


def local(hidden, query_key_value_weight, w_out, k_cache, value_cache, lengths, assign):
    tp_count = lax.axis_size("tp")
    grp_count = lax.axis_size("grp")
    ratio = grp_count // tp_count
    t = lax.axis_index("tp")
    plane = lax.axis_index("grp") // ratio
    core = lax.axis_index("grp") % ratio
    row_count, width = hidden.shape
    prompts, context, kv_local, _ = k_cache.shape

    def to_rank(value, shift):
        return lax.ppermute(value, "tp", [(i, i ^ shift) for i in range(tp_count)])

    def to_plane(value, shift):
        pairs = [(i, ((i // ratio) ^ shift) * ratio + i % ratio) for i in range(grp_count)]
        return lax.ppermute(value, "grp", pairs)

    def to_core(value, shift):
        pairs = [(i, i // ratio * ratio + (i + shift) % ratio) for i in range(grp_count)]
        return lax.ppermute(value, "grp", pairs)

    def spread(weight, size):
        mine = [lax.dynamic_slice_in_dim(weight, t * size, size, 1)]
        for shift in range(1, tp_count):
            mine.append(to_rank(lax.dynamic_slice_in_dim(weight, (t ^ shift) * size, size, 1), shift))
        pieces = list(mine)
        for turn in range(1, ratio):
            pieces += [to_core(piece, turn) for piece in mine]
        places = [
            (core - turn) % ratio * tp_count + (t ^ shift)
            for turn in range(ratio)
            for shift in range(tp_count)
        ]
        return pieces, jnp.stack(places).astype(jnp.int32)

    pieces, places = spread(query_key_value_weight, query_key_value_weight.shape[1] // tp_count)

    index = jnp.arange(row_count, dtype=jnp.int32)
    key = assign * row_count + index
    place = jnp.sum((key[None, :] < key[:, None]).astype(jnp.int32), axis=1)
    sort_rows = (place[None, :] == index[:, None]).astype(jnp.bfloat16)
    lens = jnp.sum(jnp.where(place[None, :] == index[:, None], lengths[None, :], 0), axis=1)
    cosine, sine = rotary_tables(lens)
    lens = jnp.broadcast_to(lens[:, None], (row_count, HEAD_SIZE))

    hidden = jnp.dot(sort_rows, hidden, preferred_element_type=jnp.float32).astype(jnp.bfloat16)
    full = jnp.stack([hidden] + [to_rank(hidden, shift) for shift in range(1, tp_count)])
    values32 = full.astype(jnp.float32)
    mean = jnp.sum(values32 * values32, axis=(0, 2), keepdims=True) / (tp_count * width)
    normed = (values32 * lax.rsqrt(mean + EPS)).astype(jnp.bfloat16)
    features = []
    for shift in range(tp_count):
        block = lax.dynamic_index_in_dim(normed, t ^ plane ^ shift, 0, keepdims=False)
        features.append(block if shift == 0 else to_plane(block, shift))
    features = jnp.concatenate(features, axis=0)

    partial = project(features, *at_place(pieces, places))
    partials = []
    for shift in range(tp_count):
        block = partial[shift * row_count : (shift + 1) * row_count]
        partials.append(block if shift == 0 else to_plane(block, shift))

    mixed = attention(
        partials,
        cosine,
        sine,
        lens,
        k_cache.reshape(prompts, context, kv_local * HEAD_SIZE),
        value_cache.reshape(prompts, context, kv_local * HEAD_SIZE),
        kv_local,
    )

    w_out, _ = lax.optimization_barrier((w_out, pieces))
    out_pieces, out_places = spread(w_out.T, w_out.shape[0] // tp_count)
    all_mixed = [mixed] + [to_plane(mixed, shift) for shift in range(1, tp_count)]
    partial_out = output(all_mixed, *at_place(out_pieces, out_places))

    summed = 0.0
    for shift in range(tp_count):
        block = lax.dynamic_index_in_dim(partial_out, plane ^ t ^ shift, 0, keepdims=False)
        block = block if shift == 0 else to_rank(block, shift)
        summed = summed + block.astype(jnp.float32)
    summed = summed.astype(jnp.bfloat16)
    pairs = [
        (g * tp_count + r, (r * ratio + g % ratio) * tp_count + g // ratio)
        for g in range(grp_count)
        for r in range(tp_count)
    ]
    result = lax.ppermute(summed, ("grp", "tp"), pairs)
    return lax.dot_general(
        sort_rows, result, (((0,), (0,)), ((), ())), preferred_element_type=jnp.float32
    ).astype(jnp.bfloat16)


def solution(mesh):
    return jax.shard_map(
        local,
        mesh=mesh,
        in_specs=(
            P("grp", "tp"),
            P(("grp", "tp"), None),
            P(None, ("grp", "tp")),
            P("grp", None, "tp", None),
            P("grp", None, "tp", None),
            P("grp"),
            P("grp"),
        ),
        out_specs=P("grp", "tp"),
        check_vma=False,
    )
```

```python
import functools

import jax
import jax.numpy as jnp
from jax import lax
from jax.experimental import pallas as pl
from jax.experimental.pallas import tpu as pltpu
from jax.sharding import PartitionSpec as P

QUERY_HEADS = 64
KEY_VALUE_HEADS = 8
HEAD_SIZE = 128
HEAD_GROUP = QUERY_HEADS // KEY_VALUE_HEADS


EPS = 1e-06
ROPE_BASE = 1000000.0
LOG2_E = 1.4426950408889634
MASKED = -1e30
VMEM_LIMIT = 48 * 1024 * 1024


def rotary_tables(positions):
    half = HEAD_SIZE // 2
    freq = ROPE_BASE ** (-jnp.arange(half, dtype=jnp.float32) * 2.0 / HEAD_SIZE)
    angle = positions.astype(jnp.float32)[:, None] * freq[None, :]
    cosine, sine = (jnp.cos(angle), jnp.sin(angle))
    return jnp.concatenate([cosine, cosine], axis=1), jnp.concatenate([-sine, sine], axis=1)


def column_tile(width):
    return next(tile for tile in (512, 640, 256, 128) if width % tile == 0)


def project_kernel(count, place_ref, x_ref, *refs):
    pieces, (out_ref, weight, sems) = refs[:count], refs[count:]
    rows, width = pieces[0].shape
    tile = column_tile(width)
    copies = []
    for c in range(width // tile):
        for n, piece in enumerate(pieces):
            start = pl.multiple_of(place_ref[n] * rows, 16)
            copy = pltpu.make_async_copy(
                piece.at[:, pl.ds(c * tile, tile)],
                weight.at[pl.ds(start, rows), pl.ds(c * tile, tile)],
                sems.at[c, n],
            )
            copy.start()
            copies.append(copy)
    for c in range(width // tile):
        for copy in copies[c * count : (c + 1) * count]:
            copy.wait()
        out_ref[:, c * tile : (c + 1) * tile] = jnp.dot(
            x_ref[...], weight[:, c * tile : (c + 1) * tile], preferred_element_type=jnp.float32
        ).astype(out_ref.dtype)


def project(x, pieces, places):
    rows, width = pieces[0].shape
    count = len(pieces)
    tile = column_tile(width)
    return pl.pallas_call(
        functools.partial(project_kernel, count),
        grid_spec=pltpu.PrefetchScalarGridSpec(
            num_scalar_prefetch=1,
            grid=(),
            in_specs=[pl.BlockSpec(memory_space=pltpu.VMEM)]
            + [pl.BlockSpec(memory_space=pl.ANY)] * count,
            out_specs=pl.BlockSpec(memory_space=pltpu.VMEM),
            scratch_shapes=[
                pltpu.VMEM((count * rows, width), jnp.bfloat16),
                pltpu.SemaphoreType.DMA((width // tile, count)),
            ],
        ),
        out_shape=jax.ShapeDtypeStruct((x.shape[0], width), jnp.bfloat16),
        compiler_params=pltpu.CompilerParams(vmem_limit_bytes=VMEM_LIMIT),
        cost_estimate=pl.CostEstimate(
            flops=2 * x.shape[0] * count * rows * width,
            bytes_accessed=2 * count * rows * width,
            transcendentals=0,
        ),
        name="project",
    )(places, x, *pieces)


def output_kernel(count, place_ref, x_ref, *refs):
    pieces, (out_ref, weight, sems) = refs[:count], refs[count:]
    rows = pieces[0].shape[0]
    copies = []
    for n, piece in enumerate(pieces):
        start = pl.multiple_of(place_ref[n] * rows, 16)
        copy = pltpu.make_async_copy(piece, weight.at[pl.ds(start, rows)], sems.at[n])
        copy.start()
        copies.append(copy)
    for copy in copies:
        copy.wait()
    width = count * rows
    tile = next(size for size in (256, 320, 128) if width % size == 0)
    for c in range(width // tile):
        out_ref[:, c * tile : (c + 1) * tile] = lax.dot_general(
            x_ref[...],
            weight[c * tile : (c + 1) * tile],
            (((1,), (1,)), ((), ())),
            preferred_element_type=jnp.float32,
        ).astype(out_ref.dtype)


def output(x, pieces, places):
    rows, depth = pieces[0].shape
    count = len(pieces)
    return pl.pallas_call(
        functools.partial(output_kernel, count),
        grid_spec=pltpu.PrefetchScalarGridSpec(
            num_scalar_prefetch=1,
            grid=(),
            in_specs=[pl.BlockSpec(memory_space=pltpu.VMEM)]
            + [pl.BlockSpec(memory_space=pl.ANY)] * count,
            out_specs=pl.BlockSpec(memory_space=pltpu.VMEM),
            scratch_shapes=[
                pltpu.VMEM((count * rows, depth), jnp.bfloat16),
                pltpu.SemaphoreType.DMA((count,)),
            ],
        ),
        out_shape=jax.ShapeDtypeStruct((x.shape[0], count * rows), jnp.bfloat16),
        compiler_params=pltpu.CompilerParams(vmem_limit_bytes=VMEM_LIMIT),
        cost_estimate=pl.CostEstimate(
            flops=2 * x.shape[0] * count * rows * depth,
            bytes_accessed=2 * count * rows * depth,
            transcendentals=0,
        ),
        name="output",
    )(places, x, *pieces)


def attention_kernel(kv_local, samples, *refs):
    partials, refs = refs[:kv_local], refs[kv_local:]
    cos_ref, sin_ref, lens_ref, k_ref, v_ref, out_ref, scores = refs
    together, length, _ = k_ref.shape
    scale = HEAD_SIZE ** (-0.5) * LOG2_E
    group = HEAD_GROUP * samples
    tile = 1024
    cosine, sine = cos_ref[...], sin_ref[...]
    lane = lax.broadcasted_iota(jnp.int32, (group, HEAD_SIZE), 1) % kv_local

    queries, owns, fresh = [], [], []
    for ref in partials:
        proj = ref[0].astype(jnp.float32)
        for n in range(1, ref.shape[0]):
            proj = proj + ref[n].astype(jnp.float32)

        def head(index):
            vec = proj[:, index * HEAD_SIZE : (index + 1) * HEAD_SIZE]
            vec = vec * lax.rsqrt(jnp.mean(vec * vec, axis=-1, keepdims=True) + EPS)
            vec = vec * cosine + pltpu.roll(vec, HEAD_SIZE // 2, 1) * sine
            return vec.astype(jnp.bfloat16).astype(jnp.float32)

        new_key = head(HEAD_GROUP)
        new_value = proj[:, (HEAD_GROUP + 1) * HEAD_SIZE : (HEAD_GROUP + 2) * HEAD_SIZE]
        fresh.append(new_value.astype(jnp.bfloat16).astype(jnp.float32))
        queries.append([head(j) for j in range(HEAD_GROUP)])
        owns.append([jnp.sum(q * new_key, axis=-1, keepdims=True) for q in queries[-1]])

    results = []
    for u in range(together):
        rows = slice(u * samples, (u + 1) * samples)
        query = jnp.concatenate(
            [q[rows] for head_queries in queries for q in head_queries], axis=0
        ).astype(jnp.bfloat16)
        own = [jnp.concatenate([o[rows] for o in head_owns], axis=0) for head_owns in owns]
        lens = lens_ref[rows, 0:1] * kv_local
        most = jnp.full((group, HEAD_SIZE), MASKED, jnp.float32)
        for c in range(0, length, tile):
            part = lax.dot_general(
                query,
                k_ref[u, c : c + tile],
                (((1,), (1,)), ((), ())),
                preferred_element_type=jnp.float32,
            )
            for d in range(0, tile, HEAD_SIZE):
                dense = part[:group, d : d + HEAD_SIZE]
                for h in range(1, kv_local):
                    other = part[h * group : (h + 1) * group, d : d + HEAD_SIZE]
                    dense = jnp.where(lane == h, other, dense)
                slots = lax.broadcasted_iota(jnp.int32, (samples, HEAD_SIZE), 1) + (c + d)
                bias = jnp.where(slots < lens, 0.0, MASKED)
                dense = (dense.reshape(HEAD_GROUP, samples, HEAD_SIZE) + bias[None]).reshape(
                    group, HEAD_SIZE
                )
                scores[:, c + d : c + d + HEAD_SIZE] = dense
                most = jnp.maximum(most, dense)
        tops = [
            jnp.maximum(
                jnp.max(jnp.where(lane == h, most, MASKED), axis=-1, keepdims=True), own[h]
            )
            for h in range(kv_local)
        ]
        top = jnp.broadcast_to(tops[0], (group, HEAD_SIZE))
        for h in range(1, kv_local):
            top = jnp.where(lane == h, tops[h], top)
        sums = jnp.zeros((group, HEAD_SIZE), jnp.float32)
        mixed = jnp.zeros((kv_local * group, HEAD_SIZE), jnp.float32)
        for c in range(0, length, tile):
            weights = [[] for _ in range(kv_local)]
            for d in range(0, tile, HEAD_SIZE):
                expo = jnp.exp2((scores[:, c + d : c + d + HEAD_SIZE] - top) * scale)
                sums = sums + expo
                for h in range(kv_local):
                    kept = expo if kv_local == 1 else jnp.where(lane == h, expo, 0.0)
                    weights[h].append(kept.astype(jnp.bfloat16))
            weights = jnp.concatenate([jnp.concatenate(w, axis=1) for w in weights], axis=0)
            mixed = mixed + jnp.dot(
                weights, v_ref[u, c : c + tile], preferred_element_type=jnp.float32
            )
        line = []
        for h in range(kv_local):
            own_expo = jnp.exp2((own[h] - tops[h]) * scale)
            total = jnp.sum(jnp.where(lane == h, sums, 0.0), axis=-1, keepdims=True) + own_expo
            inverse = 1.0 / total
            own_weight = own_expo * inverse
            value = fresh[h][rows]
            for j in range(HEAD_GROUP):
                at = slice(j * samples, (j + 1) * samples)
                part = mixed[h * group + j * samples : h * group + (j + 1) * samples]
                line.append(part * inverse[at] + own_weight[at] * value)
        results.append(jnp.concatenate(line, axis=1))
    out_ref[...] = jnp.concatenate(results, axis=0).astype(out_ref.dtype)


def attention(partials, cosine, sine, lens, k_cache, value_cache, chunk, chunks):
    count, rows, width = partials[0].shape
    kv_local = len(partials)
    prompts, length, _ = k_cache.shape
    samples = rows // prompts
    together = 16 // samples
    height = together * samples
    heads = kv_local * HEAD_GROUP
    steps = prompts // together // chunks
    first = chunk * steps
    small = pl.BlockSpec((height, HEAD_SIZE), lambda i: (i + first, 0))
    cache = pl.BlockSpec((together, length, HEAD_SIZE), lambda i: (i + first, 0, 0))
    return pl.pallas_call(
        functools.partial(attention_kernel, kv_local, samples),
        grid=(steps,),
        in_specs=[pl.BlockSpec((count, height, width), lambda i: (0, i + first, 0))] * kv_local
        + [small] * 3
        + [cache] * 2,
        out_specs=pl.BlockSpec((height, heads * HEAD_SIZE), lambda i: (i, 0)),
        out_shape=jax.ShapeDtypeStruct((rows // chunks, heads * HEAD_SIZE), jnp.bfloat16),
        scratch_shapes=[pltpu.VMEM((HEAD_GROUP * samples, length), jnp.float32)],
        compiler_params=pltpu.CompilerParams(vmem_limit_bytes=VMEM_LIMIT),
        cost_estimate=pl.CostEstimate(
            flops=4 * steps * together * heads * samples * length * HEAD_SIZE,
            bytes_accessed=4 * steps * together * length * HEAD_SIZE,
            transcendentals=steps * together * HEAD_GROUP * samples * length,
        ),
        name="attention",
    )(*partials, cosine, sine, lens, k_cache, value_cache)


CHUNKS = 2


def local(hidden, query_key_value_weight, w_out, k_cache, value_cache, lengths, assign):
    tp_count = lax.axis_size("tp")
    grp_count = lax.axis_size("grp")
    ratio = grp_count // tp_count
    core = lax.axis_index("grp") % ratio
    row_count, width = hidden.shape
    prompts, context, kv_local, _ = k_cache.shape
    columns = [[p * ratio + b for p in range(tp_count)] for b in range(ratio)]

    def swap(value):
        values = [value]
        for turn in range(1, ratio):
            pairs = [(i, i // ratio * ratio + (i + turn) % ratio) for i in range(grp_count)]
            values.append(lax.ppermute(value, "grp", pairs))
        return values

    owners = jnp.stack([(core - turn) % ratio for turn in range(ratio)]).astype(jnp.int32)

    piece_rows = query_key_value_weight.shape[0]
    head_width = query_key_value_weight.shape[1] // (tp_count * kv_local)
    weights = []
    for h in range(kv_local):
        starts = [(r * kv_local + h) * head_width for r in range(tp_count)]
        part = jnp.stack([query_key_value_weight[:, s : s + head_width] for s in starts])
        part = lax.all_to_all(part, "tp", split_axis=0, concat_axis=0, tiled=True)
        weights.append(part.reshape(tp_count * piece_rows, part.shape[2]))

    index = jnp.arange(row_count, dtype=jnp.int32)
    key = assign * row_count + index
    place = jnp.sum((key[None, :] < key[:, None]).astype(jnp.int32), axis=1)
    sort_rows = (place[None, :] == index[:, None]).astype(jnp.bfloat16)
    lens = jnp.sum(jnp.where(place[None, :] == index[:, None], lengths[None, :], 0), axis=1)
    cosine, sine = rotary_tables(lens)
    lens = jnp.broadcast_to(lens[:, None], (row_count, HEAD_SIZE))

    hidden = jnp.dot(sort_rows, hidden, preferred_element_type=jnp.float32).astype(jnp.bfloat16)
    full = lax.all_gather(hidden, "tp", axis=0)
    values32 = full.astype(jnp.float32)
    mean = jnp.sum(values32 * values32, axis=(0, 2), keepdims=True) / (tp_count * width)
    normed = (values32 * lax.rsqrt(mean + EPS)).astype(jnp.bfloat16)
    features = lax.all_to_all(
        normed, "grp", split_axis=0, concat_axis=0, axis_index_groups=columns, tiled=True
    ).reshape(tp_count * row_count, width)

    partials = []
    for h in range(kv_local):
        partial = project(features, swap(weights[h]), owners)
        partials.append(
            lax.all_to_all(
                partial.reshape(tp_count, row_count, -1),
                "grp", split_axis=0, concat_axis=0, axis_index_groups=columns, tiled=True,
            )
        )

    w_out, _ = lax.optimization_barrier((w_out, weights))
    out_cols = w_out.shape[1]
    depth = w_out.shape[0] // tp_count
    out_weight = jnp.stack([w_out[r * depth : (r + 1) * depth].T for r in range(tp_count)])
    out_weight = lax.all_to_all(out_weight, "tp", split_axis=0, concat_axis=0, tiled=True)
    out_weights = swap(out_weight.reshape(tp_count * out_cols, -1))

    keys = k_cache.reshape(prompts, context * kv_local, HEAD_SIZE)
    values = value_cache.reshape(prompts, context * kv_local, HEAD_SIZE)
    plane_pairs = [
        (g * tp_count + r, (r * ratio + g % ratio) * tp_count + g // ratio)
        for g in range(grp_count)
        for r in range(tp_count)
    ]
    results = []
    for chunk in range(CHUNKS):
        mixed = attention(partials, cosine, sine, lens, keys, values, chunk, CHUNKS)
        mixed = lax.all_gather(mixed, "grp", axis=0, axis_index_groups=columns, tiled=True)
        partial_out = output(mixed, out_weights, owners)
        pieces = lax.all_to_all(
            partial_out.reshape(tp_count, row_count // CHUNKS, -1),
            "tp", split_axis=0, concat_axis=0, tiled=True,
        )
        summed = jnp.sum(pieces.astype(jnp.float32), axis=0).astype(jnp.bfloat16)
        results.append(lax.ppermute(summed, ("grp", "tp"), plane_pairs))
    result = jnp.concatenate(results, axis=0)
    return lax.dot_general(
        sort_rows, result, (((0,), (0,)), ((), ())), preferred_element_type=jnp.float32
    ).astype(jnp.bfloat16)


def solution(mesh):
    return jax.shard_map(
        local,
        mesh=mesh,
        in_specs=(
            P("grp", "tp"),
            P(("grp", "tp"), None),
            P(None, ("grp", "tp")),
            P("grp", None, "tp", None),
            P("grp", None, "tp", None),
            P("grp"),
            P("grp"),
        ),
        out_specs=P("grp", "tp"),
        check_vma=False,
    )
```

```python
import functools

import jax
import jax.numpy as jnp
from jax import lax
from jax.experimental import pallas as pl
from jax.experimental.pallas import tpu as pltpu
from jax.sharding import PartitionSpec as P

QUERY_HEADS = 64
KEY_VALUE_HEADS = 8
HEAD_SIZE = 128
HEAD_GROUP = QUERY_HEADS // KEY_VALUE_HEADS


EPS = 1e-06
ROPE_BASE = 1000000.0
LOG2_E = 1.4426950408889634
MASKED = -1e30
VMEM_LIMIT = 48 * 1024 * 1024


def rotary_tables(positions):
    half = HEAD_SIZE // 2
    freq = ROPE_BASE ** (-jnp.arange(half, dtype=jnp.float32) * 2.0 / HEAD_SIZE)
    angle = positions.astype(jnp.float32)[:, None] * freq[None, :]
    cosine, sine = (jnp.cos(angle), jnp.sin(angle))
    return jnp.concatenate([cosine, cosine], axis=1), jnp.concatenate([-sine, sine], axis=1)


def column_tile(width):
    return next(tile for tile in (512, 640, 256, 128) if width % tile == 0)


def project_kernel(count, first, blocks, place_ref, *refs):
    xs, pieces, outs = refs[:blocks], refs[blocks : blocks + count], refs[blocks + count : -2]
    weight, sems = refs[-2:]
    rows = pieces[0].shape[0]
    height, width = outs[0].shape
    tile = column_tile(width)
    copies = []
    for c in range(width // tile):
        for n, piece in enumerate(pieces):
            start = pl.multiple_of(place_ref[n] * rows, 16)
            copy = pltpu.make_async_copy(
                piece.at[:, pl.ds(first + c * tile, tile)],
                weight.at[pl.ds(start, rows), pl.ds(c * tile, tile)],
                sems.at[c, n],
            )
            copy.start()
            copies.append(copy)
    x = jnp.concatenate([ref[...] for ref in xs], axis=0)
    for c in range(width // tile):
        for copy in copies[c * count : (c + 1) * count]:
            copy.wait()
        lanes = slice(c * tile, (c + 1) * tile)
        result = jnp.dot(x, weight[:, lanes], preferred_element_type=jnp.float32)
        for n in range(blocks):
            outs[n][:, lanes] = result[n * height : (n + 1) * height].astype(outs[n].dtype)


def project(xs, pieces, places, first, width):
    rows = pieces[0].shape[0]
    count, blocks, height = len(pieces), len(xs), xs[0].shape[0]
    tile = column_tile(width)
    return pl.pallas_call(
        functools.partial(project_kernel, count, first, blocks),
        grid_spec=pltpu.PrefetchScalarGridSpec(
            num_scalar_prefetch=1,
            grid=(),
            in_specs=[pl.BlockSpec(memory_space=pltpu.VMEM)] * blocks
            + [pl.BlockSpec(memory_space=pl.ANY)] * count,
            out_specs=[pl.BlockSpec(memory_space=pltpu.VMEM)] * blocks,
            scratch_shapes=[
                pltpu.VMEM((count * rows, width), jnp.bfloat16),
                pltpu.SemaphoreType.DMA((width // tile, count)),
            ],
        ),
        out_shape=[jax.ShapeDtypeStruct((height, width), jnp.bfloat16)] * blocks,
        compiler_params=pltpu.CompilerParams(vmem_limit_bytes=VMEM_LIMIT),
        cost_estimate=pl.CostEstimate(
            flops=2 * blocks * height * count * rows * width,
            bytes_accessed=2 * count * rows * width,
            transcendentals=0,
        ),
        name="project",
    )(places, *xs, *pieces)


def output_kernel(count, blocks, place_ref, x_place_ref, *refs):
    xs, pieces, outs = refs[:blocks], refs[blocks : blocks + count], refs[blocks + count : -4]
    x_held, weight, x_sems, sems = refs[-4:]
    rows = pieces[0].shape[0]
    height = xs[0].shape[0]
    copies = []
    for n, x in enumerate(xs):
        start = pl.multiple_of(x_place_ref[n] * height, 16)
        copies.append(pltpu.make_async_copy(x, x_held.at[pl.ds(start, height)], x_sems.at[n]))
    for n, piece in enumerate(pieces):
        start = pl.multiple_of(place_ref[n] * rows, 16)
        copies.append(pltpu.make_async_copy(piece, weight.at[pl.ds(start, rows)], sems.at[n]))
    for copy in copies:
        copy.start()
    for copy in copies:
        copy.wait()
    width = count * rows
    tile = next(size for size in (256, 320, 128) if width % size == 0)
    for c in range(width // tile):
        result = lax.dot_general(
            x_held[...],
            weight[c * tile : (c + 1) * tile],
            (((1,), (1,)), ((), ())),
            preferred_element_type=jnp.float32,
        )
        for n in range(blocks):
            outs[n][:, c * tile : (c + 1) * tile] = result[n * height : (n + 1) * height].astype(
                outs[n].dtype
            )


def output(xs, pieces, places, x_places):
    rows, depth = pieces[0].shape
    count, blocks, height = len(pieces), len(xs), xs[0].shape[0]
    return pl.pallas_call(
        functools.partial(output_kernel, count, blocks),
        grid_spec=pltpu.PrefetchScalarGridSpec(
            num_scalar_prefetch=2,
            grid=(),
            in_specs=[pl.BlockSpec(memory_space=pl.ANY)] * (blocks + count),
            out_specs=[pl.BlockSpec(memory_space=pltpu.VMEM)] * blocks,
            scratch_shapes=[
                pltpu.VMEM((blocks * height, depth), jnp.bfloat16),
                pltpu.VMEM((count * rows, depth), jnp.bfloat16),
                pltpu.SemaphoreType.DMA((blocks,)),
                pltpu.SemaphoreType.DMA((count,)),
            ],
        ),
        out_shape=[jax.ShapeDtypeStruct((height, count * rows), jnp.bfloat16)] * blocks,
        compiler_params=pltpu.CompilerParams(vmem_limit_bytes=VMEM_LIMIT),
        cost_estimate=pl.CostEstimate(
            flops=2 * blocks * height * count * rows * depth,
            bytes_accessed=2 * count * rows * depth,
            transcendentals=0,
        ),
        name="output",
    )(places, x_places, *xs, *pieces)


def attention_kernel(kv_local, count, samples, *refs):
    partials = [refs[h * count : (h + 1) * count] for h in range(kv_local)]
    refs = refs[kv_local * count :]
    cos_ref, sin_ref, lens_ref, k_ref, v_ref, out_ref, scores = refs
    together, length, _ = k_ref.shape
    scale = HEAD_SIZE ** (-0.5) * LOG2_E
    group = HEAD_GROUP * samples
    tile = 1024
    cosine, sine = cos_ref[...], sin_ref[...]
    lane = lax.broadcasted_iota(jnp.int32, (group, HEAD_SIZE), 1) % kv_local

    queries, owns, fresh = [], [], []
    for head_refs in partials:
        proj = head_refs[0][...].astype(jnp.float32)
        for ref in head_refs[1:]:
            proj = proj + ref[...].astype(jnp.float32)

        def head(index):
            vec = proj[:, index * HEAD_SIZE : (index + 1) * HEAD_SIZE]
            vec = vec * lax.rsqrt(jnp.mean(vec * vec, axis=-1, keepdims=True) + EPS)
            vec = vec * cosine + pltpu.roll(vec, HEAD_SIZE // 2, 1) * sine
            return vec.astype(jnp.bfloat16).astype(jnp.float32)

        new_key = head(HEAD_GROUP)
        new_value = proj[:, (HEAD_GROUP + 1) * HEAD_SIZE : (HEAD_GROUP + 2) * HEAD_SIZE]
        fresh.append(new_value.astype(jnp.bfloat16).astype(jnp.float32))
        queries.append([head(j) for j in range(HEAD_GROUP)])
        owns.append([jnp.sum(q * new_key, axis=-1, keepdims=True) for q in queries[-1]])

    results = []
    for u in range(together):
        rows = slice(u * samples, (u + 1) * samples)
        query = jnp.concatenate(
            [q[rows] for head_queries in queries for q in head_queries], axis=0
        ).astype(jnp.bfloat16)
        own = [jnp.concatenate([o[rows] for o in head_owns], axis=0) for head_owns in owns]
        lens = lens_ref[rows, 0:1] * kv_local
        most = jnp.full((group, HEAD_SIZE), MASKED, jnp.float32)
        for c in range(0, length, tile):
            part = lax.dot_general(
                query,
                k_ref[u, c : c + tile],
                (((1,), (1,)), ((), ())),
                preferred_element_type=jnp.float32,
            )
            for d in range(0, tile, HEAD_SIZE):
                dense = part[:group, d : d + HEAD_SIZE]
                for h in range(1, kv_local):
                    other = part[h * group : (h + 1) * group, d : d + HEAD_SIZE]
                    dense = jnp.where(lane == h, other, dense)
                slots = lax.broadcasted_iota(jnp.int32, (samples, HEAD_SIZE), 1) + (c + d)
                bias = jnp.where(slots < lens, 0.0, MASKED)
                dense = (dense.reshape(HEAD_GROUP, samples, HEAD_SIZE) + bias[None]).reshape(
                    group, HEAD_SIZE
                )
                scores[:, c + d : c + d + HEAD_SIZE] = dense
                most = jnp.maximum(most, dense)
        tops = [
            jnp.maximum(
                jnp.max(jnp.where(lane == h, most, MASKED), axis=-1, keepdims=True), own[h]
            )
            for h in range(kv_local)
        ]
        top = jnp.broadcast_to(tops[0], (group, HEAD_SIZE))
        for h in range(1, kv_local):
            top = jnp.where(lane == h, tops[h], top)
        sums = jnp.zeros((group, HEAD_SIZE), jnp.float32)
        mixed = jnp.zeros((kv_local * group, HEAD_SIZE), jnp.float32)
        for c in range(0, length, tile):
            weights = [[] for _ in range(kv_local)]
            for d in range(0, tile, HEAD_SIZE):
                expo = jnp.exp2((scores[:, c + d : c + d + HEAD_SIZE] - top) * scale)
                sums = sums + expo
                for h in range(kv_local):
                    kept = expo if kv_local == 1 else jnp.where(lane == h, expo, 0.0)
                    weights[h].append(kept.astype(jnp.bfloat16))
            weights = jnp.concatenate([jnp.concatenate(w, axis=1) for w in weights], axis=0)
            mixed = mixed + jnp.dot(
                weights, v_ref[u, c : c + tile], preferred_element_type=jnp.float32
            )
        line = []
        for h in range(kv_local):
            own_expo = jnp.exp2((own[h] - tops[h]) * scale)
            total = jnp.sum(jnp.where(lane == h, sums, 0.0), axis=-1, keepdims=True) + own_expo
            inverse = 1.0 / total
            own_weight = own_expo * inverse
            value = fresh[h][rows]
            for j in range(HEAD_GROUP):
                at = slice(j * samples, (j + 1) * samples)
                part = mixed[h * group + j * samples : h * group + (j + 1) * samples]
                line.append(part * inverse[at] + own_weight[at] * value)
        results.append(jnp.concatenate(line, axis=1))
    out_ref[...] = jnp.concatenate(results, axis=0).astype(out_ref.dtype)


def attention(partials, cosine, sine, lens, k_cache, value_cache, chunk, chunks):
    rows, width = partials[0][0].shape
    kv_local, count = len(partials), len(partials[0])
    prompts, length, _ = k_cache.shape
    samples = rows // prompts
    together = 16 // samples
    height = together * samples
    heads = kv_local * HEAD_GROUP
    steps = prompts // together // chunks
    first = chunk * steps
    small = pl.BlockSpec((height, HEAD_SIZE), lambda i: (i + first, 0))
    cache = pl.BlockSpec((together, length, HEAD_SIZE), lambda i: (i + first, 0, 0))
    return pl.pallas_call(
        functools.partial(attention_kernel, kv_local, count, samples),
        grid=(steps,),
        in_specs=[pl.BlockSpec((height, width), lambda i: (i + first, 0))] * (kv_local * count)
        + [small] * 3
        + [cache] * 2,
        out_specs=pl.BlockSpec((height, heads * HEAD_SIZE), lambda i: (i, 0)),
        out_shape=jax.ShapeDtypeStruct((rows // chunks, heads * HEAD_SIZE), jnp.bfloat16),
        scratch_shapes=[pltpu.VMEM((HEAD_GROUP * samples, length), jnp.float32)],
        compiler_params=pltpu.CompilerParams(vmem_limit_bytes=VMEM_LIMIT),
        cost_estimate=pl.CostEstimate(
            flops=4 * steps * together * heads * samples * length * HEAD_SIZE,
            bytes_accessed=4 * steps * together * length * HEAD_SIZE,
            transcendentals=steps * together * HEAD_GROUP * samples * length,
        ),
        name="attention",
    )(*[ref for head_refs in partials for ref in head_refs], cosine, sine, lens, k_cache, value_cache)


CHUNKS = 2


def laid(pieces, places):
    rows, width = pieces[0].shape
    whole = jnp.zeros((len(pieces) * rows, width), pieces[0].dtype)
    for piece, place in zip(pieces, places):
        whole = lax.dynamic_update_slice_in_dim(whole, piece, place * rows, 0)
    return whole


def local(hidden, query_key_value_weight, w_out, k_cache, value_cache, lengths, assign):
    tp_count = lax.axis_size("tp")
    grp_count = lax.axis_size("grp")
    ratio = grp_count // tp_count
    t = lax.axis_index("tp")
    plane = lax.axis_index("grp") // ratio
    core = lax.axis_index("grp") % ratio
    row_count, width = hidden.shape
    prompts, context, kv_local, _ = k_cache.shape
    shifts = range(tp_count)

    def to_rank(value, shift):
        if shift == 0:
            return value
        return lax.ppermute(value, "tp", [(i, i ^ shift) for i in range(tp_count)])

    def to_plane(value, shift):
        if shift == 0:
            return value
        pairs = [(i, ((i // ratio) ^ shift) * ratio + i % ratio) for i in range(grp_count)]
        return lax.ppermute(value, "grp", pairs)

    def to_core(value, turn):
        if turn == 0:
            return value
        pairs = [(i, i // ratio * ratio + (i + turn) % ratio) for i in range(grp_count)]
        return lax.ppermute(value, "grp", pairs)

    index = jnp.arange(row_count, dtype=jnp.int32)
    key = assign * row_count + index
    place = jnp.sum((key[None, :] < key[:, None]).astype(jnp.int32), axis=1)
    sort_rows = (place[None, :] == index[:, None]).astype(jnp.bfloat16)
    lens = jnp.sum(jnp.where(place[None, :] == index[:, None], lengths[None, :], 0), axis=1)
    cosine, sine = rotary_tables(lens)
    lens = jnp.broadcast_to(lens[:, None], (row_count, HEAD_SIZE))

    hidden = jnp.dot(sort_rows, hidden, preferred_element_type=jnp.float32).astype(jnp.bfloat16)
    full = [to_rank(hidden, shift) for shift in shifts]
    size = query_key_value_weight.shape[1] // tp_count
    weights = [
        to_rank(lax.dynamic_slice_in_dim(query_key_value_weight, (t ^ shift) * size, size, 1), shift)
        for shift in shifts
    ]
    values32 = jnp.stack(full).astype(jnp.float32)
    mean = jnp.sum(values32 * values32, axis=(0, 2), keepdims=True) / (tp_count * width)
    normed = (values32 * lax.rsqrt(mean + EPS)).astype(jnp.bfloat16)
    features = [
        to_plane(lax.dynamic_index_in_dim(normed, t ^ plane ^ shift, 0, keepdims=False), shift)
        for shift in shifts
    ]
    features, weights = lax.optimization_barrier((features, weights))
    places = jnp.stack(
        [(core - turn) % ratio * tp_count + (t ^ shift) for turn in range(ratio) for shift in shifts]
    ).astype(jnp.int32)
    pieces = [to_core(piece, turn) for turn in range(ratio) for piece in weights]
    if pieces[0].shape[0] % 16:
        pieces, places = [laid(pieces, places)], jnp.zeros((1,), jnp.int32)

    partials = []
    for h in range(kv_local):
        blocks = project(features, pieces, places, h * (size // kv_local), size // kv_local)
        partials.append([to_plane(block, shift) for shift, block in zip(shifts, blocks)])

    w_out, _ = lax.optimization_barrier((w_out, weights))
    depth = w_out.shape[0] // tp_count
    out_pieces = [
        to_rank(lax.dynamic_slice_in_dim(w_out, (t ^ shift) * depth, depth, 0).T, shift)
        for shift in shifts
    ]
    out_weight = laid(out_pieces, [t ^ shift for shift in shifts])
    partials, out_weight = lax.optimization_barrier((partials, out_weight))
    out_weights = [to_core(out_weight, turn) for turn in range(ratio)]
    out_places = jnp.stack([(core - turn) % ratio for turn in range(ratio)]).astype(jnp.int32)
    row_places = jnp.stack([plane ^ t ^ shift for shift in shifts]).astype(jnp.int32)

    keys = k_cache.reshape(prompts, context * kv_local, HEAD_SIZE)
    values = value_cache.reshape(prompts, context * kv_local, HEAD_SIZE)
    plane_pairs = [
        (g * tp_count + r, (r * ratio + g % ratio) * tp_count + g // ratio)
        for g in range(grp_count)
        for r in range(tp_count)
    ]
    results = []
    for chunk in range(CHUNKS):
        mixed = attention(partials, cosine, sine, lens, keys, values, chunk, CHUNKS)
        mixed = [to_plane(mixed, shift) for shift in shifts]
        blocks = output(mixed, out_weights, out_places, row_places)
        blocks = [to_rank(block, shift) for shift, block in zip(shifts, blocks)]
        summed = sum(block.astype(jnp.float32) for block in blocks).astype(jnp.bfloat16)
        results.append(lax.ppermute(summed, ("grp", "tp"), plane_pairs))
    result = jnp.concatenate(results, axis=0)
    return lax.dot_general(
        sort_rows, result, (((0,), (0,)), ((), ())), preferred_element_type=jnp.float32
    ).astype(jnp.bfloat16)


def solution(mesh):
    return jax.shard_map(
        local,
        mesh=mesh,
        in_specs=(
            P("grp", "tp"),
            P(("grp", "tp"), None),
            P(None, ("grp", "tp")),
            P("grp", None, "tp", None),
            P("grp", None, "tp", None),
            P("grp"),
            P("grp"),
        ),
        out_specs=P("grp", "tp"),
        check_vma=False,
    )
```

```python
import functools

import jax
import jax.numpy as jnp
from jax import lax
from jax.experimental import pallas as pl
from jax.experimental.pallas import tpu as pltpu
from jax.sharding import PartitionSpec as P

QUERY_HEADS = 64
KEY_VALUE_HEADS = 8
HEAD_SIZE = 128
HEAD_GROUP = QUERY_HEADS // KEY_VALUE_HEADS


EPS = 1e-06
ROPE_BASE = 1000000.0
LOG2_E = 1.4426950408889634
MASKED = -1e30
VMEM_LIMIT = 48 * 1024 * 1024


def rotary_tables(positions):
    half = HEAD_SIZE // 2
    freq = ROPE_BASE ** (-jnp.arange(half, dtype=jnp.float32) * 2.0 / HEAD_SIZE)
    angle = positions.astype(jnp.float32)[:, None] * freq[None, :]
    cosine, sine = (jnp.cos(angle), jnp.sin(angle))
    return jnp.concatenate([cosine, cosine], axis=1), jnp.concatenate([-sine, sine], axis=1)


def column_tile(width):
    return next(tile for tile in (512, 640, 256, 128) if width % tile == 0)


def project_kernel(count, blocks, place_ref, *refs):
    xs, pieces, outs = refs[:blocks], refs[blocks : blocks + count], refs[blocks + count : -2]
    weight, sems = refs[-2:]
    rows = pieces[0].shape[0]
    height, width = outs[0].shape
    tile = column_tile(width)
    copies = []
    for c in range(width // tile):
        for n, piece in enumerate(pieces):
            start = pl.multiple_of(place_ref[n] * rows, 16)
            copy = pltpu.make_async_copy(
                piece.at[:, pl.ds(c * tile, tile)],
                weight.at[pl.ds(start, rows), pl.ds(c * tile, tile)],
                sems.at[c, n],
            )
            copy.start()
            copies.append(copy)
    x = jnp.concatenate([ref[...] for ref in xs], axis=0)
    for c in range(width // tile):
        for copy in copies[c * count : (c + 1) * count]:
            copy.wait()
        lanes = slice(c * tile, (c + 1) * tile)
        result = jnp.dot(x, weight[:, lanes], preferred_element_type=jnp.float32)
        for n in range(blocks):
            outs[n][:, lanes] = result[n * height : (n + 1) * height].astype(outs[n].dtype)


def project(xs, pieces, places):
    rows, width = pieces[0].shape
    count, blocks, height = len(pieces), len(xs), xs[0].shape[0]
    tile = column_tile(width)
    return pl.pallas_call(
        functools.partial(project_kernel, count, blocks),
        grid_spec=pltpu.PrefetchScalarGridSpec(
            num_scalar_prefetch=1,
            grid=(),
            in_specs=[pl.BlockSpec(memory_space=pltpu.VMEM)] * blocks
            + [pl.BlockSpec(memory_space=pl.ANY)] * count,
            out_specs=[pl.BlockSpec(memory_space=pltpu.VMEM)] * blocks,
            scratch_shapes=[
                pltpu.VMEM((count * rows, width), jnp.bfloat16),
                pltpu.SemaphoreType.DMA((width // tile, count)),
            ],
        ),
        out_shape=[jax.ShapeDtypeStruct((height, width), jnp.bfloat16)] * blocks,
        compiler_params=pltpu.CompilerParams(vmem_limit_bytes=VMEM_LIMIT),
        cost_estimate=pl.CostEstimate(
            flops=2 * blocks * height * count * rows * width,
            bytes_accessed=2 * count * rows * width,
            transcendentals=0,
        ),
        name="project",
    )(places, *xs, *pieces)


def output_kernel(count, blocks, place_ref, x_place_ref, *refs):
    xs, pieces, outs = refs[:blocks], refs[blocks : blocks + count], refs[blocks + count : -4]
    x_held, weight, x_sems, sems = refs[-4:]
    rows = pieces[0].shape[0]
    height = xs[0].shape[0]
    copies = []
    for n, x in enumerate(xs):
        start = pl.multiple_of(x_place_ref[n] * height, 16)
        copies.append(pltpu.make_async_copy(x, x_held.at[pl.ds(start, height)], x_sems.at[n]))
    for n, piece in enumerate(pieces):
        start = pl.multiple_of(place_ref[n] * rows, 16)
        copies.append(pltpu.make_async_copy(piece, weight.at[pl.ds(start, rows)], sems.at[n]))
    for copy in copies:
        copy.start()
    for copy in copies:
        copy.wait()
    width = count * rows
    tile = next(size for size in (256, 320, 128) if width % size == 0)
    for c in range(width // tile):
        result = lax.dot_general(
            x_held[...],
            weight[c * tile : (c + 1) * tile],
            (((1,), (1,)), ((), ())),
            preferred_element_type=jnp.float32,
        )
        for n in range(blocks):
            outs[n][:, c * tile : (c + 1) * tile] = result[n * height : (n + 1) * height].astype(
                outs[n].dtype
            )


def output(xs, pieces, places, x_places):
    rows, depth = pieces[0].shape
    count, blocks, height = len(pieces), len(xs), xs[0].shape[0]
    return pl.pallas_call(
        functools.partial(output_kernel, count, blocks),
        grid_spec=pltpu.PrefetchScalarGridSpec(
            num_scalar_prefetch=2,
            grid=(),
            in_specs=[pl.BlockSpec(memory_space=pl.ANY)] * (blocks + count),
            out_specs=[pl.BlockSpec(memory_space=pltpu.VMEM)] * blocks,
            scratch_shapes=[
                pltpu.VMEM((blocks * height, depth), jnp.bfloat16),
                pltpu.VMEM((count * rows, depth), jnp.bfloat16),
                pltpu.SemaphoreType.DMA((blocks,)),
                pltpu.SemaphoreType.DMA((count,)),
            ],
        ),
        out_shape=[jax.ShapeDtypeStruct((height, count * rows), jnp.bfloat16)] * blocks,
        compiler_params=pltpu.CompilerParams(vmem_limit_bytes=VMEM_LIMIT),
        cost_estimate=pl.CostEstimate(
            flops=2 * blocks * height * count * rows * depth,
            bytes_accessed=2 * count * rows * depth,
            transcendentals=0,
        ),
        name="output",
    )(places, x_places, *xs, *pieces)


def attention_kernel(kv_local, count, samples, *refs):
    partials = [refs[h * count : (h + 1) * count] for h in range(kv_local)]
    refs = refs[kv_local * count :]
    cos_ref, sin_ref, lens_ref, k_ref, v_ref, out_ref, scores = refs
    together, length, _ = k_ref.shape
    scale = HEAD_SIZE ** (-0.5) * LOG2_E
    group = HEAD_GROUP * samples
    tile = 1024
    cosine, sine = cos_ref[...], sin_ref[...]
    lane = lax.broadcasted_iota(jnp.int32, (group, HEAD_SIZE), 1) % kv_local

    queries, owns, fresh = [], [], []
    for head_refs in partials:
        proj = head_refs[0][...].astype(jnp.float32)
        for ref in head_refs[1:]:
            proj = proj + ref[...].astype(jnp.float32)

        def head(index):
            vec = proj[:, index * HEAD_SIZE : (index + 1) * HEAD_SIZE]
            vec = vec * lax.rsqrt(jnp.mean(vec * vec, axis=-1, keepdims=True) + EPS)
            vec = vec * cosine + pltpu.roll(vec, HEAD_SIZE // 2, 1) * sine
            return vec.astype(jnp.bfloat16).astype(jnp.float32)

        new_key = head(HEAD_GROUP)
        new_value = proj[:, (HEAD_GROUP + 1) * HEAD_SIZE : (HEAD_GROUP + 2) * HEAD_SIZE]
        fresh.append(new_value.astype(jnp.bfloat16).astype(jnp.float32))
        queries.append([head(j) for j in range(HEAD_GROUP)])
        owns.append([jnp.sum(q * new_key, axis=-1, keepdims=True) for q in queries[-1]])

    results = []
    for u in range(together):
        rows = slice(u * samples, (u + 1) * samples)
        query = jnp.concatenate(
            [q[rows] for head_queries in queries for q in head_queries], axis=0
        ).astype(jnp.bfloat16)
        own = [jnp.concatenate([o[rows] for o in head_owns], axis=0) for head_owns in owns]
        lens = lens_ref[rows, 0:1] * kv_local
        most = jnp.full((group, HEAD_SIZE), MASKED, jnp.float32)
        for c in range(0, length, tile):
            part = lax.dot_general(
                query,
                k_ref[u, c : c + tile],
                (((1,), (1,)), ((), ())),
                preferred_element_type=jnp.float32,
            )
            for d in range(0, tile, HEAD_SIZE):
                dense = part[:group, d : d + HEAD_SIZE]
                for h in range(1, kv_local):
                    other = part[h * group : (h + 1) * group, d : d + HEAD_SIZE]
                    dense = jnp.where(lane == h, other, dense)
                slots = lax.broadcasted_iota(jnp.int32, (samples, HEAD_SIZE), 1) + (c + d)
                bias = jnp.where(slots < lens, 0.0, MASKED)
                dense = (dense.reshape(HEAD_GROUP, samples, HEAD_SIZE) + bias[None]).reshape(
                    group, HEAD_SIZE
                )
                scores[:, c + d : c + d + HEAD_SIZE] = dense
                most = jnp.maximum(most, dense)
        tops = [
            jnp.maximum(
                jnp.max(jnp.where(lane == h, most, MASKED), axis=-1, keepdims=True), own[h]
            )
            for h in range(kv_local)
        ]
        top = jnp.broadcast_to(tops[0], (group, HEAD_SIZE))
        for h in range(1, kv_local):
            top = jnp.where(lane == h, tops[h], top)
        sums = jnp.zeros((group, HEAD_SIZE), jnp.float32)
        mixed = jnp.zeros((kv_local * group, HEAD_SIZE), jnp.float32)
        for c in range(0, length, tile):
            weights = [[] for _ in range(kv_local)]
            for d in range(0, tile, HEAD_SIZE):
                expo = jnp.exp2((scores[:, c + d : c + d + HEAD_SIZE] - top) * scale)
                sums = sums + expo
                for h in range(kv_local):
                    kept = expo if kv_local == 1 else jnp.where(lane == h, expo, 0.0)
                    weights[h].append(kept.astype(jnp.bfloat16))
            weights = jnp.concatenate([jnp.concatenate(w, axis=1) for w in weights], axis=0)
            mixed = mixed + jnp.dot(
                weights, v_ref[u, c : c + tile], preferred_element_type=jnp.float32
            )
        line = []
        for h in range(kv_local):
            own_expo = jnp.exp2((own[h] - tops[h]) * scale)
            total = jnp.sum(jnp.where(lane == h, sums, 0.0), axis=-1, keepdims=True) + own_expo
            inverse = 1.0 / total
            own_weight = own_expo * inverse
            value = fresh[h][rows]
            for j in range(HEAD_GROUP):
                at = slice(j * samples, (j + 1) * samples)
                part = mixed[h * group + j * samples : h * group + (j + 1) * samples]
                line.append(part * inverse[at] + own_weight[at] * value)
        results.append(jnp.concatenate(line, axis=1))
    out_ref[...] = jnp.concatenate(results, axis=0).astype(out_ref.dtype)


def attention(partials, cosine, sine, lens, k_cache, value_cache, chunk, chunks):
    rows, width = partials[0][0].shape
    kv_local, count = len(partials), len(partials[0])
    prompts, length, _ = k_cache.shape
    samples = rows // prompts
    together = 16 // samples
    height = together * samples
    heads = kv_local * HEAD_GROUP
    steps = prompts // together // chunks
    first = chunk * steps
    small = pl.BlockSpec((height, HEAD_SIZE), lambda i: (i + first, 0))
    cache = pl.BlockSpec((together, length, HEAD_SIZE), lambda i: (i + first, 0, 0))
    return pl.pallas_call(
        functools.partial(attention_kernel, kv_local, count, samples),
        grid=(steps,),
        in_specs=[pl.BlockSpec((height, width), lambda i: (i + first, 0))] * (kv_local * count)
        + [small] * 3
        + [cache] * 2,
        out_specs=pl.BlockSpec((height, heads * HEAD_SIZE), lambda i: (i, 0)),
        out_shape=jax.ShapeDtypeStruct((rows // chunks, heads * HEAD_SIZE), jnp.bfloat16),
        scratch_shapes=[pltpu.VMEM((HEAD_GROUP * samples, length), jnp.float32)],
        compiler_params=pltpu.CompilerParams(vmem_limit_bytes=VMEM_LIMIT),
        cost_estimate=pl.CostEstimate(
            flops=4 * steps * together * heads * samples * length * HEAD_SIZE,
            bytes_accessed=4 * steps * together * length * HEAD_SIZE,
            transcendentals=steps * together * HEAD_GROUP * samples * length,
        ),
        name="attention",
    )(*[ref for head_refs in partials for ref in head_refs], cosine, sine, lens, k_cache, value_cache)


CHUNKS = 2


def after(value, *others):
    return lax.optimization_barrier((value, others))[0]


def placed(received, places, ratio, to_core):
    pieces = [to_core(piece, turn) for turn in range(ratio) for piece in received]
    rows, width = pieces[0].shape
    if rows % 16 == 0:
        return pieces, places
    whole = jnp.zeros((len(pieces) * rows, width), pieces[0].dtype)
    for n, piece in enumerate(pieces):
        whole = lax.dynamic_update_slice_in_dim(whole, piece, places[n] * rows, 0)
    return [whole], jnp.zeros((1,), jnp.int32)


def local(hidden, query_key_value_weight, w_out, k_cache, value_cache, lengths, assign):
    tp_count = lax.axis_size("tp")
    grp_count = lax.axis_size("grp")
    ratio = grp_count // tp_count
    t = lax.axis_index("tp")
    plane = lax.axis_index("grp") // ratio
    core = lax.axis_index("grp") % ratio
    row_count, width = hidden.shape
    prompts, context, kv_local, _ = k_cache.shape
    shifts = range(tp_count)

    def to_rank(value, shift):
        if shift == 0:
            return value
        return lax.ppermute(value, "tp", [(i, i ^ shift) for i in range(tp_count)])

    def to_plane(value, shift):
        if shift == 0:
            return value
        pairs = [(i, ((i // ratio) ^ shift) * ratio + i % ratio) for i in range(grp_count)]
        return lax.ppermute(value, "grp", pairs)

    def to_core(value, turn):
        if turn == 0:
            return value
        pairs = [(i, i // ratio * ratio + (i + turn) % ratio) for i in range(grp_count)]
        return lax.ppermute(value, "grp", pairs)

    index = jnp.arange(row_count, dtype=jnp.int32)
    key = assign * row_count + index
    place = jnp.sum((key[None, :] < key[:, None]).astype(jnp.int32), axis=1)
    sort_rows = (place[None, :] == index[:, None]).astype(jnp.bfloat16)
    lens = jnp.sum(jnp.where(place[None, :] == index[:, None], lengths[None, :], 0), axis=1)
    cosine, sine = rotary_tables(lens)
    lens = jnp.broadcast_to(lens[:, None], (row_count, HEAD_SIZE))

    hidden = jnp.dot(sort_rows, hidden, preferred_element_type=jnp.float32).astype(jnp.bfloat16)
    full = [to_rank(hidden, shift) for shift in shifts]
    values32 = jnp.stack(full).astype(jnp.float32)
    mean = jnp.sum(values32 * values32, axis=(0, 2), keepdims=True) / (tp_count * width)
    normed = (values32 * lax.rsqrt(mean + EPS)).astype(jnp.bfloat16)
    features = [
        to_plane(lax.dynamic_index_in_dim(normed, t ^ plane ^ shift, 0, keepdims=False), shift)
        for shift in shifts
    ]

    places = jnp.stack(
        [(core - turn) % ratio * tp_count + (t ^ shift) for turn in range(ratio) for shift in shifts]
    ).astype(jnp.int32)
    head_width = query_key_value_weight.shape[1] // (tp_count * kv_local)
    source, earlier = query_key_value_weight, features[:-1]
    partials = []
    for h in range(kv_local):
        received = [
            to_rank(
                lax.dynamic_slice_in_dim(
                    source, ((t ^ shift) * kv_local + h) * head_width, head_width, 1
                ),
                shift,
            )
            for shift in shifts
        ]
        received = after(received, earlier)
        source = after(query_key_value_weight, received)
        blocks = project(features, *placed(received, places, ratio, to_core))
        earlier = blocks
        partials.append([to_plane(block, shift) for shift, block in zip(shifts, blocks)])

    depth = w_out.shape[0] // tp_count
    source = after(w_out, earlier)
    out_received = [
        to_rank(lax.dynamic_slice_in_dim(source, (t ^ shift) * depth, depth, 0).T, shift)
        for shift in shifts
    ]
    row_places = jnp.stack([plane ^ t ^ shift for shift in shifts]).astype(jnp.int32)

    keys = k_cache.reshape(prompts, context * kv_local, HEAD_SIZE)
    values = value_cache.reshape(prompts, context * kv_local, HEAD_SIZE)
    plane_pairs = [
        (g * tp_count + r, (r * ratio + g % ratio) * tp_count + g // ratio)
        for g in range(grp_count)
        for r in range(tp_count)
    ]
    results = []
    for chunk in range(CHUNKS):
        mixed = attention(partials, cosine, sine, lens, keys, values, chunk, CHUNKS)
        if chunk == 0:
            out_weights, out_places = placed(after(out_received, mixed), places, ratio, to_core)
        mixed = [to_plane(mixed, shift) for shift in shifts]
        blocks = output(mixed, out_weights, out_places, row_places)
        blocks = [to_rank(block, shift) for shift, block in zip(shifts, blocks)]
        summed = sum(block.astype(jnp.float32) for block in blocks).astype(jnp.bfloat16)
        results.append(lax.ppermute(summed, ("grp", "tp"), plane_pairs))
    result = jnp.concatenate(results, axis=0)
    return lax.dot_general(
        sort_rows, result, (((0,), (0,)), ((), ())), preferred_element_type=jnp.float32
    ).astype(jnp.bfloat16)


def solution(mesh):
    return jax.shard_map(
        local,
        mesh=mesh,
        in_specs=(
            P("grp", "tp"),
            P(("grp", "tp"), None),
            P(None, ("grp", "tp")),
            P("grp", None, "tp", None),
            P("grp", None, "tp", None),
            P("grp"),
            P("grp"),
        ),
        out_specs=P("grp", "tp"),
        check_vma=False,
    )
```

```python
import functools

import jax
import jax.numpy as jnp
from jax import lax
from jax.experimental import pallas as pl
from jax.experimental.pallas import tpu as pltpu
from jax.sharding import PartitionSpec as P

QUERY_HEADS = 64
KEY_VALUE_HEADS = 8
HEAD_SIZE = 128
HEAD_GROUP = QUERY_HEADS // KEY_VALUE_HEADS


EPS = 1e-06
ROPE_BASE = 1000000.0
LOG2_E = 1.4426950408889634
MASKED = -1e30
VMEM_LIMIT = 48 * 1024 * 1024


def rotary_tables(positions):
    half = HEAD_SIZE // 2
    freq = ROPE_BASE ** (-jnp.arange(half, dtype=jnp.float32) * 2.0 / HEAD_SIZE)
    angle = positions.astype(jnp.float32)[:, None] * freq[None, :]
    cosine, sine = (jnp.cos(angle), jnp.sin(angle))
    return jnp.concatenate([cosine, cosine], axis=1), jnp.concatenate([-sine, sine], axis=1)


def column_tile(width):
    return next(tile for tile in (512, 640, 256, 128) if width % tile == 0)


def normalize_kernel(count, place_ref, *refs):
    xs, out_ref = refs[:count], refs[count]
    values = [ref[...].astype(jnp.float32) for ref in xs]
    total = sum(jnp.sum(value * value, axis=-1, keepdims=True) for value in values)
    factor = lax.rsqrt(total / (count * xs[0].shape[1]) + EPS)
    for n, value in enumerate(values):
        out_ref[place_ref[n]] = (value * factor).astype(out_ref.dtype)


def normalize(xs, places):
    count = len(xs)
    return pl.pallas_call(
        functools.partial(normalize_kernel, count),
        grid_spec=pltpu.PrefetchScalarGridSpec(
            num_scalar_prefetch=1,
            grid=(),
            in_specs=[pl.BlockSpec(memory_space=pltpu.VMEM)] * count,
            out_specs=pl.BlockSpec(memory_space=pltpu.VMEM),
        ),
        out_shape=jax.ShapeDtypeStruct((count,) + xs[0].shape, jnp.bfloat16),
        compiler_params=pltpu.CompilerParams(vmem_limit_bytes=VMEM_LIMIT),
        name="normalize",
    )(places, *xs)


def project_kernel(count, place_ref, x_ref, *refs):
    pieces, (out_ref, weight, sems) = refs[:count], refs[count:]
    rows, width = pieces[0].shape
    blocks, height, depth = x_ref.shape
    tile = column_tile(width)
    copies = []
    for c in range(width // tile):
        for n, piece in enumerate(pieces):
            start = pl.multiple_of(place_ref[n] * rows, 16)
            copy = pltpu.make_async_copy(
                piece.at[:, pl.ds(c * tile, tile)],
                weight.at[pl.ds(start, rows), pl.ds(c * tile, tile)],
                sems.at[c, n],
            )
            copy.start()
            copies.append(copy)
    x = x_ref[...].reshape(blocks * height, depth)
    for c in range(width // tile):
        for copy in copies[c * count : (c + 1) * count]:
            copy.wait()
        lanes = slice(c * tile, (c + 1) * tile)
        result = jnp.dot(x, weight[:, lanes], preferred_element_type=jnp.float32)
        out_ref[:, :, lanes] = result.reshape(blocks, height, tile).astype(out_ref.dtype)


def project(x, pieces, places):
    rows, width = pieces[0].shape
    count = len(pieces)
    blocks, height, _ = x.shape
    tile = column_tile(width)
    return pl.pallas_call(
        functools.partial(project_kernel, count),
        grid_spec=pltpu.PrefetchScalarGridSpec(
            num_scalar_prefetch=1,
            grid=(),
            in_specs=[pl.BlockSpec(memory_space=pltpu.VMEM)]
            + [pl.BlockSpec(memory_space=pl.ANY)] * count,
            out_specs=pl.BlockSpec(memory_space=pltpu.VMEM),
            scratch_shapes=[
                pltpu.VMEM((count * rows, width), jnp.bfloat16),
                pltpu.SemaphoreType.DMA((width // tile, count)),
            ],
        ),
        out_shape=jax.ShapeDtypeStruct((blocks, height, width), jnp.bfloat16),
        compiler_params=pltpu.CompilerParams(vmem_limit_bytes=VMEM_LIMIT),
        cost_estimate=pl.CostEstimate(
            flops=2 * blocks * height * count * rows * width,
            bytes_accessed=2 * count * rows * width,
            transcendentals=0,
        ),
        name="project",
    )(places, x, *pieces)


def output_kernel(count, blocks, place_ref, x_place_ref, *refs):
    xs, pieces, outs = refs[:blocks], refs[blocks : blocks + count], refs[blocks + count : -4]
    x_held, weight, x_sems, sems = refs[-4:]
    rows = pieces[0].shape[0]
    height = xs[0].shape[0]
    copies = []
    for n, x in enumerate(xs):
        start = pl.multiple_of(x_place_ref[n] * height, 16)
        copies.append(pltpu.make_async_copy(x, x_held.at[pl.ds(start, height)], x_sems.at[n]))
    for n, piece in enumerate(pieces):
        start = pl.multiple_of(place_ref[n] * rows, 16)
        copies.append(pltpu.make_async_copy(piece, weight.at[pl.ds(start, rows)], sems.at[n]))
    for copy in copies:
        copy.start()
    for copy in copies:
        copy.wait()
    width = count * rows
    tile = next(size for size in (256, 320, 128) if width % size == 0)
    for c in range(width // tile):
        result = lax.dot_general(
            x_held[...],
            weight[c * tile : (c + 1) * tile],
            (((1,), (1,)), ((), ())),
            preferred_element_type=jnp.float32,
        )
        for n in range(blocks):
            outs[n][:, c * tile : (c + 1) * tile] = result[n * height : (n + 1) * height].astype(
                outs[n].dtype
            )


def output(xs, pieces, places, x_places):
    rows, depth = pieces[0].shape
    count, blocks, height = len(pieces), len(xs), xs[0].shape[0]
    return pl.pallas_call(
        functools.partial(output_kernel, count, blocks),
        grid_spec=pltpu.PrefetchScalarGridSpec(
            num_scalar_prefetch=2,
            grid=(),
            in_specs=[pl.BlockSpec(memory_space=pl.ANY)] * (blocks + count),
            out_specs=[pl.BlockSpec(memory_space=pltpu.VMEM)] * blocks,
            scratch_shapes=[
                pltpu.VMEM((blocks * height, depth), jnp.bfloat16),
                pltpu.VMEM((count * rows, depth), jnp.bfloat16),
                pltpu.SemaphoreType.DMA((blocks,)),
                pltpu.SemaphoreType.DMA((count,)),
            ],
        ),
        out_shape=[jax.ShapeDtypeStruct((height, count * rows), jnp.bfloat16)] * blocks,
        compiler_params=pltpu.CompilerParams(vmem_limit_bytes=VMEM_LIMIT),
        cost_estimate=pl.CostEstimate(
            flops=2 * blocks * height * count * rows * depth,
            bytes_accessed=2 * count * rows * depth,
            transcendentals=0,
        ),
        name="output",
    )(places, x_places, *xs, *pieces)


def attention_kernel(kv_local, samples, *refs):
    partials, refs = refs[:kv_local], refs[kv_local:]
    cos_ref, sin_ref, lens_ref, k_ref, v_ref, out_ref, scores = refs
    together, length, _ = k_ref.shape
    scale = HEAD_SIZE ** (-0.5) * LOG2_E
    group = HEAD_GROUP * samples
    tile = 1024
    cosine, sine = cos_ref[...], sin_ref[...]
    lane = lax.broadcasted_iota(jnp.int32, (group, HEAD_SIZE), 1) % kv_local

    queries, owns, fresh = [], [], []
    for ref in partials:
        proj = ref[0].astype(jnp.float32)
        for n in range(1, ref.shape[0]):
            proj = proj + ref[n].astype(jnp.float32)

        def head(index):
            vec = proj[:, index * HEAD_SIZE : (index + 1) * HEAD_SIZE]
            vec = vec * lax.rsqrt(jnp.mean(vec * vec, axis=-1, keepdims=True) + EPS)
            vec = vec * cosine + pltpu.roll(vec, HEAD_SIZE // 2, 1) * sine
            return vec.astype(jnp.bfloat16).astype(jnp.float32)

        new_key = head(HEAD_GROUP)
        new_value = proj[:, (HEAD_GROUP + 1) * HEAD_SIZE : (HEAD_GROUP + 2) * HEAD_SIZE]
        fresh.append(new_value.astype(jnp.bfloat16).astype(jnp.float32))
        queries.append([head(j) for j in range(HEAD_GROUP)])
        owns.append([jnp.sum(q * new_key, axis=-1, keepdims=True) for q in queries[-1]])

    results = []
    for u in range(together):
        rows = slice(u * samples, (u + 1) * samples)
        query = jnp.concatenate(
            [q[rows] for head_queries in queries for q in head_queries], axis=0
        ).astype(jnp.bfloat16)
        own = [jnp.concatenate([o[rows] for o in head_owns], axis=0) for head_owns in owns]
        lens = lens_ref[rows, 0:1] * kv_local
        most = jnp.full((group, HEAD_SIZE), MASKED, jnp.float32)
        for c in range(0, length, tile):
            part = lax.dot_general(
                query,
                k_ref[u, c : c + tile],
                (((1,), (1,)), ((), ())),
                preferred_element_type=jnp.float32,
            )
            for d in range(0, tile, HEAD_SIZE):
                dense = part[:group, d : d + HEAD_SIZE]
                for h in range(1, kv_local):
                    other = part[h * group : (h + 1) * group, d : d + HEAD_SIZE]
                    dense = jnp.where(lane == h, other, dense)
                slots = lax.broadcasted_iota(jnp.int32, (samples, HEAD_SIZE), 1) + (c + d)
                bias = jnp.where(slots < lens, 0.0, MASKED)
                dense = (dense.reshape(HEAD_GROUP, samples, HEAD_SIZE) + bias[None]).reshape(
                    group, HEAD_SIZE
                )
                scores[:, c + d : c + d + HEAD_SIZE] = dense
                most = jnp.maximum(most, dense)
        tops = [
            jnp.maximum(
                jnp.max(jnp.where(lane == h, most, MASKED), axis=-1, keepdims=True), own[h]
            )
            for h in range(kv_local)
        ]
        top = jnp.broadcast_to(tops[0], (group, HEAD_SIZE))
        for h in range(1, kv_local):
            top = jnp.where(lane == h, tops[h], top)
        sums = jnp.zeros((group, HEAD_SIZE), jnp.float32)
        mixed = jnp.zeros((kv_local * group, HEAD_SIZE), jnp.float32)
        for c in range(0, length, tile):
            weights = [[] for _ in range(kv_local)]
            for d in range(0, tile, HEAD_SIZE):
                expo = jnp.exp2((scores[:, c + d : c + d + HEAD_SIZE] - top) * scale)
                sums = sums + expo
                for h in range(kv_local):
                    kept = expo if kv_local == 1 else jnp.where(lane == h, expo, 0.0)
                    weights[h].append(kept.astype(jnp.bfloat16))
            weights = jnp.concatenate([jnp.concatenate(w, axis=1) for w in weights], axis=0)
            mixed = mixed + jnp.dot(
                weights, v_ref[u, c : c + tile], preferred_element_type=jnp.float32
            )
        line = []
        for h in range(kv_local):
            own_expo = jnp.exp2((own[h] - tops[h]) * scale)
            total = jnp.sum(jnp.where(lane == h, sums, 0.0), axis=-1, keepdims=True) + own_expo
            inverse = 1.0 / total
            own_weight = own_expo * inverse
            value = fresh[h][rows]
            for j in range(HEAD_GROUP):
                at = slice(j * samples, (j + 1) * samples)
                part = mixed[h * group + j * samples : h * group + (j + 1) * samples]
                line.append(part * inverse[at] + own_weight[at] * value)
        results.append(jnp.concatenate(line, axis=1))
    out_ref[...] = jnp.concatenate(results, axis=0).astype(out_ref.dtype)


def attention(partials, cosine, sine, lens, k_cache, value_cache, chunk, chunks):
    count, rows, width = partials[0].shape
    kv_local = len(partials)
    prompts, length, _ = k_cache.shape
    samples = rows // prompts
    together = 16 // samples
    height = together * samples
    heads = kv_local * HEAD_GROUP
    steps = prompts // together // chunks
    first = chunk * steps
    small = pl.BlockSpec((height, HEAD_SIZE), lambda i: (i + first, 0))
    cache = pl.BlockSpec((together, length, HEAD_SIZE), lambda i: (i + first, 0, 0))
    return pl.pallas_call(
        functools.partial(attention_kernel, kv_local, samples),
        grid=(steps,),
        in_specs=[pl.BlockSpec((count, height, width), lambda i: (0, i + first, 0))] * kv_local
        + [small] * 3
        + [cache] * 2,
        out_specs=pl.BlockSpec((height, heads * HEAD_SIZE), lambda i: (i, 0)),
        out_shape=jax.ShapeDtypeStruct((rows // chunks, heads * HEAD_SIZE), jnp.bfloat16),
        scratch_shapes=[pltpu.VMEM((HEAD_GROUP * samples, length), jnp.float32)],
        compiler_params=pltpu.CompilerParams(vmem_limit_bytes=VMEM_LIMIT),
        cost_estimate=pl.CostEstimate(
            flops=4 * steps * together * heads * samples * length * HEAD_SIZE,
            bytes_accessed=4 * steps * together * length * HEAD_SIZE,
            transcendentals=steps * together * HEAD_GROUP * samples * length,
        ),
        name="attention",
    )(*partials, cosine, sine, lens, k_cache, value_cache)


CHUNKS = 2


def after(value, *others):
    return lax.optimization_barrier((value, others))[0]


def placed(received, places, ratio, to_core):
    pieces = [to_core(piece, turn) for turn in range(ratio) for piece in received]
    rows, width = pieces[0].shape
    if rows % 16 == 0:
        return pieces, places
    whole = jnp.zeros((len(pieces) * rows, width), pieces[0].dtype)
    for n, piece in enumerate(pieces):
        whole = lax.dynamic_update_slice_in_dim(whole, piece, places[n] * rows, 0)
    return [whole], jnp.zeros((1,), jnp.int32)


def local(hidden, query_key_value_weight, w_out, k_cache, value_cache, lengths, assign):
    tp_count = lax.axis_size("tp")
    grp_count = lax.axis_size("grp")
    ratio = grp_count // tp_count
    t = lax.axis_index("tp")
    plane = lax.axis_index("grp") // ratio
    core = lax.axis_index("grp") % ratio
    row_count, width = hidden.shape
    prompts, context, kv_local, _ = k_cache.shape
    shifts = range(tp_count)

    def to_rank(value, shift):
        if shift == 0:
            return value
        return lax.ppermute(value, "tp", [(i, i ^ shift) for i in range(tp_count)])

    def to_plane(value, shift):
        if shift == 0:
            return value
        pairs = [(i, ((i // ratio) ^ shift) * ratio + i % ratio) for i in range(grp_count)]
        return lax.ppermute(value, "grp", pairs)

    def to_core(value, turn):
        if turn == 0:
            return value
        pairs = [(i, i // ratio * ratio + (i + turn) % ratio) for i in range(grp_count)]
        return lax.ppermute(value, "grp", pairs)

    def between_planes(value):
        columns = [[p * ratio + b for p in range(tp_count)] for b in range(ratio)]
        return lax.all_to_all(
            value, "grp", split_axis=0, concat_axis=0, axis_index_groups=columns, tiled=True
        )

    index = jnp.arange(row_count, dtype=jnp.int32)
    key = assign * row_count + index
    place = jnp.sum((key[None, :] < key[:, None]).astype(jnp.int32), axis=1)
    sort_rows = (place[None, :] == index[:, None]).astype(jnp.bfloat16)
    lens = jnp.sum(jnp.where(place[None, :] == index[:, None], lengths[None, :], 0), axis=1)
    cosine, sine = rotary_tables(lens)
    lens = jnp.broadcast_to(lens[:, None], (row_count, HEAD_SIZE))

    hidden = jnp.dot(sort_rows, hidden, preferred_element_type=jnp.float32).astype(jnp.bfloat16)
    ranks = jnp.stack([t ^ shift for shift in shifts]).astype(jnp.int32)
    normed = normalize([to_rank(hidden, shift) for shift in shifts], ranks)
    features = between_planes(normed)

    places = jnp.stack(
        [(core - turn) % ratio * tp_count + (t ^ shift) for turn in range(ratio) for shift in shifts]
    ).astype(jnp.int32)
    head_width = query_key_value_weight.shape[1] // (tp_count * kv_local)
    source, earlier = query_key_value_weight, features
    partials = []
    for h in range(kv_local):
        own, *received = [
            to_rank(
                lax.dynamic_slice_in_dim(
                    source, ((t ^ shift) * kv_local + h) * head_width, head_width, 1
                ),
                shift,
            )
            for shift in shifts
        ]
        received = [own] + after(received, earlier)
        source = after(query_key_value_weight, normed)
        earlier = project(features, *placed(received, places, ratio, to_core))
        partials.append(between_planes(earlier))

    depth = w_out.shape[0] // tp_count
    source = after(w_out, earlier)
    out_received = [
        to_rank(lax.dynamic_slice_in_dim(source, (t ^ shift) * depth, depth, 0).T, shift)
        for shift in shifts
    ]
    row_places = jnp.stack([plane ^ t ^ shift for shift in shifts]).astype(jnp.int32)

    keys = k_cache.reshape(prompts, context * kv_local, HEAD_SIZE)
    values = value_cache.reshape(prompts, context * kv_local, HEAD_SIZE)
    plane_pairs = [
        (g * tp_count + r, (r * ratio + g % ratio) * tp_count + g // ratio)
        for g in range(grp_count)
        for r in range(tp_count)
    ]
    gathered = []
    for chunk in range(CHUNKS):
        if chunk == CHUNKS - 1:
            lens = after(lens, out_received)
        mixed = attention(partials, cosine, sine, lens, keys, values, chunk, CHUNKS)
        if chunk == CHUNKS - 1:
            out_weights, out_places = placed(after(out_received, mixed), places, ratio, to_core)
        gathered.append([to_plane(mixed, shift) for shift in shifts])
    results = []
    for mixed in gathered:
        blocks = output(mixed, out_weights, out_places, row_places)
        blocks = [to_rank(block, shift) for shift, block in zip(shifts, blocks)]
        summed = sum(block.astype(jnp.float32) for block in blocks).astype(jnp.bfloat16)
        results.append(lax.ppermute(summed, ("grp", "tp"), plane_pairs))
    result = jnp.concatenate(results, axis=0)
    return lax.dot_general(
        sort_rows, result, (((0,), (0,)), ((), ())), preferred_element_type=jnp.float32
    ).astype(jnp.bfloat16)


def solution(mesh):
    return jax.shard_map(
        local,
        mesh=mesh,
        in_specs=(
            P("grp", "tp"),
            P(("grp", "tp"), None),
            P(None, ("grp", "tp")),
            P("grp", None, "tp", None),
            P("grp", None, "tp", None),
            P("grp"),
            P("grp"),
        ),
        out_specs=P("grp", "tp"),
        check_vma=False,
    )
```

```python
import functools

import jax
import jax.numpy as jnp
from jax import lax
from jax.experimental import pallas as pl
from jax.experimental.pallas import tpu as pltpu
from jax.sharding import PartitionSpec as P

QUERY_HEADS = 64
KEY_VALUE_HEADS = 8
HEAD_SIZE = 128
HEAD_GROUP = QUERY_HEADS // KEY_VALUE_HEADS


EPS = 1e-06
ROPE_BASE = 1000000.0
LOG2_E = 1.4426950408889634
MASKED = -1e30
VMEM_LIMIT = 48 * 1024 * 1024


def rotary_tables(positions):
    half = HEAD_SIZE // 2
    freq = ROPE_BASE ** (-jnp.arange(half, dtype=jnp.float32) * 2.0 / HEAD_SIZE)
    angle = positions.astype(jnp.float32)[:, None] * freq[None, :]
    cosine, sine = (jnp.cos(angle), jnp.sin(angle))
    return jnp.concatenate([cosine, cosine], axis=1), jnp.concatenate([-sine, sine], axis=1)


def column_tile(width):
    return next(tile for tile in (512, 640, 256, 128) if width % tile == 0)


def normalize_kernel(count, place_ref, *refs):
    xs, outs, held = refs[:count], refs[count : 2 * count], refs[2 * count]
    values = [ref[...].astype(jnp.float32) for ref in xs]
    total = sum(jnp.sum(value * value, axis=-1, keepdims=True) for value in values)
    factor = lax.rsqrt(total / (count * xs[0].shape[1]) + EPS)
    for n, value in enumerate(values):
        held[place_ref[n]] = (value * factor).astype(held.dtype)
    for n, out_ref in enumerate(outs):
        out_ref[...] = held[n]


def normalize(xs, places):
    count = len(xs)
    return pl.pallas_call(
        functools.partial(normalize_kernel, count),
        grid_spec=pltpu.PrefetchScalarGridSpec(
            num_scalar_prefetch=1,
            grid=(),
            in_specs=[pl.BlockSpec(memory_space=pltpu.VMEM)] * count,
            out_specs=[pl.BlockSpec(memory_space=pltpu.VMEM)] * count,
            scratch_shapes=[pltpu.VMEM((count,) + xs[0].shape, jnp.bfloat16)],
        ),
        out_shape=[jax.ShapeDtypeStruct(xs[0].shape, jnp.bfloat16)] * count,
        compiler_params=pltpu.CompilerParams(vmem_limit_bytes=VMEM_LIMIT),
        name="normalize",
    )(places, *xs)


def lay_kernel(count, place_ref, *refs):
    pieces, (out_ref, sems) = refs[:count], refs[count:]
    rows = pieces[0].shape[0]
    copies = []
    for n, piece in enumerate(pieces):
        start = pl.multiple_of(place_ref[n] * rows, 16)
        copies.append(pltpu.make_async_copy(piece, out_ref.at[pl.ds(start, rows)], sems.at[n]))
    for copy in copies:
        copy.start()
    for copy in copies:
        copy.wait()


def lay(pieces, places):
    count = len(pieces)
    rows, width = pieces[0].shape
    if rows % 16:
        whole = jnp.zeros((count * rows, width), pieces[0].dtype)
        for n, piece in enumerate(pieces):
            whole = lax.dynamic_update_slice_in_dim(whole, piece, places[n] * rows, 0)
        return whole
    return pl.pallas_call(
        functools.partial(lay_kernel, count),
        grid_spec=pltpu.PrefetchScalarGridSpec(
            num_scalar_prefetch=1,
            grid=(),
            in_specs=[pl.BlockSpec(memory_space=pl.ANY)] * count,
            out_specs=pl.BlockSpec(memory_space=pl.ANY),
            scratch_shapes=[pltpu.SemaphoreType.DMA((count,))],
        ),
        out_shape=jax.ShapeDtypeStruct((count * rows, width), pieces[0].dtype),
        cost_estimate=pl.CostEstimate(
            flops=0, bytes_accessed=4 * count * rows * width, transcendentals=0
        ),
        name="lay",
    )(places, *pieces)


def project_kernel(count, blocks, place_ref, *refs):
    xs, pieces = refs[:blocks], refs[blocks : blocks + count]
    even_ref, odd_ref, weight, sems = refs[blocks + count :]
    rows, width = pieces[0].shape
    height = xs[0].shape[0]
    tile = column_tile(width)
    copies = []
    for c in range(width // tile):
        for n, piece in enumerate(pieces):
            start = pl.multiple_of(place_ref[n] * rows, 16)
            copy = pltpu.make_async_copy(
                piece.at[:, pl.ds(c * tile, tile)],
                weight.at[pl.ds(start, rows), pl.ds(c * tile, tile)],
                sems.at[c, n],
            )
            copy.start()
            copies.append(copy)
    x = jnp.concatenate([ref[...] for ref in xs], axis=0)
    for c in range(width // tile):
        for copy in copies[c * count : (c + 1) * count]:
            copy.wait()
        lanes = slice(c * tile, (c + 1) * tile)
        result = jnp.dot(x, weight[:, lanes], preferred_element_type=jnp.float32)
        result = result.astype(jnp.bfloat16)
        for n in range(blocks):
            out_ref = odd_ref if n % 2 else even_ref
            out_ref[n // 2, :, lanes] = result[n * height : (n + 1) * height]


def project(xs, pieces, places):
    rows, width = pieces[0].shape
    count, blocks, height = len(pieces), len(xs), xs[0].shape[0]
    tile = column_tile(width)
    return pl.pallas_call(
        functools.partial(project_kernel, count, blocks),
        grid_spec=pltpu.PrefetchScalarGridSpec(
            num_scalar_prefetch=1,
            grid=(),
            in_specs=[pl.BlockSpec(memory_space=pltpu.VMEM)] * blocks
            + [pl.BlockSpec(memory_space=pl.ANY)] * count,
            out_specs=[pl.BlockSpec(memory_space=pltpu.VMEM)] * 2,
            scratch_shapes=[
                pltpu.VMEM((count * rows, width), jnp.bfloat16),
                pltpu.SemaphoreType.DMA((width // tile, count)),
            ],
        ),
        out_shape=[jax.ShapeDtypeStruct((blocks // 2, height, width), jnp.bfloat16)] * 2,
        compiler_params=pltpu.CompilerParams(vmem_limit_bytes=VMEM_LIMIT),
        cost_estimate=pl.CostEstimate(
            flops=2 * blocks * height * count * rows * width,
            bytes_accessed=2 * count * rows * width,
            transcendentals=0,
        ),
        name="project",
    )(places, *xs, *pieces)


def output_kernel(count, blocks, place_ref, x_place_ref, *refs):
    xs, pieces, outs = refs[:blocks], refs[blocks : blocks + count], refs[blocks + count : -4]
    x_held, weight, x_sems, sems = refs[-4:]
    rows = pieces[0].shape[0]
    height = xs[0].shape[0]
    copies = []
    for n, x in enumerate(xs):
        start = pl.multiple_of(x_place_ref[n] * height, 16)
        copies.append(pltpu.make_async_copy(x, x_held.at[pl.ds(start, height)], x_sems.at[n]))
    for n, piece in enumerate(pieces):
        start = pl.multiple_of(place_ref[n] * rows, 16)
        copies.append(pltpu.make_async_copy(piece, weight.at[pl.ds(start, rows)], sems.at[n]))
    for copy in copies:
        copy.start()
    for copy in copies:
        copy.wait()
    width = count * rows
    tile = next(size for size in (256, 320, 128) if width % size == 0)
    for c in range(width // tile):
        result = lax.dot_general(
            x_held[...],
            weight[c * tile : (c + 1) * tile],
            (((1,), (1,)), ((), ())),
            preferred_element_type=jnp.float32,
        )
        for n in range(blocks):
            outs[n][:, c * tile : (c + 1) * tile] = result[n * height : (n + 1) * height].astype(
                outs[n].dtype
            )


def output(xs, pieces, places, x_places):
    rows, depth = pieces[0].shape
    count, blocks, height = len(pieces), len(xs), xs[0].shape[0]
    return pl.pallas_call(
        functools.partial(output_kernel, count, blocks),
        grid_spec=pltpu.PrefetchScalarGridSpec(
            num_scalar_prefetch=2,
            grid=(),
            in_specs=[pl.BlockSpec(memory_space=pl.ANY)] * (blocks + count),
            out_specs=[pl.BlockSpec(memory_space=pltpu.VMEM)] * blocks,
            scratch_shapes=[
                pltpu.VMEM((blocks * height, depth), jnp.bfloat16),
                pltpu.VMEM((count * rows, depth), jnp.bfloat16),
                pltpu.SemaphoreType.DMA((blocks,)),
                pltpu.SemaphoreType.DMA((count,)),
            ],
        ),
        out_shape=[jax.ShapeDtypeStruct((height, count * rows), jnp.bfloat16)] * blocks,
        compiler_params=pltpu.CompilerParams(vmem_limit_bytes=VMEM_LIMIT),
        cost_estimate=pl.CostEstimate(
            flops=2 * blocks * height * count * rows * depth,
            bytes_accessed=2 * count * rows * depth,
            transcendentals=0,
        ),
        name="output",
    )(places, x_places, *xs, *pieces)


def attention_kernel(kv_local, terms, samples, *refs):
    partials = [refs[h * terms : (h + 1) * terms] for h in range(kv_local)]
    refs = refs[kv_local * terms :]
    cos_ref, sin_ref, lens_ref, k_ref, v_ref, out_ref, scores = refs
    together, length, _ = k_ref.shape
    scale = HEAD_SIZE ** (-0.5) * LOG2_E
    group = HEAD_GROUP * samples
    tile = 1024
    cosine, sine = cos_ref[...], sin_ref[...]
    lane = lax.broadcasted_iota(jnp.int32, (group, HEAD_SIZE), 1) % kv_local

    queries, owns, fresh = [], [], []
    for term_refs in partials:
        proj = sum(ref[0].astype(jnp.float32) for ref in term_refs)

        def head(index):
            vec = proj[:, index * HEAD_SIZE : (index + 1) * HEAD_SIZE]
            vec = vec * lax.rsqrt(jnp.mean(vec * vec, axis=-1, keepdims=True) + EPS)
            vec = vec * cosine + pltpu.roll(vec, HEAD_SIZE // 2, 1) * sine
            return vec.astype(jnp.bfloat16).astype(jnp.float32)

        new_key = head(HEAD_GROUP)
        new_value = proj[:, (HEAD_GROUP + 1) * HEAD_SIZE : (HEAD_GROUP + 2) * HEAD_SIZE]
        fresh.append(new_value.astype(jnp.bfloat16).astype(jnp.float32))
        queries.append([head(j) for j in range(HEAD_GROUP)])
        owns.append([jnp.sum(q * new_key, axis=-1, keepdims=True) for q in queries[-1]])

    results = []
    for u in range(together):
        rows = slice(u * samples, (u + 1) * samples)
        query = jnp.concatenate(
            [q[rows] for head_queries in queries for q in head_queries], axis=0
        ).astype(jnp.bfloat16)
        own = [jnp.concatenate([o[rows] for o in head_owns], axis=0) for head_owns in owns]
        lens = lens_ref[rows, 0:1] * kv_local
        most = jnp.full((group, HEAD_SIZE), MASKED, jnp.float32)
        for c in range(0, length, tile):
            part = lax.dot_general(
                query,
                k_ref[u, c : c + tile],
                (((1,), (1,)), ((), ())),
                preferred_element_type=jnp.float32,
            )
            for d in range(0, tile, HEAD_SIZE):
                dense = part[:group, d : d + HEAD_SIZE]
                for h in range(1, kv_local):
                    other = part[h * group : (h + 1) * group, d : d + HEAD_SIZE]
                    dense = jnp.where(lane == h, other, dense)
                slots = lax.broadcasted_iota(jnp.int32, (samples, HEAD_SIZE), 1) + (c + d)
                bias = jnp.where(slots < lens, 0.0, MASKED)
                dense = (dense.reshape(HEAD_GROUP, samples, HEAD_SIZE) + bias[None]).reshape(
                    group, HEAD_SIZE
                )
                scores[:, c + d : c + d + HEAD_SIZE] = dense
                most = jnp.maximum(most, dense)
        tops = [
            jnp.maximum(
                jnp.max(jnp.where(lane == h, most, MASKED), axis=-1, keepdims=True), own[h]
            )
            for h in range(kv_local)
        ]
        top = jnp.broadcast_to(tops[0], (group, HEAD_SIZE))
        for h in range(1, kv_local):
            top = jnp.where(lane == h, tops[h], top)
        sums = jnp.zeros((group, HEAD_SIZE), jnp.float32)
        mixed = jnp.zeros((kv_local * group, HEAD_SIZE), jnp.float32)
        for c in range(0, length, tile):
            weights = [[] for _ in range(kv_local)]
            for d in range(0, tile, HEAD_SIZE):
                expo = jnp.exp2((scores[:, c + d : c + d + HEAD_SIZE] - top) * scale)
                sums = sums + expo
                for h in range(kv_local):
                    kept = expo if kv_local == 1 else jnp.where(lane == h, expo, 0.0)
                    weights[h].append(kept.astype(jnp.bfloat16))
            weights = jnp.concatenate([jnp.concatenate(w, axis=1) for w in weights], axis=0)
            mixed = mixed + jnp.dot(
                weights, v_ref[u, c : c + tile], preferred_element_type=jnp.float32
            )
        line = []
        for h in range(kv_local):
            own_expo = jnp.exp2((own[h] - tops[h]) * scale)
            total = jnp.sum(jnp.where(lane == h, sums, 0.0), axis=-1, keepdims=True) + own_expo
            inverse = 1.0 / total
            own_weight = own_expo * inverse
            value = fresh[h][rows]
            for j in range(HEAD_GROUP):
                at = slice(j * samples, (j + 1) * samples)
                part = mixed[h * group + j * samples : h * group + (j + 1) * samples]
                line.append(part * inverse[at] + own_weight[at] * value)
        results.append(jnp.concatenate(line, axis=1))
    out_ref[...] = jnp.concatenate(results, axis=0).astype(out_ref.dtype)


def attention(partials, cosine, sine, lens, k_cache, value_cache, chunk, chunks):
    _, rows, width = partials[0][0].shape
    kv_local, terms = len(partials), len(partials[0])
    prompts, length, _ = k_cache.shape
    samples = rows // prompts
    together = 16 // samples
    height = together * samples
    heads = kv_local * HEAD_GROUP
    steps = prompts // together // chunks
    first = chunk * steps
    small = pl.BlockSpec((height, HEAD_SIZE), lambda i: (i + first, 0))
    cache = pl.BlockSpec((together, length, HEAD_SIZE), lambda i: (i + first, 0, 0))
    return pl.pallas_call(
        functools.partial(attention_kernel, kv_local, terms, samples),
        grid=(steps,),
        in_specs=[pl.BlockSpec((1, height, width), lambda i: (0, i + first, 0))] * (kv_local * terms)
        + [small] * 3
        + [cache] * 2,
        out_specs=pl.BlockSpec((height, heads * HEAD_SIZE), lambda i: (i, 0)),
        out_shape=jax.ShapeDtypeStruct((rows // chunks, heads * HEAD_SIZE), jnp.bfloat16),
        scratch_shapes=[pltpu.VMEM((HEAD_GROUP * samples, length), jnp.float32)],
        compiler_params=pltpu.CompilerParams(vmem_limit_bytes=VMEM_LIMIT),
        cost_estimate=pl.CostEstimate(
            flops=4 * steps * together * heads * samples * length * HEAD_SIZE,
            bytes_accessed=4 * steps * together * length * HEAD_SIZE,
            transcendentals=steps * together * HEAD_GROUP * samples * length,
        ),
        name="attention",
    )(*[term for head_terms in partials for term in head_terms], cosine, sine, lens, k_cache, value_cache)


CHUNKS = 2


def after(value, *others):
    return lax.optimization_barrier((value, others))[0]


def local(hidden, query_key_value_weight, w_out, k_cache, value_cache, lengths, assign):
    tp_count = lax.axis_size("tp")
    grp_count = lax.axis_size("grp")
    ratio = grp_count // tp_count
    t = lax.axis_index("tp")
    plane = lax.axis_index("grp") // ratio
    core = lax.axis_index("grp") % ratio
    row_count, width = hidden.shape
    prompts, context, kv_local, _ = k_cache.shape
    shifts = range(tp_count)

    def to_rank(value, shift):
        if shift == 0:
            return value
        return lax.ppermute(value, "tp", [(i, i ^ shift) for i in range(tp_count)])

    def to_plane(value, shift):
        if shift == 0:
            return value
        pairs = [(i, ((i // ratio) ^ shift) * ratio + i % ratio) for i in range(grp_count)]
        return lax.ppermute(value, "grp", pairs)

    def to_core(value, turn):
        if turn == 0:
            return value
        pairs = [(i, i // ratio * ratio + (i + turn) % ratio) for i in range(grp_count)]
        return lax.ppermute(value, "grp", pairs)

    def sum_over_planes(even, odd):
        terms, shift = [(even, 1)], 1
        received = to_plane(odd, shift)
        while received.shape[0] > 1:
            terms.append((received, 1))
            passed = sum(term[step :: 2 * step].astype(jnp.float32) for term, step in terms)
            terms = [(term, 2 * step) for term, step in terms]
            shift *= 2
            received = to_plane(passed.astype(jnp.bfloat16), shift)
        return [term for term, _ in terms] + [received]

    index = jnp.arange(row_count, dtype=jnp.int32)
    key = assign * row_count + index
    place = jnp.sum((key[None, :] < key[:, None]).astype(jnp.int32), axis=1)
    sort_rows = (place[None, :] == index[:, None]).astype(jnp.bfloat16)
    lens = jnp.sum(jnp.where(place[None, :] == index[:, None], lengths[None, :], 0), axis=1)
    cosine, sine = rotary_tables(lens)
    lens = jnp.broadcast_to(lens[:, None], (row_count, HEAD_SIZE))

    hidden = jnp.dot(sort_rows, hidden, preferred_element_type=jnp.float32).astype(jnp.bfloat16)
    full = [to_rank(hidden, shift) for shift in shifts]
    ranks = jnp.stack([t ^ shift for shift in shifts]).astype(jnp.int32)
    owners = jnp.stack([(core - turn) % ratio for turn in range(ratio)]).astype(jnp.int32)
    row_places = jnp.stack([plane ^ t ^ shift for shift in shifts]).astype(jnp.int32)
    head_width = query_key_value_weight.shape[1] // (tp_count * kv_local)
    slices = [
        [
            lax.dynamic_slice_in_dim(
                query_key_value_weight, ((t ^ shift) * kv_local + h) * head_width, head_width, 1
            )
            for shift in shifts
        ]
        for h in range(kv_local)
    ]
    full = after(full, slices)
    normed = normalize(full, row_places)
    features = [to_plane(block, shift) for shift, block in zip(shifts, normed)]

    awaited = features
    partials = []
    for h in range(kv_local):
        sent = slices[h] if h == 0 else after(slices[h], received)
        received = after([to_rank(part, shift) for shift, part in zip(shifts, sent)], awaited)
        laid = lay(received, ranks)
        awaited = project(features, [to_core(laid, turn) for turn in range(ratio)], owners)
        partials.append(sum_over_planes(*awaited))

    depth = w_out.shape[0] // tp_count
    source = after(w_out, awaited)
    out_received = [
        to_rank(lax.dynamic_slice_in_dim(source, (t ^ shift) * depth, depth, 0).T, shift)
        for shift in shifts
    ]

    keys = k_cache.reshape(prompts, context * kv_local, HEAD_SIZE)
    values = value_cache.reshape(prompts, context * kv_local, HEAD_SIZE)
    plane_pairs = [
        (g * tp_count + r, (r * ratio + g % ratio) * tp_count + g // ratio)
        for g in range(grp_count)
        for r in range(tp_count)
    ]
    gathered = []
    for chunk in range(CHUNKS):
        if chunk > 0:
            lens = after(lens, mixed, out_received)
        mixed = attention(partials, cosine, sine, lens, keys, values, chunk, CHUNKS)
        gathered.append([to_plane(mixed, shift) for shift in shifts])
    laid = lay(after(out_received, mixed), ranks)
    out_weights = [to_core(laid, turn) for turn in range(ratio)]
    results = []
    for mixed in gathered:
        blocks = output(mixed, out_weights, owners, row_places)
        blocks = [to_rank(block, shift) for shift, block in zip(shifts, blocks)]
        summed = sum(block.astype(jnp.float32) for block in blocks).astype(jnp.bfloat16)
        results.append(lax.ppermute(summed, ("grp", "tp"), plane_pairs))
    result = jnp.concatenate(results, axis=0)
    return lax.dot_general(
        sort_rows, result, (((0,), (0,)), ((), ())), preferred_element_type=jnp.float32
    ).astype(jnp.bfloat16)


def solution(mesh):
    return jax.shard_map(
        local,
        mesh=mesh,
        in_specs=(
            P("grp", "tp"),
            P(("grp", "tp"), None),
            P(None, ("grp", "tp")),
            P("grp", None, "tp", None),
            P("grp", None, "tp", None),
            P("grp"),
            P("grp"),
        ),
        out_specs=P("grp", "tp"),
        check_vma=False,
    )
```

```python
import functools

import jax
import jax.numpy as jnp
from jax import lax
from jax.experimental import pallas as pl
from jax.experimental.pallas import tpu as pltpu
from jax.sharding import PartitionSpec as P

QUERY_HEADS = 64
KEY_VALUE_HEADS = 8
HEAD_SIZE = 128
HEAD_GROUP = QUERY_HEADS // KEY_VALUE_HEADS


EPS = 1e-06
ROPE_BASE = 1000000.0
LOG2_E = 1.4426950408889634
MASKED = -1e30
VMEM_LIMIT = 48 * 1024 * 1024


def rotary_tables(positions):
    half = HEAD_SIZE // 2
    freq = ROPE_BASE ** (-jnp.arange(half, dtype=jnp.float32) * 2.0 / HEAD_SIZE)
    angle = positions.astype(jnp.float32)[:, None] * freq[None, :]
    cosine, sine = (jnp.cos(angle), jnp.sin(angle))
    return jnp.concatenate([cosine, cosine], axis=1), jnp.concatenate([-sine, sine], axis=1)


def column_tile(width):
    return next(tile for tile in (512, 640, 256, 128) if width % tile == 0)


def normalize_kernel(count, place_ref, *refs):
    xs, outs, held = refs[:count], refs[count : 2 * count], refs[2 * count]
    values = [ref[...].astype(jnp.float32) for ref in xs]
    total = sum(jnp.sum(value * value, axis=-1, keepdims=True) for value in values)
    factor = lax.rsqrt(total / (count * xs[0].shape[1]) + EPS)
    for n, value in enumerate(values):
        held[place_ref[n]] = (value * factor).astype(held.dtype)
    for n, out_ref in enumerate(outs):
        out_ref[...] = held[n]


def normalize(xs, places):
    count = len(xs)
    return pl.pallas_call(
        functools.partial(normalize_kernel, count),
        grid_spec=pltpu.PrefetchScalarGridSpec(
            num_scalar_prefetch=1,
            grid=(),
            in_specs=[pl.BlockSpec(memory_space=pltpu.VMEM)] * count,
            out_specs=[pl.BlockSpec(memory_space=pltpu.VMEM)] * count,
            scratch_shapes=[pltpu.VMEM((count,) + xs[0].shape, jnp.bfloat16)],
        ),
        out_shape=[jax.ShapeDtypeStruct(xs[0].shape, jnp.bfloat16)] * count,
        compiler_params=pltpu.CompilerParams(vmem_limit_bytes=VMEM_LIMIT),
        name="normalize",
    )(places, *xs)


def lay_kernel(count, place_ref, *refs):
    pieces, (out_ref, sems) = refs[:count], refs[count:]
    rows = pieces[0].shape[0]
    copies = []
    for n, piece in enumerate(pieces):
        start = pl.multiple_of(place_ref[n] * rows, 16)
        copies.append(pltpu.make_async_copy(piece, out_ref.at[pl.ds(start, rows)], sems.at[n]))
    for copy in copies:
        copy.start()
    for copy in copies:
        copy.wait()


def lay(pieces, places):
    count = len(pieces)
    rows, width = pieces[0].shape
    if rows % 16:
        whole = jnp.zeros((count * rows, width), pieces[0].dtype)
        for n, piece in enumerate(pieces):
            whole = lax.dynamic_update_slice_in_dim(whole, piece, places[n] * rows, 0)
        return whole
    return pl.pallas_call(
        functools.partial(lay_kernel, count),
        grid_spec=pltpu.PrefetchScalarGridSpec(
            num_scalar_prefetch=1,
            grid=(),
            in_specs=[pl.BlockSpec(memory_space=pl.ANY)] * count,
            out_specs=pl.BlockSpec(memory_space=pltpu.VMEM),
            scratch_shapes=[pltpu.SemaphoreType.DMA((count,))],
        ),
        out_shape=jax.ShapeDtypeStruct((count * rows, width), pieces[0].dtype),
        compiler_params=pltpu.CompilerParams(vmem_limit_bytes=VMEM_LIMIT),
        cost_estimate=pl.CostEstimate(
            flops=0, bytes_accessed=4 * count * rows * width, transcendentals=0
        ),
        name="lay",
    )(places, *pieces)


def project_kernel(count, blocks, place_ref, *refs):
    xs, pieces = refs[:blocks], refs[blocks : blocks + count]
    even_ref, odd_ref, weight, sems = refs[blocks + count :]
    rows, width = pieces[0].shape
    height = xs[0].shape[0]
    tile = column_tile(width)
    copies = []
    for c in range(width // tile):
        for n, piece in enumerate(pieces):
            start = pl.multiple_of(place_ref[n] * rows, 16)
            copy = pltpu.make_async_copy(
                piece.at[:, pl.ds(c * tile, tile)],
                weight.at[pl.ds(start, rows), pl.ds(c * tile, tile)],
                sems.at[c, n],
            )
            copy.start()
            copies.append(copy)
    x = jnp.concatenate([ref[...] for ref in xs], axis=0)
    for c in range(width // tile):
        for copy in copies[c * count : (c + 1) * count]:
            copy.wait()
        lanes = slice(c * tile, (c + 1) * tile)
        result = jnp.dot(x, weight[:, lanes], preferred_element_type=jnp.float32)
        result = result.astype(jnp.bfloat16)
        for n in range(blocks):
            out_ref = odd_ref if n % 2 else even_ref
            out_ref[n // 2, :, lanes] = result[n * height : (n + 1) * height]


def project(xs, pieces, places):
    rows, width = pieces[0].shape
    count, blocks, height = len(pieces), len(xs), xs[0].shape[0]
    tile = column_tile(width)
    return pl.pallas_call(
        functools.partial(project_kernel, count, blocks),
        grid_spec=pltpu.PrefetchScalarGridSpec(
            num_scalar_prefetch=1,
            grid=(),
            in_specs=[pl.BlockSpec(memory_space=pltpu.VMEM)] * blocks
            + [pl.BlockSpec(memory_space=pl.ANY)] * count,
            out_specs=[pl.BlockSpec(memory_space=pltpu.VMEM)] * 2,
            scratch_shapes=[
                pltpu.VMEM((count * rows, width), jnp.bfloat16),
                pltpu.SemaphoreType.DMA((width // tile, count)),
            ],
        ),
        out_shape=[jax.ShapeDtypeStruct((blocks // 2, height, width), jnp.bfloat16)] * 2,
        compiler_params=pltpu.CompilerParams(vmem_limit_bytes=VMEM_LIMIT),
        cost_estimate=pl.CostEstimate(
            flops=2 * blocks * height * count * rows * width,
            bytes_accessed=2 * count * rows * width,
            transcendentals=0,
        ),
        name="project",
    )(places, *xs, *pieces)


def output_kernel(count, blocks, place_ref, x_place_ref, *refs):
    xs, pieces, outs = refs[:blocks], refs[blocks : blocks + count], refs[blocks + count : -4]
    x_held, weight, x_sems, sems = refs[-4:]
    rows = pieces[0].shape[0]
    height = xs[0].shape[0]
    copies = []
    for n, x in enumerate(xs):
        start = pl.multiple_of(x_place_ref[n] * height, 16)
        copies.append(pltpu.make_async_copy(x, x_held.at[pl.ds(start, height)], x_sems.at[n]))
    for n, piece in enumerate(pieces):
        start = pl.multiple_of(place_ref[n] * rows, 16)
        copies.append(pltpu.make_async_copy(piece, weight.at[pl.ds(start, rows)], sems.at[n]))
    for copy in copies:
        copy.start()
    for copy in copies:
        copy.wait()
    width = count * rows
    tile = next(size for size in (256, 320, 128) if width % size == 0)
    for c in range(width // tile):
        result = lax.dot_general(
            x_held[...],
            weight[c * tile : (c + 1) * tile],
            (((1,), (1,)), ((), ())),
            preferred_element_type=jnp.float32,
        )
        for n in range(blocks):
            outs[n][:, c * tile : (c + 1) * tile] = result[n * height : (n + 1) * height].astype(
                outs[n].dtype
            )


def output(xs, pieces, places, x_places):
    rows, depth = pieces[0].shape
    count, blocks, height = len(pieces), len(xs), xs[0].shape[0]
    return pl.pallas_call(
        functools.partial(output_kernel, count, blocks),
        grid_spec=pltpu.PrefetchScalarGridSpec(
            num_scalar_prefetch=2,
            grid=(),
            in_specs=[pl.BlockSpec(memory_space=pl.ANY)] * (blocks + count),
            out_specs=[pl.BlockSpec(memory_space=pltpu.VMEM)] * blocks,
            scratch_shapes=[
                pltpu.VMEM((blocks * height, depth), jnp.bfloat16),
                pltpu.VMEM((count * rows, depth), jnp.bfloat16),
                pltpu.SemaphoreType.DMA((blocks,)),
                pltpu.SemaphoreType.DMA((count,)),
            ],
        ),
        out_shape=[jax.ShapeDtypeStruct((height, count * rows), jnp.bfloat16)] * blocks,
        compiler_params=pltpu.CompilerParams(vmem_limit_bytes=VMEM_LIMIT),
        cost_estimate=pl.CostEstimate(
            flops=2 * blocks * height * count * rows * depth,
            bytes_accessed=2 * count * rows * depth,
            transcendentals=0,
        ),
        name="output",
    )(places, x_places, *xs, *pieces)


def attention_kernel(kv_local, terms, samples, *refs):
    partials = [refs[h * terms : (h + 1) * terms] for h in range(kv_local)]
    refs = refs[kv_local * terms :]
    cos_ref, sin_ref, lens_ref, k_ref, v_ref, out_ref, scores = refs
    together, length, _ = k_ref.shape
    scale = HEAD_SIZE ** (-0.5) * LOG2_E
    group = HEAD_GROUP * samples
    tile = 1024
    cosine, sine = cos_ref[...], sin_ref[...]
    lane = lax.broadcasted_iota(jnp.int32, (group, HEAD_SIZE), 1) % kv_local

    queries, owns, fresh = [], [], []
    for term_refs in partials:
        proj = sum(ref[0].astype(jnp.float32) for ref in term_refs)

        def head(index):
            vec = proj[:, index * HEAD_SIZE : (index + 1) * HEAD_SIZE]
            vec = vec * lax.rsqrt(jnp.mean(vec * vec, axis=-1, keepdims=True) + EPS)
            vec = vec * cosine + pltpu.roll(vec, HEAD_SIZE // 2, 1) * sine
            return vec.astype(jnp.bfloat16).astype(jnp.float32)

        new_key = head(HEAD_GROUP)
        new_value = proj[:, (HEAD_GROUP + 1) * HEAD_SIZE : (HEAD_GROUP + 2) * HEAD_SIZE]
        fresh.append(new_value.astype(jnp.bfloat16).astype(jnp.float32))
        queries.append([head(j) for j in range(HEAD_GROUP)])
        owns.append([jnp.sum(q * new_key, axis=-1, keepdims=True) for q in queries[-1]])

    results = []
    for u in range(together):
        rows = slice(u * samples, (u + 1) * samples)
        query = jnp.concatenate(
            [q[rows] for head_queries in queries for q in head_queries], axis=0
        ).astype(jnp.bfloat16)
        own = [jnp.concatenate([o[rows] for o in head_owns], axis=0) for head_owns in owns]
        lens = lens_ref[rows, 0:1] * kv_local
        most = jnp.full((group, HEAD_SIZE), MASKED, jnp.float32)
        for c in range(0, length, tile):
            part = lax.dot_general(
                query,
                k_ref[u, c : c + tile],
                (((1,), (1,)), ((), ())),
                preferred_element_type=jnp.float32,
            )
            for d in range(0, tile, HEAD_SIZE):
                dense = part[:group, d : d + HEAD_SIZE]
                for h in range(1, kv_local):
                    other = part[h * group : (h + 1) * group, d : d + HEAD_SIZE]
                    dense = jnp.where(lane == h, other, dense)
                slots = lax.broadcasted_iota(jnp.int32, (samples, HEAD_SIZE), 1) + (c + d)
                bias = jnp.where(slots < lens, 0.0, MASKED)
                dense = (dense.reshape(HEAD_GROUP, samples, HEAD_SIZE) + bias[None]).reshape(
                    group, HEAD_SIZE
                )
                scores[:, c + d : c + d + HEAD_SIZE] = dense
                most = jnp.maximum(most, dense)
        tops = [
            jnp.maximum(
                jnp.max(jnp.where(lane == h, most, MASKED), axis=-1, keepdims=True), own[h]
            )
            for h in range(kv_local)
        ]
        top = jnp.broadcast_to(tops[0], (group, HEAD_SIZE))
        for h in range(1, kv_local):
            top = jnp.where(lane == h, tops[h], top)
        sums = jnp.zeros((group, HEAD_SIZE), jnp.float32)
        mixed = jnp.zeros((kv_local * group, HEAD_SIZE), jnp.float32)
        for c in range(0, length, tile):
            weights = [[] for _ in range(kv_local)]
            for d in range(0, tile, HEAD_SIZE):
                expo = jnp.exp2((scores[:, c + d : c + d + HEAD_SIZE] - top) * scale)
                sums = sums + expo
                for h in range(kv_local):
                    kept = expo if kv_local == 1 else jnp.where(lane == h, expo, 0.0)
                    weights[h].append(kept.astype(jnp.bfloat16))
            weights = jnp.concatenate([jnp.concatenate(w, axis=1) for w in weights], axis=0)
            mixed = mixed + jnp.dot(
                weights, v_ref[u, c : c + tile], preferred_element_type=jnp.float32
            )
        line = []
        for h in range(kv_local):
            own_expo = jnp.exp2((own[h] - tops[h]) * scale)
            total = jnp.sum(jnp.where(lane == h, sums, 0.0), axis=-1, keepdims=True) + own_expo
            inverse = 1.0 / total
            own_weight = own_expo * inverse
            value = fresh[h][rows]
            for j in range(HEAD_GROUP):
                at = slice(j * samples, (j + 1) * samples)
                part = mixed[h * group + j * samples : h * group + (j + 1) * samples]
                line.append(part * inverse[at] + own_weight[at] * value)
        results.append(jnp.concatenate(line, axis=1))
    out_ref[...] = jnp.concatenate(results, axis=0).astype(out_ref.dtype)


def attention(partials, cosine, sine, lens, k_cache, value_cache, chunk, chunks):
    _, rows, width = partials[0][0].shape
    kv_local, terms = len(partials), len(partials[0])
    prompts, length, _ = k_cache.shape
    samples = rows // prompts
    together = 16 // samples
    height = together * samples
    heads = kv_local * HEAD_GROUP
    steps = prompts // together // chunks
    first = chunk * steps
    small = pl.BlockSpec((height, HEAD_SIZE), lambda i: (i + first, 0))
    cache = pl.BlockSpec((together, length, HEAD_SIZE), lambda i: (i + first, 0, 0))
    return pl.pallas_call(
        functools.partial(attention_kernel, kv_local, terms, samples),
        grid=(steps,),
        in_specs=[pl.BlockSpec((1, height, width), lambda i: (0, i + first, 0))] * (kv_local * terms)
        + [small] * 3
        + [cache] * 2,
        out_specs=pl.BlockSpec((height, heads * HEAD_SIZE), lambda i: (i, 0)),
        out_shape=jax.ShapeDtypeStruct((rows // chunks, heads * HEAD_SIZE), jnp.bfloat16),
        scratch_shapes=[pltpu.VMEM((HEAD_GROUP * samples, length), jnp.float32)],
        compiler_params=pltpu.CompilerParams(vmem_limit_bytes=VMEM_LIMIT),
        cost_estimate=pl.CostEstimate(
            flops=4 * steps * together * heads * samples * length * HEAD_SIZE,
            bytes_accessed=4 * steps * together * length * HEAD_SIZE,
            transcendentals=steps * together * HEAD_GROUP * samples * length,
        ),
        name="attention",
    )(*[term for head_terms in partials for term in head_terms], cosine, sine, lens, k_cache, value_cache)


CHUNKS = 2


def after(value, *others):
    return lax.optimization_barrier((value, others))[0]


def local(hidden, query_key_value_weight, w_out, k_cache, value_cache, lengths, assign):
    tp_count = lax.axis_size("tp")
    grp_count = lax.axis_size("grp")
    ratio = grp_count // tp_count
    t = lax.axis_index("tp")
    plane = lax.axis_index("grp") // ratio
    core = lax.axis_index("grp") % ratio
    row_count, width = hidden.shape
    prompts, context, kv_local, _ = k_cache.shape
    shifts = range(tp_count)

    def to_rank(value, shift):
        if shift == 0:
            return value
        return lax.ppermute(value, "tp", [(i, i ^ shift) for i in range(tp_count)])

    def to_plane(value, shift):
        if shift == 0:
            return value
        pairs = [(i, ((i // ratio) ^ shift) * ratio + i % ratio) for i in range(grp_count)]
        return lax.ppermute(value, "grp", pairs)

    def to_core(value, turn):
        if turn == 0:
            return value
        pairs = [(i, i // ratio * ratio + (i + turn) % ratio) for i in range(grp_count)]
        return lax.ppermute(value, "grp", pairs)

    def sum_over_planes(even, odd):
        terms, shift = [(even, 1)], 1
        received = to_plane(odd, shift)
        while received.shape[0] > 1:
            terms.append((received, 1))
            passed = sum(term[step :: 2 * step].astype(jnp.float32) for term, step in terms)
            terms = [(term, 2 * step) for term, step in terms]
            shift *= 2
            received = to_plane(passed.astype(jnp.bfloat16), shift)
        return [term for term, _ in terms] + [received]

    index = jnp.arange(row_count, dtype=jnp.int32)
    key = assign * row_count + index
    place = jnp.sum((key[None, :] < key[:, None]).astype(jnp.int32), axis=1)
    sort_rows = (place[None, :] == index[:, None]).astype(jnp.bfloat16)
    lens = jnp.sum(jnp.where(place[None, :] == index[:, None], lengths[None, :], 0), axis=1)
    cosine, sine = rotary_tables(lens)
    lens = jnp.broadcast_to(lens[:, None], (row_count, HEAD_SIZE))

    hidden = jnp.dot(sort_rows, hidden, preferred_element_type=jnp.float32).astype(jnp.bfloat16)
    full = [to_rank(hidden, shift) for shift in shifts]
    ranks = jnp.stack([t ^ shift for shift in shifts]).astype(jnp.int32)
    owners = jnp.stack([(core - turn) % ratio for turn in range(ratio)]).astype(jnp.int32)
    row_places = jnp.stack([plane ^ t ^ shift for shift in shifts]).astype(jnp.int32)
    head_width = query_key_value_weight.shape[1] // (tp_count * kv_local)
    slices = [
        [
            lax.dynamic_slice_in_dim(
                query_key_value_weight, ((t ^ shift) * kv_local + h) * head_width, head_width, 1
            )
            for shift in shifts
        ]
        for h in range(kv_local)
    ]
    full = after(full, slices)
    normed = normalize(full, row_places)
    features = [to_plane(block, shift) for shift, block in zip(shifts, normed)]

    awaited = features
    partials = []
    for h in range(kv_local):
        sent = slices[h] if h == 0 else after(slices[h], received)
        received = after([to_rank(part, shift) for shift, part in zip(shifts, sent)], awaited)
        laid = lay(received, ranks)
        partial = project(features, [to_core(laid, turn) for turn in range(ratio)], owners)
        awaited = sum_over_planes(*partial)
        partials.append(awaited)

    depth = w_out.shape[0] // tp_count
    source = after(w_out, partial)
    out_received = [
        to_rank(lax.dynamic_slice_in_dim(source, (t ^ shift) * depth, depth, 0).T, shift)
        for shift in shifts
    ]

    keys = k_cache.reshape(prompts, context * kv_local, HEAD_SIZE)
    values = value_cache.reshape(prompts, context * kv_local, HEAD_SIZE)
    plane_pairs = [
        (g * tp_count + r, (r * ratio + g % ratio) * tp_count + g // ratio)
        for g in range(grp_count)
        for r in range(tp_count)
    ]
    gathered = []
    for chunk in range(CHUNKS):
        if chunk > 0:
            lens = after(lens, mixed, out_received)
        mixed = attention(partials, cosine, sine, lens, keys, values, chunk, CHUNKS)
        gathered.append([to_plane(mixed, shift) for shift in shifts])
    laid = lay(after(out_received, mixed, gathered[:-1]), ranks)
    out_weights = [to_core(laid, turn) for turn in range(ratio)]
    results = []
    for mixed in gathered:
        blocks = output(mixed, out_weights, owners, row_places)
        blocks = [to_rank(block, shift) for shift, block in zip(shifts, blocks)]
        summed = sum(block.astype(jnp.float32) for block in blocks).astype(jnp.bfloat16)
        results.append(lax.ppermute(summed, ("grp", "tp"), plane_pairs))
    result = jnp.concatenate(results, axis=0)
    return lax.dot_general(
        sort_rows, result, (((0,), (0,)), ((), ())), preferred_element_type=jnp.float32
    ).astype(jnp.bfloat16)


def solution(mesh):
    return jax.shard_map(
        local,
        mesh=mesh,
        in_specs=(
            P("grp", "tp"),
            P(("grp", "tp"), None),
            P(None, ("grp", "tp")),
            P("grp", None, "tp", None),
            P("grp", None, "tp", None),
            P("grp"),
            P("grp"),
        ),
        out_specs=P("grp", "tp"),
        check_vma=False,
    )
```

```python
import functools

import jax
import jax.numpy as jnp
from jax import lax
from jax.experimental import pallas as pl
from jax.experimental.pallas import tpu as pltpu
from jax.sharding import PartitionSpec as P

QUERY_HEADS = 64
KEY_VALUE_HEADS = 8
HEAD_SIZE = 128
HEAD_GROUP = QUERY_HEADS // KEY_VALUE_HEADS


EPS = 1e-06
ROPE_BASE = 1000000.0
LOG2_E = 1.4426950408889634
MASKED = -1e30
MIB = 1024 * 1024


def rotary_tables(positions):
    half = HEAD_SIZE // 2
    freq = ROPE_BASE ** (-jnp.arange(half, dtype=jnp.float32) * 2.0 / HEAD_SIZE)
    angle = positions.astype(jnp.float32)[:, None] * freq[None, :]
    cosine, sine = (jnp.cos(angle), jnp.sin(angle))
    return jnp.concatenate([cosine, cosine], axis=1), jnp.concatenate([-sine, sine], axis=1)


def column_tile(width):
    return next(tile for tile in (512, 640, 256, 128) if width % tile == 0)


def normalize_kernel(count, place_ref, *refs):
    xs, outs, held = refs[:count], refs[count : 2 * count], refs[2 * count]
    values = [ref[...].astype(jnp.float32) for ref in xs]
    total = sum(jnp.sum(value * value, axis=-1, keepdims=True) for value in values)
    factor = lax.rsqrt(total / (count * xs[0].shape[1]) + EPS)
    for n, value in enumerate(values):
        held[place_ref[n]] = (value * factor).astype(held.dtype)
    for n, out_ref in enumerate(outs):
        out_ref[...] = held[n]


def normalize(xs, places):
    count = len(xs)
    return pl.pallas_call(
        functools.partial(normalize_kernel, count),
        grid_spec=pltpu.PrefetchScalarGridSpec(
            num_scalar_prefetch=1,
            grid=(),
            in_specs=[pl.BlockSpec(memory_space=pltpu.VMEM)] * count,
            out_specs=[pl.BlockSpec(memory_space=pltpu.VMEM)] * count,
            scratch_shapes=[pltpu.VMEM((count,) + xs[0].shape, jnp.bfloat16)],
        ),
        out_shape=[jax.ShapeDtypeStruct(xs[0].shape, jnp.bfloat16)] * count,
        compiler_params=pltpu.CompilerParams(vmem_limit_bytes=6 * MIB),
        name="normalize",
    )(places, *xs)


def lay_kernel(count, place_ref, *refs):
    pieces, (out_ref, sems) = refs[:count], refs[count:]
    rows = pieces[0].shape[0]
    copies = []
    for n, piece in enumerate(pieces):
        start = pl.multiple_of(place_ref[n] * rows, 16)
        copies.append(pltpu.make_async_copy(piece, out_ref.at[pl.ds(start, rows)], sems.at[n]))
    for copy in copies:
        copy.start()
    for copy in copies:
        copy.wait()


def lay(pieces, places):
    count = len(pieces)
    rows, width = pieces[0].shape
    if rows % 16:
        whole = jnp.zeros((count * rows, width), pieces[0].dtype)
        for n, piece in enumerate(pieces):
            whole = lax.dynamic_update_slice_in_dim(whole, piece, places[n] * rows, 0)
        return whole
    return pl.pallas_call(
        functools.partial(lay_kernel, count),
        grid_spec=pltpu.PrefetchScalarGridSpec(
            num_scalar_prefetch=1,
            grid=(),
            in_specs=[pl.BlockSpec(memory_space=pl.ANY)] * count,
            out_specs=pl.BlockSpec(memory_space=pltpu.VMEM),
            scratch_shapes=[pltpu.SemaphoreType.DMA((count,))],
        ),
        out_shape=jax.ShapeDtypeStruct((count * rows, width), pieces[0].dtype),
        compiler_params=pltpu.CompilerParams(vmem_limit_bytes=6 * MIB),
        cost_estimate=pl.CostEstimate(
            flops=0, bytes_accessed=4 * count * rows * width, transcendentals=0
        ),
        name="lay",
    )(places, *pieces)


def project_kernel(count, blocks, place_ref, *refs):
    xs, pieces, outs = refs[:blocks], refs[blocks : blocks + count], refs[blocks + count : -2]
    weight, sems = refs[-2:]
    rows = pieces[0].shape[0]
    height, width = outs[0].shape
    tile = column_tile(width)
    copies = []
    for c in range(width // tile):
        for n, piece in enumerate(pieces):
            start = pl.multiple_of(place_ref[n] * rows, 16)
            copy = pltpu.make_async_copy(
                piece.at[:, pl.ds(c * tile, tile)],
                weight.at[pl.ds(start, rows), pl.ds(c * tile, tile)],
                sems.at[c, n],
            )
            copy.start()
            copies.append(copy)
    x = jnp.concatenate([ref[...] for ref in xs], axis=0)
    for c in range(width // tile):
        for copy in copies[c * count : (c + 1) * count]:
            copy.wait()
        lanes = slice(c * tile, (c + 1) * tile)
        result = jnp.dot(x, weight[:, lanes], preferred_element_type=jnp.float32)
        for n in range(blocks):
            outs[n][:, lanes] = result[n * height : (n + 1) * height].astype(outs[n].dtype)


def project(xs, pieces, places):
    rows, width = pieces[0].shape
    count, blocks, height = len(pieces), len(xs), xs[0].shape[0]
    tile = column_tile(width)
    return pl.pallas_call(
        functools.partial(project_kernel, count, blocks),
        grid_spec=pltpu.PrefetchScalarGridSpec(
            num_scalar_prefetch=1,
            grid=(),
            in_specs=[pl.BlockSpec(memory_space=pltpu.VMEM)] * blocks
            + [pl.BlockSpec(memory_space=pl.ANY)] * count,
            out_specs=[pl.BlockSpec(memory_space=pltpu.VMEM)] * blocks,
            scratch_shapes=[
                pltpu.VMEM((count * rows, width), jnp.bfloat16),
                pltpu.SemaphoreType.DMA((width // tile, count)),
            ],
        ),
        out_shape=[jax.ShapeDtypeStruct((height, width), jnp.bfloat16)] * blocks,
        compiler_params=pltpu.CompilerParams(vmem_limit_bytes=12 * MIB),
        cost_estimate=pl.CostEstimate(
            flops=2 * blocks * height * count * rows * width,
            bytes_accessed=2 * count * rows * width,
            transcendentals=0,
        ),
        name="project",
    )(places, *xs, *pieces)


def output_kernel(count, blocks, place_ref, x_place_ref, *refs):
    xs, pieces, outs = refs[:blocks], refs[blocks : blocks + count], refs[blocks + count : -4]
    x_held, weight, x_sems, sems = refs[-4:]
    rows = pieces[0].shape[0]
    height = xs[0].shape[0]
    copies = []
    for n, x in enumerate(xs):
        start = pl.multiple_of(x_place_ref[n] * height, 16)
        copies.append(pltpu.make_async_copy(x, x_held.at[pl.ds(start, height)], x_sems.at[n]))
    for n, piece in enumerate(pieces):
        start = pl.multiple_of(place_ref[n] * rows, 16)
        copies.append(pltpu.make_async_copy(piece, weight.at[pl.ds(start, rows)], sems.at[n]))
    for copy in copies:
        copy.start()
    for copy in copies:
        copy.wait()
    width = count * rows
    tile = next(size for size in (256, 320, 128) if width % size == 0)
    for c in range(width // tile):
        result = lax.dot_general(
            x_held[...],
            weight[c * tile : (c + 1) * tile],
            (((1,), (1,)), ((), ())),
            preferred_element_type=jnp.float32,
        )
        for n in range(blocks):
            outs[n][:, c * tile : (c + 1) * tile] = result[n * height : (n + 1) * height].astype(
                outs[n].dtype
            )


def output(xs, pieces, places, x_places):
    rows, depth = pieces[0].shape
    count, blocks, height = len(pieces), len(xs), xs[0].shape[0]
    return pl.pallas_call(
        functools.partial(output_kernel, count, blocks),
        grid_spec=pltpu.PrefetchScalarGridSpec(
            num_scalar_prefetch=2,
            grid=(),
            in_specs=[pl.BlockSpec(memory_space=pl.ANY)] * (blocks + count),
            out_specs=[pl.BlockSpec(memory_space=pltpu.VMEM)] * blocks,
            scratch_shapes=[
                pltpu.VMEM((blocks * height, depth), jnp.bfloat16),
                pltpu.VMEM((count * rows, depth), jnp.bfloat16),
                pltpu.SemaphoreType.DMA((blocks,)),
                pltpu.SemaphoreType.DMA((count,)),
            ],
        ),
        out_shape=[jax.ShapeDtypeStruct((height, count * rows), jnp.bfloat16)] * blocks,
        compiler_params=pltpu.CompilerParams(vmem_limit_bytes=14 * MIB),
        cost_estimate=pl.CostEstimate(
            flops=2 * blocks * height * count * rows * depth,
            bytes_accessed=2 * count * rows * depth,
            transcendentals=0,
        ),
        name="output",
    )(places, x_places, *xs, *pieces)


def attention_kernel(kv_local, terms, samples, *refs):
    partials = [refs[h * terms : (h + 1) * terms] for h in range(kv_local)]
    refs = refs[kv_local * terms :]
    cos_ref, sin_ref, lens_ref, k_ref, v_ref, out_ref, scores = refs
    together, length, _ = k_ref.shape
    scale = HEAD_SIZE ** (-0.5) * LOG2_E
    group = HEAD_GROUP * samples
    tile = 1024
    cosine, sine = cos_ref[...], sin_ref[...]
    lane = lax.broadcasted_iota(jnp.int32, (group, HEAD_SIZE), 1) % kv_local

    queries, owns, fresh = [], [], []
    for term_refs in partials:
        proj = sum(ref[...].astype(jnp.float32) for ref in term_refs)

        def head(index):
            vec = proj[:, index * HEAD_SIZE : (index + 1) * HEAD_SIZE]
            vec = vec * lax.rsqrt(jnp.mean(vec * vec, axis=-1, keepdims=True) + EPS)
            vec = vec * cosine + pltpu.roll(vec, HEAD_SIZE // 2, 1) * sine
            return vec.astype(jnp.bfloat16).astype(jnp.float32)

        new_key = head(HEAD_GROUP)
        new_value = proj[:, (HEAD_GROUP + 1) * HEAD_SIZE : (HEAD_GROUP + 2) * HEAD_SIZE]
        fresh.append(new_value.astype(jnp.bfloat16).astype(jnp.float32))
        queries.append([head(j) for j in range(HEAD_GROUP)])
        owns.append([jnp.sum(q * new_key, axis=-1, keepdims=True) for q in queries[-1]])

    results = []
    for u in range(together):
        rows = slice(u * samples, (u + 1) * samples)
        query = jnp.concatenate(
            [q[rows] for head_queries in queries for q in head_queries], axis=0
        ).astype(jnp.bfloat16)
        own = [jnp.concatenate([o[rows] for o in head_owns], axis=0) for head_owns in owns]
        lens = lens_ref[rows, 0:1] * kv_local
        most = jnp.full((group, HEAD_SIZE), MASKED, jnp.float32)
        for c in range(0, length, tile):
            part = lax.dot_general(
                query,
                k_ref[u, c : c + tile],
                (((1,), (1,)), ((), ())),
                preferred_element_type=jnp.float32,
            )
            for d in range(0, tile, HEAD_SIZE):
                dense = part[:group, d : d + HEAD_SIZE]
                for h in range(1, kv_local):
                    other = part[h * group : (h + 1) * group, d : d + HEAD_SIZE]
                    dense = jnp.where(lane == h, other, dense)
                slots = lax.broadcasted_iota(jnp.int32, (samples, HEAD_SIZE), 1) + (c + d)
                bias = jnp.where(slots < lens, 0.0, MASKED)
                dense = (dense.reshape(HEAD_GROUP, samples, HEAD_SIZE) + bias[None]).reshape(
                    group, HEAD_SIZE
                )
                scores[:, c + d : c + d + HEAD_SIZE] = dense
                most = jnp.maximum(most, dense)
        tops = [
            jnp.maximum(
                jnp.max(jnp.where(lane == h, most, MASKED), axis=-1, keepdims=True), own[h]
            )
            for h in range(kv_local)
        ]
        top = jnp.broadcast_to(tops[0], (group, HEAD_SIZE))
        for h in range(1, kv_local):
            top = jnp.where(lane == h, tops[h], top)
        sums = jnp.zeros((group, HEAD_SIZE), jnp.float32)
        mixed = jnp.zeros((kv_local * group, HEAD_SIZE), jnp.float32)
        for c in range(0, length, tile):
            weights = [[] for _ in range(kv_local)]
            for d in range(0, tile, HEAD_SIZE):
                expo = jnp.exp2((scores[:, c + d : c + d + HEAD_SIZE] - top) * scale)
                sums = sums + expo
                for h in range(kv_local):
                    kept = expo if kv_local == 1 else jnp.where(lane == h, expo, 0.0)
                    weights[h].append(kept.astype(jnp.bfloat16))
            weights = jnp.concatenate([jnp.concatenate(w, axis=1) for w in weights], axis=0)
            mixed = mixed + jnp.dot(
                weights, v_ref[u, c : c + tile], preferred_element_type=jnp.float32
            )
        line = []
        for h in range(kv_local):
            own_expo = jnp.exp2((own[h] - tops[h]) * scale)
            total = jnp.sum(jnp.where(lane == h, sums, 0.0), axis=-1, keepdims=True) + own_expo
            inverse = 1.0 / total
            own_weight = own_expo * inverse
            value = fresh[h][rows]
            for j in range(HEAD_GROUP):
                at = slice(j * samples, (j + 1) * samples)
                part = mixed[h * group + j * samples : h * group + (j + 1) * samples]
                line.append(part * inverse[at] + own_weight[at] * value)
        results.append(jnp.concatenate(line, axis=1))
    out_ref[...] = jnp.concatenate(results, axis=0).astype(out_ref.dtype)


def attention(partials, cosine, sine, lens, k_cache, value_cache, chunk, chunks):
    rows, width = partials[0][0].shape
    kv_local, terms = len(partials), len(partials[0])
    prompts, length, _ = k_cache.shape
    samples = rows // prompts
    together = 16 // samples
    height = together * samples
    heads = kv_local * HEAD_GROUP
    steps = prompts // together // chunks
    first = chunk * steps
    small = pl.BlockSpec((height, HEAD_SIZE), lambda i: (i + first, 0))
    cache = pl.BlockSpec((together, length, HEAD_SIZE), lambda i: (i + first, 0, 0))
    return pl.pallas_call(
        functools.partial(attention_kernel, kv_local, terms, samples),
        grid=(steps,),
        in_specs=[pl.BlockSpec((height, width), lambda i: (i + first, 0))] * (kv_local * terms)
        + [small] * 3
        + [cache] * 2,
        out_specs=pl.BlockSpec((height, heads * HEAD_SIZE), lambda i: (i, 0)),
        out_shape=jax.ShapeDtypeStruct((rows // chunks, heads * HEAD_SIZE), jnp.bfloat16),
        scratch_shapes=[pltpu.VMEM((HEAD_GROUP * samples, length), jnp.float32)],
        compiler_params=pltpu.CompilerParams(vmem_limit_bytes=32 * MIB),
        cost_estimate=pl.CostEstimate(
            flops=4 * steps * together * heads * samples * length * HEAD_SIZE,
            bytes_accessed=4 * steps * together * length * HEAD_SIZE,
            transcendentals=steps * together * HEAD_GROUP * samples * length,
        ),
        name="attention",
    )(*[term for head_terms in partials for term in head_terms], cosine, sine, lens, k_cache, value_cache)


CHUNKS = 2


def after(value, *others):
    return lax.optimization_barrier((value, others))[0]


def local(hidden, query_key_value_weight, w_out, k_cache, value_cache, lengths, assign):
    tp_count = lax.axis_size("tp")
    grp_count = lax.axis_size("grp")
    ratio = grp_count // tp_count
    t = lax.axis_index("tp")
    plane = lax.axis_index("grp") // ratio
    core = lax.axis_index("grp") % ratio
    row_count, width = hidden.shape
    prompts, context, kv_local, _ = k_cache.shape
    shifts = range(tp_count)

    def to_rank(value, shift):
        if shift == 0:
            return value
        return lax.ppermute(value, "tp", [(i, i ^ shift) for i in range(tp_count)])

    def to_plane(value, shift):
        if shift == 0:
            return value
        pairs = [(i, ((i // ratio) ^ shift) * ratio + i % ratio) for i in range(grp_count)]
        return lax.ppermute(value, "grp", pairs)

    def to_core(value, turn):
        if turn == 0:
            return value
        pairs = [(i, i // ratio * ratio + (i + turn) % ratio) for i in range(grp_count)]
        return lax.ppermute(value, "grp", pairs)

    index = jnp.arange(row_count, dtype=jnp.int32)
    key = assign * row_count + index
    place = jnp.sum((key[None, :] < key[:, None]).astype(jnp.int32), axis=1)
    sort_rows = (place[None, :] == index[:, None]).astype(jnp.bfloat16)
    lens = jnp.sum(jnp.where(place[None, :] == index[:, None], lengths[None, :], 0), axis=1)
    cosine, sine = rotary_tables(lens)
    lens = jnp.broadcast_to(lens[:, None], (row_count, HEAD_SIZE))

    hidden = jnp.dot(sort_rows, hidden, preferred_element_type=jnp.float32).astype(jnp.bfloat16)
    full = [to_rank(hidden, shift) for shift in shifts]
    ranks = jnp.stack([t ^ shift for shift in shifts]).astype(jnp.int32)
    owners = jnp.stack([(core - turn) % ratio for turn in range(ratio)]).astype(jnp.int32)
    row_places = jnp.stack([plane ^ t ^ shift for shift in shifts]).astype(jnp.int32)
    head_width = query_key_value_weight.shape[1] // (tp_count * kv_local)
    slices = [
        [
            lax.dynamic_slice_in_dim(
                query_key_value_weight, ((t ^ shift) * kv_local + h) * head_width, head_width, 1
            )
            for shift in shifts
        ]
        for h in range(kv_local)
    ]
    full = after(full, slices)
    normed = normalize(full, row_places)
    features = [to_plane(block, shift) for shift, block in zip(shifts, normed)]

    def exchanged(parts):
        return [to_rank(part, shift) for shift, part in zip(shifts, parts)]

    received = after(exchanged(slices[0]), features)
    partials = []
    for h in range(kv_local):
        laid = lay(received, ranks)
        xs = features
        if h + 1 < kv_local:
            coming = exchanged(after(slices[h + 1], received))
            xs = after(features, coming[1:3])
        blocks = project(xs, [to_core(laid, turn) for turn in range(ratio)], owners)
        partials.append([to_plane(block, shift) for shift, block in zip(shifts, blocks)])
        if h + 1 < kv_local:
            received = after(coming, partials[h])

    depth = w_out.shape[0] // tp_count
    source = after(w_out, blocks)
    out_received = [
        to_rank(lax.dynamic_slice_in_dim(source, (t ^ shift) * depth, depth, 0).T, shift)
        for shift in shifts
    ]

    keys = k_cache.reshape(prompts, context * kv_local, HEAD_SIZE)
    values = value_cache.reshape(prompts, context * kv_local, HEAD_SIZE)
    plane_pairs = [
        (g * tp_count + r, (r * ratio + g % ratio) * tp_count + g // ratio)
        for g in range(grp_count)
        for r in range(tp_count)
    ]
    gathered = []
    for chunk in range(CHUNKS):
        if chunk > 0:
            lens = after(lens, mixed, out_received)
        mixed = attention(partials, cosine, sine, lens, keys, values, chunk, CHUNKS)
        gathered.append([to_plane(mixed, shift) for shift in shifts])
    laid = lay(after(out_received, mixed, gathered[:-1]), ranks)
    out_weights = [to_core(laid, turn) for turn in range(ratio)]
    results = []
    for mixed in gathered:
        blocks = output(mixed, out_weights, owners, row_places)
        blocks = [to_rank(block, shift) for shift, block in zip(shifts, blocks)]
        summed = sum(block.astype(jnp.float32) for block in blocks).astype(jnp.bfloat16)
        results.append(lax.ppermute(summed, ("grp", "tp"), plane_pairs))
    result = jnp.concatenate(results, axis=0)
    return lax.dot_general(
        sort_rows, result, (((0,), (0,)), ((), ())), preferred_element_type=jnp.float32
    ).astype(jnp.bfloat16)


def solution(mesh):
    return jax.shard_map(
        local,
        mesh=mesh,
        in_specs=(
            P("grp", "tp"),
            P(("grp", "tp"), None),
            P(None, ("grp", "tp")),
            P("grp", None, "tp", None),
            P("grp", None, "tp", None),
            P("grp"),
            P("grp"),
        ),
        out_specs=P("grp", "tp"),
        check_vma=False,
    )
```

```python
import functools

import jax
import jax.numpy as jnp
from jax import lax
from jax.experimental import pallas as pl
from jax.experimental.pallas import tpu as pltpu
from jax.sharding import PartitionSpec as P

QUERY_HEADS = 64
KEY_VALUE_HEADS = 8
HEAD_SIZE = 128
HEAD_GROUP = QUERY_HEADS // KEY_VALUE_HEADS


EPS = 1e-06
ROPE_BASE = 1000000.0
LOG2_E = 1.4426950408889634
MASKED = -1e30
MIB = 1024 * 1024


def rotary_tables(positions):
    half = HEAD_SIZE // 2
    freq = ROPE_BASE ** (-jnp.arange(half, dtype=jnp.float32) * 2.0 / HEAD_SIZE)
    angle = positions.astype(jnp.float32)[:, None] * freq[None, :]
    cosine, sine = (jnp.cos(angle), jnp.sin(angle))
    return jnp.concatenate([cosine, cosine], axis=1), jnp.concatenate([-sine, sine], axis=1)


def column_tile(width):
    return next(tile for tile in (512, 640, 256, 128) if width % tile == 0)


def normalize_kernel(count, place_ref, *refs):
    xs, outs, held = refs[:count], refs[count : 2 * count], refs[2 * count]
    values = [ref[...].astype(jnp.float32) for ref in xs]
    total = sum(jnp.sum(value * value, axis=-1, keepdims=True) for value in values)
    factor = lax.rsqrt(total / (count * xs[0].shape[1]) + EPS)
    for n, value in enumerate(values):
        held[place_ref[n]] = (value * factor).astype(held.dtype)
    for n, out_ref in enumerate(outs):
        out_ref[...] = held[n]


def normalize(xs, places):
    count = len(xs)
    return pl.pallas_call(
        functools.partial(normalize_kernel, count),
        grid_spec=pltpu.PrefetchScalarGridSpec(
            num_scalar_prefetch=1,
            grid=(),
            in_specs=[pl.BlockSpec(memory_space=pltpu.VMEM)] * count,
            out_specs=[pl.BlockSpec(memory_space=pltpu.VMEM)] * count,
            scratch_shapes=[pltpu.VMEM((count,) + xs[0].shape, jnp.bfloat16)],
        ),
        out_shape=[jax.ShapeDtypeStruct(xs[0].shape, jnp.bfloat16)] * count,
        compiler_params=pltpu.CompilerParams(vmem_limit_bytes=6 * MIB),
        name="normalize",
    )(places, *xs)


def lay_kernel(count, place_ref, *refs):
    pieces, (out_ref, sems) = refs[:count], refs[count:]
    rows = pieces[0].shape[0]
    copies = []
    for n, piece in enumerate(pieces):
        start = pl.multiple_of(place_ref[n] * rows, 16)
        copies.append(pltpu.make_async_copy(piece, out_ref.at[pl.ds(start, rows)], sems.at[n]))
    for copy in copies:
        copy.start()
    for copy in copies:
        copy.wait()


def lay(pieces, places):
    count = len(pieces)
    rows, width = pieces[0].shape
    if rows % 16:
        whole = jnp.zeros((count * rows, width), pieces[0].dtype)
        for n, piece in enumerate(pieces):
            whole = lax.dynamic_update_slice_in_dim(whole, piece, places[n] * rows, 0)
        return whole
    return pl.pallas_call(
        functools.partial(lay_kernel, count),
        grid_spec=pltpu.PrefetchScalarGridSpec(
            num_scalar_prefetch=1,
            grid=(),
            in_specs=[pl.BlockSpec(memory_space=pl.ANY)] * count,
            out_specs=pl.BlockSpec(memory_space=pltpu.VMEM),
            scratch_shapes=[pltpu.SemaphoreType.DMA((count,))],
        ),
        out_shape=jax.ShapeDtypeStruct((count * rows, width), pieces[0].dtype),
        compiler_params=pltpu.CompilerParams(vmem_limit_bytes=6 * MIB),
        cost_estimate=pl.CostEstimate(
            flops=0, bytes_accessed=4 * count * rows * width, transcendentals=0
        ),
        name="lay",
    )(places, *pieces)


def project_kernel(count, blocks, place_ref, *refs):
    xs, pieces, outs = refs[:blocks], refs[blocks : blocks + count], refs[blocks + count : -2]
    weight, sems = refs[-2:]
    rows = pieces[0].shape[0]
    height, width = outs[0].shape
    tile = column_tile(width)
    copies = []
    for c in range(width // tile):
        for n, piece in enumerate(pieces):
            start = pl.multiple_of(place_ref[n] * rows, 16)
            copy = pltpu.make_async_copy(
                piece.at[:, pl.ds(c * tile, tile)],
                weight.at[pl.ds(start, rows), pl.ds(c * tile, tile)],
                sems.at[c, n],
            )
            copy.start()
            copies.append(copy)
    x = jnp.concatenate([ref[...] for ref in xs], axis=0)
    for c in range(width // tile):
        for copy in copies[c * count : (c + 1) * count]:
            copy.wait()
        lanes = slice(c * tile, (c + 1) * tile)
        result = jnp.dot(x, weight[:, lanes], preferred_element_type=jnp.float32)
        for n in range(blocks):
            outs[n][:, lanes] = result[n * height : (n + 1) * height].astype(outs[n].dtype)


def project(xs, pieces, places):
    rows, width = pieces[0].shape
    count, blocks, height = len(pieces), len(xs), xs[0].shape[0]
    tile = column_tile(width)
    return pl.pallas_call(
        functools.partial(project_kernel, count, blocks),
        grid_spec=pltpu.PrefetchScalarGridSpec(
            num_scalar_prefetch=1,
            grid=(),
            in_specs=[pl.BlockSpec(memory_space=pltpu.VMEM)] * blocks
            + [pl.BlockSpec(memory_space=pl.ANY)] * count,
            out_specs=[pl.BlockSpec(memory_space=pltpu.VMEM)] * blocks,
            scratch_shapes=[
                pltpu.VMEM((count * rows, width), jnp.bfloat16),
                pltpu.SemaphoreType.DMA((width // tile, count)),
            ],
        ),
        out_shape=[jax.ShapeDtypeStruct((height, width), jnp.bfloat16)] * blocks,
        compiler_params=pltpu.CompilerParams(vmem_limit_bytes=12 * MIB),
        cost_estimate=pl.CostEstimate(
            flops=2 * blocks * height * count * rows * width,
            bytes_accessed=2 * count * rows * width,
            transcendentals=0,
        ),
        name="project",
    )(places, *xs, *pieces)


def output_kernel(count, blocks, place_ref, x_place_ref, *refs):
    xs, pieces, outs = refs[:blocks], refs[blocks : blocks + count], refs[blocks + count : -4]
    x_held, weight, x_sems, sems = refs[-4:]
    rows = pieces[0].shape[0]
    height = xs[0].shape[0]
    copies = []
    for n, x in enumerate(xs):
        start = pl.multiple_of(x_place_ref[n] * height, 16)
        copies.append(pltpu.make_async_copy(x, x_held.at[pl.ds(start, height)], x_sems.at[n]))
    for n, piece in enumerate(pieces):
        start = pl.multiple_of(place_ref[n] * rows, 16)
        copies.append(pltpu.make_async_copy(piece, weight.at[pl.ds(start, rows)], sems.at[n]))
    for copy in copies:
        copy.start()
    for copy in copies:
        copy.wait()
    width = count * rows
    tile = next(size for size in (256, 320, 128) if width % size == 0)
    for c in range(width // tile):
        result = lax.dot_general(
            x_held[...],
            weight[c * tile : (c + 1) * tile],
            (((1,), (1,)), ((), ())),
            preferred_element_type=jnp.float32,
        )
        for n in range(blocks):
            outs[n][:, c * tile : (c + 1) * tile] = result[n * height : (n + 1) * height].astype(
                outs[n].dtype
            )


def output(xs, pieces, places, x_places):
    rows, depth = pieces[0].shape
    count, blocks, height = len(pieces), len(xs), xs[0].shape[0]
    return pl.pallas_call(
        functools.partial(output_kernel, count, blocks),
        grid_spec=pltpu.PrefetchScalarGridSpec(
            num_scalar_prefetch=2,
            grid=(),
            in_specs=[pl.BlockSpec(memory_space=pl.ANY)] * (blocks + count),
            out_specs=[pl.BlockSpec(memory_space=pltpu.VMEM)] * blocks,
            scratch_shapes=[
                pltpu.VMEM((blocks * height, depth), jnp.bfloat16),
                pltpu.VMEM((count * rows, depth), jnp.bfloat16),
                pltpu.SemaphoreType.DMA((blocks,)),
                pltpu.SemaphoreType.DMA((count,)),
            ],
        ),
        out_shape=[jax.ShapeDtypeStruct((height, count * rows), jnp.bfloat16)] * blocks,
        compiler_params=pltpu.CompilerParams(vmem_limit_bytes=14 * MIB),
        cost_estimate=pl.CostEstimate(
            flops=2 * blocks * height * count * rows * depth,
            bytes_accessed=2 * count * rows * depth,
            transcendentals=0,
        ),
        name="output",
    )(places, x_places, *xs, *pieces)


def attention_kernel(kv_local, terms, samples, *refs):
    partials = [refs[h * terms : (h + 1) * terms] for h in range(kv_local)]
    refs = refs[kv_local * terms :]
    cos_ref, sin_ref, lens_ref, k_ref, v_ref, out_ref, scores = refs
    together, length, _ = k_ref.shape
    scale = HEAD_SIZE ** (-0.5) * LOG2_E
    group = HEAD_GROUP * samples
    tile = 1024
    cosine, sine = cos_ref[...], sin_ref[...]
    lane = lax.broadcasted_iota(jnp.int32, (group, HEAD_SIZE), 1) % kv_local

    queries, owns, fresh = [], [], []
    for term_refs in partials:
        proj = sum(ref[...].astype(jnp.float32) for ref in term_refs)

        def head(index):
            vec = proj[:, index * HEAD_SIZE : (index + 1) * HEAD_SIZE]
            vec = vec * lax.rsqrt(jnp.mean(vec * vec, axis=-1, keepdims=True) + EPS)
            vec = vec * cosine + pltpu.roll(vec, HEAD_SIZE // 2, 1) * sine
            return vec.astype(jnp.bfloat16).astype(jnp.float32)

        new_key = head(HEAD_GROUP)
        new_value = proj[:, (HEAD_GROUP + 1) * HEAD_SIZE : (HEAD_GROUP + 2) * HEAD_SIZE]
        fresh.append(new_value.astype(jnp.bfloat16).astype(jnp.float32))
        queries.append([head(j) for j in range(HEAD_GROUP)])
        owns.append([jnp.sum(q * new_key, axis=-1, keepdims=True) for q in queries[-1]])

    results = []
    for u in range(together):
        rows = slice(u * samples, (u + 1) * samples)
        query = jnp.concatenate(
            [q[rows] for head_queries in queries for q in head_queries], axis=0
        ).astype(jnp.bfloat16)
        own = [jnp.concatenate([o[rows] for o in head_owns], axis=0) for head_owns in owns]
        lens = lens_ref[rows, 0:1] * kv_local
        most = jnp.full((group, HEAD_SIZE), MASKED, jnp.float32)
        for c in range(0, length, tile):
            part = lax.dot_general(
                query,
                k_ref[u, c : c + tile],
                (((1,), (1,)), ((), ())),
                preferred_element_type=jnp.float32,
            )
            for d in range(0, tile, HEAD_SIZE):
                dense = part[:group, d : d + HEAD_SIZE]
                for h in range(1, kv_local):
                    other = part[h * group : (h + 1) * group, d : d + HEAD_SIZE]
                    dense = jnp.where(lane == h, other, dense)
                slots = lax.broadcasted_iota(jnp.int32, (samples, HEAD_SIZE), 1) + (c + d)
                bias = jnp.where(slots < lens, 0.0, MASKED)
                dense = (dense.reshape(HEAD_GROUP, samples, HEAD_SIZE) + bias[None]).reshape(
                    group, HEAD_SIZE
                )
                scores[:, c + d : c + d + HEAD_SIZE] = dense
                most = jnp.maximum(most, dense)
        tops = [
            jnp.maximum(
                jnp.max(jnp.where(lane == h, most, MASKED), axis=-1, keepdims=True), own[h]
            )
            for h in range(kv_local)
        ]
        top = jnp.broadcast_to(tops[0], (group, HEAD_SIZE))
        for h in range(1, kv_local):
            top = jnp.where(lane == h, tops[h], top)
        sums = jnp.zeros((group, HEAD_SIZE), jnp.float32)
        mixed = jnp.zeros((kv_local * group, HEAD_SIZE), jnp.float32)
        for c in range(0, length, tile):
            weights = [[] for _ in range(kv_local)]
            for d in range(0, tile, HEAD_SIZE):
                expo = jnp.exp2((scores[:, c + d : c + d + HEAD_SIZE] - top) * scale)
                sums = sums + expo
                for h in range(kv_local):
                    kept = expo if kv_local == 1 else jnp.where(lane == h, expo, 0.0)
                    weights[h].append(kept.astype(jnp.bfloat16))
            weights = jnp.concatenate([jnp.concatenate(w, axis=1) for w in weights], axis=0)
            mixed = mixed + jnp.dot(
                weights, v_ref[u, c : c + tile], preferred_element_type=jnp.float32
            )
        line = []
        for h in range(kv_local):
            own_expo = jnp.exp2((own[h] - tops[h]) * scale)
            total = jnp.sum(jnp.where(lane == h, sums, 0.0), axis=-1, keepdims=True) + own_expo
            inverse = 1.0 / total
            own_weight = own_expo * inverse
            value = fresh[h][rows]
            for j in range(HEAD_GROUP):
                at = slice(j * samples, (j + 1) * samples)
                part = mixed[h * group + j * samples : h * group + (j + 1) * samples]
                line.append(part * inverse[at] + own_weight[at] * value)
        results.append(jnp.concatenate(line, axis=1))
    out_ref[...] = jnp.concatenate(results, axis=0).astype(out_ref.dtype)


def attention(partials, cosine, sine, lens, k_cache, value_cache, chunk, chunks):
    rows, width = partials[0][0].shape
    kv_local, terms = len(partials), len(partials[0])
    prompts, length, _ = k_cache.shape
    samples = rows // prompts
    together = 16 // samples
    height = together * samples
    heads = kv_local * HEAD_GROUP
    steps = prompts // together // chunks
    first = chunk * steps
    small = pl.BlockSpec((height, HEAD_SIZE), lambda i: (i + first, 0))
    cache = pl.BlockSpec((together, length, HEAD_SIZE), lambda i: (i + first, 0, 0))
    return pl.pallas_call(
        functools.partial(attention_kernel, kv_local, terms, samples),
        grid=(steps,),
        in_specs=[pl.BlockSpec((height, width), lambda i: (i + first, 0))] * (kv_local * terms)
        + [small] * 3
        + [cache] * 2,
        out_specs=pl.BlockSpec((height, heads * HEAD_SIZE), lambda i: (i, 0)),
        out_shape=jax.ShapeDtypeStruct((rows // chunks, heads * HEAD_SIZE), jnp.bfloat16),
        scratch_shapes=[pltpu.VMEM((HEAD_GROUP * samples, length), jnp.float32)],
        compiler_params=pltpu.CompilerParams(vmem_limit_bytes=52 * MIB),
        cost_estimate=pl.CostEstimate(
            flops=4 * steps * together * heads * samples * length * HEAD_SIZE,
            bytes_accessed=4 * steps * together * length * HEAD_SIZE,
            transcendentals=steps * together * HEAD_GROUP * samples * length,
        ),
        name="attention",
    )(*[term for head_terms in partials for term in head_terms], cosine, sine, lens, k_cache, value_cache)


CHUNKS = 2


def after(value, *others):
    return lax.optimization_barrier((value, others))[0]


def local(hidden, query_key_value_weight, w_out, k_cache, value_cache, lengths, assign):
    tp_count = lax.axis_size("tp")
    grp_count = lax.axis_size("grp")
    ratio = grp_count // tp_count
    t = lax.axis_index("tp")
    plane = lax.axis_index("grp") // ratio
    core = lax.axis_index("grp") % ratio
    row_count, width = hidden.shape
    prompts, context, kv_local, _ = k_cache.shape
    shifts = range(tp_count)

    def to_rank(value, shift):
        if shift == 0:
            return value
        return lax.ppermute(value, "tp", [(i, i ^ shift) for i in range(tp_count)])

    def to_plane(value, shift):
        if shift == 0:
            return value
        pairs = [(i, ((i // ratio) ^ shift) * ratio + i % ratio) for i in range(grp_count)]
        return lax.ppermute(value, "grp", pairs)

    def to_core(value, turn):
        if turn == 0:
            return value
        pairs = [(i, i // ratio * ratio + (i + turn) % ratio) for i in range(grp_count)]
        return lax.ppermute(value, "grp", pairs)

    index = jnp.arange(row_count, dtype=jnp.int32)
    key = assign * row_count + index
    place = jnp.sum((key[None, :] < key[:, None]).astype(jnp.int32), axis=1)
    sort_rows = (place[None, :] == index[:, None]).astype(jnp.bfloat16)
    lens = jnp.sum(jnp.where(place[None, :] == index[:, None], lengths[None, :], 0), axis=1)
    cosine, sine = rotary_tables(lens)
    lens = jnp.broadcast_to(lens[:, None], (row_count, HEAD_SIZE))

    hidden = jnp.dot(sort_rows, hidden, preferred_element_type=jnp.float32).astype(jnp.bfloat16)
    full = [to_rank(hidden, shift) for shift in shifts]
    ranks = jnp.stack([t ^ shift for shift in shifts]).astype(jnp.int32)
    owners = jnp.stack([(core - turn) % ratio for turn in range(ratio)]).astype(jnp.int32)
    row_places = jnp.stack([plane ^ t ^ shift for shift in shifts]).astype(jnp.int32)
    head_width = query_key_value_weight.shape[1] // (tp_count * kv_local)
    slices, source = [], query_key_value_weight
    for h in range(kv_local):
        slices.append(
            [
                lax.dynamic_slice_in_dim(
                    source, ((t ^ shift) * kv_local + h) * head_width, head_width, 1
                )
                for shift in shifts
            ]
        )
        source = after(query_key_value_weight, slices[h])
    full = after(full, slices)
    normed = normalize(full, row_places)
    features = [to_plane(block, shift) for shift, block in zip(shifts, normed)]

    def exchanged(parts):
        return [to_rank(part, shift) for shift, part in zip(shifts, parts)]

    received = after(exchanged(slices[0]), features)
    partials = []
    for h in range(kv_local):
        laid = lay(received, ranks)
        if h + 1 < kv_local:
            coming = exchanged(after(slices[h + 1], received))
        blocks = project(features, [to_core(laid, turn) for turn in range(ratio)], owners)
        partials.append([to_plane(block, shift) for shift, block in zip(shifts, blocks)])
        if h + 1 < kv_local:
            received = after(coming, partials[h])

    depth = w_out.shape[0] // tp_count
    source = after(w_out, blocks)
    out_received = [
        to_rank(lax.dynamic_slice_in_dim(source, (t ^ shift) * depth, depth, 0).T, shift)
        for shift in shifts
    ]

    keys = k_cache.reshape(prompts, context * kv_local, HEAD_SIZE)
    values = value_cache.reshape(prompts, context * kv_local, HEAD_SIZE)
    plane_pairs = [
        (g * tp_count + r, (r * ratio + g % ratio) * tp_count + g // ratio)
        for g in range(grp_count)
        for r in range(tp_count)
    ]
    gathered = []
    for chunk in range(CHUNKS):
        if chunk > 0:
            lens = after(lens, mixed, out_received)
        mixed = attention(partials, cosine, sine, lens, keys, values, chunk, CHUNKS)
        gathered.append([to_plane(mixed, shift) for shift in shifts])
    laid = lay(after(out_received, mixed, gathered[:-1]), ranks)
    out_weights = [to_core(laid, turn) for turn in range(ratio)]
    results = []
    for mixed in gathered:
        blocks = output(mixed, out_weights, owners, row_places)
        blocks = [to_rank(block, shift) for shift, block in zip(shifts, blocks)]
        summed = sum(block.astype(jnp.float32) for block in blocks).astype(jnp.bfloat16)
        results.append(lax.ppermute(summed, ("grp", "tp"), plane_pairs))
    result = jnp.concatenate(results, axis=0)
    return lax.dot_general(
        sort_rows, result, (((0,), (0,)), ((), ())), preferred_element_type=jnp.float32
    ).astype(jnp.bfloat16)


def solution(mesh):
    return jax.shard_map(
        local,
        mesh=mesh,
        in_specs=(
            P("grp", "tp"),
            P(("grp", "tp"), None),
            P(None, ("grp", "tp")),
            P("grp", None, "tp", None),
            P("grp", None, "tp", None),
            P("grp"),
            P("grp"),
        ),
        out_specs=P("grp", "tp"),
        check_vma=False,
    )
```

```python
import functools

import jax
import jax.numpy as jnp
from jax import lax
from jax.experimental import pallas as pl
from jax.experimental.pallas import tpu as pltpu
from jax.sharding import PartitionSpec as P

QUERY_HEADS = 64
KEY_VALUE_HEADS = 8
HEAD_SIZE = 128
HEAD_GROUP = QUERY_HEADS // KEY_VALUE_HEADS


EPS = 1e-06
ROPE_BASE = 1000000.0
LOG2_E = 1.4426950408889634
MASKED = -1e30
MIB = 1024 * 1024


def rotary_tables(positions):
    half = HEAD_SIZE // 2
    freq = ROPE_BASE ** (-jnp.arange(half, dtype=jnp.float32) * 2.0 / HEAD_SIZE)
    angle = positions.astype(jnp.float32)[:, None] * freq[None, :]
    cosine, sine = (jnp.cos(angle), jnp.sin(angle))
    return jnp.concatenate([cosine, cosine], axis=1), jnp.concatenate([-sine, sine], axis=1)


def column_tile(width):
    return next(tile for tile in (512, 640, 256, 128) if width % tile == 0)


def normalize_kernel(count, place_ref, *refs):
    xs, outs, held = refs[:count], refs[count : 2 * count], refs[2 * count]
    values = [ref[...].astype(jnp.float32) for ref in xs]
    total = sum(jnp.sum(value * value, axis=-1, keepdims=True) for value in values)
    factor = lax.rsqrt(total / (count * xs[0].shape[1]) + EPS)
    for n, value in enumerate(values):
        held[place_ref[n]] = (value * factor).astype(held.dtype)
    for n, out_ref in enumerate(outs):
        out_ref[...] = held[n]


def normalize(xs, places):
    count = len(xs)
    return pl.pallas_call(
        functools.partial(normalize_kernel, count),
        grid_spec=pltpu.PrefetchScalarGridSpec(
            num_scalar_prefetch=1,
            grid=(),
            in_specs=[pl.BlockSpec(memory_space=pltpu.VMEM)] * count,
            out_specs=[pl.BlockSpec(memory_space=pltpu.VMEM)] * count,
            scratch_shapes=[pltpu.VMEM((count,) + xs[0].shape, jnp.bfloat16)],
        ),
        out_shape=[jax.ShapeDtypeStruct(xs[0].shape, jnp.bfloat16)] * count,
        compiler_params=pltpu.CompilerParams(vmem_limit_bytes=6 * MIB),
        name="normalize",
    )(places, *xs)


def lay_kernel(count, place_ref, *refs):
    pieces, (out_ref, sems) = refs[:count], refs[count:]
    rows = pieces[0].shape[0]
    copies = []
    for n, piece in enumerate(pieces):
        start = pl.multiple_of(place_ref[n] * rows, 16)
        copies.append(pltpu.make_async_copy(piece, out_ref.at[pl.ds(start, rows)], sems.at[n]))
    for copy in copies:
        copy.start()
    for copy in copies:
        copy.wait()


def lay(pieces, places):
    count = len(pieces)
    rows, width = pieces[0].shape
    if rows % 16:
        whole = jnp.zeros((count * rows, width), pieces[0].dtype)
        for n, piece in enumerate(pieces):
            whole = lax.dynamic_update_slice_in_dim(whole, piece, places[n] * rows, 0)
        return whole
    return pl.pallas_call(
        functools.partial(lay_kernel, count),
        grid_spec=pltpu.PrefetchScalarGridSpec(
            num_scalar_prefetch=1,
            grid=(),
            in_specs=[pl.BlockSpec(memory_space=pl.ANY)] * count,
            out_specs=pl.BlockSpec(memory_space=pltpu.VMEM),
            scratch_shapes=[pltpu.SemaphoreType.DMA((count,))],
        ),
        out_shape=jax.ShapeDtypeStruct((count * rows, width), pieces[0].dtype),
        compiler_params=pltpu.CompilerParams(vmem_limit_bytes=6 * MIB),
        cost_estimate=pl.CostEstimate(
            flops=0, bytes_accessed=4 * count * rows * width, transcendentals=0
        ),
        name="lay",
    )(places, *pieces)


def project_kernel(count, blocks, place_ref, *refs):
    xs, pieces, outs = refs[:blocks], refs[blocks : blocks + count], refs[blocks + count : -4]
    x_held, weight, x_sems, sems = refs[-4:]
    rows, width = pieces[0].shape
    height = xs[0].shape[0]
    tile = column_tile(width)
    x_copies = [
        pltpu.make_async_copy(x, x_held.at[pl.ds(n * height, height)], x_sems.at[n])
        for n, x in enumerate(xs)
    ]
    copies = []
    for c in range(width // tile):
        for n, piece in enumerate(pieces):
            start = pl.multiple_of(place_ref[n] * rows, 16)
            copies.append(
                pltpu.make_async_copy(
                    piece.at[:, pl.ds(c * tile, tile)],
                    weight.at[pl.ds(start, rows), pl.ds(c * tile, tile)],
                    sems.at[c, n],
                )
            )
    for copy in x_copies + copies:
        copy.start()
    for copy in x_copies:
        copy.wait()
    for c in range(width // tile):
        for copy in copies[c * count : (c + 1) * count]:
            copy.wait()
        lanes = slice(c * tile, (c + 1) * tile)
        result = jnp.dot(x_held[...], weight[:, lanes], preferred_element_type=jnp.float32)
        for n in range(blocks):
            outs[n][:, lanes] = result[n * height : (n + 1) * height].astype(outs[n].dtype)


def project(xs, pieces, places):
    rows, width = pieces[0].shape
    count, blocks, height = len(pieces), len(xs), xs[0].shape[0]
    tile = column_tile(width)
    return pl.pallas_call(
        functools.partial(project_kernel, count, blocks),
        grid_spec=pltpu.PrefetchScalarGridSpec(
            num_scalar_prefetch=1,
            grid=(),
            in_specs=[pl.BlockSpec(memory_space=pl.ANY)] * (blocks + count),
            out_specs=[pl.BlockSpec(memory_space=pltpu.VMEM)] * blocks,
            scratch_shapes=[
                pltpu.VMEM((blocks * height, count * rows), jnp.bfloat16),
                pltpu.VMEM((count * rows, width), jnp.bfloat16),
                pltpu.SemaphoreType.DMA((blocks,)),
                pltpu.SemaphoreType.DMA((width // tile, count)),
            ],
        ),
        out_shape=[jax.ShapeDtypeStruct((height, width), jnp.bfloat16)] * blocks,
        compiler_params=pltpu.CompilerParams(vmem_limit_bytes=12 * MIB),
        cost_estimate=pl.CostEstimate(
            flops=2 * blocks * height * count * rows * width,
            bytes_accessed=2 * count * rows * width,
            transcendentals=0,
        ),
        name="project",
    )(places, *xs, *pieces)


def output_kernel(count, blocks, place_ref, x_place_ref, *refs):
    xs, pieces, outs = refs[:blocks], refs[blocks : blocks + count], refs[blocks + count : -4]
    x_held, weight, x_sems, sems = refs[-4:]
    rows = pieces[0].shape[0]
    height = xs[0].shape[0]
    copies = []
    for n, x in enumerate(xs):
        start = pl.multiple_of(x_place_ref[n] * height, 16)
        copies.append(pltpu.make_async_copy(x, x_held.at[pl.ds(start, height)], x_sems.at[n]))
    for n, piece in enumerate(pieces):
        start = pl.multiple_of(place_ref[n] * rows, 16)
        copies.append(pltpu.make_async_copy(piece, weight.at[pl.ds(start, rows)], sems.at[n]))
    for copy in copies:
        copy.start()
    for copy in copies:
        copy.wait()
    width = count * rows
    tile = next(size for size in (256, 320, 128) if width % size == 0)
    for c in range(width // tile):
        result = lax.dot_general(
            x_held[...],
            weight[c * tile : (c + 1) * tile],
            (((1,), (1,)), ((), ())),
            preferred_element_type=jnp.float32,
        )
        for n in range(blocks):
            outs[n][:, c * tile : (c + 1) * tile] = result[n * height : (n + 1) * height].astype(
                outs[n].dtype
            )


def output(xs, pieces, places, x_places):
    rows, depth = pieces[0].shape
    count, blocks, height = len(pieces), len(xs), xs[0].shape[0]
    return pl.pallas_call(
        functools.partial(output_kernel, count, blocks),
        grid_spec=pltpu.PrefetchScalarGridSpec(
            num_scalar_prefetch=2,
            grid=(),
            in_specs=[pl.BlockSpec(memory_space=pl.ANY)] * (blocks + count),
            out_specs=[pl.BlockSpec(memory_space=pltpu.VMEM)] * blocks,
            scratch_shapes=[
                pltpu.VMEM((blocks * height, depth), jnp.bfloat16),
                pltpu.VMEM((count * rows, depth), jnp.bfloat16),
                pltpu.SemaphoreType.DMA((blocks,)),
                pltpu.SemaphoreType.DMA((count,)),
            ],
        ),
        out_shape=[jax.ShapeDtypeStruct((height, count * rows), jnp.bfloat16)] * blocks,
        compiler_params=pltpu.CompilerParams(vmem_limit_bytes=14 * MIB),
        cost_estimate=pl.CostEstimate(
            flops=2 * blocks * height * count * rows * depth,
            bytes_accessed=2 * count * rows * depth,
            transcendentals=0,
        ),
        name="output",
    )(places, x_places, *xs, *pieces)


def attention_kernel(kv_local, terms, samples, first, *refs):
    total_terms = kv_local * terms
    partials = refs[:total_terms]
    cos_ref, sin_ref, lens_ref, k_ref, v_ref, out_ref = refs[total_terms : total_terms + 6]
    scores, k_held, v_held, held, tables, lens_held, k_sems, v_sems, sems = refs[total_terms + 6 :]
    height = out_ref.shape[0]
    here = height // samples
    length = k_ref.shape[1]
    pieces = k_sems.shape[1]
    piece = length // pieces
    scale = HEAD_SIZE ** (-0.5) * LOG2_E
    group = HEAD_GROUP * samples
    tile = 1024

    chunk = pl.ds(first * samples, height)
    small = [
        pltpu.make_async_copy(ref.at[chunk], held.at[n], sems.at[n])
        for n, ref in enumerate(partials)
    ]
    small += [
        pltpu.make_async_copy(ref.at[chunk], to, sems.at[total_terms + n])
        for n, (ref, to) in enumerate(
            [(cos_ref, tables.at[0]), (sin_ref, tables.at[1]), (lens_ref, lens_held)]
        )
    ]

    def fetch(ref, buffer, buffer_sems, u):
        return [
            pltpu.make_async_copy(
                ref.at[first + u, pl.ds(c * piece, piece)],
                buffer.at[u % 2, pl.ds(c * piece, piece)],
                buffer_sems.at[u % 2, c],
            )
            for c in range(pieces)
        ]

    keys = [fetch(k_ref, k_held, k_sems, u) for u in range(here)]
    values = [fetch(v_ref, v_held, v_sems, u) for u in range(here)]
    for copy in small:
        copy.start()
    for u in range(min(2, here)):
        for copy in keys[u] + values[u]:
            copy.start()
    for copy in small:
        copy.wait()
    cosine, sine = tables[0], tables[1]
    lane = lax.broadcasted_iota(jnp.int32, (group, HEAD_SIZE), 1) % kv_local

    queries, owns, fresh = [], [], []
    for h in range(kv_local):
        proj = sum(held[h * terms + n].astype(jnp.float32) for n in range(terms))

        def head(index):
            vec = proj[:, index * HEAD_SIZE : (index + 1) * HEAD_SIZE]
            vec = vec * lax.rsqrt(jnp.mean(vec * vec, axis=-1, keepdims=True) + EPS)
            vec = vec * cosine + pltpu.roll(vec, HEAD_SIZE // 2, 1) * sine
            return vec.astype(jnp.bfloat16).astype(jnp.float32)

        new_key = head(HEAD_GROUP)
        new_value = proj[:, (HEAD_GROUP + 1) * HEAD_SIZE : (HEAD_GROUP + 2) * HEAD_SIZE]
        fresh.append(new_value.astype(jnp.bfloat16).astype(jnp.float32))
        queries.append([head(j) for j in range(HEAD_GROUP)])
        owns.append([jnp.sum(q * new_key, axis=-1, keepdims=True) for q in queries[-1]])

    results = []
    for u in range(here):
        rows = slice(u * samples, (u + 1) * samples)
        query = jnp.concatenate(
            [q[rows] for head_queries in queries for q in head_queries], axis=0
        ).astype(jnp.bfloat16)
        own = [jnp.concatenate([o[rows] for o in head_owns], axis=0) for head_owns in owns]
        lens = lens_held[rows, 0:1] * kv_local
        most = jnp.full((group, HEAD_SIZE), MASKED, jnp.float32)
        for c in range(0, length, tile):
            if c % piece == 0:
                keys[u][c // piece].wait()
            part = lax.dot_general(
                query,
                k_held[u % 2, c : c + tile],
                (((1,), (1,)), ((), ())),
                preferred_element_type=jnp.float32,
            )
            for d in range(0, tile, HEAD_SIZE):
                dense = part[:group, d : d + HEAD_SIZE]
                for h in range(1, kv_local):
                    other = part[h * group : (h + 1) * group, d : d + HEAD_SIZE]
                    dense = jnp.where(lane == h, other, dense)
                slots = lax.broadcasted_iota(jnp.int32, (samples, HEAD_SIZE), 1) + (c + d)
                bias = jnp.where(slots < lens, 0.0, MASKED)
                dense = (dense.reshape(HEAD_GROUP, samples, HEAD_SIZE) + bias[None]).reshape(
                    group, HEAD_SIZE
                )
                scores[:, c + d : c + d + HEAD_SIZE] = dense
                most = jnp.maximum(most, dense)
        if u + 2 < here:
            for copy in keys[u + 2]:
                copy.start()
        tops = [
            jnp.maximum(
                jnp.max(jnp.where(lane == h, most, MASKED), axis=-1, keepdims=True), own[h]
            )
            for h in range(kv_local)
        ]
        top = jnp.broadcast_to(tops[0], (group, HEAD_SIZE))
        for h in range(1, kv_local):
            top = jnp.where(lane == h, tops[h], top)
        sums = jnp.zeros((group, HEAD_SIZE), jnp.float32)
        mixed = jnp.zeros((kv_local * group, HEAD_SIZE), jnp.float32)
        for c in range(0, length, tile):
            if c % piece == 0:
                values[u][c // piece].wait()
            weights = [[] for _ in range(kv_local)]
            for d in range(0, tile, HEAD_SIZE):
                expo = jnp.exp2((scores[:, c + d : c + d + HEAD_SIZE] - top) * scale)
                sums = sums + expo
                for h in range(kv_local):
                    kept = expo if kv_local == 1 else jnp.where(lane == h, expo, 0.0)
                    weights[h].append(kept.astype(jnp.bfloat16))
            weights = jnp.concatenate([jnp.concatenate(w, axis=1) for w in weights], axis=0)
            mixed = mixed + jnp.dot(
                weights, v_held[u % 2, c : c + tile], preferred_element_type=jnp.float32
            )
        if u + 2 < here:
            for copy in values[u + 2]:
                copy.start()
        line = []
        for h in range(kv_local):
            own_expo = jnp.exp2((own[h] - tops[h]) * scale)
            total = jnp.sum(jnp.where(lane == h, sums, 0.0), axis=-1, keepdims=True) + own_expo
            inverse = 1.0 / total
            own_weight = own_expo * inverse
            value = fresh[h][rows]
            for j in range(HEAD_GROUP):
                at = slice(j * samples, (j + 1) * samples)
                part = mixed[h * group + j * samples : h * group + (j + 1) * samples]
                line.append(part * inverse[at] + own_weight[at] * value)
        results.append(jnp.concatenate(line, axis=1))
    out_ref[...] = jnp.concatenate(results, axis=0).astype(out_ref.dtype)


def attention(partials, cosine, sine, lens, k_cache, value_cache, chunk, chunks):
    rows, width = partials[0][0].shape
    kv_local, terms = len(partials), len(partials[0])
    prompts, length, _ = k_cache.shape
    samples = rows // prompts
    here = prompts // chunks
    height = here * samples
    heads = kv_local * HEAD_GROUP
    pieces = length // 2048
    return pl.pallas_call(
        functools.partial(attention_kernel, kv_local, terms, samples, chunk * here),
        in_specs=[pl.BlockSpec(memory_space=pl.ANY)] * (kv_local * terms + 5),
        out_specs=pl.BlockSpec(memory_space=pltpu.VMEM),
        out_shape=jax.ShapeDtypeStruct((height, heads * HEAD_SIZE), jnp.bfloat16),
        scratch_shapes=[
            pltpu.VMEM((HEAD_GROUP * samples, length), jnp.float32),
            pltpu.VMEM((2, length, HEAD_SIZE), jnp.bfloat16),
            pltpu.VMEM((2, length, HEAD_SIZE), jnp.bfloat16),
            pltpu.VMEM((kv_local * terms, height, width), jnp.bfloat16),
            pltpu.VMEM((2, height, HEAD_SIZE), jnp.float32),
            pltpu.VMEM((height, HEAD_SIZE), jnp.int32),
            pltpu.SemaphoreType.DMA((2, pieces)),
            pltpu.SemaphoreType.DMA((2, pieces)),
            pltpu.SemaphoreType.DMA((kv_local * terms + 3,)),
        ],
        compiler_params=pltpu.CompilerParams(vmem_limit_bytes=52 * MIB),
        cost_estimate=pl.CostEstimate(
            flops=4 * here * heads * samples * length * HEAD_SIZE,
            bytes_accessed=4 * here * length * HEAD_SIZE,
            transcendentals=here * HEAD_GROUP * samples * length,
        ),
        name="attention",
    )(*[term for head_terms in partials for term in head_terms], cosine, sine, lens, k_cache, value_cache)


CHUNKS = 2


def after(value, *others):
    return lax.optimization_barrier((value, others))[0]


def local(hidden, query_key_value_weight, w_out, k_cache, value_cache, lengths, assign):
    tp_count = lax.axis_size("tp")
    grp_count = lax.axis_size("grp")
    ratio = grp_count // tp_count
    t = lax.axis_index("tp")
    plane = lax.axis_index("grp") // ratio
    core = lax.axis_index("grp") % ratio
    row_count, width = hidden.shape
    prompts, context, kv_local, _ = k_cache.shape
    shifts = range(tp_count)

    def to_rank(value, shift):
        if shift == 0:
            return value
        return lax.ppermute(value, "tp", [(i, i ^ shift) for i in range(tp_count)])

    def to_plane(value, shift):
        if shift == 0:
            return value
        pairs = [(i, ((i // ratio) ^ shift) * ratio + i % ratio) for i in range(grp_count)]
        return lax.ppermute(value, "grp", pairs)

    def to_core(value, turn):
        if turn == 0:
            return value
        pairs = [(i, i // ratio * ratio + (i + turn) % ratio) for i in range(grp_count)]
        return lax.ppermute(value, "grp", pairs)

    index = jnp.arange(row_count, dtype=jnp.int32)
    key = assign * row_count + index
    place = jnp.sum((key[None, :] < key[:, None]).astype(jnp.int32), axis=1)
    sort_rows = (place[None, :] == index[:, None]).astype(jnp.bfloat16)
    lens = jnp.sum(jnp.where(place[None, :] == index[:, None], lengths[None, :], 0), axis=1)
    cosine, sine = rotary_tables(lens)
    lens = jnp.broadcast_to(lens[:, None], (row_count, HEAD_SIZE))

    hidden = jnp.dot(sort_rows, hidden, preferred_element_type=jnp.float32).astype(jnp.bfloat16)
    full = [to_rank(hidden, shift) for shift in shifts]
    ranks = jnp.stack([t ^ shift for shift in shifts]).astype(jnp.int32)
    owners = jnp.stack([(core - turn) % ratio for turn in range(ratio)]).astype(jnp.int32)
    row_places = jnp.stack([plane ^ t ^ shift for shift in shifts]).astype(jnp.int32)
    head_width = query_key_value_weight.shape[1] // (tp_count * kv_local)
    slices, source = [], query_key_value_weight
    for h in range(kv_local):
        slices.append(
            [
                lax.dynamic_slice_in_dim(
                    source, ((t ^ shift) * kv_local + h) * head_width, head_width, 1
                )
                for shift in shifts
            ]
        )
        source = after(query_key_value_weight, slices[h])
    full = after(full, slices)
    normed = normalize(full, row_places)
    features = [to_plane(block, shift) for shift, block in zip(shifts, normed)]

    def exchanged(parts):
        return [to_rank(part, shift) for shift, part in zip(shifts, parts)]

    received = after(exchanged(slices[0]), features)
    partials = []
    for h in range(kv_local):
        laid = lay(received, ranks)
        if h + 1 < kv_local:
            coming = exchanged(after(slices[h + 1], received))
        blocks = project(features, [to_core(laid, turn) for turn in range(ratio)], owners)
        partials.append([to_plane(block, shift) for shift, block in zip(shifts, blocks)])
        if h + 1 < kv_local:
            received = after(coming, partials[h])

    depth = w_out.shape[0] // tp_count
    source = after(w_out, partials[-1][1])
    out_received = [
        to_rank(lax.dynamic_slice_in_dim(source, (t ^ shift) * depth, depth, 0).T, shift)
        for shift in shifts
    ]

    keys = k_cache.reshape(prompts, context * kv_local, HEAD_SIZE)
    values = value_cache.reshape(prompts, context * kv_local, HEAD_SIZE)
    plane_pairs = [
        (g * tp_count + r, (r * ratio + g % ratio) * tp_count + g // ratio)
        for g in range(grp_count)
        for r in range(tp_count)
    ]
    gathered = []
    for chunk in range(CHUNKS):
        if chunk > 0:
            lens = after(lens, mixed, out_received[:-1])
        mixed = attention(partials, cosine, sine, lens, keys, values, chunk, CHUNKS)
        gathered.append([to_plane(mixed, shift) for shift in shifts])
    laid = lay(after(out_received, mixed, gathered[:-1]), ranks)
    out_weights = [to_core(laid, turn) for turn in range(ratio)]
    results = []
    for mixed in gathered:
        blocks = output(mixed, out_weights, owners, row_places)
        blocks = [to_rank(block, shift) for shift, block in zip(shifts, blocks)]
        results.append(sum(block.astype(jnp.float32) for block in blocks).astype(jnp.bfloat16))
    result = lax.ppermute(jnp.concatenate(results, axis=0), ("grp", "tp"), plane_pairs)
    return lax.dot_general(
        sort_rows, result, (((0,), (0,)), ((), ())), preferred_element_type=jnp.float32
    ).astype(jnp.bfloat16)


def solution(mesh):
    return jax.shard_map(
        local,
        mesh=mesh,
        in_specs=(
            P("grp", "tp"),
            P(("grp", "tp"), None),
            P(None, ("grp", "tp")),
            P("grp", None, "tp", None),
            P("grp", None, "tp", None),
            P("grp"),
            P("grp"),
        ),
        out_specs=P("grp", "tp"),
        check_vma=False,
    )
```

```python
import functools

import jax
import jax.numpy as jnp
from jax import lax
from jax.experimental import pallas as pl
from jax.experimental.pallas import tpu as pltpu
from jax.sharding import PartitionSpec as P

QUERY_HEADS = 64
KEY_VALUE_HEADS = 8
HEAD_SIZE = 128
HEAD_GROUP = QUERY_HEADS // KEY_VALUE_HEADS


EPS = 1e-06
ROPE_BASE = 1000000.0
LOG2_E = 1.4426950408889634
MASKED = -1e30
MIB = 1024 * 1024


def rotary_tables(positions):
    half = HEAD_SIZE // 2
    freq = ROPE_BASE ** (-jnp.arange(half, dtype=jnp.float32) * 2.0 / HEAD_SIZE)
    angle = positions.astype(jnp.float32)[:, None] * freq[None, :]
    cosine, sine = (jnp.cos(angle), jnp.sin(angle))
    return jnp.concatenate([cosine, cosine], axis=1), jnp.concatenate([-sine, sine], axis=1)


def column_tile(width):
    return next(tile for tile in (512, 640, 256, 128) if width % tile == 0)


def normalize_kernel(count, place_ref, *refs):
    xs, outs, held = refs[:count], refs[count : 2 * count], refs[2 * count]
    values = [ref[...].astype(jnp.float32) for ref in xs]
    total = sum(jnp.sum(value * value, axis=-1, keepdims=True) for value in values)
    factor = lax.rsqrt(total / (count * xs[0].shape[1]) + EPS)
    for n, value in enumerate(values):
        held[place_ref[n]] = (value * factor).astype(held.dtype)
    for n, out_ref in enumerate(outs):
        out_ref[...] = held[n]


def normalize(xs, places):
    count = len(xs)
    return pl.pallas_call(
        functools.partial(normalize_kernel, count),
        grid_spec=pltpu.PrefetchScalarGridSpec(
            num_scalar_prefetch=1,
            grid=(),
            in_specs=[pl.BlockSpec(memory_space=pltpu.VMEM)] * count,
            out_specs=[pl.BlockSpec(memory_space=pltpu.VMEM)] * count,
            scratch_shapes=[pltpu.VMEM((count,) + xs[0].shape, jnp.bfloat16)],
        ),
        out_shape=[jax.ShapeDtypeStruct(xs[0].shape, jnp.bfloat16)] * count,
        compiler_params=pltpu.CompilerParams(vmem_limit_bytes=48 * MIB),
        name="normalize",
    )(places, *xs)


def lay_kernel(count, place_ref, *refs):
    pieces, (out_ref, sems) = refs[:count], refs[count:]
    rows = pieces[0].shape[0]
    copies = []
    for n, piece in enumerate(pieces):
        start = pl.multiple_of(place_ref[n] * rows, 16)
        copies.append(pltpu.make_async_copy(piece, out_ref.at[pl.ds(start, rows)], sems.at[n]))
    for copy in copies:
        copy.start()
    for copy in copies:
        copy.wait()


def lay(pieces, places):
    count = len(pieces)
    rows, width = pieces[0].shape
    if rows % 16:
        whole = jnp.zeros((count * rows, width), pieces[0].dtype)
        for n, piece in enumerate(pieces):
            whole = lax.dynamic_update_slice_in_dim(whole, piece, places[n] * rows, 0)
        return whole
    return pl.pallas_call(
        functools.partial(lay_kernel, count),
        grid_spec=pltpu.PrefetchScalarGridSpec(
            num_scalar_prefetch=1,
            grid=(),
            in_specs=[pl.BlockSpec(memory_space=pl.ANY)] * count,
            out_specs=pl.BlockSpec(memory_space=pltpu.VMEM),
            scratch_shapes=[pltpu.SemaphoreType.DMA((count,))],
        ),
        out_shape=jax.ShapeDtypeStruct((count * rows, width), pieces[0].dtype),
        compiler_params=pltpu.CompilerParams(vmem_limit_bytes=6 * MIB),
        cost_estimate=pl.CostEstimate(
            flops=0, bytes_accessed=4 * count * rows * width, transcendentals=0
        ),
        name="lay",
    )(places, *pieces)


def project_kernel(count, blocks, place_ref, *refs):
    xs, pieces, outs = refs[:blocks], refs[blocks : blocks + count], refs[blocks + count : -2]
    weight, sems = refs[-2:]
    rows = pieces[0].shape[0]
    height, width = outs[0].shape
    tile = column_tile(width)
    copies = []
    for c in range(width // tile):
        for n, piece in enumerate(pieces):
            start = pl.multiple_of(place_ref[n] * rows, 16)
            copy = pltpu.make_async_copy(
                piece.at[:, pl.ds(c * tile, tile)],
                weight.at[pl.ds(start, rows), pl.ds(c * tile, tile)],
                sems.at[c, n],
            )
            copy.start()
            copies.append(copy)
    x = jnp.concatenate([ref[...] for ref in xs], axis=0)
    for c in range(width // tile):
        for copy in copies[c * count : (c + 1) * count]:
            copy.wait()
        lanes = slice(c * tile, (c + 1) * tile)
        result = jnp.dot(x, weight[:, lanes], preferred_element_type=jnp.float32)
        for n in range(blocks):
            outs[n][:, lanes] = result[n * height : (n + 1) * height].astype(outs[n].dtype)


def project(xs, pieces, places):
    rows, width = pieces[0].shape
    count, blocks, height = len(pieces), len(xs), xs[0].shape[0]
    tile = column_tile(width)
    return pl.pallas_call(
        functools.partial(project_kernel, count, blocks),
        grid_spec=pltpu.PrefetchScalarGridSpec(
            num_scalar_prefetch=1,
            grid=(),
            in_specs=[pl.BlockSpec(memory_space=pltpu.VMEM)] * blocks
            + [pl.BlockSpec(memory_space=pl.ANY)] * count,
            out_specs=[pl.BlockSpec(memory_space=pltpu.VMEM)] * blocks,
            scratch_shapes=[
                pltpu.VMEM((count * rows, width), jnp.bfloat16),
                pltpu.SemaphoreType.DMA((width // tile, count)),
            ],
        ),
        out_shape=[jax.ShapeDtypeStruct((height, width), jnp.bfloat16)] * blocks,
        compiler_params=pltpu.CompilerParams(vmem_limit_bytes=48 * MIB),
        cost_estimate=pl.CostEstimate(
            flops=2 * blocks * height * count * rows * width,
            bytes_accessed=2 * count * rows * width,
            transcendentals=0,
        ),
        name="project",
    )(places, *xs, *pieces)


def output_kernel(count, blocks, place_ref, x_place_ref, *refs):
    xs, pieces, outs = refs[:blocks], refs[blocks : blocks + count], refs[blocks + count : -4]
    x_held, weight, x_sems, sems = refs[-4:]
    rows = pieces[0].shape[0]
    height = xs[0].shape[0]
    copies = []
    for n, x in enumerate(xs):
        start = pl.multiple_of(x_place_ref[n] * height, 16)
        copies.append(pltpu.make_async_copy(x, x_held.at[pl.ds(start, height)], x_sems.at[n]))
    for n, piece in enumerate(pieces):
        start = pl.multiple_of(place_ref[n] * rows, 16)
        copies.append(pltpu.make_async_copy(piece, weight.at[pl.ds(start, rows)], sems.at[n]))
    for copy in copies:
        copy.start()
    for copy in copies:
        copy.wait()
    width = count * rows
    tile = next(size for size in (256, 320, 128) if width % size == 0)
    for c in range(width // tile):
        result = lax.dot_general(
            x_held[...],
            weight[c * tile : (c + 1) * tile],
            (((1,), (1,)), ((), ())),
            preferred_element_type=jnp.float32,
        )
        for n in range(blocks):
            outs[n][:, c * tile : (c + 1) * tile] = result[n * height : (n + 1) * height].astype(
                outs[n].dtype
            )


def output(xs, pieces, places, x_places):
    rows, depth = pieces[0].shape
    count, blocks, height = len(pieces), len(xs), xs[0].shape[0]
    return pl.pallas_call(
        functools.partial(output_kernel, count, blocks),
        grid_spec=pltpu.PrefetchScalarGridSpec(
            num_scalar_prefetch=2,
            grid=(),
            in_specs=[pl.BlockSpec(memory_space=pl.ANY)] * (blocks + count),
            out_specs=[pl.BlockSpec(memory_space=pltpu.VMEM)] * blocks,
            scratch_shapes=[
                pltpu.VMEM((blocks * height, depth), jnp.bfloat16),
                pltpu.VMEM((count * rows, depth), jnp.bfloat16),
                pltpu.SemaphoreType.DMA((blocks,)),
                pltpu.SemaphoreType.DMA((count,)),
            ],
        ),
        out_shape=[jax.ShapeDtypeStruct((height, count * rows), jnp.bfloat16)] * blocks,
        compiler_params=pltpu.CompilerParams(vmem_limit_bytes=48 * MIB),
        cost_estimate=pl.CostEstimate(
            flops=2 * blocks * height * count * rows * depth,
            bytes_accessed=2 * count * rows * depth,
            transcendentals=0,
        ),
        name="output",
    )(places, x_places, *xs, *pieces)


def attention_kernel(kv_local, terms, samples, *refs):
    partials = [refs[h * terms : (h + 1) * terms] for h in range(kv_local)]
    refs = refs[kv_local * terms :]
    cos_ref, sin_ref, lens_ref, k_ref, v_ref, out_ref, scores = refs
    together, length, _ = k_ref.shape
    scale = HEAD_SIZE ** (-0.5) * LOG2_E
    group = HEAD_GROUP * samples
    tile = 1024
    cosine, sine = cos_ref[...], sin_ref[...]
    lane = lax.broadcasted_iota(jnp.int32, (group, HEAD_SIZE), 1) % kv_local

    queries, owns, fresh = [], [], []
    for term_refs in partials:
        proj = sum(ref[...].astype(jnp.float32) for ref in term_refs)

        def head(index):
            vec = proj[:, index * HEAD_SIZE : (index + 1) * HEAD_SIZE]
            vec = vec * lax.rsqrt(jnp.mean(vec * vec, axis=-1, keepdims=True) + EPS)
            vec = vec * cosine + pltpu.roll(vec, HEAD_SIZE // 2, 1) * sine
            return vec.astype(jnp.bfloat16).astype(jnp.float32)

        new_key = head(HEAD_GROUP)
        new_value = proj[:, (HEAD_GROUP + 1) * HEAD_SIZE : (HEAD_GROUP + 2) * HEAD_SIZE]
        fresh.append(new_value.astype(jnp.bfloat16).astype(jnp.float32))
        queries.append([head(j) for j in range(HEAD_GROUP)])
        owns.append([jnp.sum(q * new_key, axis=-1, keepdims=True) for q in queries[-1]])

    results = []
    for u in range(together):
        rows = slice(u * samples, (u + 1) * samples)
        query = jnp.concatenate(
            [q[rows] for head_queries in queries for q in head_queries], axis=0
        ).astype(jnp.bfloat16)
        own = [jnp.concatenate([o[rows] for o in head_owns], axis=0) for head_owns in owns]
        lens = lens_ref[rows, 0:1] * kv_local
        most = jnp.full((group, HEAD_SIZE), MASKED, jnp.float32)
        for c in range(0, length, tile):
            part = lax.dot_general(
                query,
                k_ref[u, c : c + tile],
                (((1,), (1,)), ((), ())),
                preferred_element_type=jnp.float32,
            )
            for d in range(0, tile, HEAD_SIZE):
                dense = part[:group, d : d + HEAD_SIZE]
                for h in range(1, kv_local):
                    other = part[h * group : (h + 1) * group, d : d + HEAD_SIZE]
                    dense = jnp.where(lane == h, other, dense)
                slots = lax.broadcasted_iota(jnp.int32, (samples, HEAD_SIZE), 1) + (c + d)
                bias = jnp.where(slots < lens, 0.0, MASKED)
                dense = (dense.reshape(HEAD_GROUP, samples, HEAD_SIZE) + bias[None]).reshape(
                    group, HEAD_SIZE
                )
                scores[:, c + d : c + d + HEAD_SIZE] = dense
                most = jnp.maximum(most, dense)
        tops = [
            jnp.maximum(
                jnp.max(jnp.where(lane == h, most, MASKED), axis=-1, keepdims=True), own[h]
            )
            for h in range(kv_local)
        ]
        top = jnp.broadcast_to(tops[0], (group, HEAD_SIZE))
        for h in range(1, kv_local):
            top = jnp.where(lane == h, tops[h], top)
        sums = jnp.zeros((group, HEAD_SIZE), jnp.float32)
        mixed = jnp.zeros((kv_local * group, HEAD_SIZE), jnp.float32)
        for c in range(0, length, tile):
            weights = [[] for _ in range(kv_local)]
            for d in range(0, tile, HEAD_SIZE):
                expo = jnp.exp2((scores[:, c + d : c + d + HEAD_SIZE] - top) * scale)
                sums = sums + expo
                for h in range(kv_local):
                    kept = expo if kv_local == 1 else jnp.where(lane == h, expo, 0.0)
                    weights[h].append(kept.astype(jnp.bfloat16))
            weights = jnp.concatenate([jnp.concatenate(w, axis=1) for w in weights], axis=0)
            mixed = mixed + jnp.dot(
                weights, v_ref[u, c : c + tile], preferred_element_type=jnp.float32
            )
        line = []
        for h in range(kv_local):
            own_expo = jnp.exp2((own[h] - tops[h]) * scale)
            total = jnp.sum(jnp.where(lane == h, sums, 0.0), axis=-1, keepdims=True) + own_expo
            inverse = 1.0 / total
            own_weight = own_expo * inverse
            value = fresh[h][rows]
            for j in range(HEAD_GROUP):
                at = slice(j * samples, (j + 1) * samples)
                part = mixed[h * group + j * samples : h * group + (j + 1) * samples]
                line.append(part * inverse[at] + own_weight[at] * value)
        results.append(jnp.concatenate(line, axis=1))
    out_ref[...] = jnp.concatenate(results, axis=0).astype(out_ref.dtype)


def attention(partials, cosine, sine, lens, k_cache, value_cache, chunk, chunks):
    rows, width = partials[0][0].shape
    kv_local, terms = len(partials), len(partials[0])
    prompts, length, _ = k_cache.shape
    samples = rows // prompts
    together = 16 // samples
    height = together * samples
    heads = kv_local * HEAD_GROUP
    steps = prompts // together // chunks
    first = chunk * steps
    small = pl.BlockSpec((height, HEAD_SIZE), lambda i: (i + first, 0))
    cache = pl.BlockSpec((together, length, HEAD_SIZE), lambda i: (i + first, 0, 0))
    return pl.pallas_call(
        functools.partial(attention_kernel, kv_local, terms, samples),
        grid=(steps,),
        in_specs=[pl.BlockSpec((height, width), lambda i: (i + first, 0))] * (kv_local * terms)
        + [small] * 3
        + [cache] * 2,
        out_specs=pl.BlockSpec((height, heads * HEAD_SIZE), lambda i: (i, 0)),
        out_shape=jax.ShapeDtypeStruct((rows // chunks, heads * HEAD_SIZE), jnp.bfloat16),
        scratch_shapes=[pltpu.VMEM((HEAD_GROUP * samples, length), jnp.float32)],
        compiler_params=pltpu.CompilerParams(vmem_limit_bytes=48 * MIB),
        cost_estimate=pl.CostEstimate(
            flops=4 * steps * together * heads * samples * length * HEAD_SIZE,
            bytes_accessed=4 * steps * together * length * HEAD_SIZE,
            transcendentals=steps * together * HEAD_GROUP * samples * length,
        ),
        name="attention",
    )(*[term for head_terms in partials for term in head_terms], cosine, sine, lens, k_cache, value_cache)


CHUNKS = 2


def after(value, *others):
    return lax.optimization_barrier((value, others))[0]


def local(hidden, query_key_value_weight, w_out, k_cache, value_cache, lengths, assign):
    tp_count = lax.axis_size("tp")
    grp_count = lax.axis_size("grp")
    ratio = grp_count // tp_count
    t = lax.axis_index("tp")
    plane = lax.axis_index("grp") // ratio
    core = lax.axis_index("grp") % ratio
    row_count, width = hidden.shape
    prompts, context, kv_local, _ = k_cache.shape
    shifts = range(tp_count)

    def to_rank(value, shift):
        if shift == 0:
            return value
        return lax.ppermute(value, "tp", [(i, i ^ shift) for i in range(tp_count)])

    def to_plane(value, shift):
        if shift == 0:
            return value
        pairs = [(i, ((i // ratio) ^ shift) * ratio + i % ratio) for i in range(grp_count)]
        return lax.ppermute(value, "grp", pairs)

    def to_core(value, turn):
        if turn == 0:
            return value
        pairs = [(i, i // ratio * ratio + (i + turn) % ratio) for i in range(grp_count)]
        return lax.ppermute(value, "grp", pairs)

    index = jnp.arange(row_count, dtype=jnp.int32)
    key = assign * row_count + index
    place = jnp.sum((key[None, :] < key[:, None]).astype(jnp.int32), axis=1)
    sort_rows = (place[None, :] == index[:, None]).astype(jnp.bfloat16)
    lens = jnp.sum(jnp.where(place[None, :] == index[:, None], lengths[None, :], 0), axis=1)
    cosine, sine = rotary_tables(lens)
    lens = jnp.broadcast_to(lens[:, None], (row_count, HEAD_SIZE))

    hidden = jnp.dot(sort_rows, hidden, preferred_element_type=jnp.float32).astype(jnp.bfloat16)
    full = [to_rank(hidden, shift) for shift in shifts]
    ranks = jnp.stack([t ^ shift for shift in shifts]).astype(jnp.int32)
    owners = jnp.stack([(core - turn) % ratio for turn in range(ratio)]).astype(jnp.int32)
    row_places = jnp.stack([plane ^ t ^ shift for shift in shifts]).astype(jnp.int32)
    head_width = query_key_value_weight.shape[1] // (tp_count * kv_local)
    slices, source = [], query_key_value_weight
    for h in range(kv_local):
        slices.append(
            [
                lax.dynamic_slice_in_dim(
                    source, ((t ^ shift) * kv_local + h) * head_width, head_width, 1
                )
                for shift in shifts
            ]
        )
        source = after(query_key_value_weight, slices[h])
    full = after(full, slices)
    normed = normalize(full, row_places)
    features = [to_plane(block, shift) for shift, block in zip(shifts, normed)]

    def exchanged(parts):
        return [to_rank(part, shift) for shift, part in zip(shifts, parts)]

    coming = exchanged(slices[0])
    received = after(coming, features)
    partials = []
    for h in range(kv_local):
        laid = lay(received, ranks)
        if h + 1 < kv_local:
            coming = exchanged(after(slices[h + 1], received))
        blocks = project(features, [to_core(laid, turn) for turn in range(ratio)], owners)
        partials.append([to_plane(block, shift) for shift, block in zip(shifts, blocks)])
        if h + 1 < kv_local:
            received = after(coming, partials[h])

    depth = w_out.shape[0] // tp_count
    source = after(w_out, coming)
    out_received = [
        to_rank(lax.dynamic_slice_in_dim(source, (t ^ shift) * depth, depth, 0).T, shift)
        for shift in shifts
    ]

    keys = k_cache.reshape(prompts, context * kv_local, HEAD_SIZE)
    values = value_cache.reshape(prompts, context * kv_local, HEAD_SIZE)
    plane_pairs = [
        (g * tp_count + r, (r * ratio + g % ratio) * tp_count + g // ratio)
        for g in range(grp_count)
        for r in range(tp_count)
    ]
    gathered = []
    for chunk in range(CHUNKS):
        if chunk > 0:
            lens = after(lens, mixed, out_received)
        mixed = attention(partials, cosine, sine, lens, keys, values, chunk, CHUNKS)
        gathered.append([to_plane(mixed, shift) for shift in shifts])
    laid = lay(after(out_received, mixed, gathered[:-1]), ranks)
    out_weights = [to_core(laid, turn) for turn in range(ratio)]
    results = []
    for mixed in gathered:
        blocks = output(mixed, out_weights, owners, row_places)
        blocks = [to_rank(block, shift) for shift, block in zip(shifts, blocks)]
        results.append(sum(block.astype(jnp.float32) for block in blocks).astype(jnp.bfloat16))
    result = lax.ppermute(jnp.concatenate(results, axis=0), ("grp", "tp"), plane_pairs)
    return lax.dot_general(
        sort_rows, result, (((0,), (0,)), ((), ())), preferred_element_type=jnp.float32
    ).astype(jnp.bfloat16)


def solution(mesh):
    return jax.shard_map(
        local,
        mesh=mesh,
        in_specs=(
            P("grp", "tp"),
            P(("grp", "tp"), None),
            P(None, ("grp", "tp")),
            P("grp", None, "tp", None),
            P("grp", None, "tp", None),
            P("grp"),
            P("grp"),
        ),
        out_specs=P("grp", "tp"),
        check_vma=False,
    )
```

```python
import functools

import jax
import jax.numpy as jnp
from jax import lax
from jax.experimental import pallas as pl
from jax.experimental.pallas import tpu as pltpu
from jax.sharding import PartitionSpec as P

QUERY_HEADS = 64
KEY_VALUE_HEADS = 8
HEAD_SIZE = 128
HEAD_GROUP = QUERY_HEADS // KEY_VALUE_HEADS


EPS = 1e-06
ROPE_BASE = 1000000.0
LOG2_E = 1.4426950408889634
MASKED = -1e30
MIB = 1024 * 1024


def rotary_tables(positions):
    half = HEAD_SIZE // 2
    freq = ROPE_BASE ** (-jnp.arange(half, dtype=jnp.float32) * 2.0 / HEAD_SIZE)
    angle = positions.astype(jnp.float32)[:, None] * freq[None, :]
    cosine, sine = (jnp.cos(angle), jnp.sin(angle))
    return jnp.concatenate([cosine, cosine], axis=1), jnp.concatenate([-sine, sine], axis=1)


def column_tile(width):
    return next(tile for tile in (512, 640, 256, 128) if width % tile == 0)


def normalize_kernel(count, place_ref, *refs):
    xs, outs, held = refs[:count], refs[count : 2 * count], refs[2 * count]
    values = [ref[...].astype(jnp.float32) for ref in xs]
    total = sum(jnp.sum(value * value, axis=-1, keepdims=True) for value in values)
    factor = lax.rsqrt(total / (count * xs[0].shape[1]) + EPS)
    for n, value in enumerate(values):
        held[place_ref[n]] = (value * factor).astype(held.dtype)
    for n, out_ref in enumerate(outs):
        out_ref[...] = held[n]


def normalize(xs, places):
    count = len(xs)
    return pl.pallas_call(
        functools.partial(normalize_kernel, count),
        grid_spec=pltpu.PrefetchScalarGridSpec(
            num_scalar_prefetch=1,
            grid=(),
            in_specs=[pl.BlockSpec(memory_space=pltpu.VMEM)] * count,
            out_specs=[pl.BlockSpec(memory_space=pltpu.VMEM)] * count,
            scratch_shapes=[pltpu.VMEM((count,) + xs[0].shape, jnp.bfloat16)],
        ),
        out_shape=[jax.ShapeDtypeStruct(xs[0].shape, jnp.bfloat16)] * count,
        compiler_params=pltpu.CompilerParams(vmem_limit_bytes=48 * MIB),
        name="normalize",
    )(places, *xs)


def lay_kernel(count, place_ref, *refs):
    pieces, (out_ref, sems) = refs[:count], refs[count:]
    rows = pieces[0].shape[0]
    copies = []
    for n, piece in enumerate(pieces):
        start = pl.multiple_of(place_ref[n] * rows, 16)
        copies.append(pltpu.make_async_copy(piece, out_ref.at[pl.ds(start, rows)], sems.at[n]))
    for copy in copies:
        copy.start()
    for copy in copies:
        copy.wait()


def lay(pieces, places):
    count = len(pieces)
    rows, width = pieces[0].shape
    if rows % 16:
        whole = jnp.zeros((count * rows, width), pieces[0].dtype)
        for n, piece in enumerate(pieces):
            whole = lax.dynamic_update_slice_in_dim(whole, piece, places[n] * rows, 0)
        return whole
    return pl.pallas_call(
        functools.partial(lay_kernel, count),
        grid_spec=pltpu.PrefetchScalarGridSpec(
            num_scalar_prefetch=1,
            grid=(),
            in_specs=[pl.BlockSpec(memory_space=pl.ANY)] * count,
            out_specs=pl.BlockSpec(memory_space=pltpu.VMEM),
            scratch_shapes=[pltpu.SemaphoreType.DMA((count,))],
        ),
        out_shape=jax.ShapeDtypeStruct((count * rows, width), pieces[0].dtype),
        compiler_params=pltpu.CompilerParams(vmem_limit_bytes=6 * MIB),
        cost_estimate=pl.CostEstimate(
            flops=0, bytes_accessed=4 * count * rows * width, transcendentals=0
        ),
        name="lay",
    )(places, *pieces)


def project_kernel(count, blocks, place_ref, *refs):
    xs, pieces, outs = refs[:blocks], refs[blocks : blocks + count], refs[blocks + count : -4]
    x_held, weight, x_sems, sems = refs[-4:]
    rows, width = pieces[0].shape
    height = xs[0].shape[0]
    tile = column_tile(width)
    x_copies = [
        pltpu.make_async_copy(x, x_held.at[pl.ds(n * height, height)], x_sems.at[n])
        for n, x in enumerate(xs)
    ]
    copies = []
    for c in range(width // tile):
        for n, piece in enumerate(pieces):
            start = pl.multiple_of(place_ref[n] * rows, 16)
            copies.append(
                pltpu.make_async_copy(
                    piece.at[:, pl.ds(c * tile, tile)],
                    weight.at[pl.ds(start, rows), pl.ds(c * tile, tile)],
                    sems.at[c, n],
                )
            )
    for copy in x_copies + copies:
        copy.start()
    for copy in x_copies:
        copy.wait()
    for c in range(width // tile):
        for copy in copies[c * count : (c + 1) * count]:
            copy.wait()
        lanes = slice(c * tile, (c + 1) * tile)
        result = jnp.dot(x_held[...], weight[:, lanes], preferred_element_type=jnp.float32)
        for n in range(blocks):
            outs[n][:, lanes] = result[n * height : (n + 1) * height].astype(outs[n].dtype)


def project(xs, pieces, places):
    rows, width = pieces[0].shape
    count, blocks, height = len(pieces), len(xs), xs[0].shape[0]
    tile = column_tile(width)
    return pl.pallas_call(
        functools.partial(project_kernel, count, blocks),
        grid_spec=pltpu.PrefetchScalarGridSpec(
            num_scalar_prefetch=1,
            grid=(),
            in_specs=[pl.BlockSpec(memory_space=pltpu.HBM)] * blocks
            + [pl.BlockSpec(memory_space=pl.ANY)] * count,
            out_specs=[pl.BlockSpec(memory_space=pltpu.VMEM)] * blocks,
            scratch_shapes=[
                pltpu.VMEM((blocks * height, count * rows), jnp.bfloat16),
                pltpu.VMEM((count * rows, width), jnp.bfloat16),
                pltpu.SemaphoreType.DMA((blocks,)),
                pltpu.SemaphoreType.DMA((width // tile, count)),
            ],
        ),
        out_shape=[jax.ShapeDtypeStruct((height, width), jnp.bfloat16)] * blocks,
        compiler_params=pltpu.CompilerParams(vmem_limit_bytes=48 * MIB),
        cost_estimate=pl.CostEstimate(
            flops=2 * blocks * height * count * rows * width,
            bytes_accessed=2 * count * rows * width,
            transcendentals=0,
        ),
        name="project",
    )(places, *xs, *pieces)


def output_kernel(count, blocks, place_ref, x_place_ref, *refs):
    xs, pieces, outs = refs[:blocks], refs[blocks : blocks + count], refs[blocks + count : -4]
    x_held, weight, x_sems, sems = refs[-4:]
    rows = pieces[0].shape[0]
    height = xs[0].shape[0]
    copies = []
    for n, x in enumerate(xs):
        start = pl.multiple_of(x_place_ref[n] * height, 16)
        copies.append(pltpu.make_async_copy(x, x_held.at[pl.ds(start, height)], x_sems.at[n]))
    for n, piece in enumerate(pieces):
        start = pl.multiple_of(place_ref[n] * rows, 16)
        copies.append(pltpu.make_async_copy(piece, weight.at[pl.ds(start, rows)], sems.at[n]))
    for copy in copies:
        copy.start()
    for copy in copies:
        copy.wait()
    width = count * rows
    tile = next(size for size in (256, 320, 128) if width % size == 0)
    for c in range(width // tile):
        result = lax.dot_general(
            x_held[...],
            weight[c * tile : (c + 1) * tile],
            (((1,), (1,)), ((), ())),
            preferred_element_type=jnp.float32,
        )
        for n in range(blocks):
            outs[n][:, c * tile : (c + 1) * tile] = result[n * height : (n + 1) * height].astype(
                outs[n].dtype
            )


def output(xs, pieces, places, x_places):
    rows, depth = pieces[0].shape
    count, blocks, height = len(pieces), len(xs), xs[0].shape[0]
    return pl.pallas_call(
        functools.partial(output_kernel, count, blocks),
        grid_spec=pltpu.PrefetchScalarGridSpec(
            num_scalar_prefetch=2,
            grid=(),
            in_specs=[pl.BlockSpec(memory_space=pl.ANY)] * (blocks + count),
            out_specs=[pl.BlockSpec(memory_space=pltpu.VMEM)] * blocks,
            scratch_shapes=[
                pltpu.VMEM((blocks * height, depth), jnp.bfloat16),
                pltpu.VMEM((count * rows, depth), jnp.bfloat16),
                pltpu.SemaphoreType.DMA((blocks,)),
                pltpu.SemaphoreType.DMA((count,)),
            ],
        ),
        out_shape=[jax.ShapeDtypeStruct((height, count * rows), jnp.bfloat16)] * blocks,
        compiler_params=pltpu.CompilerParams(vmem_limit_bytes=48 * MIB),
        cost_estimate=pl.CostEstimate(
            flops=2 * blocks * height * count * rows * depth,
            bytes_accessed=2 * count * rows * depth,
            transcendentals=0,
        ),
        name="output",
    )(places, x_places, *xs, *pieces)


def attention_kernel(kv_local, terms, samples, *refs):
    partials = [refs[h * terms : (h + 1) * terms] for h in range(kv_local)]
    refs = refs[kv_local * terms :]
    cos_ref, sin_ref, lens_ref, k_ref, v_ref, out_ref, scores = refs
    together, length, _ = k_ref.shape
    scale = HEAD_SIZE ** (-0.5) * LOG2_E
    group = HEAD_GROUP * samples
    tile = 1024
    cosine, sine = cos_ref[...], sin_ref[...]
    lane = lax.broadcasted_iota(jnp.int32, (group, HEAD_SIZE), 1) % kv_local

    queries, owns, fresh = [], [], []
    for term_refs in partials:
        proj = sum(ref[...].astype(jnp.float32) for ref in term_refs)

        def head(index):
            vec = proj[:, index * HEAD_SIZE : (index + 1) * HEAD_SIZE]
            vec = vec * lax.rsqrt(jnp.mean(vec * vec, axis=-1, keepdims=True) + EPS)
            vec = vec * cosine + pltpu.roll(vec, HEAD_SIZE // 2, 1) * sine
            return vec.astype(jnp.bfloat16).astype(jnp.float32)

        new_key = head(HEAD_GROUP)
        new_value = proj[:, (HEAD_GROUP + 1) * HEAD_SIZE : (HEAD_GROUP + 2) * HEAD_SIZE]
        fresh.append(new_value.astype(jnp.bfloat16).astype(jnp.float32))
        queries.append([head(j) for j in range(HEAD_GROUP)])
        owns.append([jnp.sum(q * new_key, axis=-1, keepdims=True) for q in queries[-1]])

    class Prompt:
        def __init__(self, u):
            self.u = u
            self.rows = slice(u * samples, (u + 1) * samples)
            self.query = jnp.concatenate(
                [q[self.rows] for head_queries in queries for q in head_queries], axis=0
            ).astype(jnp.bfloat16)
            self.own = [
                jnp.concatenate([o[self.rows] for o in head_owns], axis=0) for head_owns in owns
            ]
            self.lens = lens_ref[self.rows, 0:1] * kv_local
            self.most = jnp.full((group, HEAD_SIZE), MASKED, jnp.float32)
            self.sums = jnp.zeros((group, HEAD_SIZE), jnp.float32)
            self.mixed = jnp.zeros((kv_local * group, HEAD_SIZE), jnp.float32)

        def score(self, c):
            part = lax.dot_general(
                self.query,
                k_ref[self.u, c : c + tile],
                (((1,), (1,)), ((), ())),
                preferred_element_type=jnp.float32,
            )
            for d in range(0, tile, HEAD_SIZE):
                dense = part[:group, d : d + HEAD_SIZE]
                for h in range(1, kv_local):
                    other = part[h * group : (h + 1) * group, d : d + HEAD_SIZE]
                    dense = jnp.where(lane == h, other, dense)
                slots = lax.broadcasted_iota(jnp.int32, (samples, HEAD_SIZE), 1) + (c + d)
                bias = jnp.where(slots < self.lens, 0.0, MASKED)
                dense = (dense.reshape(HEAD_GROUP, samples, HEAD_SIZE) + bias[None]).reshape(
                    group, HEAD_SIZE
                )
                scores[self.u, :, c + d : c + d + HEAD_SIZE] = dense
                self.most = jnp.maximum(self.most, dense)

        def find_top(self):
            self.tops = [
                jnp.maximum(
                    jnp.max(jnp.where(lane == h, self.most, MASKED), axis=-1, keepdims=True),
                    self.own[h],
                )
                for h in range(kv_local)
            ]
            self.top = jnp.broadcast_to(self.tops[0], (group, HEAD_SIZE))
            for h in range(1, kv_local):
                self.top = jnp.where(lane == h, self.tops[h], self.top)

        def mix(self, c):
            weights = [[] for _ in range(kv_local)]
            for d in range(0, tile, HEAD_SIZE):
                score = scores[self.u, :, c + d : c + d + HEAD_SIZE]
                expo = jnp.exp2((score - self.top) * scale)
                self.sums = self.sums + expo
                for h in range(kv_local):
                    kept = expo if kv_local == 1 else jnp.where(lane == h, expo, 0.0)
                    weights[h].append(kept.astype(jnp.bfloat16))
            weights = jnp.concatenate([jnp.concatenate(w, axis=1) for w in weights], axis=0)
            self.mixed = self.mixed + jnp.dot(
                weights, v_ref[self.u, c : c + tile], preferred_element_type=jnp.float32
            )

        def result(self):
            line = []
            for h in range(kv_local):
                own_expo = jnp.exp2((self.own[h] - self.tops[h]) * scale)
                kept = jnp.where(lane == h, self.sums, 0.0)
                inverse = 1.0 / (jnp.sum(kept, axis=-1, keepdims=True) + own_expo)
                own_weight = own_expo * inverse
                value = fresh[h][self.rows]
                for j in range(HEAD_GROUP):
                    at = slice(j * samples, (j + 1) * samples)
                    part = self.mixed[h * group + j * samples : h * group + (j + 1) * samples]
                    line.append(part * inverse[at] + own_weight[at] * value)
            return jnp.concatenate(line, axis=1)

    line_up = [Prompt(u) for u in range(together)]
    for u in range(together + 1):
        for c in range(0, length, tile):
            if u < together:
                line_up[u].score(c)
            if u > 0:
                line_up[u - 1].mix(c)
        if u < together:
            line_up[u].find_top()
    results = [prompt.result() for prompt in line_up]
    out_ref[...] = jnp.concatenate(results, axis=0).astype(out_ref.dtype)


def attention(partials, cosine, sine, lens, k_cache, value_cache, chunk, chunks):
    rows, width = partials[0][0].shape
    kv_local, terms = len(partials), len(partials[0])
    prompts, length, _ = k_cache.shape
    samples = rows // prompts
    together = 16 // samples
    height = together * samples
    heads = kv_local * HEAD_GROUP
    steps = prompts // together // chunks
    first = chunk * steps
    small = pl.BlockSpec((height, HEAD_SIZE), lambda i: (i + first, 0))
    cache = pl.BlockSpec((together, length, HEAD_SIZE), lambda i: (i + first, 0, 0))
    return pl.pallas_call(
        functools.partial(attention_kernel, kv_local, terms, samples),
        grid=(steps,),
        in_specs=[pl.BlockSpec((height, width), lambda i: (i + first, 0))] * (kv_local * terms)
        + [small] * 3
        + [cache] * 2,
        out_specs=pl.BlockSpec((height, heads * HEAD_SIZE), lambda i: (i, 0)),
        out_shape=jax.ShapeDtypeStruct((rows // chunks, heads * HEAD_SIZE), jnp.bfloat16),
        scratch_shapes=[pltpu.VMEM((together, HEAD_GROUP * samples, length), jnp.float32)],
        compiler_params=pltpu.CompilerParams(vmem_limit_bytes=48 * MIB),
        cost_estimate=pl.CostEstimate(
            flops=4 * steps * together * heads * samples * length * HEAD_SIZE,
            bytes_accessed=4 * steps * together * length * HEAD_SIZE,
            transcendentals=steps * together * HEAD_GROUP * samples * length,
        ),
        name="attention",
    )(*[term for head_terms in partials for term in head_terms], cosine, sine, lens, k_cache, value_cache)


CHUNKS = 2


def after(value, *others):
    return lax.optimization_barrier((value, others))[0]


def local(hidden, query_key_value_weight, w_out, k_cache, value_cache, lengths, assign):
    tp_count = lax.axis_size("tp")
    grp_count = lax.axis_size("grp")
    ratio = grp_count // tp_count
    t = lax.axis_index("tp")
    plane = lax.axis_index("grp") // ratio
    core = lax.axis_index("grp") % ratio
    row_count, width = hidden.shape
    prompts, context, kv_local, _ = k_cache.shape
    shifts = range(tp_count)

    def to_rank(value, shift):
        if shift == 0:
            return value
        return lax.ppermute(value, "tp", [(i, i ^ shift) for i in range(tp_count)])

    def to_plane(value, shift):
        if shift == 0:
            return value
        pairs = [(i, ((i // ratio) ^ shift) * ratio + i % ratio) for i in range(grp_count)]
        return lax.ppermute(value, "grp", pairs)

    def to_core(value, turn):
        if turn == 0:
            return value
        pairs = [(i, i // ratio * ratio + (i + turn) % ratio) for i in range(grp_count)]
        return lax.ppermute(value, "grp", pairs)

    index = jnp.arange(row_count, dtype=jnp.int32)
    key = assign * row_count + index
    place = jnp.sum((key[None, :] < key[:, None]).astype(jnp.int32), axis=1)
    sort_rows = (place[None, :] == index[:, None]).astype(jnp.bfloat16)
    lens = jnp.sum(jnp.where(place[None, :] == index[:, None], lengths[None, :], 0), axis=1)
    cosine, sine = rotary_tables(lens)
    lens = jnp.broadcast_to(lens[:, None], (row_count, HEAD_SIZE))

    hidden = jnp.dot(sort_rows, hidden, preferred_element_type=jnp.float32).astype(jnp.bfloat16)
    full = [to_rank(hidden, shift) for shift in shifts]
    ranks = jnp.stack([t ^ shift for shift in shifts]).astype(jnp.int32)
    owners = jnp.stack([(core - turn) % ratio for turn in range(ratio)]).astype(jnp.int32)
    row_places = jnp.stack([plane ^ t ^ shift for shift in shifts]).astype(jnp.int32)
    head_width = query_key_value_weight.shape[1] // (tp_count * kv_local)
    slices, source = [], query_key_value_weight
    for h in range(kv_local):
        slices.append(
            [
                lax.dynamic_slice_in_dim(
                    source, ((t ^ shift) * kv_local + h) * head_width, head_width, 1
                )
                for shift in shifts
            ]
        )
        source = after(query_key_value_weight, slices[h])
    full = after(full, slices)
    normed = normalize(full, row_places)
    features = [to_plane(block, shift) for shift, block in zip(shifts, normed)]

    def exchanged(parts):
        return [to_rank(part, shift) for shift, part in zip(shifts, parts)]

    coming = exchanged(slices[0])
    received = after(coming, features)
    partials = []
    for h in range(kv_local):
        laid = lay(received, ranks)
        if h + 1 < kv_local:
            coming = exchanged(after(slices[h + 1], received))
        blocks = project(features, [to_core(laid, turn) for turn in range(ratio)], owners)
        partials.append([to_plane(block, shift) for shift, block in zip(shifts, blocks)])
        if h + 1 < kv_local:
            received = after(coming, partials[h])

    depth = w_out.shape[0] // tp_count
    source = after(w_out, coming)
    out_received = []
    for shift in shifts:
        if shift > 2:
            source = after(source, out_received[1])
        part = lax.dynamic_slice_in_dim(source, (t ^ shift) * depth, depth, 0).T
        out_received.append(to_rank(part, shift))

    keys = k_cache.reshape(prompts, context * kv_local, HEAD_SIZE)
    values = value_cache.reshape(prompts, context * kv_local, HEAD_SIZE)
    plane_pairs = [
        (g * tp_count + r, (r * ratio + g % ratio) * tp_count + g // ratio)
        for g in range(grp_count)
        for r in range(tp_count)
    ]
    gathered = []
    for chunk in range(CHUNKS):
        if chunk > 0:
            lens = after(lens, mixed, out_received)
        mixed = attention(partials, cosine, sine, lens, keys, values, chunk, CHUNKS)
        gathered.append([to_plane(mixed, shift) for shift in shifts])
    laid = lay(after(out_received, mixed, gathered[:-1]), ranks)
    out_weights = [to_core(laid, turn) for turn in range(ratio)]
    results = []
    for mixed in gathered:
        if results:
            mixed = after(mixed, blocks)
        blocks = output(mixed, out_weights, owners, row_places)
        blocks = [to_rank(block, shift) for shift, block in zip(shifts, blocks)]
        results.append(sum(block.astype(jnp.float32) for block in blocks).astype(jnp.bfloat16))
    result = lax.ppermute(jnp.concatenate(results, axis=0), ("grp", "tp"), plane_pairs)
    return lax.dot_general(
        sort_rows, result, (((0,), (0,)), ((), ())), preferred_element_type=jnp.float32
    ).astype(jnp.bfloat16)


def solution(mesh):
    return jax.shard_map(
        local,
        mesh=mesh,
        in_specs=(
            P("grp", "tp"),
            P(("grp", "tp"), None),
            P(None, ("grp", "tp")),
            P("grp", None, "tp", None),
            P("grp", None, "tp", None),
            P("grp"),
            P("grp"),
        ),
        out_specs=P("grp", "tp"),
        check_vma=False,
    )
```

```python
import functools

import jax
import jax.numpy as jnp
from jax import lax
from jax.experimental import pallas as pl
from jax.experimental.pallas import tpu as pltpu
from jax.sharding import PartitionSpec as P

QUERY_HEADS = 64
KEY_VALUE_HEADS = 8
HEAD_SIZE = 128
HEAD_GROUP = QUERY_HEADS // KEY_VALUE_HEADS


EPS = 1e-06
ROPE_BASE = 1000000.0
LOG2_E = 1.4426950408889634
MASKED = -1e30
MIB = 1024 * 1024


def rotary_tables(positions):
    half = HEAD_SIZE // 2
    freq = ROPE_BASE ** (-jnp.arange(half, dtype=jnp.float32) * 2.0 / HEAD_SIZE)
    angle = positions.astype(jnp.float32)[:, None] * freq[None, :]
    cosine, sine = (jnp.cos(angle), jnp.sin(angle))
    return jnp.concatenate([cosine, cosine], axis=1), jnp.concatenate([-sine, sine], axis=1)


def column_tile(width):
    return next(tile for tile in (512, 640, 256, 128) if width % tile == 0)


def normalize_kernel(count, place_ref, *refs):
    xs, outs, held = refs[:count], refs[count : 2 * count], refs[2 * count]
    values = [ref[...].astype(jnp.float32) for ref in xs]
    total = sum(jnp.sum(value * value, axis=-1, keepdims=True) for value in values)
    factor = lax.rsqrt(total / (count * xs[0].shape[1]) + EPS)
    for n, value in enumerate(values):
        held[place_ref[n]] = (value * factor).astype(held.dtype)
    for n, out_ref in enumerate(outs):
        out_ref[...] = held[n]


def normalize(xs, places):
    count = len(xs)
    return pl.pallas_call(
        functools.partial(normalize_kernel, count),
        grid_spec=pltpu.PrefetchScalarGridSpec(
            num_scalar_prefetch=1,
            grid=(),
            in_specs=[pl.BlockSpec(memory_space=pltpu.VMEM)] * count,
            out_specs=[pl.BlockSpec(memory_space=pltpu.VMEM)] * count,
            scratch_shapes=[pltpu.VMEM((count,) + xs[0].shape, jnp.bfloat16)],
        ),
        out_shape=[jax.ShapeDtypeStruct(xs[0].shape, jnp.bfloat16)] * count,
        compiler_params=pltpu.CompilerParams(vmem_limit_bytes=48 * MIB),
        name="normalize",
    )(places, *xs)


def lay_kernel(count, first, place_ref, *refs):
    pieces, (out_ref, sems) = refs[:count], refs[count:]
    rows = pieces[0].shape[0]
    lanes = pl.ds(first, out_ref.shape[1])
    copies = []
    for n, piece in enumerate(pieces):
        start = pl.multiple_of(place_ref[n] * rows, 16)
        copies.append(
            pltpu.make_async_copy(piece.at[:, lanes], out_ref.at[pl.ds(start, rows)], sems.at[n])
        )
    for copy in copies:
        copy.start()
    for copy in copies:
        copy.wait()


def lay(pieces, places, first, width):
    count = len(pieces)
    rows = pieces[0].shape[0]
    if rows % 16:
        whole = jnp.zeros((count * rows, width), pieces[0].dtype)
        for n, piece in enumerate(pieces):
            piece = piece[:, first : first + width]
            whole = lax.dynamic_update_slice_in_dim(whole, piece, places[n] * rows, 0)
        return whole
    return pl.pallas_call(
        functools.partial(lay_kernel, count, first),
        grid_spec=pltpu.PrefetchScalarGridSpec(
            num_scalar_prefetch=1,
            grid=(),
            in_specs=[pl.BlockSpec(memory_space=pl.ANY)] * count,
            out_specs=pl.BlockSpec(memory_space=pltpu.VMEM),
            scratch_shapes=[pltpu.SemaphoreType.DMA((count,))],
        ),
        out_shape=jax.ShapeDtypeStruct((count * rows, width), pieces[0].dtype),
        compiler_params=pltpu.CompilerParams(vmem_limit_bytes=6 * MIB),
        cost_estimate=pl.CostEstimate(
            flops=0, bytes_accessed=4 * count * rows * width, transcendentals=0
        ),
        name="lay",
    )(places, *pieces)


def project_kernel(count, blocks, place_ref, *refs):
    xs, pieces, outs = refs[:blocks], refs[blocks : blocks + count], refs[blocks + count : -2]
    weight, sems = refs[-2:]
    rows = pieces[0].shape[0]
    height, width = outs[0].shape
    tile = column_tile(width)
    copies = []
    for c in range(width // tile):
        for n, piece in enumerate(pieces):
            start = pl.multiple_of(place_ref[n] * rows, 16)
            copy = pltpu.make_async_copy(
                piece.at[:, pl.ds(c * tile, tile)],
                weight.at[pl.ds(start, rows), pl.ds(c * tile, tile)],
                sems.at[c, n],
            )
            copy.start()
            copies.append(copy)
    x = jnp.concatenate([ref[...] for ref in xs], axis=0)
    for c in range(width // tile):
        for copy in copies[c * count : (c + 1) * count]:
            copy.wait()
        lanes = slice(c * tile, (c + 1) * tile)
        result = jnp.dot(x, weight[:, lanes], preferred_element_type=jnp.float32)
        for n in range(blocks):
            outs[n][:, lanes] = result[n * height : (n + 1) * height].astype(outs[n].dtype)


def project(xs, pieces, places):
    rows, width = pieces[0].shape
    count, blocks, height = len(pieces), len(xs), xs[0].shape[0]
    tile = column_tile(width)
    return pl.pallas_call(
        functools.partial(project_kernel, count, blocks),
        grid_spec=pltpu.PrefetchScalarGridSpec(
            num_scalar_prefetch=1,
            grid=(),
            in_specs=[pl.BlockSpec(memory_space=pltpu.VMEM)] * blocks
            + [pl.BlockSpec(memory_space=pl.ANY)] * count,
            out_specs=[pl.BlockSpec(memory_space=pltpu.VMEM)] * blocks,
            scratch_shapes=[
                pltpu.VMEM((count * rows, width), jnp.bfloat16),
                pltpu.SemaphoreType.DMA((width // tile, count)),
            ],
        ),
        out_shape=[jax.ShapeDtypeStruct((height, width), jnp.bfloat16)] * blocks,
        compiler_params=pltpu.CompilerParams(vmem_limit_bytes=48 * MIB),
        cost_estimate=pl.CostEstimate(
            flops=2 * blocks * height * count * rows * width,
            bytes_accessed=2 * count * rows * width,
            transcendentals=0,
        ),
        name="project",
    )(places, *xs, *pieces)


def output_kernel(count, blocks, place_ref, x_place_ref, *refs):
    xs, pieces, outs = refs[:blocks], refs[blocks : blocks + count], refs[blocks + count : -4]
    x_held, weight, x_sems, sems = refs[-4:]
    rows = pieces[0].shape[0]
    height = xs[0].shape[0]
    copies = []
    for n, x in enumerate(xs):
        start = pl.multiple_of(x_place_ref[n] * height, 16)
        copies.append(pltpu.make_async_copy(x, x_held.at[pl.ds(start, height)], x_sems.at[n]))
    for n, piece in enumerate(pieces):
        start = pl.multiple_of(place_ref[n] * rows, 16)
        copies.append(pltpu.make_async_copy(piece, weight.at[pl.ds(start, rows)], sems.at[n]))
    for copy in copies:
        copy.start()
    for copy in copies:
        copy.wait()
    width = count * rows
    tile = next(size for size in (256, 320, 128) if width % size == 0)
    for c in range(width // tile):
        result = lax.dot_general(
            x_held[...],
            weight[c * tile : (c + 1) * tile],
            (((1,), (1,)), ((), ())),
            preferred_element_type=jnp.float32,
        )
        for n in range(blocks):
            outs[n][:, c * tile : (c + 1) * tile] = result[n * height : (n + 1) * height].astype(
                outs[n].dtype
            )


def output(xs, pieces, places, x_places):
    rows, depth = pieces[0].shape
    count, blocks, height = len(pieces), len(xs), xs[0].shape[0]
    return pl.pallas_call(
        functools.partial(output_kernel, count, blocks),
        grid_spec=pltpu.PrefetchScalarGridSpec(
            num_scalar_prefetch=2,
            grid=(),
            in_specs=[pl.BlockSpec(memory_space=pl.ANY)] * (blocks + count),
            out_specs=[pl.BlockSpec(memory_space=pltpu.VMEM)] * blocks,
            scratch_shapes=[
                pltpu.VMEM((blocks * height, depth), jnp.bfloat16),
                pltpu.VMEM((count * rows, depth), jnp.bfloat16),
                pltpu.SemaphoreType.DMA((blocks,)),
                pltpu.SemaphoreType.DMA((count,)),
            ],
        ),
        out_shape=[jax.ShapeDtypeStruct((height, count * rows), jnp.bfloat16)] * blocks,
        compiler_params=pltpu.CompilerParams(vmem_limit_bytes=48 * MIB),
        cost_estimate=pl.CostEstimate(
            flops=2 * blocks * height * count * rows * depth,
            bytes_accessed=2 * count * rows * depth,
            transcendentals=0,
        ),
        name="output",
    )(places, x_places, *xs, *pieces)


def attention_kernel(kv_local, terms, samples, *refs):
    partials = [refs[h * terms : (h + 1) * terms] for h in range(kv_local)]
    refs = refs[kv_local * terms :]
    cos_ref, sin_ref, lens_ref, k_ref, v_ref, out_ref, scores = refs
    together, length, _ = k_ref.shape
    scale = HEAD_SIZE ** (-0.5) * LOG2_E
    group = HEAD_GROUP * samples
    tile = 1024
    cosine, sine = cos_ref[...], sin_ref[...]
    lane = lax.broadcasted_iota(jnp.int32, (group, HEAD_SIZE), 1) % kv_local

    queries, owns, fresh = [], [], []
    for term_refs in partials:
        proj = sum(ref[...].astype(jnp.float32) for ref in term_refs)

        def head(index):
            vec = proj[:, index * HEAD_SIZE : (index + 1) * HEAD_SIZE]
            vec = vec * lax.rsqrt(jnp.mean(vec * vec, axis=-1, keepdims=True) + EPS)
            vec = vec * cosine + pltpu.roll(vec, HEAD_SIZE // 2, 1) * sine
            return vec.astype(jnp.bfloat16).astype(jnp.float32)

        new_key = head(HEAD_GROUP)
        new_value = proj[:, (HEAD_GROUP + 1) * HEAD_SIZE : (HEAD_GROUP + 2) * HEAD_SIZE]
        fresh.append(new_value.astype(jnp.bfloat16).astype(jnp.float32))
        queries.append([head(j) for j in range(HEAD_GROUP)])
        owns.append([jnp.sum(q * new_key, axis=-1, keepdims=True) for q in queries[-1]])

    class Prompt:
        def __init__(self, u):
            self.u = u
            self.rows = slice(u * samples, (u + 1) * samples)
            self.query = jnp.concatenate(
                [q[self.rows] for head_queries in queries for q in head_queries], axis=0
            ).astype(jnp.bfloat16)
            self.own = [
                jnp.concatenate([o[self.rows] for o in head_owns], axis=0) for head_owns in owns
            ]
            self.lens = lens_ref[self.rows, 0:1] * kv_local
            self.most = jnp.full((group, HEAD_SIZE), MASKED, jnp.float32)
            self.sums = jnp.zeros((group, HEAD_SIZE), jnp.float32)
            self.mixed = jnp.zeros((kv_local * group, HEAD_SIZE), jnp.float32)

        def score(self, c):
            part = lax.dot_general(
                self.query,
                k_ref[self.u, c : c + tile],
                (((1,), (1,)), ((), ())),
                preferred_element_type=jnp.float32,
            )
            for d in range(0, tile, HEAD_SIZE):
                dense = part[:group, d : d + HEAD_SIZE]
                for h in range(1, kv_local):
                    other = part[h * group : (h + 1) * group, d : d + HEAD_SIZE]
                    dense = jnp.where(lane == h, other, dense)
                slots = lax.broadcasted_iota(jnp.int32, (samples, HEAD_SIZE), 1) + (c + d)
                bias = jnp.where(slots < self.lens, 0.0, MASKED)
                dense = (dense.reshape(HEAD_GROUP, samples, HEAD_SIZE) + bias[None]).reshape(
                    group, HEAD_SIZE
                )
                scores[self.u, :, c + d : c + d + HEAD_SIZE] = dense
                self.most = jnp.maximum(self.most, dense)

        def find_top(self):
            self.tops = [
                jnp.maximum(
                    jnp.max(jnp.where(lane == h, self.most, MASKED), axis=-1, keepdims=True),
                    self.own[h],
                )
                for h in range(kv_local)
            ]
            self.top = jnp.broadcast_to(self.tops[0], (group, HEAD_SIZE))
            for h in range(1, kv_local):
                self.top = jnp.where(lane == h, self.tops[h], self.top)

        def mix(self, c):
            weights = [[] for _ in range(kv_local)]
            for d in range(0, tile, HEAD_SIZE):
                score = scores[self.u, :, c + d : c + d + HEAD_SIZE]
                expo = jnp.exp2((score - self.top) * scale)
                self.sums = self.sums + expo
                for h in range(kv_local):
                    kept = expo if kv_local == 1 else jnp.where(lane == h, expo, 0.0)
                    weights[h].append(kept.astype(jnp.bfloat16))
            weights = jnp.concatenate([jnp.concatenate(w, axis=1) for w in weights], axis=0)
            self.mixed = self.mixed + jnp.dot(
                weights, v_ref[self.u, c : c + tile], preferred_element_type=jnp.float32
            )

        def result(self):
            line = []
            for h in range(kv_local):
                own_expo = jnp.exp2((self.own[h] - self.tops[h]) * scale)
                kept = jnp.where(lane == h, self.sums, 0.0)
                inverse = 1.0 / (jnp.sum(kept, axis=-1, keepdims=True) + own_expo)
                own_weight = own_expo * inverse
                value = fresh[h][self.rows]
                for j in range(HEAD_GROUP):
                    at = slice(j * samples, (j + 1) * samples)
                    part = self.mixed[h * group + j * samples : h * group + (j + 1) * samples]
                    line.append(part * inverse[at] + own_weight[at] * value)
            return jnp.concatenate(line, axis=1)

    line_up = [Prompt(u) for u in range(together)]
    for u in range(together + 1):
        for c in range(0, length, tile):
            if u < together:
                line_up[u].score(c)
            if u > 0:
                line_up[u - 1].mix(c)
        if u < together:
            line_up[u].find_top()
    results = [prompt.result() for prompt in line_up]
    out_ref[...] = jnp.concatenate(results, axis=0).astype(out_ref.dtype)


def attention(partials, cosine, sine, lens, k_cache, value_cache, chunk, chunks):
    rows, width = partials[0][0].shape
    kv_local, terms = len(partials), len(partials[0])
    prompts, length, _ = k_cache.shape
    samples = rows // prompts
    together = 16 // samples
    height = together * samples
    heads = kv_local * HEAD_GROUP
    steps = prompts // together // chunks
    first = chunk * steps
    small = pl.BlockSpec((height, HEAD_SIZE), lambda i: (i + first, 0))
    cache = pl.BlockSpec((together, length, HEAD_SIZE), lambda i: (i + first, 0, 0))
    return pl.pallas_call(
        functools.partial(attention_kernel, kv_local, terms, samples),
        grid=(steps,),
        in_specs=[pl.BlockSpec((height, width), lambda i: (i + first, 0))] * (kv_local * terms)
        + [small] * 3
        + [cache] * 2,
        out_specs=pl.BlockSpec((height, heads * HEAD_SIZE), lambda i: (i, 0)),
        out_shape=jax.ShapeDtypeStruct((rows // chunks, heads * HEAD_SIZE), jnp.bfloat16),
        scratch_shapes=[pltpu.VMEM((together, HEAD_GROUP * samples, length), jnp.float32)],
        compiler_params=pltpu.CompilerParams(vmem_limit_bytes=48 * MIB),
        cost_estimate=pl.CostEstimate(
            flops=4 * steps * together * heads * samples * length * HEAD_SIZE,
            bytes_accessed=4 * steps * together * length * HEAD_SIZE,
            transcendentals=steps * together * HEAD_GROUP * samples * length,
        ),
        name="attention",
    )(*[term for head_terms in partials for term in head_terms], cosine, sine, lens, k_cache, value_cache)


CHUNKS = 2


def after(value, *others):
    return lax.optimization_barrier((value, others))[0]


def local(hidden, query_key_value_weight, w_out, k_cache, value_cache, lengths, assign):
    tp_count = lax.axis_size("tp")
    grp_count = lax.axis_size("grp")
    ratio = grp_count // tp_count
    t = lax.axis_index("tp")
    plane = lax.axis_index("grp") // ratio
    core = lax.axis_index("grp") % ratio
    row_count, width = hidden.shape
    prompts, context, kv_local, _ = k_cache.shape
    shifts = range(tp_count)

    def to_rank(value, shift):
        if shift == 0:
            return value
        return lax.ppermute(value, "tp", [(i, i ^ shift) for i in range(tp_count)])

    def to_plane(value, shift):
        if shift == 0:
            return value
        pairs = [(i, ((i // ratio) ^ shift) * ratio + i % ratio) for i in range(grp_count)]
        return lax.ppermute(value, "grp", pairs)

    def to_core(value, turn):
        if turn == 0:
            return value
        pairs = [(i, i // ratio * ratio + (i + turn) % ratio) for i in range(grp_count)]
        return lax.ppermute(value, "grp", pairs)

    index = jnp.arange(row_count, dtype=jnp.int32)
    key = assign * row_count + index
    place = jnp.sum((key[None, :] < key[:, None]).astype(jnp.int32), axis=1)
    sort_rows = (place[None, :] == index[:, None]).astype(jnp.bfloat16)
    lens = jnp.sum(jnp.where(place[None, :] == index[:, None], lengths[None, :], 0), axis=1)
    cosine, sine = rotary_tables(lens)
    lens = jnp.broadcast_to(lens[:, None], (row_count, HEAD_SIZE))

    hidden = jnp.dot(sort_rows, hidden, preferred_element_type=jnp.float32).astype(jnp.bfloat16)
    ranks = jnp.stack([t ^ shift for shift in shifts]).astype(jnp.int32)
    owners = jnp.stack([(core - turn) % ratio for turn in range(ratio)]).astype(jnp.int32)
    row_places = jnp.stack([plane ^ t ^ shift for shift in shifts]).astype(jnp.int32)
    size = query_key_value_weight.shape[1] // tp_count
    slices = [
        lax.dynamic_slice_in_dim(query_key_value_weight, (t ^ shift) * size, size, 1)
        for shift in shifts
    ]
    hidden = after(hidden, slices)
    full = [to_rank(hidden, shift) for shift in shifts]
    received = [to_rank(part, shift) for shift, part in zip(shifts, slices)]
    normed = normalize(full, row_places)
    features = [to_plane(block, shift) for shift, block in zip(shifts, normed)]
    received = after(received, features)

    head_width = size // kv_local
    partials = []
    for h in range(kv_local):
        laid = lay(received, ranks, h * head_width, head_width)
        blocks = project(features, [to_core(laid, turn) for turn in range(ratio)], owners)
        partials.append([to_plane(block, shift) for shift, block in zip(shifts, blocks)])

    depth = w_out.shape[0] // tp_count
    source = after(w_out, partials[0])
    out_received = [
        to_rank(lax.dynamic_slice_in_dim(source, (t ^ shift) * depth, depth, 0).T, shift)
        for shift in shifts
    ]

    keys = k_cache.reshape(prompts, context * kv_local, HEAD_SIZE)
    values = value_cache.reshape(prompts, context * kv_local, HEAD_SIZE)
    plane_pairs = [
        (g * tp_count + r, (r * ratio + g % ratio) * tp_count + g // ratio)
        for g in range(grp_count)
        for r in range(tp_count)
    ]
    gathered = []
    for chunk in range(CHUNKS):
        if chunk > 0:
            lens = after(lens, mixed, out_received)
        mixed = attention(partials, cosine, sine, lens, keys, values, chunk, CHUNKS)
        gathered.append([to_plane(mixed, shift) for shift in shifts])
    laid = lay(after(out_received, mixed, gathered[:-1]), ranks, 0, depth)
    out_weights = [to_core(laid, turn) for turn in range(ratio)]
    results = []
    for mixed in gathered:
        if results:
            mixed = after(mixed, blocks)
        blocks = output(mixed, out_weights, owners, row_places)
        blocks = [to_rank(block, shift) for shift, block in zip(shifts, blocks)]
        results.append(sum(block.astype(jnp.float32) for block in blocks).astype(jnp.bfloat16))
    result = lax.ppermute(jnp.concatenate(results, axis=0), ("grp", "tp"), plane_pairs)
    return lax.dot_general(
        sort_rows, result, (((0,), (0,)), ((), ())), preferred_element_type=jnp.float32
    ).astype(jnp.bfloat16)


def solution(mesh):
    return jax.shard_map(
        local,
        mesh=mesh,
        in_specs=(
            P("grp", "tp"),
            P(("grp", "tp"), None),
            P(None, ("grp", "tp")),
            P("grp", None, "tp", None),
            P("grp", None, "tp", None),
            P("grp"),
            P("grp"),
        ),
        out_specs=P("grp", "tp"),
        check_vma=False,
    )
```

```python
import functools

import jax
import jax.numpy as jnp
from jax import lax
from jax.experimental import pallas as pl
from jax.experimental.pallas import tpu as pltpu
from jax.sharding import PartitionSpec as P

QUERY_HEADS = 64
KEY_VALUE_HEADS = 8
HEAD_SIZE = 128
HEAD_GROUP = QUERY_HEADS // KEY_VALUE_HEADS


EPS = 1e-06
ROPE_BASE = 1000000.0
LOG2_E = 1.4426950408889634
MASKED = -1e30
MIB = 1024 * 1024


def rotary_tables(positions):
    half = HEAD_SIZE // 2
    freq = ROPE_BASE ** (-jnp.arange(half, dtype=jnp.float32) * 2.0 / HEAD_SIZE)
    angle = positions.astype(jnp.float32)[:, None] * freq[None, :]
    cosine, sine = (jnp.cos(angle), jnp.sin(angle))
    return jnp.concatenate([cosine, cosine], axis=1), jnp.concatenate([-sine, sine], axis=1)


def column_tile(width):
    return next(tile for tile in (512, 640, 256, 128) if width % tile == 0)


def normalize_kernel(count, place_ref, *refs):
    xs, outs, held = refs[:count], refs[count : 2 * count], refs[2 * count]
    values = [ref[...].astype(jnp.float32) for ref in xs]
    total = sum(jnp.sum(value * value, axis=-1, keepdims=True) for value in values)
    factor = lax.rsqrt(total / (count * xs[0].shape[1]) + EPS)
    for n, value in enumerate(values):
        held[place_ref[n]] = (value * factor).astype(held.dtype)
    for n, out_ref in enumerate(outs):
        out_ref[...] = held[n]


def normalize(xs, places):
    count = len(xs)
    return pl.pallas_call(
        functools.partial(normalize_kernel, count),
        grid_spec=pltpu.PrefetchScalarGridSpec(
            num_scalar_prefetch=1,
            grid=(),
            in_specs=[pl.BlockSpec(memory_space=pltpu.VMEM)] * count,
            out_specs=[pl.BlockSpec(memory_space=pltpu.VMEM)] * count,
            scratch_shapes=[pltpu.VMEM((count,) + xs[0].shape, jnp.bfloat16)],
        ),
        out_shape=[jax.ShapeDtypeStruct(xs[0].shape, jnp.bfloat16)] * count,
        compiler_params=pltpu.CompilerParams(vmem_limit_bytes=48 * MIB),
        name="normalize",
    )(places, *xs)


def lay_kernel(count, first, place_ref, *refs):
    pieces, (out_ref, sems) = refs[:count], refs[count:]
    rows = pieces[0].shape[0]
    lanes = pl.ds(first, out_ref.shape[1])
    copies = []
    for n, piece in enumerate(pieces):
        start = pl.multiple_of(place_ref[n] * rows, 16)
        copies.append(
            pltpu.make_async_copy(piece.at[:, lanes], out_ref.at[pl.ds(start, rows)], sems.at[n])
        )
    for copy in copies:
        copy.start()
    for copy in copies:
        copy.wait()


def lay(pieces, places, first, width):
    count = len(pieces)
    rows = pieces[0].shape[0]
    if rows % 16:
        whole = jnp.zeros((count * rows, width), pieces[0].dtype)
        for n, piece in enumerate(pieces):
            piece = piece[:, first : first + width]
            whole = lax.dynamic_update_slice_in_dim(whole, piece, places[n] * rows, 0)
        return whole
    return pl.pallas_call(
        functools.partial(lay_kernel, count, first),
        grid_spec=pltpu.PrefetchScalarGridSpec(
            num_scalar_prefetch=1,
            grid=(),
            in_specs=[pl.BlockSpec(memory_space=pl.ANY)] * count,
            out_specs=pl.BlockSpec(memory_space=pltpu.VMEM),
            scratch_shapes=[pltpu.SemaphoreType.DMA((count,))],
        ),
        out_shape=jax.ShapeDtypeStruct((count * rows, width), pieces[0].dtype),
        compiler_params=pltpu.CompilerParams(vmem_limit_bytes=6 * MIB),
        cost_estimate=pl.CostEstimate(
            flops=0, bytes_accessed=4 * count * rows * width, transcendentals=0
        ),
        name="lay",
    )(places, *pieces)


def project_kernel(count, place_ref, x_ref, *refs):
    pieces, outs, (weight, sems) = refs[:count], refs[count:-2], refs[-2:]
    rows = pieces[0].shape[0]
    height, width = outs[0].shape
    tile = column_tile(width)
    copies = []
    for c in range(width // tile):
        for n, piece in enumerate(pieces):
            start = pl.multiple_of(place_ref[n] * rows, 16)
            copy = pltpu.make_async_copy(
                piece.at[:, pl.ds(c * tile, tile)],
                weight.at[pl.ds(start, rows), pl.ds(c * tile, tile)],
                sems.at[c, n],
            )
            copy.start()
            copies.append(copy)
    for c in range(width // tile):
        for copy in copies[c * count : (c + 1) * count]:
            copy.wait()
        lanes = slice(c * tile, (c + 1) * tile)
        result = jnp.dot(x_ref[...], weight[:, lanes], preferred_element_type=jnp.float32)
        for n, out_ref in enumerate(outs):
            out_ref[:, lanes] = result[n * height : (n + 1) * height].astype(out_ref.dtype)


def project(x, pieces, places, blocks):
    rows, width = pieces[0].shape
    count, height = len(pieces), x.shape[0] // blocks
    tile = column_tile(width)
    return pl.pallas_call(
        functools.partial(project_kernel, count),
        grid_spec=pltpu.PrefetchScalarGridSpec(
            num_scalar_prefetch=1,
            grid=(),
            in_specs=[pl.BlockSpec(memory_space=pltpu.VMEM)]
            + [pl.BlockSpec(memory_space=pl.ANY)] * count,
            out_specs=[pl.BlockSpec(memory_space=pltpu.VMEM)] * blocks,
            scratch_shapes=[
                pltpu.VMEM((count * rows, width), jnp.bfloat16),
                pltpu.SemaphoreType.DMA((width // tile, count)),
            ],
        ),
        out_shape=[jax.ShapeDtypeStruct((height, width), jnp.bfloat16)] * blocks,
        compiler_params=pltpu.CompilerParams(vmem_limit_bytes=48 * MIB),
        cost_estimate=pl.CostEstimate(
            flops=2 * blocks * height * count * rows * width,
            bytes_accessed=2 * count * rows * width,
            transcendentals=0,
        ),
        name="project",
    )(places, x, *pieces)


def output_kernel(count, blocks, place_ref, x_place_ref, *refs):
    xs, pieces, outs = refs[:blocks], refs[blocks : blocks + count], refs[blocks + count : -4]
    x_held, weight, x_sems, sems = refs[-4:]
    rows = pieces[0].shape[0]
    height = xs[0].shape[0]
    copies = []
    for n, x in enumerate(xs):
        start = pl.multiple_of(x_place_ref[n] * height, 16)
        copies.append(pltpu.make_async_copy(x, x_held.at[pl.ds(start, height)], x_sems.at[n]))
    for n, piece in enumerate(pieces):
        start = pl.multiple_of(place_ref[n] * rows, 16)
        copies.append(pltpu.make_async_copy(piece, weight.at[pl.ds(start, rows)], sems.at[n]))
    for copy in copies:
        copy.start()
    for copy in copies:
        copy.wait()
    width = count * rows
    tile = next(size for size in (256, 320, 128) if width % size == 0)
    for c in range(width // tile):
        result = lax.dot_general(
            x_held[...],
            weight[c * tile : (c + 1) * tile],
            (((1,), (1,)), ((), ())),
            preferred_element_type=jnp.float32,
        )
        for n in range(blocks):
            outs[n][:, c * tile : (c + 1) * tile] = result[n * height : (n + 1) * height].astype(
                outs[n].dtype
            )


def output(xs, pieces, places, x_places):
    rows, depth = pieces[0].shape
    count, blocks, height = len(pieces), len(xs), xs[0].shape[0]
    return pl.pallas_call(
        functools.partial(output_kernel, count, blocks),
        grid_spec=pltpu.PrefetchScalarGridSpec(
            num_scalar_prefetch=2,
            grid=(),
            in_specs=[pl.BlockSpec(memory_space=pl.ANY)] * (blocks + count),
            out_specs=[pl.BlockSpec(memory_space=pltpu.VMEM)] * blocks,
            scratch_shapes=[
                pltpu.VMEM((blocks * height, depth), jnp.bfloat16),
                pltpu.VMEM((count * rows, depth), jnp.bfloat16),
                pltpu.SemaphoreType.DMA((blocks,)),
                pltpu.SemaphoreType.DMA((count,)),
            ],
        ),
        out_shape=[jax.ShapeDtypeStruct((height, count * rows), jnp.bfloat16)] * blocks,
        compiler_params=pltpu.CompilerParams(vmem_limit_bytes=48 * MIB),
        cost_estimate=pl.CostEstimate(
            flops=2 * blocks * height * count * rows * depth,
            bytes_accessed=2 * count * rows * depth,
            transcendentals=0,
        ),
        name="output",
    )(places, x_places, *xs, *pieces)


def attention_kernel(kv_local, terms, samples, *refs):
    partials = [refs[h * terms : (h + 1) * terms] for h in range(kv_local)]
    refs = refs[kv_local * terms :]
    cos_ref, sin_ref, lens_ref, k_ref, v_ref, out_ref, scores = refs
    together, length, _ = k_ref.shape
    scale = HEAD_SIZE ** (-0.5) * LOG2_E
    group = HEAD_GROUP * samples
    tile = 1024
    cosine, sine = cos_ref[...], sin_ref[...]
    lane = lax.broadcasted_iota(jnp.int32, (group, HEAD_SIZE), 1) % kv_local

    queries, owns, fresh = [], [], []
    for term_refs in partials:
        proj = sum(ref[...].astype(jnp.float32) for ref in term_refs)

        def head(index):
            vec = proj[:, index * HEAD_SIZE : (index + 1) * HEAD_SIZE]
            vec = vec * lax.rsqrt(jnp.mean(vec * vec, axis=-1, keepdims=True) + EPS)
            vec = vec * cosine + pltpu.roll(vec, HEAD_SIZE // 2, 1) * sine
            return vec.astype(jnp.bfloat16).astype(jnp.float32)

        new_key = head(HEAD_GROUP)
        new_value = proj[:, (HEAD_GROUP + 1) * HEAD_SIZE : (HEAD_GROUP + 2) * HEAD_SIZE]
        fresh.append(new_value.astype(jnp.bfloat16).astype(jnp.float32))
        queries.append([head(j) for j in range(HEAD_GROUP)])
        owns.append([jnp.sum(q * new_key, axis=-1, keepdims=True) for q in queries[-1]])

    class Prompt:
        def __init__(self, u):
            self.u = u
            self.rows = slice(u * samples, (u + 1) * samples)
            self.query = jnp.concatenate(
                [q[self.rows] for head_queries in queries for q in head_queries], axis=0
            ).astype(jnp.bfloat16)
            self.own = [
                jnp.concatenate([o[self.rows] for o in head_owns], axis=0) for head_owns in owns
            ]
            self.lens = lens_ref[self.rows, 0:1] * kv_local
            self.most = jnp.full((group, HEAD_SIZE), MASKED, jnp.float32)
            self.sums = jnp.zeros((group, HEAD_SIZE), jnp.float32)
            self.mixed = jnp.zeros((kv_local * group, HEAD_SIZE), jnp.float32)

        def score(self, c):
            part = lax.dot_general(
                self.query,
                k_ref[self.u, c : c + tile],
                (((1,), (1,)), ((), ())),
                preferred_element_type=jnp.float32,
            )
            for d in range(0, tile, HEAD_SIZE):
                dense = part[:group, d : d + HEAD_SIZE]
                for h in range(1, kv_local):
                    other = part[h * group : (h + 1) * group, d : d + HEAD_SIZE]
                    dense = jnp.where(lane == h, other, dense)
                slots = lax.broadcasted_iota(jnp.int32, (samples, HEAD_SIZE), 1) + (c + d)
                bias = jnp.where(slots < self.lens, 0.0, MASKED)
                dense = (dense.reshape(HEAD_GROUP, samples, HEAD_SIZE) + bias[None]).reshape(
                    group, HEAD_SIZE
                )
                scores[self.u, :, c + d : c + d + HEAD_SIZE] = dense
                self.most = jnp.maximum(self.most, dense)

        def find_top(self):
            self.tops = [
                jnp.maximum(
                    jnp.max(jnp.where(lane == h, self.most, MASKED), axis=-1, keepdims=True),
                    self.own[h],
                )
                for h in range(kv_local)
            ]
            self.top = jnp.broadcast_to(self.tops[0], (group, HEAD_SIZE))
            for h in range(1, kv_local):
                self.top = jnp.where(lane == h, self.tops[h], self.top)

        def mix(self, c):
            weights = [[] for _ in range(kv_local)]
            for d in range(0, tile, HEAD_SIZE):
                score = scores[self.u, :, c + d : c + d + HEAD_SIZE]
                expo = jnp.exp2((score - self.top) * scale)
                self.sums = self.sums + expo
                for h in range(kv_local):
                    kept = expo if kv_local == 1 else jnp.where(lane == h, expo, 0.0)
                    weights[h].append(kept.astype(jnp.bfloat16))
            weights = jnp.concatenate([jnp.concatenate(w, axis=1) for w in weights], axis=0)
            self.mixed = self.mixed + jnp.dot(
                weights, v_ref[self.u, c : c + tile], preferred_element_type=jnp.float32
            )

        def result(self):
            line = []
            for h in range(kv_local):
                own_expo = jnp.exp2((self.own[h] - self.tops[h]) * scale)
                kept = jnp.where(lane == h, self.sums, 0.0)
                inverse = 1.0 / (jnp.sum(kept, axis=-1, keepdims=True) + own_expo)
                own_weight = own_expo * inverse
                value = fresh[h][self.rows]
                for j in range(HEAD_GROUP):
                    at = slice(j * samples, (j + 1) * samples)
                    part = self.mixed[h * group + j * samples : h * group + (j + 1) * samples]
                    line.append(part * inverse[at] + own_weight[at] * value)
            return jnp.concatenate(line, axis=1)

    line_up = [Prompt(u) for u in range(together)]
    for u in range(together + 1):
        for c in range(0, length, tile):
            if u < together:
                line_up[u].score(c)
            if u > 0:
                line_up[u - 1].mix(c)
        if u < together:
            line_up[u].find_top()
    results = [prompt.result() for prompt in line_up]
    out_ref[...] = jnp.concatenate(results, axis=0).astype(out_ref.dtype)


def attention(partials, cosine, sine, lens, k_cache, value_cache, chunk, chunks):
    rows, width = partials[0][0].shape
    kv_local, terms = len(partials), len(partials[0])
    prompts, length, _ = k_cache.shape
    samples = rows // prompts
    together = 16 // samples
    height = together * samples
    heads = kv_local * HEAD_GROUP
    steps = prompts // together // chunks
    first = chunk * steps
    small = pl.BlockSpec((height, HEAD_SIZE), lambda i: (i + first, 0))
    cache = pl.BlockSpec((together, length, HEAD_SIZE), lambda i: (i + first, 0, 0))
    return pl.pallas_call(
        functools.partial(attention_kernel, kv_local, terms, samples),
        grid=(steps,),
        in_specs=[pl.BlockSpec((height, width), lambda i: (i + first, 0))] * (kv_local * terms)
        + [small] * 3
        + [cache] * 2,
        out_specs=pl.BlockSpec((height, heads * HEAD_SIZE), lambda i: (i, 0)),
        out_shape=jax.ShapeDtypeStruct((rows // chunks, heads * HEAD_SIZE), jnp.bfloat16),
        scratch_shapes=[pltpu.VMEM((together, HEAD_GROUP * samples, length), jnp.float32)],
        compiler_params=pltpu.CompilerParams(vmem_limit_bytes=48 * MIB),
        cost_estimate=pl.CostEstimate(
            flops=4 * steps * together * heads * samples * length * HEAD_SIZE,
            bytes_accessed=4 * steps * together * length * HEAD_SIZE,
            transcendentals=steps * together * HEAD_GROUP * samples * length,
        ),
        name="attention",
    )(*[term for head_terms in partials for term in head_terms], cosine, sine, lens, k_cache, value_cache)


CHUNKS = 2


def after(value, *others):
    return lax.optimization_barrier((value, others))[0]


def local(hidden, query_key_value_weight, w_out, k_cache, value_cache, lengths, assign):
    tp_count = lax.axis_size("tp")
    grp_count = lax.axis_size("grp")
    ratio = grp_count // tp_count
    t = lax.axis_index("tp")
    plane = lax.axis_index("grp") // ratio
    core = lax.axis_index("grp") % ratio
    row_count, width = hidden.shape
    prompts, context, kv_local, _ = k_cache.shape
    shifts = range(tp_count)

    def to_rank(value, shift):
        if shift == 0:
            return value
        return lax.ppermute(value, "tp", [(i, i ^ shift) for i in range(tp_count)])

    def to_plane(value, shift):
        if shift == 0:
            return value
        pairs = [(i, ((i // ratio) ^ shift) * ratio + i % ratio) for i in range(grp_count)]
        return lax.ppermute(value, "grp", pairs)

    def to_core(value, turn):
        if turn == 0:
            return value
        pairs = [(i, i // ratio * ratio + (i + turn) % ratio) for i in range(grp_count)]
        return lax.ppermute(value, "grp", pairs)

    index = jnp.arange(row_count, dtype=jnp.int32)
    key = assign * row_count + index
    place = jnp.sum((key[None, :] < key[:, None]).astype(jnp.int32), axis=1)
    sort_rows = (place[None, :] == index[:, None]).astype(jnp.bfloat16)
    lens = jnp.sum(jnp.where(place[None, :] == index[:, None], lengths[None, :], 0), axis=1)
    cosine, sine = rotary_tables(lens)
    lens = jnp.broadcast_to(lens[:, None], (row_count, HEAD_SIZE))

    hidden = jnp.dot(sort_rows, hidden, preferred_element_type=jnp.float32).astype(jnp.bfloat16)
    full = [to_rank(hidden, shift) for shift in shifts]
    ranks = jnp.stack([t ^ shift for shift in shifts]).astype(jnp.int32)
    owners = jnp.stack([(core - turn) % ratio for turn in range(ratio)]).astype(jnp.int32)
    row_places = jnp.stack([plane ^ t ^ shift for shift in shifts]).astype(jnp.int32)
    head_width = query_key_value_weight.shape[1] // (tp_count * kv_local)
    slices, source = [], query_key_value_weight
    for h in range(kv_local):
        slices.append(
            [
                lax.dynamic_slice_in_dim(
                    source, ((t ^ shift) * kv_local + h) * head_width, head_width, 1
                )
                for shift in shifts
            ]
        )
        source = after(query_key_value_weight, slices[h])
    full = after(full, slices)
    normed = normalize(full, row_places)
    features = [to_plane(block, shift) for shift, block in zip(shifts, normed)]

    def exchanged(parts):
        return [to_rank(part, shift) for shift, part in zip(shifts, parts)]

    coming = exchanged(slices[0])
    received = after(coming, features)
    features = lay(features, jnp.arange(tp_count, dtype=jnp.int32), 0, width)
    partials = []
    for h in range(kv_local):
        laid = lay(received, ranks, 0, head_width)
        if h + 1 < kv_local:
            coming = exchanged(after(slices[h + 1], received))
        laid = [to_core(laid, turn) for turn in range(ratio)]
        blocks = project(features, laid, owners, tp_count)
        partials.append([to_plane(block, shift) for shift, block in zip(shifts, blocks)])
        if h + 1 < kv_local:
            received = after(coming, partials[h][1:3])

    depth = w_out.shape[0] // tp_count
    source = after(w_out, coming)
    parts = [lax.dynamic_slice_in_dim(source, (t ^ shift) * depth, depth, 0).T for shift in shifts]
    out_received = exchanged(after(parts, partials))

    keys = k_cache.reshape(prompts, context * kv_local, HEAD_SIZE)
    values = value_cache.reshape(prompts, context * kv_local, HEAD_SIZE)
    plane_pairs = [
        (g * tp_count + r, (r * ratio + g % ratio) * tp_count + g // ratio)
        for g in range(grp_count)
        for r in range(tp_count)
    ]
    gathered = []
    for chunk in range(CHUNKS):
        if chunk > 0:
            lens = after(lens, mixed, out_received[1])
        mixed = attention(partials, cosine, sine, lens, keys, values, chunk, CHUNKS)
        gathered.append([to_plane(mixed, shift) for shift in shifts])
    laid = lay(after(out_received, mixed, gathered[:-1]), ranks, 0, depth)
    out_weights = [to_core(laid, turn) for turn in range(ratio)]
    results = []
    for mixed in gathered:
        if results:
            mixed = after(mixed, blocks)
        blocks = output(mixed, out_weights, owners, row_places)
        blocks = [to_rank(block, shift) for shift, block in zip(shifts, blocks)]
        results.append(sum(block.astype(jnp.float32) for block in blocks).astype(jnp.bfloat16))
    result = lax.ppermute(jnp.concatenate(results, axis=0), ("grp", "tp"), plane_pairs)
    return lax.dot_general(
        sort_rows, result, (((0,), (0,)), ((), ())), preferred_element_type=jnp.float32
    ).astype(jnp.bfloat16)


def solution(mesh):
    return jax.shard_map(
        local,
        mesh=mesh,
        in_specs=(
            P("grp", "tp"),
            P(("grp", "tp"), None),
            P(None, ("grp", "tp")),
            P("grp", None, "tp", None),
            P("grp", None, "tp", None),
            P("grp"),
            P("grp"),
        ),
        out_specs=P("grp", "tp"),
        check_vma=False,
    )
```

```python
import functools

import jax
import jax.numpy as jnp
from jax import lax
from jax.experimental import pallas as pl
from jax.experimental.pallas import tpu as pltpu
from jax.sharding import PartitionSpec as P

QUERY_HEADS = 64
KEY_VALUE_HEADS = 8
HEAD_SIZE = 128
HEAD_GROUP = QUERY_HEADS // KEY_VALUE_HEADS


EPS = 1e-06
ROPE_BASE = 1000000.0
LOG2_E = 1.4426950408889634
MASKED = -1e30
MIB = 1024 * 1024


def rotary_tables(positions):
    half = HEAD_SIZE // 2
    freq = ROPE_BASE ** (-jnp.arange(half, dtype=jnp.float32) * 2.0 / HEAD_SIZE)
    angle = positions.astype(jnp.float32)[:, None] * freq[None, :]
    cosine, sine = (jnp.cos(angle), jnp.sin(angle))
    return jnp.concatenate([cosine, cosine], axis=1), jnp.concatenate([-sine, sine], axis=1)


def column_tile(width):
    return next(tile for tile in (512, 640, 256, 128) if width % tile == 0)


def normalize_kernel(count, place_ref, *refs):
    xs, outs, held = refs[:count], refs[count : 2 * count], refs[2 * count]
    values = [ref[...].astype(jnp.float32) for ref in xs]
    total = sum(jnp.sum(value * value, axis=-1, keepdims=True) for value in values)
    factor = lax.rsqrt(total / (count * xs[0].shape[1]) + EPS)
    for n, value in enumerate(values):
        held[place_ref[n]] = (value * factor).astype(held.dtype)
    for n, out_ref in enumerate(outs):
        out_ref[...] = held[n]


def normalize(xs, places):
    count = len(xs)
    return pl.pallas_call(
        functools.partial(normalize_kernel, count),
        grid_spec=pltpu.PrefetchScalarGridSpec(
            num_scalar_prefetch=1,
            grid=(),
            in_specs=[pl.BlockSpec(memory_space=pltpu.VMEM)] * count,
            out_specs=[pl.BlockSpec(memory_space=pltpu.VMEM)] * count,
            scratch_shapes=[pltpu.VMEM((count,) + xs[0].shape, jnp.bfloat16)],
        ),
        out_shape=[jax.ShapeDtypeStruct(xs[0].shape, jnp.bfloat16)] * count,
        compiler_params=pltpu.CompilerParams(vmem_limit_bytes=48 * MIB),
        name="normalize",
    )(places, *xs)


def lay_kernel(count, first, place_ref, *refs):
    pieces, (out_ref, sems) = refs[:count], refs[count:]
    rows = pieces[0].shape[0]
    lanes = pl.ds(first, out_ref.shape[1])
    copies = []
    for n, piece in enumerate(pieces):
        start = pl.multiple_of(place_ref[n] * rows, 16)
        copies.append(
            pltpu.make_async_copy(piece.at[:, lanes], out_ref.at[pl.ds(start, rows)], sems.at[n])
        )
    for copy in copies:
        copy.start()
    for copy in copies:
        copy.wait()


def lay(pieces, places, first, width):
    count = len(pieces)
    rows = pieces[0].shape[0]
    if rows % 16:
        whole = jnp.zeros((count * rows, width), pieces[0].dtype)
        for n, piece in enumerate(pieces):
            piece = piece[:, first : first + width]
            whole = lax.dynamic_update_slice_in_dim(whole, piece, places[n] * rows, 0)
        return whole
    return pl.pallas_call(
        functools.partial(lay_kernel, count, first),
        grid_spec=pltpu.PrefetchScalarGridSpec(
            num_scalar_prefetch=1,
            grid=(),
            in_specs=[pl.BlockSpec(memory_space=pl.ANY)] * count,
            out_specs=pl.BlockSpec(memory_space=pltpu.VMEM),
            scratch_shapes=[pltpu.SemaphoreType.DMA((count,))],
        ),
        out_shape=jax.ShapeDtypeStruct((count * rows, width), pieces[0].dtype),
        compiler_params=pltpu.CompilerParams(vmem_limit_bytes=6 * MIB),
        cost_estimate=pl.CostEstimate(
            flops=0, bytes_accessed=4 * count * rows * width, transcendentals=0
        ),
        name="lay",
    )(places, *pieces)


def project_kernel(count, groups, place_ref, x_ref, *refs):
    pieces, outs, (weight, sems) = refs[:count], refs[count:-2], refs[-2:]
    rows = pieces[0].shape[0]
    width = outs[0].shape[1]
    height = x_ref.shape[0] // sum(len(group) for group in groups)
    tile = column_tile(width)
    copies = []
    for c in range(width // tile):
        for n, piece in enumerate(pieces):
            start = pl.multiple_of(place_ref[n] * rows, 16)
            copy = pltpu.make_async_copy(
                piece.at[:, pl.ds(c * tile, tile)],
                weight.at[pl.ds(start, rows), pl.ds(c * tile, tile)],
                sems.at[c, n],
            )
            copy.start()
            copies.append(copy)
    for c in range(width // tile):
        for copy in copies[c * count : (c + 1) * count]:
            copy.wait()
        lanes = slice(c * tile, (c + 1) * tile)
        result = jnp.dot(x_ref[...], weight[:, lanes], preferred_element_type=jnp.float32)
        result = result.astype(jnp.bfloat16)
        for group, out_ref in zip(groups, outs):
            for at, n in enumerate(group):
                out_ref[at * height : (at + 1) * height, lanes] = result[
                    n * height : (n + 1) * height
                ]


def project(x, pieces, places, groups):
    rows, width = pieces[0].shape
    count, blocks = len(pieces), sum(len(group) for group in groups)
    height = x.shape[0] // blocks
    tile = column_tile(width)
    return pl.pallas_call(
        functools.partial(project_kernel, count, groups),
        grid_spec=pltpu.PrefetchScalarGridSpec(
            num_scalar_prefetch=1,
            grid=(),
            in_specs=[pl.BlockSpec(memory_space=pltpu.VMEM)]
            + [pl.BlockSpec(memory_space=pl.ANY)] * count,
            out_specs=[pl.BlockSpec(memory_space=pltpu.VMEM)] * len(groups),
            scratch_shapes=[
                pltpu.VMEM((count * rows, width), jnp.bfloat16),
                pltpu.SemaphoreType.DMA((width // tile, count)),
            ],
        ),
        out_shape=[
            jax.ShapeDtypeStruct((len(group) * height, width), jnp.bfloat16) for group in groups
        ],
        compiler_params=pltpu.CompilerParams(vmem_limit_bytes=48 * MIB),
        cost_estimate=pl.CostEstimate(
            flops=2 * blocks * height * count * rows * width,
            bytes_accessed=2 * count * rows * width,
            transcendentals=0,
        ),
        name="project",
    )(places, x, *pieces)


def output_kernel(count, blocks, place_ref, x_place_ref, *refs):
    xs, pieces, outs = refs[:blocks], refs[blocks : blocks + count], refs[blocks + count : -4]
    x_held, weight, x_sems, sems = refs[-4:]
    rows = pieces[0].shape[0]
    height = xs[0].shape[0]
    copies = []
    for n, x in enumerate(xs):
        start = pl.multiple_of(x_place_ref[n] * height, 16)
        copies.append(pltpu.make_async_copy(x, x_held.at[pl.ds(start, height)], x_sems.at[n]))
    for n, piece in enumerate(pieces):
        start = pl.multiple_of(place_ref[n] * rows, 16)
        copies.append(pltpu.make_async_copy(piece, weight.at[pl.ds(start, rows)], sems.at[n]))
    for copy in copies:
        copy.start()
    for copy in copies:
        copy.wait()
    width = count * rows
    tile = next(size for size in (256, 320, 128) if width % size == 0)
    for c in range(width // tile):
        result = lax.dot_general(
            x_held[...],
            weight[c * tile : (c + 1) * tile],
            (((1,), (1,)), ((), ())),
            preferred_element_type=jnp.float32,
        )
        for n in range(blocks):
            outs[n][:, c * tile : (c + 1) * tile] = result[n * height : (n + 1) * height].astype(
                outs[n].dtype
            )


def output(xs, pieces, places, x_places):
    rows, depth = pieces[0].shape
    count, blocks, height = len(pieces), len(xs), xs[0].shape[0]
    return pl.pallas_call(
        functools.partial(output_kernel, count, blocks),
        grid_spec=pltpu.PrefetchScalarGridSpec(
            num_scalar_prefetch=2,
            grid=(),
            in_specs=[pl.BlockSpec(memory_space=pl.ANY)] * (blocks + count),
            out_specs=[pl.BlockSpec(memory_space=pltpu.VMEM)] * blocks,
            scratch_shapes=[
                pltpu.VMEM((blocks * height, depth), jnp.bfloat16),
                pltpu.VMEM((count * rows, depth), jnp.bfloat16),
                pltpu.SemaphoreType.DMA((blocks,)),
                pltpu.SemaphoreType.DMA((count,)),
            ],
        ),
        out_shape=[jax.ShapeDtypeStruct((height, count * rows), jnp.bfloat16)] * blocks,
        compiler_params=pltpu.CompilerParams(vmem_limit_bytes=48 * MIB),
        cost_estimate=pl.CostEstimate(
            flops=2 * blocks * height * count * rows * depth,
            bytes_accessed=2 * count * rows * depth,
            transcendentals=0,
        ),
        name="output",
    )(places, x_places, *xs, *pieces)


def attention_kernel(terms, samples, *refs):
    kv_local, partials = len(terms), []
    for count in terms:
        partials.append(refs[:count])
        refs = refs[count:]
    cos_ref, sin_ref, lens_ref, k_ref, v_ref, out_ref, scores = refs
    together, length, _ = k_ref.shape
    scale = HEAD_SIZE ** (-0.5) * LOG2_E
    group = HEAD_GROUP * samples
    tile = 1024
    cosine, sine = cos_ref[...], sin_ref[...]
    lane = lax.broadcasted_iota(jnp.int32, (group, HEAD_SIZE), 1) % kv_local

    queries, owns, fresh = [], [], []
    for term_refs in partials:
        proj = sum(ref[...].astype(jnp.float32) for ref in term_refs)

        def head(index):
            vec = proj[:, index * HEAD_SIZE : (index + 1) * HEAD_SIZE]
            vec = vec * lax.rsqrt(jnp.mean(vec * vec, axis=-1, keepdims=True) + EPS)
            vec = vec * cosine + pltpu.roll(vec, HEAD_SIZE // 2, 1) * sine
            return vec.astype(jnp.bfloat16).astype(jnp.float32)

        new_key = head(HEAD_GROUP)
        new_value = proj[:, (HEAD_GROUP + 1) * HEAD_SIZE : (HEAD_GROUP + 2) * HEAD_SIZE]
        fresh.append(new_value.astype(jnp.bfloat16).astype(jnp.float32))
        queries.append([head(j) for j in range(HEAD_GROUP)])
        owns.append([jnp.sum(q * new_key, axis=-1, keepdims=True) for q in queries[-1]])

    class Prompt:
        def __init__(self, u):
            self.u = u
            self.rows = slice(u * samples, (u + 1) * samples)
            self.query = jnp.concatenate(
                [q[self.rows] for head_queries in queries for q in head_queries], axis=0
            ).astype(jnp.bfloat16)
            self.own = [
                jnp.concatenate([o[self.rows] for o in head_owns], axis=0) for head_owns in owns
            ]
            self.lens = lens_ref[self.rows, 0:1] * kv_local
            self.most = jnp.full((group, HEAD_SIZE), MASKED, jnp.float32)
            self.sums = jnp.zeros((group, HEAD_SIZE), jnp.float32)
            self.mixed = jnp.zeros((kv_local * group, HEAD_SIZE), jnp.float32)

        def score(self, c):
            part = lax.dot_general(
                self.query,
                k_ref[self.u, c : c + tile],
                (((1,), (1,)), ((), ())),
                preferred_element_type=jnp.float32,
            )
            for d in range(0, tile, HEAD_SIZE):
                dense = part[:group, d : d + HEAD_SIZE]
                for h in range(1, kv_local):
                    other = part[h * group : (h + 1) * group, d : d + HEAD_SIZE]
                    dense = jnp.where(lane == h, other, dense)
                slots = lax.broadcasted_iota(jnp.int32, (samples, HEAD_SIZE), 1) + (c + d)
                bias = jnp.where(slots < self.lens, 0.0, MASKED)
                dense = (dense.reshape(HEAD_GROUP, samples, HEAD_SIZE) + bias[None]).reshape(
                    group, HEAD_SIZE
                )
                scores[self.u, :, c + d : c + d + HEAD_SIZE] = dense
                self.most = jnp.maximum(self.most, dense)

        def find_top(self):
            self.tops = [
                jnp.maximum(
                    jnp.max(jnp.where(lane == h, self.most, MASKED), axis=-1, keepdims=True),
                    self.own[h],
                )
                for h in range(kv_local)
            ]
            self.top = jnp.broadcast_to(self.tops[0], (group, HEAD_SIZE))
            for h in range(1, kv_local):
                self.top = jnp.where(lane == h, self.tops[h], self.top)

        def mix(self, c):
            weights = [[] for _ in range(kv_local)]
            for d in range(0, tile, HEAD_SIZE):
                score = scores[self.u, :, c + d : c + d + HEAD_SIZE]
                expo = jnp.exp2((score - self.top) * scale)
                self.sums = self.sums + expo
                for h in range(kv_local):
                    kept = expo if kv_local == 1 else jnp.where(lane == h, expo, 0.0)
                    weights[h].append(kept.astype(jnp.bfloat16))
            weights = jnp.concatenate([jnp.concatenate(w, axis=1) for w in weights], axis=0)
            self.mixed = self.mixed + jnp.dot(
                weights, v_ref[self.u, c : c + tile], preferred_element_type=jnp.float32
            )

        def result(self):
            line = []
            for h in range(kv_local):
                own_expo = jnp.exp2((self.own[h] - self.tops[h]) * scale)
                kept = jnp.where(lane == h, self.sums, 0.0)
                inverse = 1.0 / (jnp.sum(kept, axis=-1, keepdims=True) + own_expo)
                own_weight = own_expo * inverse
                value = fresh[h][self.rows]
                for j in range(HEAD_GROUP):
                    at = slice(j * samples, (j + 1) * samples)
                    part = self.mixed[h * group + j * samples : h * group + (j + 1) * samples]
                    line.append(part * inverse[at] + own_weight[at] * value)
            return jnp.concatenate(line, axis=1)

    line_up = [Prompt(u) for u in range(together)]
    for u in range(together + 1):
        for c in range(0, length, tile):
            if u < together:
                line_up[u].score(c)
            if u > 0:
                line_up[u - 1].mix(c)
        if u < together:
            line_up[u].find_top()
    results = [prompt.result() for prompt in line_up]
    out_ref[...] = jnp.concatenate(results, axis=0).astype(out_ref.dtype)


def attention(partials, cosine, sine, lens, k_cache, value_cache, chunk, chunks):
    rows, width = cosine.shape[0], partials[0][0].shape[1]
    kv_local, terms = len(partials), [len(head_terms) for head_terms in partials]
    prompts, length, _ = k_cache.shape
    samples = rows // prompts
    together = 16 // samples
    height = together * samples
    heads = kv_local * HEAD_GROUP
    steps = prompts // together // chunks
    first = chunk * steps
    small = pl.BlockSpec((height, HEAD_SIZE), lambda i: (i + first, 0))
    cache = pl.BlockSpec((together, length, HEAD_SIZE), lambda i: (i + first, 0, 0))
    return pl.pallas_call(
        functools.partial(attention_kernel, terms, samples),
        grid=(steps,),
        in_specs=[pl.BlockSpec((height, width), lambda i: (i + first, 0))] * sum(terms)
        + [small] * 3
        + [cache] * 2,
        out_specs=pl.BlockSpec((height, heads * HEAD_SIZE), lambda i: (i, 0)),
        out_shape=jax.ShapeDtypeStruct((rows // chunks, heads * HEAD_SIZE), jnp.bfloat16),
        scratch_shapes=[pltpu.VMEM((together, HEAD_GROUP * samples, length), jnp.float32)],
        compiler_params=pltpu.CompilerParams(vmem_limit_bytes=48 * MIB),
        cost_estimate=pl.CostEstimate(
            flops=4 * steps * together * heads * samples * length * HEAD_SIZE,
            bytes_accessed=4 * steps * together * length * HEAD_SIZE,
            transcendentals=steps * together * HEAD_GROUP * samples * length,
        ),
        name="attention",
    )(*[term for head_terms in partials for term in head_terms], cosine, sine, lens, k_cache, value_cache)


CHUNKS = 2


def after(value, *others):
    return lax.optimization_barrier((value, others))[0]


def local(hidden, query_key_value_weight, w_out, k_cache, value_cache, lengths, assign):
    tp_count = lax.axis_size("tp")
    grp_count = lax.axis_size("grp")
    ratio = grp_count // tp_count
    t = lax.axis_index("tp")
    plane = lax.axis_index("grp") // ratio
    core = lax.axis_index("grp") % ratio
    row_count, width = hidden.shape
    prompts, context, kv_local, _ = k_cache.shape
    shifts = range(tp_count)

    def to_rank(value, shift):
        if shift == 0:
            return value
        return lax.ppermute(value, "tp", [(i, i ^ shift) for i in range(tp_count)])

    def to_plane(value, shift):
        if shift == 0:
            return value
        pairs = [(i, ((i // ratio) ^ shift) * ratio + i % ratio) for i in range(grp_count)]
        return lax.ppermute(value, "grp", pairs)

    def to_core(value, turn):
        if turn == 0:
            return value
        pairs = [(i, i // ratio * ratio + (i + turn) % ratio) for i in range(grp_count)]
        return lax.ppermute(value, "grp", pairs)

    def sum_by_halves(kept, sent):
        received, shift = to_plane(sent, 1), 1
        terms = [[(block, 0), (received, n * row_count)] for n, block in enumerate(kept)]
        while len(terms) > 1:
            passed = [
                sum(array[at : at + row_count].astype(jnp.float32) for array, at in pair)
                for pair in terms[1::2]
            ]
            shift *= 2
            received = to_plane(jnp.concatenate(passed, axis=0).astype(jnp.bfloat16), shift)
            terms = [pair + [(received, n * row_count)] for n, pair in enumerate(terms[::2])]
        return [array for array, _ in terms[0]]

    index = jnp.arange(row_count, dtype=jnp.int32)
    key = assign * row_count + index
    place = jnp.sum((key[None, :] < key[:, None]).astype(jnp.int32), axis=1)
    sort_rows = (place[None, :] == index[:, None]).astype(jnp.bfloat16)
    lens = jnp.sum(jnp.where(place[None, :] == index[:, None], lengths[None, :], 0), axis=1)
    cosine, sine = rotary_tables(lens)
    lens = jnp.broadcast_to(lens[:, None], (row_count, HEAD_SIZE))

    hidden = jnp.dot(sort_rows, hidden, preferred_element_type=jnp.float32).astype(jnp.bfloat16)
    full = [to_rank(hidden, shift) for shift in shifts]
    ranks = jnp.stack([t ^ shift for shift in shifts]).astype(jnp.int32)
    owners = jnp.stack([(core - turn) % ratio for turn in range(ratio)]).astype(jnp.int32)
    row_places = jnp.stack([plane ^ t ^ shift for shift in shifts]).astype(jnp.int32)
    head_width = query_key_value_weight.shape[1] // (tp_count * kv_local)
    slices, source = [], query_key_value_weight
    for h in range(kv_local):
        slices.append(
            [
                lax.dynamic_slice_in_dim(
                    source, ((t ^ shift) * kv_local + h) * head_width, head_width, 1
                )
                for shift in shifts
            ]
        )
        source = after(query_key_value_weight, slices[h])
    full = after(full, slices)
    normed = normalize(full, row_places)
    features = [to_plane(block, shift) for shift, block in zip(shifts, normed)]

    def exchanged(parts):
        return [to_rank(part, shift) for shift, part in zip(shifts, parts)]

    coming = exchanged(slices[0])
    features = lay(features, jnp.arange(tp_count, dtype=jnp.int32), 0, width)
    received = after(coming, features)
    partials = []
    for h in range(kv_local):
        laid = lay(received, ranks, 0, head_width)
        if h + 1 < kv_local:
            coming = exchanged(after(slices[h + 1], received))
        laid = [to_core(laid, turn) for turn in range(ratio)]
        if h + 1 < kv_local:
            blocks = project(features, laid, owners, [[n] for n in shifts])
            partials.append([to_plane(block, shift) for shift, block in zip(shifts, blocks)])
            received = after(coming, partials[h][1:3])
        else:
            groups = [[n] for n in shifts[::2]] + [list(shifts[1::2])]
            *blocks, sent = project(features, laid, owners, groups)
            partials.append(sum_by_halves(blocks, sent))

    depth = w_out.shape[0] // tp_count
    source = after(w_out, blocks)
    out_received = exchanged(
        [lax.dynamic_slice_in_dim(source, (t ^ shift) * depth, depth, 0).T for shift in shifts]
    )

    keys = k_cache.reshape(prompts, context * kv_local, HEAD_SIZE)
    values = value_cache.reshape(prompts, context * kv_local, HEAD_SIZE)
    plane_pairs = [
        (g * tp_count + r, (r * ratio + g % ratio) * tp_count + g // ratio)
        for g in range(grp_count)
        for r in range(tp_count)
    ]
    gathered = []
    for chunk in range(CHUNKS):
        if chunk == 1:
            laid = lay(after(out_received, mixed), ranks, 0, depth)
            out_weights = [to_core(laid, turn) for turn in range(ratio)]
            lens = after(lens, laid)
        mixed = attention(partials, cosine, sine, lens, keys, values, chunk, CHUNKS)
        gathered.append([to_plane(mixed, shift) for shift in shifts])
    results = []
    for mixed in gathered:
        if results:
            mixed = after(mixed, products)
        products = output(mixed, out_weights, owners, row_places)
        blocks = exchanged(products)
        results.append(sum(block.astype(jnp.float32) for block in blocks).astype(jnp.bfloat16))
    result = lax.ppermute(jnp.concatenate(results, axis=0), ("grp", "tp"), plane_pairs)
    return lax.dot_general(
        sort_rows, result, (((0,), (0,)), ((), ())), preferred_element_type=jnp.float32
    ).astype(jnp.bfloat16)


def solution(mesh):
    return jax.shard_map(
        local,
        mesh=mesh,
        in_specs=(
            P("grp", "tp"),
            P(("grp", "tp"), None),
            P(None, ("grp", "tp")),
            P("grp", None, "tp", None),
            P("grp", None, "tp", None),
            P("grp"),
            P("grp"),
        ),
        out_specs=P("grp", "tp"),
        check_vma=False,
    )
```

```python
import functools

import jax
import jax.numpy as jnp
from jax import lax
from jax.experimental import pallas as pl
from jax.experimental.pallas import tpu as pltpu
from jax.sharding import PartitionSpec as P

QUERY_HEADS = 64
KEY_VALUE_HEADS = 8
HEAD_SIZE = 128
HEAD_GROUP = QUERY_HEADS // KEY_VALUE_HEADS


EPS = 1e-06
ROPE_BASE = 1000000.0
LOG2_E = 1.4426950408889634
MASKED = -1e30
MIB = 1024 * 1024


def rotary_tables(positions):
    half = HEAD_SIZE // 2
    freq = ROPE_BASE ** (-jnp.arange(half, dtype=jnp.float32) * 2.0 / HEAD_SIZE)
    angle = positions.astype(jnp.float32)[:, None] * freq[None, :]
    cosine, sine = (jnp.cos(angle), jnp.sin(angle))
    return jnp.concatenate([cosine, cosine], axis=1), jnp.concatenate([-sine, sine], axis=1)


def column_tile(width):
    return next(tile for tile in (512, 640, 256, 128) if width % tile == 0)


def normalize_kernel(count, place_ref, *refs):
    xs, outs, held = refs[:count], refs[count : 2 * count], refs[2 * count]
    values = [ref[...].astype(jnp.float32) for ref in xs]
    total = sum(jnp.sum(value * value, axis=-1, keepdims=True) for value in values)
    factor = lax.rsqrt(total / (count * xs[0].shape[1]) + EPS)
    for n, value in enumerate(values):
        held[place_ref[n]] = (value * factor).astype(held.dtype)
    for n, out_ref in enumerate(outs):
        out_ref[...] = held[n]


def normalize(xs, places):
    count = len(xs)
    return pl.pallas_call(
        functools.partial(normalize_kernel, count),
        grid_spec=pltpu.PrefetchScalarGridSpec(
            num_scalar_prefetch=1,
            grid=(),
            in_specs=[pl.BlockSpec(memory_space=pltpu.VMEM)] * count,
            out_specs=[pl.BlockSpec(memory_space=pltpu.VMEM)] * count,
            scratch_shapes=[pltpu.VMEM((count,) + xs[0].shape, jnp.bfloat16)],
        ),
        out_shape=[jax.ShapeDtypeStruct(xs[0].shape, jnp.bfloat16)] * count,
        compiler_params=pltpu.CompilerParams(vmem_limit_bytes=48 * MIB),
        name="normalize",
    )(places, *xs)


def lay_kernel(count, first, place_ref, *refs):
    pieces, (out_ref, sems) = refs[:count], refs[count:]
    rows = pieces[0].shape[0]
    lanes = pl.ds(first, out_ref.shape[1])
    copies = []
    for n, piece in enumerate(pieces):
        start = pl.multiple_of(place_ref[n] * rows, 16)
        copies.append(
            pltpu.make_async_copy(piece.at[:, lanes], out_ref.at[pl.ds(start, rows)], sems.at[n])
        )
    for copy in copies:
        copy.start()
    for copy in copies:
        copy.wait()


def lay(pieces, places, first, width):
    count = len(pieces)
    rows = pieces[0].shape[0]
    if rows % 16:
        whole = jnp.zeros((count * rows, width), pieces[0].dtype)
        for n, piece in enumerate(pieces):
            piece = piece[:, first : first + width]
            whole = lax.dynamic_update_slice_in_dim(whole, piece, places[n] * rows, 0)
        return whole
    return pl.pallas_call(
        functools.partial(lay_kernel, count, first),
        grid_spec=pltpu.PrefetchScalarGridSpec(
            num_scalar_prefetch=1,
            grid=(),
            in_specs=[pl.BlockSpec(memory_space=pl.ANY)] * count,
            out_specs=pl.BlockSpec(memory_space=pltpu.VMEM),
            scratch_shapes=[pltpu.SemaphoreType.DMA((count,))],
        ),
        out_shape=jax.ShapeDtypeStruct((count * rows, width), pieces[0].dtype),
        compiler_params=pltpu.CompilerParams(vmem_limit_bytes=6 * MIB),
        cost_estimate=pl.CostEstimate(
            flops=0, bytes_accessed=4 * count * rows * width, transcendentals=0
        ),
        name="lay",
    )(places, *pieces)


def project_kernel(count, groups, place_ref, x_ref, *refs):
    pieces, outs, (weight, sems) = refs[:count], refs[count:-2], refs[-2:]
    rows = pieces[0].shape[0]
    width = outs[0].shape[1]
    height = x_ref.shape[0] // sum(len(group) for group in groups)
    tile = column_tile(width)
    copies = []
    for c in range(width // tile):
        for n, piece in enumerate(pieces):
            start = pl.multiple_of(place_ref[n] * rows, 16)
            copy = pltpu.make_async_copy(
                piece.at[:, pl.ds(c * tile, tile)],
                weight.at[pl.ds(start, rows), pl.ds(c * tile, tile)],
                sems.at[c, n],
            )
            copy.start()
            copies.append(copy)
    for c in range(width // tile):
        for copy in copies[c * count : (c + 1) * count]:
            copy.wait()
        lanes = slice(c * tile, (c + 1) * tile)
        result = jnp.dot(x_ref[...], weight[:, lanes], preferred_element_type=jnp.float32)
        result = result.astype(jnp.bfloat16)
        for group, out_ref in zip(groups, outs):
            for at, n in enumerate(group):
                out_ref[at * height : (at + 1) * height, lanes] = result[
                    n * height : (n + 1) * height
                ]


def project(x, pieces, places, groups):
    rows, width = pieces[0].shape
    count, blocks = len(pieces), sum(len(group) for group in groups)
    height = x.shape[0] // blocks
    tile = column_tile(width)
    return pl.pallas_call(
        functools.partial(project_kernel, count, groups),
        grid_spec=pltpu.PrefetchScalarGridSpec(
            num_scalar_prefetch=1,
            grid=(),
            in_specs=[pl.BlockSpec(memory_space=pltpu.VMEM)]
            + [pl.BlockSpec(memory_space=pl.ANY)] * count,
            out_specs=[pl.BlockSpec(memory_space=pltpu.VMEM)] * len(groups),
            scratch_shapes=[
                pltpu.VMEM((count * rows, width), jnp.bfloat16),
                pltpu.SemaphoreType.DMA((width // tile, count)),
            ],
        ),
        out_shape=[
            jax.ShapeDtypeStruct((len(group) * height, width), jnp.bfloat16) for group in groups
        ],
        compiler_params=pltpu.CompilerParams(vmem_limit_bytes=48 * MIB),
        cost_estimate=pl.CostEstimate(
            flops=2 * blocks * height * count * rows * width,
            bytes_accessed=2 * count * rows * width,
            transcendentals=0,
        ),
        name="project",
    )(places, x, *pieces)


def output_kernel(count, blocks, place_ref, x_place_ref, *refs):
    xs, pieces, outs = refs[:blocks], refs[blocks : blocks + count], refs[blocks + count : -4]
    x_held, weight, x_sems, sems = refs[-4:]
    rows = pieces[0].shape[0]
    height = xs[0].shape[0]
    copies = []
    for n, x in enumerate(xs):
        start = pl.multiple_of(x_place_ref[n] * height, 16)
        copies.append(pltpu.make_async_copy(x, x_held.at[pl.ds(start, height)], x_sems.at[n]))
    for n, piece in enumerate(pieces):
        start = pl.multiple_of(place_ref[n] * rows, 16)
        copies.append(pltpu.make_async_copy(piece, weight.at[pl.ds(start, rows)], sems.at[n]))
    for copy in copies:
        copy.start()
    for copy in copies:
        copy.wait()
    width = count * rows
    tile = next(size for size in (256, 320, 128) if width % size == 0)
    for c in range(width // tile):
        result = lax.dot_general(
            x_held[...],
            weight[c * tile : (c + 1) * tile],
            (((1,), (1,)), ((), ())),
            preferred_element_type=jnp.float32,
        )
        for n in range(blocks):
            outs[n][:, c * tile : (c + 1) * tile] = result[n * height : (n + 1) * height].astype(
                outs[n].dtype
            )


def output(xs, pieces, places, x_places):
    rows, depth = pieces[0].shape
    count, blocks, height = len(pieces), len(xs), xs[0].shape[0]
    return pl.pallas_call(
        functools.partial(output_kernel, count, blocks),
        grid_spec=pltpu.PrefetchScalarGridSpec(
            num_scalar_prefetch=2,
            grid=(),
            in_specs=[pl.BlockSpec(memory_space=pl.ANY)] * (blocks + count),
            out_specs=[pl.BlockSpec(memory_space=pltpu.VMEM)] * blocks,
            scratch_shapes=[
                pltpu.VMEM((blocks * height, depth), jnp.bfloat16),
                pltpu.VMEM((count * rows, depth), jnp.bfloat16),
                pltpu.SemaphoreType.DMA((blocks,)),
                pltpu.SemaphoreType.DMA((count,)),
            ],
        ),
        out_shape=[jax.ShapeDtypeStruct((height, count * rows), jnp.bfloat16)] * blocks,
        compiler_params=pltpu.CompilerParams(vmem_limit_bytes=48 * MIB),
        cost_estimate=pl.CostEstimate(
            flops=2 * blocks * height * count * rows * depth,
            bytes_accessed=2 * count * rows * depth,
            transcendentals=0,
        ),
        name="output",
    )(places, x_places, *xs, *pieces)


def attention_kernel(terms, samples, *refs):
    kv_local, partials = len(terms), []
    for count in terms:
        partials.append(refs[:count])
        refs = refs[count:]
    cos_ref, sin_ref, lens_ref, k_ref, v_ref, out_ref, scores = refs
    together, length, _ = k_ref.shape
    scale = HEAD_SIZE ** (-0.5) * LOG2_E
    group = HEAD_GROUP * samples
    tile = 1024
    cosine, sine = cos_ref[...], sin_ref[...]
    lane = lax.broadcasted_iota(jnp.int32, (group, HEAD_SIZE), 1) % kv_local

    queries, owns, fresh = [], [], []
    for term_refs in partials:
        proj = sum(ref[...].astype(jnp.float32) for ref in term_refs)

        def head(index):
            vec = proj[:, index * HEAD_SIZE : (index + 1) * HEAD_SIZE]
            vec = vec * lax.rsqrt(jnp.mean(vec * vec, axis=-1, keepdims=True) + EPS)
            vec = vec * cosine + pltpu.roll(vec, HEAD_SIZE // 2, 1) * sine
            return vec.astype(jnp.bfloat16).astype(jnp.float32)

        new_key = head(HEAD_GROUP)
        new_value = proj[:, (HEAD_GROUP + 1) * HEAD_SIZE : (HEAD_GROUP + 2) * HEAD_SIZE]
        fresh.append(new_value.astype(jnp.bfloat16).astype(jnp.float32))
        queries.append([head(j) for j in range(HEAD_GROUP)])
        owns.append([jnp.sum(q * new_key, axis=-1, keepdims=True) for q in queries[-1]])

    class Prompt:
        def __init__(self, u):
            self.u = u
            self.rows = slice(u * samples, (u + 1) * samples)
            self.query = jnp.concatenate(
                [q[self.rows] for head_queries in queries for q in head_queries], axis=0
            ).astype(jnp.bfloat16)
            self.own = [
                jnp.concatenate([o[self.rows] for o in head_owns], axis=0) for head_owns in owns
            ]
            self.lens = lens_ref[self.rows, 0:1] * kv_local
            self.most = jnp.full((group, HEAD_SIZE), MASKED, jnp.float32)
            self.sums = jnp.zeros((group, HEAD_SIZE), jnp.float32)
            self.mixed = jnp.zeros((kv_local * group, HEAD_SIZE), jnp.float32)

        def score(self, c):
            part = lax.dot_general(
                self.query,
                k_ref[self.u, c : c + tile],
                (((1,), (1,)), ((), ())),
                preferred_element_type=jnp.float32,
            )
            for d in range(0, tile, HEAD_SIZE):
                dense = part[:group, d : d + HEAD_SIZE]
                for h in range(1, kv_local):
                    other = part[h * group : (h + 1) * group, d : d + HEAD_SIZE]
                    dense = jnp.where(lane == h, other, dense)
                slots = lax.broadcasted_iota(jnp.int32, (samples, HEAD_SIZE), 1) + (c + d)
                bias = jnp.where(slots < self.lens, 0.0, MASKED)
                dense = (dense.reshape(HEAD_GROUP, samples, HEAD_SIZE) + bias[None]).reshape(
                    group, HEAD_SIZE
                )
                scores[self.u, :, c + d : c + d + HEAD_SIZE] = dense
                self.most = jnp.maximum(self.most, dense)

        def find_top(self):
            self.tops = [
                jnp.maximum(
                    jnp.max(jnp.where(lane == h, self.most, MASKED), axis=-1, keepdims=True),
                    self.own[h],
                )
                for h in range(kv_local)
            ]
            self.top = jnp.broadcast_to(self.tops[0], (group, HEAD_SIZE))
            for h in range(1, kv_local):
                self.top = jnp.where(lane == h, self.tops[h], self.top)

        def mix(self, c):
            weights = [[] for _ in range(kv_local)]
            for d in range(0, tile, HEAD_SIZE):
                score = scores[self.u, :, c + d : c + d + HEAD_SIZE]
                expo = jnp.exp2((score - self.top) * scale)
                self.sums = self.sums + expo
                for h in range(kv_local):
                    kept = expo if kv_local == 1 else jnp.where(lane == h, expo, 0.0)
                    weights[h].append(kept.astype(jnp.bfloat16))
            weights = jnp.concatenate([jnp.concatenate(w, axis=1) for w in weights], axis=0)
            self.mixed = self.mixed + jnp.dot(
                weights, v_ref[self.u, c : c + tile], preferred_element_type=jnp.float32
            )

        def result(self):
            line = []
            for h in range(kv_local):
                own_expo = jnp.exp2((self.own[h] - self.tops[h]) * scale)
                kept = jnp.where(lane == h, self.sums, 0.0)
                inverse = 1.0 / (jnp.sum(kept, axis=-1, keepdims=True) + own_expo)
                own_weight = own_expo * inverse
                value = fresh[h][self.rows]
                for j in range(HEAD_GROUP):
                    at = slice(j * samples, (j + 1) * samples)
                    part = self.mixed[h * group + j * samples : h * group + (j + 1) * samples]
                    line.append(part * inverse[at] + own_weight[at] * value)
            return jnp.concatenate(line, axis=1)

    line_up = [Prompt(u) for u in range(together)]
    for u in range(together + 1):
        for c in range(0, length, tile):
            if u < together:
                line_up[u].score(c)
            if u > 0:
                line_up[u - 1].mix(c)
        if u < together:
            line_up[u].find_top()
    results = [prompt.result() for prompt in line_up]
    out_ref[...] = jnp.concatenate(results, axis=0).astype(out_ref.dtype)


def attention(partials, cosine, sine, lens, k_cache, value_cache, chunk, chunks):
    rows, width = cosine.shape[0], partials[0][0].shape[1]
    kv_local, terms = len(partials), [len(head_terms) for head_terms in partials]
    prompts, length, _ = k_cache.shape
    samples = rows // prompts
    together = 16 // samples
    height = together * samples
    heads = kv_local * HEAD_GROUP
    steps = prompts // together // chunks
    first = chunk * steps
    small = pl.BlockSpec((height, HEAD_SIZE), lambda i: (i + first, 0))
    cache = pl.BlockSpec((together, length, HEAD_SIZE), lambda i: (i + first, 0, 0))
    return pl.pallas_call(
        functools.partial(attention_kernel, terms, samples),
        grid=(steps,),
        in_specs=[pl.BlockSpec((height, width), lambda i: (i + first, 0))] * sum(terms)
        + [small] * 3
        + [cache] * 2,
        out_specs=pl.BlockSpec((height, heads * HEAD_SIZE), lambda i: (i, 0)),
        out_shape=jax.ShapeDtypeStruct((rows // chunks, heads * HEAD_SIZE), jnp.bfloat16),
        scratch_shapes=[pltpu.VMEM((together, HEAD_GROUP * samples, length), jnp.float32)],
        compiler_params=pltpu.CompilerParams(vmem_limit_bytes=48 * MIB),
        cost_estimate=pl.CostEstimate(
            flops=4 * steps * together * heads * samples * length * HEAD_SIZE,
            bytes_accessed=4 * steps * together * length * HEAD_SIZE,
            transcendentals=steps * together * HEAD_GROUP * samples * length,
        ),
        name="attention",
    )(*[term for head_terms in partials for term in head_terms], cosine, sine, lens, k_cache, value_cache)


CHUNKS = 2


def after(value, *others):
    return lax.optimization_barrier((value, others))[0]


def local(hidden, query_key_value_weight, w_out, k_cache, value_cache, lengths, assign):
    tp_count = lax.axis_size("tp")
    grp_count = lax.axis_size("grp")
    ratio = grp_count // tp_count
    t = lax.axis_index("tp")
    plane = lax.axis_index("grp") // ratio
    core = lax.axis_index("grp") % ratio
    row_count, width = hidden.shape
    prompts, context, kv_local, _ = k_cache.shape
    shifts = range(tp_count)

    def to_rank(value, shift):
        if shift == 0:
            return value
        return lax.ppermute(value, "tp", [(i, i ^ shift) for i in range(tp_count)])

    def to_plane(value, shift):
        if shift == 0:
            return value
        pairs = [(i, ((i // ratio) ^ shift) * ratio + i % ratio) for i in range(grp_count)]
        return lax.ppermute(value, "grp", pairs)

    def to_core(value, turn):
        if turn == 0:
            return value
        pairs = [(i, i // ratio * ratio + (i + turn) % ratio) for i in range(grp_count)]
        return lax.ppermute(value, "grp", pairs)

    index = jnp.arange(row_count, dtype=jnp.int32)
    key = assign * row_count + index
    place = jnp.sum((key[None, :] < key[:, None]).astype(jnp.int32), axis=1)
    sort_rows = (place[None, :] == index[:, None]).astype(jnp.bfloat16)
    lens = jnp.sum(jnp.where(place[None, :] == index[:, None], lengths[None, :], 0), axis=1)
    cosine, sine = rotary_tables(lens)
    lens = jnp.broadcast_to(lens[:, None], (row_count, HEAD_SIZE))

    hidden = jnp.dot(sort_rows, hidden, preferred_element_type=jnp.float32).astype(jnp.bfloat16)
    full = [to_rank(hidden, shift) for shift in shifts]
    ranks = jnp.stack([t ^ shift for shift in shifts]).astype(jnp.int32)
    owners = jnp.stack([(core - turn) % ratio for turn in range(ratio)]).astype(jnp.int32)
    row_places = jnp.stack([plane ^ t ^ shift for shift in shifts]).astype(jnp.int32)
    head_width = query_key_value_weight.shape[1] // (tp_count * kv_local)
    slices, source = [], query_key_value_weight
    for h in range(kv_local):
        slices.append(
            [
                lax.dynamic_slice_in_dim(
                    source, ((t ^ shift) * kv_local + h) * head_width, head_width, 1
                )
                for shift in shifts
            ]
        )
        source = after(query_key_value_weight, slices[h])
    full = after(full, slices)
    normed = normalize(full, row_places)
    features = [to_plane(block, shift) for shift, block in zip(shifts, normed)]

    def exchanged(parts):
        return [to_rank(part, shift) for shift, part in zip(shifts, parts)]

    coming = exchanged(slices[0])
    features = lay(features, jnp.arange(tp_count, dtype=jnp.int32), 0, width)
    received = after(coming, features)
    partials = []
    for h in range(kv_local):
        laid = lay(received, ranks, 0, head_width)
        if h + 1 < kv_local:
            coming = exchanged(after(slices[h + 1], received))
        laid = [to_core(laid, turn) for turn in range(ratio)]
        blocks = project(features, laid, owners, [[n] for n in shifts])
        partials.append([to_plane(block, shift) for shift, block in zip(shifts, blocks)])
        if h + 1 < kv_local:
            received = after(coming, partials[h][1:3])

    depth = w_out.shape[0] // tp_count
    source = after(w_out, blocks)
    out_received = exchanged(
        [lax.dynamic_slice_in_dim(source, (t ^ shift) * depth, depth, 0).T for shift in shifts]
    )

    keys = k_cache.reshape(prompts, context * kv_local, HEAD_SIZE)
    values = value_cache.reshape(prompts, context * kv_local, HEAD_SIZE)
    plane_pairs = [
        (g * tp_count + r, (r * ratio + g % ratio) * tp_count + g // ratio)
        for g in range(grp_count)
        for r in range(tp_count)
    ]
    gathered = []
    for chunk in range(CHUNKS):
        if chunk > 0:
            lens = after(lens, mixed, out_received)
        mixed = attention(partials, cosine, sine, lens, keys, values, chunk, CHUNKS)
        gathered.append([to_plane(mixed, shift) for shift in shifts])
    laid = lay(after(out_received, mixed, gathered[:-1]), ranks, 0, depth)
    out_weights = [to_core(laid, turn) for turn in range(ratio)]
    results = []
    for mixed in gathered:
        if results:
            mixed = after(mixed, products)
        products = output(mixed, out_weights, owners, row_places)
        blocks = exchanged(products)
        summed = sum(block.astype(jnp.float32) for block in blocks).astype(jnp.bfloat16)
        results.append(lax.ppermute(summed, ("grp", "tp"), plane_pairs))
    result = jnp.concatenate(results, axis=0)
    return lax.dot_general(
        sort_rows, result, (((0,), (0,)), ((), ())), preferred_element_type=jnp.float32
    ).astype(jnp.bfloat16)


def solution(mesh):
    return jax.shard_map(
        local,
        mesh=mesh,
        in_specs=(
            P("grp", "tp"),
            P(("grp", "tp"), None),
            P(None, ("grp", "tp")),
            P("grp", None, "tp", None),
            P("grp", None, "tp", None),
            P("grp"),
            P("grp"),
        ),
        out_specs=P("grp", "tp"),
        check_vma=False,
    )
```

```python
import functools

import jax
import jax.numpy as jnp
from jax import lax
from jax.experimental import pallas as pl
from jax.experimental.pallas import tpu as pltpu
from jax.sharding import PartitionSpec as P

QUERY_HEADS = 64
KEY_VALUE_HEADS = 8
HEAD_SIZE = 128
HEAD_GROUP = QUERY_HEADS // KEY_VALUE_HEADS


EPS = 1e-06
ROPE_BASE = 1000000.0
LOG2_E = 1.4426950408889634
MASKED = -1e30
MIB = 1024 * 1024


def rotary_tables(positions):
    half = HEAD_SIZE // 2
    freq = ROPE_BASE ** (-jnp.arange(half, dtype=jnp.float32) * 2.0 / HEAD_SIZE)
    angle = positions.astype(jnp.float32)[:, None] * freq[None, :]
    cosine, sine = (jnp.cos(angle), jnp.sin(angle))
    return jnp.concatenate([cosine, cosine], axis=1), jnp.concatenate([-sine, sine], axis=1)


def column_tile(width):
    return next(tile for tile in (512, 640, 256, 128) if width % tile == 0)


def normalize_kernel(count, place_ref, *refs):
    xs, outs, held = refs[:count], refs[count : 2 * count], refs[2 * count]
    values = [ref[...].astype(jnp.float32) for ref in xs]
    total = sum(jnp.sum(value * value, axis=-1, keepdims=True) for value in values)
    factor = lax.rsqrt(total / (count * xs[0].shape[1]) + EPS)
    for n, value in enumerate(values):
        held[place_ref[n]] = (value * factor).astype(held.dtype)
    for n, out_ref in enumerate(outs):
        out_ref[...] = held[n]


def normalize(xs, places):
    count = len(xs)
    return pl.pallas_call(
        functools.partial(normalize_kernel, count),
        grid_spec=pltpu.PrefetchScalarGridSpec(
            num_scalar_prefetch=1,
            grid=(),
            in_specs=[pl.BlockSpec(memory_space=pltpu.VMEM)] * count,
            out_specs=[pl.BlockSpec(memory_space=pltpu.VMEM)] * count,
            scratch_shapes=[pltpu.VMEM((count,) + xs[0].shape, jnp.bfloat16)],
        ),
        out_shape=[jax.ShapeDtypeStruct(xs[0].shape, jnp.bfloat16)] * count,
        compiler_params=pltpu.CompilerParams(vmem_limit_bytes=48 * MIB),
        name="normalize",
    )(places, *xs)


def lay_kernel(count, first, place_ref, *refs):
    pieces, (out_ref, sems) = refs[:count], refs[count:]
    rows = pieces[0].shape[0]
    lanes = pl.ds(first, out_ref.shape[1])
    copies = []
    for n, piece in enumerate(pieces):
        start = pl.multiple_of(place_ref[n] * rows, 16)
        copies.append(
            pltpu.make_async_copy(piece.at[:, lanes], out_ref.at[pl.ds(start, rows)], sems.at[n])
        )
    for copy in copies:
        copy.start()
    for copy in copies:
        copy.wait()


def lay(pieces, places, first, width):
    count = len(pieces)
    rows = pieces[0].shape[0]
    if rows % 16:
        whole = jnp.zeros((count * rows, width), pieces[0].dtype)
        for n, piece in enumerate(pieces):
            piece = piece[:, first : first + width]
            whole = lax.dynamic_update_slice_in_dim(whole, piece, places[n] * rows, 0)
        return whole
    return pl.pallas_call(
        functools.partial(lay_kernel, count, first),
        grid_spec=pltpu.PrefetchScalarGridSpec(
            num_scalar_prefetch=1,
            grid=(),
            in_specs=[pl.BlockSpec(memory_space=pl.ANY)] * count,
            out_specs=pl.BlockSpec(memory_space=pltpu.VMEM),
            scratch_shapes=[pltpu.SemaphoreType.DMA((count,))],
        ),
        out_shape=jax.ShapeDtypeStruct((count * rows, width), pieces[0].dtype),
        compiler_params=pltpu.CompilerParams(vmem_limit_bytes=6 * MIB),
        cost_estimate=pl.CostEstimate(
            flops=0, bytes_accessed=4 * count * rows * width, transcendentals=0
        ),
        name="lay",
    )(places, *pieces)


def project_kernel(count, groups, place_ref, x_ref, *refs):
    pieces, outs, (weight, sems) = refs[:count], refs[count:-2], refs[-2:]
    rows = pieces[0].shape[0]
    width = outs[0].shape[1]
    height = x_ref.shape[0] // sum(len(group) for group in groups)
    tile = column_tile(width)
    copies = []
    for c in range(width // tile):
        for n, piece in enumerate(pieces):
            start = pl.multiple_of(place_ref[n] * rows, 16)
            copy = pltpu.make_async_copy(
                piece.at[:, pl.ds(c * tile, tile)],
                weight.at[pl.ds(start, rows), pl.ds(c * tile, tile)],
                sems.at[c, n],
            )
            copy.start()
            copies.append(copy)
    for c in range(width // tile):
        for copy in copies[c * count : (c + 1) * count]:
            copy.wait()
        lanes = slice(c * tile, (c + 1) * tile)
        result = jnp.dot(x_ref[...], weight[:, lanes], preferred_element_type=jnp.float32)
        result = result.astype(jnp.bfloat16)
        for group, out_ref in zip(groups, outs):
            for at, n in enumerate(group):
                out_ref[at * height : (at + 1) * height, lanes] = result[
                    n * height : (n + 1) * height
                ]


def project(x, pieces, places, groups):
    rows, width = pieces[0].shape
    count, blocks = len(pieces), sum(len(group) for group in groups)
    height = x.shape[0] // blocks
    tile = column_tile(width)
    return pl.pallas_call(
        functools.partial(project_kernel, count, groups),
        grid_spec=pltpu.PrefetchScalarGridSpec(
            num_scalar_prefetch=1,
            grid=(),
            in_specs=[pl.BlockSpec(memory_space=pltpu.VMEM)]
            + [pl.BlockSpec(memory_space=pl.ANY)] * count,
            out_specs=[pl.BlockSpec(memory_space=pltpu.VMEM)] * len(groups),
            scratch_shapes=[
                pltpu.VMEM((count * rows, width), jnp.bfloat16),
                pltpu.SemaphoreType.DMA((width // tile, count)),
            ],
        ),
        out_shape=[
            jax.ShapeDtypeStruct((len(group) * height, width), jnp.bfloat16) for group in groups
        ],
        compiler_params=pltpu.CompilerParams(vmem_limit_bytes=48 * MIB),
        cost_estimate=pl.CostEstimate(
            flops=2 * blocks * height * count * rows * width,
            bytes_accessed=2 * count * rows * width,
            transcendentals=0,
        ),
        name="project",
    )(places, x, *pieces)


def output_kernel(count, blocks, place_ref, x_place_ref, *refs):
    xs, pieces, outs = refs[:blocks], refs[blocks : blocks + count], refs[blocks + count : -4]
    x_held, weight, x_sems, sems = refs[-4:]
    rows = pieces[0].shape[0]
    height = xs[0].shape[0]
    copies = []
    for n, x in enumerate(xs):
        start = pl.multiple_of(x_place_ref[n] * height, 16)
        copies.append(pltpu.make_async_copy(x, x_held.at[pl.ds(start, height)], x_sems.at[n]))
    for n, piece in enumerate(pieces):
        start = pl.multiple_of(place_ref[n] * rows, 16)
        copies.append(pltpu.make_async_copy(piece, weight.at[pl.ds(start, rows)], sems.at[n]))
    for copy in copies:
        copy.start()
    for copy in copies:
        copy.wait()
    width = count * rows
    tile = next(size for size in (256, 320, 128) if width % size == 0)
    for c in range(width // tile):
        result = lax.dot_general(
            x_held[...],
            weight[c * tile : (c + 1) * tile],
            (((1,), (1,)), ((), ())),
            preferred_element_type=jnp.float32,
        )
        for n in range(blocks):
            outs[n][:, c * tile : (c + 1) * tile] = result[n * height : (n + 1) * height].astype(
                outs[n].dtype
            )


def output(xs, pieces, places, x_places):
    rows, depth = pieces[0].shape
    count, blocks, height = len(pieces), len(xs), xs[0].shape[0]
    return pl.pallas_call(
        functools.partial(output_kernel, count, blocks),
        grid_spec=pltpu.PrefetchScalarGridSpec(
            num_scalar_prefetch=2,
            grid=(),
            in_specs=[pl.BlockSpec(memory_space=pl.ANY)] * (blocks + count),
            out_specs=[pl.BlockSpec(memory_space=pltpu.VMEM)] * blocks,
            scratch_shapes=[
                pltpu.VMEM((blocks * height, depth), jnp.bfloat16),
                pltpu.VMEM((count * rows, depth), jnp.bfloat16),
                pltpu.SemaphoreType.DMA((blocks,)),
                pltpu.SemaphoreType.DMA((count,)),
            ],
        ),
        out_shape=[jax.ShapeDtypeStruct((height, count * rows), jnp.bfloat16)] * blocks,
        compiler_params=pltpu.CompilerParams(vmem_limit_bytes=48 * MIB),
        cost_estimate=pl.CostEstimate(
            flops=2 * blocks * height * count * rows * depth,
            bytes_accessed=2 * count * rows * depth,
            transcendentals=0,
        ),
        name="output",
    )(places, x_places, *xs, *pieces)


def attention_kernel(terms, samples, first, *refs):
    kv_local, count = len(terms), sum(terms)
    cos_ref, sin_ref, lens_ref, k_ref, v_ref, out_ref = refs[count : count + 6]
    scores, k_held, v_held, held, tables, lens_held, k_sems, v_sems, sems = refs[count + 6 :]
    height = out_ref.shape[0]
    here = height // samples
    length = k_ref.shape[1]
    pieces = k_sems.shape[1]
    piece = length // pieces
    scale = HEAD_SIZE ** (-0.5) * LOG2_E
    group = HEAD_GROUP * samples
    tile = 1024

    chunk = pl.ds(first * samples, height)
    small = [
        pltpu.make_async_copy(ref.at[chunk], held.at[n], sems.at[n])
        for n, ref in enumerate(refs[:count])
    ]
    small += [
        pltpu.make_async_copy(ref.at[chunk], to, sems.at[count + n])
        for n, (ref, to) in enumerate(
            [(cos_ref, tables.at[0]), (sin_ref, tables.at[1]), (lens_ref, lens_held)]
        )
    ]

    def fetch(ref, buffer, buffer_sems, u):
        return [
            pltpu.make_async_copy(
                ref.at[first + u, pl.ds(c * piece, piece)],
                buffer.at[u % 2, pl.ds(c * piece, piece)],
                buffer_sems.at[u % 2, c],
            )
            for c in range(pieces)
        ]

    def start(copies):
        for copy in copies:
            copy.start()

    def wait(copies):
        for copy in copies:
            copy.wait()

    keys = [fetch(k_ref, k_held, k_sems, u) for u in range(here)]
    values = [fetch(v_ref, v_held, v_sems, u) for u in range(here)]
    start(small)
    for u in range(min(2, here)):
        start(keys[u] + values[u])
    wait(small)
    cosine, sine = tables[0], tables[1]
    lane = lax.broadcasted_iota(jnp.int32, (group, HEAD_SIZE), 1) % kv_local

    queries, owns, fresh = [], [], []
    for h in range(kv_local):
        at = sum(terms[:h])
        proj = sum(held[n].astype(jnp.float32) for n in range(at, at + terms[h]))

        def head(index):
            vec = proj[:, index * HEAD_SIZE : (index + 1) * HEAD_SIZE]
            vec = vec * lax.rsqrt(jnp.mean(vec * vec, axis=-1, keepdims=True) + EPS)
            vec = vec * cosine + pltpu.roll(vec, HEAD_SIZE // 2, 1) * sine
            return vec.astype(jnp.bfloat16).astype(jnp.float32)

        new_key = head(HEAD_GROUP)
        new_value = proj[:, (HEAD_GROUP + 1) * HEAD_SIZE : (HEAD_GROUP + 2) * HEAD_SIZE]
        fresh.append(new_value.astype(jnp.bfloat16).astype(jnp.float32))
        queries.append([head(j) for j in range(HEAD_GROUP)])
        owns.append([jnp.sum(q * new_key, axis=-1, keepdims=True) for q in queries[-1]])

    class Prompt:
        def __init__(self, u):
            self.u = u
            self.rows = slice(u * samples, (u + 1) * samples)
            self.query = jnp.concatenate(
                [q[self.rows] for head_queries in queries for q in head_queries], axis=0
            ).astype(jnp.bfloat16)
            self.own = [
                jnp.concatenate([o[self.rows] for o in head_owns], axis=0) for head_owns in owns
            ]
            self.lens = lens_held[self.rows, 0:1] * kv_local
            self.most = jnp.full((group, HEAD_SIZE), MASKED, jnp.float32)
            self.sums = jnp.zeros((group, HEAD_SIZE), jnp.float32)
            self.mixed = jnp.zeros((kv_local * group, HEAD_SIZE), jnp.float32)

        def score(self, c):
            part = lax.dot_general(
                self.query,
                k_held[self.u % 2, c : c + tile],
                (((1,), (1,)), ((), ())),
                preferred_element_type=jnp.float32,
            )
            for d in range(0, tile, HEAD_SIZE):
                dense = part[:group, d : d + HEAD_SIZE]
                for h in range(1, kv_local):
                    other = part[h * group : (h + 1) * group, d : d + HEAD_SIZE]
                    dense = jnp.where(lane == h, other, dense)
                slots = lax.broadcasted_iota(jnp.int32, (samples, HEAD_SIZE), 1) + (c + d)
                bias = jnp.where(slots < self.lens, 0.0, MASKED)
                dense = (dense.reshape(HEAD_GROUP, samples, HEAD_SIZE) + bias[None]).reshape(
                    group, HEAD_SIZE
                )
                scores[self.u % 2, :, c + d : c + d + HEAD_SIZE] = dense
                self.most = jnp.maximum(self.most, dense)

        def find_top(self):
            self.tops = [
                jnp.maximum(
                    jnp.max(jnp.where(lane == h, self.most, MASKED), axis=-1, keepdims=True),
                    self.own[h],
                )
                for h in range(kv_local)
            ]
            self.top = jnp.broadcast_to(self.tops[0], (group, HEAD_SIZE))
            for h in range(1, kv_local):
                self.top = jnp.where(lane == h, self.tops[h], self.top)

        def mix(self, c):
            weights = [[] for _ in range(kv_local)]
            for d in range(0, tile, HEAD_SIZE):
                score = scores[self.u % 2, :, c + d : c + d + HEAD_SIZE]
                expo = jnp.exp2((score - self.top) * scale)
                self.sums = self.sums + expo
                for h in range(kv_local):
                    kept = expo if kv_local == 1 else jnp.where(lane == h, expo, 0.0)
                    weights[h].append(kept.astype(jnp.bfloat16))
            weights = jnp.concatenate([jnp.concatenate(w, axis=1) for w in weights], axis=0)
            self.mixed = self.mixed + jnp.dot(
                weights, v_held[self.u % 2, c : c + tile], preferred_element_type=jnp.float32
            )

        def result(self):
            line = []
            for h in range(kv_local):
                own_expo = jnp.exp2((self.own[h] - self.tops[h]) * scale)
                kept = jnp.where(lane == h, self.sums, 0.0)
                inverse = 1.0 / (jnp.sum(kept, axis=-1, keepdims=True) + own_expo)
                own_weight = own_expo * inverse
                value = fresh[h][self.rows]
                for j in range(HEAD_GROUP):
                    at = slice(j * samples, (j + 1) * samples)
                    part = self.mixed[h * group + j * samples : h * group + (j + 1) * samples]
                    line.append(part * inverse[at] + own_weight[at] * value)
            return jnp.concatenate(line, axis=1)

    line_up = [Prompt(u) for u in range(here)]
    for u in range(here + 1):
        if u < here:
            wait(keys[u])
        if u > 0:
            wait(values[u - 1])
        for c in range(0, length, tile):
            if u < here:
                line_up[u].score(c)
            if u > 0:
                line_up[u - 1].mix(c)
        if u + 2 < here:
            start(keys[u + 2])
        if 0 < u and u + 1 < here:
            start(values[u + 1])
        if u < here:
            line_up[u].find_top()
    out_ref[...] = jnp.concatenate([prompt.result() for prompt in line_up], axis=0).astype(
        out_ref.dtype
    )


def attention(partials, cosine, sine, lens, k_cache, value_cache, chunk, chunks):
    rows, width = cosine.shape[0], partials[0][0].shape[1]
    kv_local, terms = len(partials), [len(head_terms) for head_terms in partials]
    prompts, length, _ = k_cache.shape
    samples = rows // prompts
    here = prompts // chunks
    height = here * samples
    heads = kv_local * HEAD_GROUP
    pieces = length // 2048
    return pl.pallas_call(
        functools.partial(attention_kernel, terms, samples, chunk * here),
        in_specs=[pl.BlockSpec(memory_space=pl.ANY)] * (sum(terms) + 5),
        out_specs=pl.BlockSpec(memory_space=pltpu.VMEM),
        out_shape=jax.ShapeDtypeStruct((height, heads * HEAD_SIZE), jnp.bfloat16),
        scratch_shapes=[
            pltpu.VMEM((2, HEAD_GROUP * samples, length), jnp.float32),
            pltpu.VMEM((2, length, HEAD_SIZE), jnp.bfloat16),
            pltpu.VMEM((2, length, HEAD_SIZE), jnp.bfloat16),
            pltpu.VMEM((sum(terms), height, width), jnp.bfloat16),
            pltpu.VMEM((2, height, HEAD_SIZE), jnp.float32),
            pltpu.VMEM((height, HEAD_SIZE), jnp.int32),
            pltpu.SemaphoreType.DMA((2, pieces)),
            pltpu.SemaphoreType.DMA((2, pieces)),
            pltpu.SemaphoreType.DMA((sum(terms) + 3,)),
        ],
        compiler_params=pltpu.CompilerParams(vmem_limit_bytes=48 * MIB),
        cost_estimate=pl.CostEstimate(
            flops=4 * here * heads * samples * length * HEAD_SIZE,
            bytes_accessed=4 * here * length * HEAD_SIZE,
            transcendentals=here * HEAD_GROUP * samples * length,
        ),
        name="attention",
    )(*[term for head_terms in partials for term in head_terms], cosine, sine, lens, k_cache, value_cache)


CHUNKS = 2


def after(value, *others):
    return lax.optimization_barrier((value, others))[0]


def local(hidden, query_key_value_weight, w_out, k_cache, value_cache, lengths, assign):
    tp_count = lax.axis_size("tp")
    grp_count = lax.axis_size("grp")
    ratio = grp_count // tp_count
    t = lax.axis_index("tp")
    plane = lax.axis_index("grp") // ratio
    core = lax.axis_index("grp") % ratio
    row_count, width = hidden.shape
    prompts, context, kv_local, _ = k_cache.shape
    shifts = range(tp_count)

    def to_rank(value, shift):
        if shift == 0:
            return value
        return lax.ppermute(value, "tp", [(i, i ^ shift) for i in range(tp_count)])

    def to_plane(value, shift):
        if shift == 0:
            return value
        pairs = [(i, ((i // ratio) ^ shift) * ratio + i % ratio) for i in range(grp_count)]
        return lax.ppermute(value, "grp", pairs)

    def to_core(value, turn):
        if turn == 0:
            return value
        pairs = [(i, i // ratio * ratio + (i + turn) % ratio) for i in range(grp_count)]
        return lax.ppermute(value, "grp", pairs)

    index = jnp.arange(row_count, dtype=jnp.int32)
    key = assign * row_count + index
    place = jnp.sum((key[None, :] < key[:, None]).astype(jnp.int32), axis=1)
    sort_rows = (place[None, :] == index[:, None]).astype(jnp.bfloat16)
    lens = jnp.sum(jnp.where(place[None, :] == index[:, None], lengths[None, :], 0), axis=1)
    cosine, sine = rotary_tables(lens)
    lens = jnp.broadcast_to(lens[:, None], (row_count, HEAD_SIZE))

    hidden = jnp.dot(sort_rows, hidden, preferred_element_type=jnp.float32).astype(jnp.bfloat16)
    full = [to_rank(hidden, shift) for shift in shifts]
    ranks = jnp.stack([t ^ shift for shift in shifts]).astype(jnp.int32)
    owners = jnp.stack([(core - turn) % ratio for turn in range(ratio)]).astype(jnp.int32)
    row_places = jnp.stack([plane ^ t ^ shift for shift in shifts]).astype(jnp.int32)
    head_width = query_key_value_weight.shape[1] // (tp_count * kv_local)
    slices, source = [], query_key_value_weight
    for h in range(kv_local):
        slices.append(
            [
                lax.dynamic_slice_in_dim(
                    source, ((t ^ shift) * kv_local + h) * head_width, head_width, 1
                )
                for shift in shifts
            ]
        )
        source = after(query_key_value_weight, slices[h])
    full = after(full, slices)
    normed = normalize(full, row_places)
    features = [to_plane(block, shift) for shift, block in zip(shifts, normed)]

    def exchanged(parts):
        return [to_rank(part, shift) for shift, part in zip(shifts, parts)]

    coming = exchanged(slices[0])
    features = lay(features, jnp.arange(tp_count, dtype=jnp.int32), 0, width)
    received = after(coming, features)
    partials = []
    for h in range(kv_local):
        laid = lay(received, ranks, 0, head_width)
        if h + 1 < kv_local:
            coming = exchanged(after(slices[h + 1], received))
        laid = [to_core(laid, turn) for turn in range(ratio)]
        blocks = project(features, laid, owners, [[n] for n in shifts])
        partials.append([to_plane(block, shift) for shift, block in zip(shifts, blocks)])
        if h + 1 < kv_local:
            received = after(coming, partials[h][1:3])

    depth = w_out.shape[0] // tp_count
    source = after(w_out, blocks)
    out_received = exchanged(
        [lax.dynamic_slice_in_dim(source, (t ^ shift) * depth, depth, 0).T for shift in shifts]
    )

    keys = k_cache.reshape(prompts, context * kv_local, HEAD_SIZE)
    values = value_cache.reshape(prompts, context * kv_local, HEAD_SIZE)
    plane_pairs = [
        (g * tp_count + r, (r * ratio + g % ratio) * tp_count + g // ratio)
        for g in range(grp_count)
        for r in range(tp_count)
    ]
    gathered = []
    for chunk in range(CHUNKS):
        if chunk > 0:
            lens = after(lens, mixed, out_received)
        mixed = attention(partials, cosine, sine, lens, keys, values, chunk, CHUNKS)
        gathered.append([to_plane(mixed, shift) for shift in shifts])
    laid = lay(after(out_received, mixed, gathered[:-1]), ranks, 0, depth)
    out_weights = [to_core(laid, turn) for turn in range(ratio)]
    results = []
    for mixed in gathered:
        if results:
            mixed = after(mixed, products)
        products = output(mixed, out_weights, owners, row_places)
        blocks = exchanged(products)
        summed = sum(block.astype(jnp.float32) for block in blocks).astype(jnp.bfloat16)
        results.append(lax.ppermute(summed, ("grp", "tp"), plane_pairs))
    result = jnp.concatenate(results, axis=0)
    return lax.dot_general(
        sort_rows, result, (((0,), (0,)), ((), ())), preferred_element_type=jnp.float32
    ).astype(jnp.bfloat16)


def solution(mesh):
    return jax.shard_map(
        local,
        mesh=mesh,
        in_specs=(
            P("grp", "tp"),
            P(("grp", "tp"), None),
            P(None, ("grp", "tp")),
            P("grp", None, "tp", None),
            P("grp", None, "tp", None),
            P("grp"),
            P("grp"),
        ),
        out_specs=P("grp", "tp"),
        check_vma=False,
    )
```

```python
import functools

import jax
import jax.numpy as jnp
from jax import lax
from jax.experimental import pallas as pl
from jax.experimental.pallas import tpu as pltpu
from jax.sharding import PartitionSpec as P

QUERY_HEADS = 64
KEY_VALUE_HEADS = 8
HEAD_SIZE = 128
HEAD_GROUP = QUERY_HEADS // KEY_VALUE_HEADS


EPS = 1e-06
ROPE_BASE = 1000000.0
LOG2_E = 1.4426950408889634
MASKED = -1e30
MIB = 1024 * 1024


def rotary_tables(positions):
    half = HEAD_SIZE // 2
    freq = ROPE_BASE ** (-jnp.arange(half, dtype=jnp.float32) * 2.0 / HEAD_SIZE)
    angle = positions.astype(jnp.float32)[:, None] * freq[None, :]
    cosine, sine = (jnp.cos(angle), jnp.sin(angle))
    return jnp.concatenate([cosine, cosine], axis=1), jnp.concatenate([-sine, sine], axis=1)


def column_tile(width):
    return next(tile for tile in (512, 640, 256, 128) if width % tile == 0)


def normalize_kernel(count, place_ref, *refs):
    xs, outs, held = refs[:count], refs[count : 2 * count], refs[2 * count]
    values = [ref[...].astype(jnp.float32) for ref in xs]
    total = sum(jnp.sum(value * value, axis=-1, keepdims=True) for value in values)
    factor = lax.rsqrt(total / (count * xs[0].shape[1]) + EPS)
    for n, value in enumerate(values):
        held[place_ref[n]] = (value * factor).astype(held.dtype)
    for n, out_ref in enumerate(outs):
        out_ref[...] = held[n]


def normalize(xs, places):
    count = len(xs)
    return pl.pallas_call(
        functools.partial(normalize_kernel, count),
        grid_spec=pltpu.PrefetchScalarGridSpec(
            num_scalar_prefetch=1,
            grid=(),
            in_specs=[pl.BlockSpec(memory_space=pltpu.VMEM)] * count,
            out_specs=[pl.BlockSpec(memory_space=pltpu.VMEM)] * count,
            scratch_shapes=[pltpu.VMEM((count,) + xs[0].shape, jnp.bfloat16)],
        ),
        out_shape=[jax.ShapeDtypeStruct(xs[0].shape, jnp.bfloat16)] * count,
        compiler_params=pltpu.CompilerParams(vmem_limit_bytes=48 * MIB),
        name="normalize",
    )(places, *xs)


def lay_kernel(firsts, place_ref, *refs):
    pieces, (out_ref, sems) = refs[: len(firsts)], refs[len(firsts) :]
    rows, width = pieces[0].shape[0], out_ref.shape[1]
    copies = []
    for n, piece in enumerate(pieces):
        start = pl.multiple_of(place_ref[n] * rows, 16)
        copies.append(
            pltpu.make_async_copy(
                piece.at[:, pl.ds(firsts[n], width)], out_ref.at[pl.ds(start, rows)], sems.at[n]
            )
        )
    for copy in copies:
        copy.start()
    for copy in copies:
        copy.wait()


def lay(pieces, places, firsts, width):
    count = len(pieces)
    rows = pieces[0].shape[0]
    if rows % 16:
        whole = jnp.zeros((count * rows, width), pieces[0].dtype)
        for n, piece in enumerate(pieces):
            piece = piece[:, firsts[n] : firsts[n] + width]
            whole = lax.dynamic_update_slice_in_dim(whole, piece, places[n] * rows, 0)
        return whole
    return pl.pallas_call(
        functools.partial(lay_kernel, tuple(firsts)),
        grid_spec=pltpu.PrefetchScalarGridSpec(
            num_scalar_prefetch=1,
            grid=(),
            in_specs=[pl.BlockSpec(memory_space=pl.ANY)] * count,
            out_specs=pl.BlockSpec(memory_space=pltpu.VMEM),
            scratch_shapes=[pltpu.SemaphoreType.DMA((count,))],
        ),
        out_shape=jax.ShapeDtypeStruct((count * rows, width), pieces[0].dtype),
        compiler_params=pltpu.CompilerParams(vmem_limit_bytes=6 * MIB),
        cost_estimate=pl.CostEstimate(
            flops=0, bytes_accessed=4 * count * rows * width, transcendentals=0
        ),
        name="lay",
    )(places, *pieces)


def project_kernel(count, groups, place_ref, x_ref, *refs):
    pieces, outs, (weight, sems) = refs[:count], refs[count:-2], refs[-2:]
    rows = pieces[0].shape[0]
    width = outs[0].shape[1]
    height = x_ref.shape[0] // sum(len(group) for group in groups)
    tile = column_tile(width)
    copies = []
    for c in range(width // tile):
        for n, piece in enumerate(pieces):
            start = pl.multiple_of(place_ref[n] * rows, 16)
            copy = pltpu.make_async_copy(
                piece.at[:, pl.ds(c * tile, tile)],
                weight.at[pl.ds(start, rows), pl.ds(c * tile, tile)],
                sems.at[c, n],
            )
            copy.start()
            copies.append(copy)
    for c in range(width // tile):
        for copy in copies[c * count : (c + 1) * count]:
            copy.wait()
        lanes = slice(c * tile, (c + 1) * tile)
        result = jnp.dot(x_ref[...], weight[:, lanes], preferred_element_type=jnp.float32)
        result = result.astype(jnp.bfloat16)
        for group, out_ref in zip(groups, outs):
            for at, n in enumerate(group):
                out_ref[at * height : (at + 1) * height, lanes] = result[
                    n * height : (n + 1) * height
                ]


def project(x, pieces, places, groups):
    rows, width = pieces[0].shape
    count, blocks = len(pieces), sum(len(group) for group in groups)
    height = x.shape[0] // blocks
    tile = column_tile(width)
    return pl.pallas_call(
        functools.partial(project_kernel, count, groups),
        grid_spec=pltpu.PrefetchScalarGridSpec(
            num_scalar_prefetch=1,
            grid=(),
            in_specs=[pl.BlockSpec(memory_space=pltpu.VMEM)]
            + [pl.BlockSpec(memory_space=pl.ANY)] * count,
            out_specs=[pl.BlockSpec(memory_space=pltpu.VMEM)] * len(groups),
            scratch_shapes=[
                pltpu.VMEM((count * rows, width), jnp.bfloat16),
                pltpu.SemaphoreType.DMA((width // tile, count)),
            ],
        ),
        out_shape=[
            jax.ShapeDtypeStruct((len(group) * height, width), jnp.bfloat16) for group in groups
        ],
        compiler_params=pltpu.CompilerParams(vmem_limit_bytes=48 * MIB),
        cost_estimate=pl.CostEstimate(
            flops=2 * blocks * height * count * rows * width,
            bytes_accessed=2 * count * rows * width,
            transcendentals=0,
        ),
        name="project",
    )(places, x, *pieces)


def output_kernel(count, blocks, place_ref, x_place_ref, *refs):
    xs, pieces, outs = refs[:blocks], refs[blocks : blocks + count], refs[blocks + count : -4]
    x_held, weight, x_sems, sems = refs[-4:]
    rows = pieces[0].shape[0]
    height = xs[0].shape[0]
    copies = []
    for n, x in enumerate(xs):
        start = pl.multiple_of(x_place_ref[n] * height, 16)
        copies.append(pltpu.make_async_copy(x, x_held.at[pl.ds(start, height)], x_sems.at[n]))
    for n, piece in enumerate(pieces):
        start = pl.multiple_of(place_ref[n] * rows, 16)
        copies.append(pltpu.make_async_copy(piece, weight.at[pl.ds(start, rows)], sems.at[n]))
    for copy in copies:
        copy.start()
    for copy in copies:
        copy.wait()
    width = count * rows
    tile = next(size for size in (256, 320, 128) if width % size == 0)
    for c in range(width // tile):
        result = lax.dot_general(
            x_held[...],
            weight[c * tile : (c + 1) * tile],
            (((1,), (1,)), ((), ())),
            preferred_element_type=jnp.float32,
        )
        for n in range(blocks):
            outs[n][:, c * tile : (c + 1) * tile] = result[n * height : (n + 1) * height].astype(
                outs[n].dtype
            )


def output(xs, pieces, places, x_places):
    rows, depth = pieces[0].shape
    count, blocks, height = len(pieces), len(xs), xs[0].shape[0]
    return pl.pallas_call(
        functools.partial(output_kernel, count, blocks),
        grid_spec=pltpu.PrefetchScalarGridSpec(
            num_scalar_prefetch=2,
            grid=(),
            in_specs=[pl.BlockSpec(memory_space=pl.ANY)] * (blocks + count),
            out_specs=[pl.BlockSpec(memory_space=pltpu.VMEM)] * blocks,
            scratch_shapes=[
                pltpu.VMEM((blocks * height, depth), jnp.bfloat16),
                pltpu.VMEM((count * rows, depth), jnp.bfloat16),
                pltpu.SemaphoreType.DMA((blocks,)),
                pltpu.SemaphoreType.DMA((count,)),
            ],
        ),
        out_shape=[jax.ShapeDtypeStruct((height, count * rows), jnp.bfloat16)] * blocks,
        compiler_params=pltpu.CompilerParams(vmem_limit_bytes=48 * MIB),
        cost_estimate=pl.CostEstimate(
            flops=2 * blocks * height * count * rows * depth,
            bytes_accessed=2 * count * rows * depth,
            transcendentals=0,
        ),
        name="output",
    )(places, x_places, *xs, *pieces)


def attention_kernel(terms, samples, first, *refs):
    kv_local, count = len(terms), sum(terms)
    cos_ref, sin_ref, lens_ref, k_ref, v_ref, out_ref = refs[count : count + 6]
    scores, k_held, v_held, held, tables, lens_held, k_sems, v_sems, sems = refs[count + 6 :]
    height = out_ref.shape[0]
    here = height // samples
    length = k_ref.shape[1]
    pieces = k_sems.shape[1]
    piece = length // pieces
    scale = HEAD_SIZE ** (-0.5) * LOG2_E
    group = HEAD_GROUP * samples
    tile = 1024

    chunk = pl.ds(first * samples, height)
    small = [
        pltpu.make_async_copy(ref.at[chunk], held.at[n], sems.at[n])
        for n, ref in enumerate(refs[:count])
    ]
    small += [
        pltpu.make_async_copy(ref.at[chunk], to, sems.at[count + n])
        for n, (ref, to) in enumerate(
            [(cos_ref, tables.at[0]), (sin_ref, tables.at[1]), (lens_ref, lens_held)]
        )
    ]

    def fetch(ref, buffer, buffer_sems, u):
        return [
            pltpu.make_async_copy(
                ref.at[first + u, pl.ds(c * piece, piece)],
                buffer.at[u % 2, pl.ds(c * piece, piece)],
                buffer_sems.at[u % 2, c],
            )
            for c in range(pieces)
        ]

    def start(copies):
        for copy in copies:
            copy.start()

    def wait(copies):
        for copy in copies:
            copy.wait()

    keys = [fetch(k_ref, k_held, k_sems, u) for u in range(here)]
    values = [fetch(v_ref, v_held, v_sems, u) for u in range(here)]
    start(small)
    for u in range(min(2, here)):
        start(keys[u] + values[u])
    wait(small)
    cosine, sine = tables[0], tables[1]
    lane = lax.broadcasted_iota(jnp.int32, (group, HEAD_SIZE), 1) % kv_local

    queries, owns, fresh = [], [], []
    for h in range(kv_local):
        at = sum(terms[:h])
        proj = sum(held[n].astype(jnp.float32) for n in range(at, at + terms[h]))

        def head(index):
            vec = proj[:, index * HEAD_SIZE : (index + 1) * HEAD_SIZE]
            vec = vec * lax.rsqrt(jnp.mean(vec * vec, axis=-1, keepdims=True) + EPS)
            vec = vec * cosine + pltpu.roll(vec, HEAD_SIZE // 2, 1) * sine
            return vec.astype(jnp.bfloat16).astype(jnp.float32)

        new_key = head(HEAD_GROUP)
        new_value = proj[:, (HEAD_GROUP + 1) * HEAD_SIZE : (HEAD_GROUP + 2) * HEAD_SIZE]
        fresh.append(new_value.astype(jnp.bfloat16).astype(jnp.float32))
        queries.append([head(j) for j in range(HEAD_GROUP)])
        owns.append([jnp.sum(q * new_key, axis=-1, keepdims=True) for q in queries[-1]])

    class Prompt:
        def __init__(self, u):
            self.u = u
            self.rows = slice(u * samples, (u + 1) * samples)
            self.query = jnp.concatenate(
                [q[self.rows] for head_queries in queries for q in head_queries], axis=0
            ).astype(jnp.bfloat16)
            self.own = [
                jnp.concatenate([o[self.rows] for o in head_owns], axis=0) for head_owns in owns
            ]
            self.lens = lens_held[self.rows, 0:1] * kv_local
            self.most = jnp.full((group, HEAD_SIZE), MASKED, jnp.float32)
            self.sums = jnp.zeros((group, HEAD_SIZE), jnp.float32)
            self.mixed = jnp.zeros((kv_local * group, HEAD_SIZE), jnp.float32)

        def score(self, c):
            part = lax.dot_general(
                self.query,
                k_held[self.u % 2, c : c + tile],
                (((1,), (1,)), ((), ())),
                preferred_element_type=jnp.float32,
            )
            for d in range(0, tile, HEAD_SIZE):
                dense = part[:group, d : d + HEAD_SIZE]
                for h in range(1, kv_local):
                    other = part[h * group : (h + 1) * group, d : d + HEAD_SIZE]
                    dense = jnp.where(lane == h, other, dense)
                slots = lax.broadcasted_iota(jnp.int32, (samples, HEAD_SIZE), 1) + (c + d)
                bias = jnp.where(slots < self.lens, 0.0, MASKED)
                dense = (dense.reshape(HEAD_GROUP, samples, HEAD_SIZE) + bias[None]).reshape(
                    group, HEAD_SIZE
                )
                scores[self.u % 2, :, c + d : c + d + HEAD_SIZE] = dense
                self.most = jnp.maximum(self.most, dense)

        def find_top(self):
            self.tops = [
                jnp.maximum(
                    jnp.max(jnp.where(lane == h, self.most, MASKED), axis=-1, keepdims=True),
                    self.own[h],
                )
                for h in range(kv_local)
            ]
            self.top = jnp.broadcast_to(self.tops[0], (group, HEAD_SIZE))
            for h in range(1, kv_local):
                self.top = jnp.where(lane == h, self.tops[h], self.top)

        def mix(self, c):
            weights = [[] for _ in range(kv_local)]
            for d in range(0, tile, HEAD_SIZE):
                score = scores[self.u % 2, :, c + d : c + d + HEAD_SIZE]
                expo = jnp.exp2((score - self.top) * scale)
                self.sums = self.sums + expo
                for h in range(kv_local):
                    kept = expo if kv_local == 1 else jnp.where(lane == h, expo, 0.0)
                    weights[h].append(kept.astype(jnp.bfloat16))
            weights = jnp.concatenate([jnp.concatenate(w, axis=1) for w in weights], axis=0)
            self.mixed = self.mixed + jnp.dot(
                weights, v_held[self.u % 2, c : c + tile], preferred_element_type=jnp.float32
            )

        def result(self):
            line = []
            for h in range(kv_local):
                own_expo = jnp.exp2((self.own[h] - self.tops[h]) * scale)
                kept = jnp.where(lane == h, self.sums, 0.0)
                inverse = 1.0 / (jnp.sum(kept, axis=-1, keepdims=True) + own_expo)
                own_weight = own_expo * inverse
                value = fresh[h][self.rows]
                for j in range(HEAD_GROUP):
                    at = slice(j * samples, (j + 1) * samples)
                    part = self.mixed[h * group + j * samples : h * group + (j + 1) * samples]
                    line.append(part * inverse[at] + own_weight[at] * value)
            return jnp.concatenate(line, axis=1)

    line_up = [Prompt(u) for u in range(here)]
    for u in range(here + 1):
        if u < here:
            wait(keys[u])
        if u > 0:
            wait(values[u - 1])
        for c in range(0, length, tile):
            if u < here:
                line_up[u].score(c)
            if u > 0:
                line_up[u - 1].mix(c)
        if u + 2 < here:
            start(keys[u + 2])
        if 0 < u and u + 1 < here:
            start(values[u + 1])
        if u < here:
            line_up[u].find_top()
    out_ref[...] = jnp.concatenate([prompt.result() for prompt in line_up], axis=0).astype(
        out_ref.dtype
    )


def attention(partials, cosine, sine, lens, k_cache, value_cache, chunk, chunks):
    rows, width = cosine.shape[0], partials[0][0].shape[1]
    kv_local, terms = len(partials), [len(head_terms) for head_terms in partials]
    prompts, length, _ = k_cache.shape
    samples = rows // prompts
    here = prompts // chunks
    height = here * samples
    heads = kv_local * HEAD_GROUP
    pieces = length // 2048
    return pl.pallas_call(
        functools.partial(attention_kernel, terms, samples, chunk * here),
        in_specs=[pl.BlockSpec(memory_space=pl.ANY)] * (sum(terms) + 5),
        out_specs=pl.BlockSpec(memory_space=pltpu.VMEM),
        out_shape=jax.ShapeDtypeStruct((height, heads * HEAD_SIZE), jnp.bfloat16),
        scratch_shapes=[
            pltpu.VMEM((2, HEAD_GROUP * samples, length), jnp.float32),
            pltpu.VMEM((2, length, HEAD_SIZE), jnp.bfloat16),
            pltpu.VMEM((2, length, HEAD_SIZE), jnp.bfloat16),
            pltpu.VMEM((sum(terms), height, width), jnp.bfloat16),
            pltpu.VMEM((2, height, HEAD_SIZE), jnp.float32),
            pltpu.VMEM((height, HEAD_SIZE), jnp.int32),
            pltpu.SemaphoreType.DMA((2, pieces)),
            pltpu.SemaphoreType.DMA((2, pieces)),
            pltpu.SemaphoreType.DMA((sum(terms) + 3,)),
        ],
        compiler_params=pltpu.CompilerParams(vmem_limit_bytes=48 * MIB),
        cost_estimate=pl.CostEstimate(
            flops=4 * here * heads * samples * length * HEAD_SIZE,
            bytes_accessed=4 * here * length * HEAD_SIZE,
            transcendentals=here * HEAD_GROUP * samples * length,
        ),
        name="attention",
    )(*[term for head_terms in partials for term in head_terms], cosine, sine, lens, k_cache, value_cache)


CHUNKS = 2


def after(value, *others):
    return lax.optimization_barrier((value, others))[0]


def local(hidden, query_key_value_weight, w_out, k_cache, value_cache, lengths, assign):
    tp_count = lax.axis_size("tp")
    grp_count = lax.axis_size("grp")
    ratio = grp_count // tp_count
    t = lax.axis_index("tp")
    plane = lax.axis_index("grp") // ratio
    core = lax.axis_index("grp") % ratio
    row_count, width = hidden.shape
    prompts, context, kv_local, _ = k_cache.shape
    shifts = range(tp_count)

    def to_rank(value, shift):
        if shift == 0:
            return value
        return lax.ppermute(value, "tp", [(i, i ^ shift) for i in range(tp_count)])

    def to_plane(value, shift):
        if shift == 0:
            return value
        pairs = [(i, ((i // ratio) ^ shift) * ratio + i % ratio) for i in range(grp_count)]
        return lax.ppermute(value, "grp", pairs)

    def to_core(value, turn):
        if turn == 0:
            return value
        pairs = [(i, i // ratio * ratio + (i + turn) % ratio) for i in range(grp_count)]
        return lax.ppermute(value, "grp", pairs)

    index = jnp.arange(row_count, dtype=jnp.int32)
    key = assign * row_count + index
    place = jnp.sum((key[None, :] < key[:, None]).astype(jnp.int32), axis=1)
    sort_rows = (place[None, :] == index[:, None]).astype(jnp.bfloat16)
    lens = jnp.sum(jnp.where(place[None, :] == index[:, None], lengths[None, :], 0), axis=1)
    cosine, sine = rotary_tables(lens)
    lens = jnp.broadcast_to(lens[:, None], (row_count, HEAD_SIZE))

    hidden = jnp.dot(sort_rows, hidden, preferred_element_type=jnp.float32).astype(jnp.bfloat16)
    full = [to_rank(hidden, shift) for shift in shifts]
    ranks = jnp.stack([t ^ shift for shift in shifts]).astype(jnp.int32)
    owners = jnp.stack([(core - turn) % ratio for turn in range(ratio)]).astype(jnp.int32)
    row_places = jnp.stack([plane ^ t ^ shift for shift in shifts]).astype(jnp.int32)
    head_width = query_key_value_weight.shape[1] // (tp_count * kv_local)
    size = kv_local * head_width
    *near, far = [(t ^ shift) * size for shift in shifts]
    whole = [lax.dynamic_slice_in_dim(query_key_value_weight, at, size, 1) for at in near]
    split = [
        lax.dynamic_slice_in_dim(query_key_value_weight, far + h * head_width, head_width, 1)
        for h in range(kv_local)
    ]
    full = after(full, whole, split)
    normed = normalize(full, row_places)
    features = [to_plane(block, shift) for shift, block in zip(shifts, normed)]

    def exchanged(parts):
        return [to_rank(part, shift) for shift, part in zip(shifts, parts)]

    coming = exchanged(whole) + [to_rank(split[0], shifts[-1])]
    features = lay(features, jnp.arange(tp_count, dtype=jnp.int32), [0] * tp_count, width)
    received = after(coming, features)
    partials = []
    for h in range(kv_local):
        firsts = [h * head_width] * (tp_count - 1) + [0]
        laid = lay(received, ranks, firsts, head_width)
        if h + 1 < kv_local:
            coming = to_rank(after(split[h + 1], received), shifts[-1])
        laid = [to_core(laid, turn) for turn in range(ratio)]
        blocks = project(features, laid, owners, [[n] for n in shifts])
        partials.append([to_plane(block, shift) for shift, block in zip(shifts, blocks)])
        if h + 1 < kv_local:
            received = received[:-1] + [after(coming, partials[h][1])]

    depth = w_out.shape[0] // tp_count
    source = after(w_out, blocks)
    out_received = exchanged(
        [lax.dynamic_slice_in_dim(source, (t ^ shift) * depth, depth, 0).T for shift in shifts]
    )

    keys = k_cache.reshape(prompts, context * kv_local, HEAD_SIZE)
    values = value_cache.reshape(prompts, context * kv_local, HEAD_SIZE)
    plane_pairs = [
        (g * tp_count + r, (r * ratio + g % ratio) * tp_count + g // ratio)
        for g in range(grp_count)
        for r in range(tp_count)
    ]
    gathered = []
    for chunk in range(CHUNKS):
        if chunk > 0:
            lens = after(lens, mixed, out_received)
        mixed = attention(partials, cosine, sine, lens, keys, values, chunk, CHUNKS)
        gathered.append([to_plane(mixed, shift) for shift in shifts])
    laid = lay(after(out_received, mixed, gathered[:-1]), ranks, [0] * tp_count, depth)
    out_weights = [to_core(laid, turn) for turn in range(ratio)]
    results = []
    for mixed in gathered:
        if results:
            mixed = after(mixed, products)
        products = output(mixed, out_weights, owners, row_places)
        blocks = exchanged(products)
        summed = sum(block.astype(jnp.float32) for block in blocks).astype(jnp.bfloat16)
        results.append(lax.ppermute(summed, ("grp", "tp"), plane_pairs))
    result = jnp.concatenate(results, axis=0)
    return lax.dot_general(
        sort_rows, result, (((0,), (0,)), ((), ())), preferred_element_type=jnp.float32
    ).astype(jnp.bfloat16)


def solution(mesh):
    return jax.shard_map(
        local,
        mesh=mesh,
        in_specs=(
            P("grp", "tp"),
            P(("grp", "tp"), None),
            P(None, ("grp", "tp")),
            P("grp", None, "tp", None),
            P("grp", None, "tp", None),
            P("grp"),
            P("grp"),
        ),
        out_specs=P("grp", "tp"),
        check_vma=False,
    )
```

```python
import functools

import jax
import jax.numpy as jnp
from jax import lax
from jax.experimental import pallas as pl
from jax.experimental.pallas import tpu as pltpu
from jax.sharding import PartitionSpec as P

QUERY_HEADS = 64
KEY_VALUE_HEADS = 8
HEAD_SIZE = 128
HEAD_GROUP = QUERY_HEADS // KEY_VALUE_HEADS


EPS = 1e-06
ROPE_BASE = 1000000.0
LOG2_E = 1.4426950408889634
MASKED = -1e30
MIB = 1024 * 1024


def rotary_tables(positions):
    half = HEAD_SIZE // 2
    freq = ROPE_BASE ** (-jnp.arange(half, dtype=jnp.float32) * 2.0 / HEAD_SIZE)
    angle = positions.astype(jnp.float32)[:, None] * freq[None, :]
    cosine, sine = (jnp.cos(angle), jnp.sin(angle))
    return jnp.concatenate([cosine, cosine], axis=1), jnp.concatenate([-sine, sine], axis=1)


def column_tile(width):
    return next(tile for tile in (512, 640, 256, 128) if width % tile == 0)


def normalize_kernel(count, place_ref, *refs):
    xs, outs, held = refs[:count], refs[count : 2 * count], refs[2 * count]
    values = [ref[...].astype(jnp.float32) for ref in xs]
    total = sum(jnp.sum(value * value, axis=-1, keepdims=True) for value in values)
    factor = lax.rsqrt(total / (count * xs[0].shape[1]) + EPS)
    for n, value in enumerate(values):
        held[place_ref[n]] = (value * factor).astype(held.dtype)
    for n, out_ref in enumerate(outs):
        out_ref[...] = held[n]


def normalize(xs, places):
    count = len(xs)
    return pl.pallas_call(
        functools.partial(normalize_kernel, count),
        grid_spec=pltpu.PrefetchScalarGridSpec(
            num_scalar_prefetch=1,
            grid=(),
            in_specs=[pl.BlockSpec(memory_space=pltpu.VMEM)] * count,
            out_specs=[pl.BlockSpec(memory_space=pltpu.VMEM)] * count,
            scratch_shapes=[pltpu.VMEM((count,) + xs[0].shape, jnp.bfloat16)],
        ),
        out_shape=[jax.ShapeDtypeStruct(xs[0].shape, jnp.bfloat16)] * count,
        compiler_params=pltpu.CompilerParams(vmem_limit_bytes=48 * MIB),
        name="normalize",
    )(places, *xs)


def lay_kernel(count, first, place_ref, *refs):
    pieces, (out_ref, sems) = refs[:count], refs[count:]
    rows = pieces[0].shape[0]
    lanes = pl.ds(first, out_ref.shape[1])
    copies = []
    for n, piece in enumerate(pieces):
        start = pl.multiple_of(place_ref[n] * rows, 16)
        copies.append(
            pltpu.make_async_copy(piece.at[:, lanes], out_ref.at[pl.ds(start, rows)], sems.at[n])
        )
    for copy in copies:
        copy.start()
    for copy in copies:
        copy.wait()


def lay(pieces, places, first, width):
    count = len(pieces)
    rows = pieces[0].shape[0]
    if rows % 16:
        whole = jnp.zeros((count * rows, width), pieces[0].dtype)
        for n, piece in enumerate(pieces):
            piece = piece[:, first : first + width]
            whole = lax.dynamic_update_slice_in_dim(whole, piece, places[n] * rows, 0)
        return whole
    return pl.pallas_call(
        functools.partial(lay_kernel, count, first),
        grid_spec=pltpu.PrefetchScalarGridSpec(
            num_scalar_prefetch=1,
            grid=(),
            in_specs=[pl.BlockSpec(memory_space=pl.ANY)] * count,
            out_specs=pl.BlockSpec(memory_space=pltpu.VMEM),
            scratch_shapes=[pltpu.SemaphoreType.DMA((count,))],
        ),
        out_shape=jax.ShapeDtypeStruct((count * rows, width), pieces[0].dtype),
        compiler_params=pltpu.CompilerParams(vmem_limit_bytes=6 * MIB),
        cost_estimate=pl.CostEstimate(
            flops=0, bytes_accessed=4 * count * rows * width, transcendentals=0
        ),
        name="lay",
    )(places, *pieces)


def project_kernel(count, groups, place_ref, x_ref, *refs):
    pieces, outs, (weight, sems) = refs[:count], refs[count:-2], refs[-2:]
    rows = pieces[0].shape[0]
    width = outs[0].shape[1]
    height = x_ref.shape[0] // sum(len(group) for group in groups)
    tile = column_tile(width)
    copies = []
    for c in range(width // tile):
        for n, piece in enumerate(pieces):
            start = pl.multiple_of(place_ref[n] * rows, 16)
            copy = pltpu.make_async_copy(
                piece.at[:, pl.ds(c * tile, tile)],
                weight.at[pl.ds(start, rows), pl.ds(c * tile, tile)],
                sems.at[c, n],
            )
            copy.start()
            copies.append(copy)
    for c in range(width // tile):
        for copy in copies[c * count : (c + 1) * count]:
            copy.wait()
        lanes = slice(c * tile, (c + 1) * tile)
        result = jnp.dot(x_ref[...], weight[:, lanes], preferred_element_type=jnp.float32)
        result = result.astype(jnp.bfloat16)
        for group, out_ref in zip(groups, outs):
            for at, n in enumerate(group):
                out_ref[at * height : (at + 1) * height, lanes] = result[
                    n * height : (n + 1) * height
                ]


def project(x, pieces, places, groups):
    rows, width = pieces[0].shape
    count, blocks = len(pieces), sum(len(group) for group in groups)
    height = x.shape[0] // blocks
    tile = column_tile(width)
    return pl.pallas_call(
        functools.partial(project_kernel, count, groups),
        grid_spec=pltpu.PrefetchScalarGridSpec(
            num_scalar_prefetch=1,
            grid=(),
            in_specs=[pl.BlockSpec(memory_space=pltpu.VMEM)]
            + [pl.BlockSpec(memory_space=pl.ANY)] * count,
            out_specs=[pl.BlockSpec(memory_space=pltpu.VMEM)] * len(groups),
            scratch_shapes=[
                pltpu.VMEM((count * rows, width), jnp.bfloat16),
                pltpu.SemaphoreType.DMA((width // tile, count)),
            ],
        ),
        out_shape=[
            jax.ShapeDtypeStruct((len(group) * height, width), jnp.bfloat16) for group in groups
        ],
        compiler_params=pltpu.CompilerParams(vmem_limit_bytes=48 * MIB),
        cost_estimate=pl.CostEstimate(
            flops=2 * blocks * height * count * rows * width,
            bytes_accessed=2 * count * rows * width,
            transcendentals=0,
        ),
        name="project",
    )(places, x, *pieces)


def output_kernel(count, blocks, place_ref, x_place_ref, *refs):
    xs, pieces, outs = refs[:blocks], refs[blocks : blocks + count], refs[blocks + count : -2]
    x_held, x_sems = refs[-2:]
    rows = pieces[0].shape[0]
    height = xs[0].shape[0]
    copies = []
    for n, x in enumerate(xs):
        start = pl.multiple_of(x_place_ref[n] * height, 16)
        copies.append(pltpu.make_async_copy(x, x_held.at[pl.ds(start, height)], x_sems.at[n]))
    for copy in copies:
        copy.start()
    for copy in copies:
        copy.wait()

    def multiply(piece, at):
        result = lax.dot_general(
            x_held[...], piece[...], (((1,), (1,)), ((), ())), preferred_element_type=jnp.float32
        ).astype(jnp.bfloat16)
        for n in range(blocks):
            outs[n][:, at * rows : (at + 1) * rows] = result[n * height : (n + 1) * height]

    for n, piece in enumerate(pieces):
        for at in range(count):
            pl.when(place_ref[n] == at)(functools.partial(multiply, piece, at))


def output(xs, pieces, places, x_places):
    rows, depth = pieces[0].shape
    count, blocks, height = len(pieces), len(xs), xs[0].shape[0]
    return pl.pallas_call(
        functools.partial(output_kernel, count, blocks),
        grid_spec=pltpu.PrefetchScalarGridSpec(
            num_scalar_prefetch=2,
            grid=(),
            in_specs=[pl.BlockSpec(memory_space=pl.ANY)] * blocks
            + [pl.BlockSpec(memory_space=pltpu.VMEM)] * count,
            out_specs=[pl.BlockSpec(memory_space=pltpu.VMEM)] * blocks,
            scratch_shapes=[
                pltpu.VMEM((blocks * height, depth), jnp.bfloat16),
                pltpu.SemaphoreType.DMA((blocks,)),
            ],
        ),
        out_shape=[jax.ShapeDtypeStruct((height, count * rows), jnp.bfloat16)] * blocks,
        compiler_params=pltpu.CompilerParams(vmem_limit_bytes=48 * MIB),
        cost_estimate=pl.CostEstimate(
            flops=2 * blocks * height * count * rows * depth,
            bytes_accessed=2 * count * rows * depth,
            transcendentals=0,
        ),
        name="output",
    )(places, x_places, *xs, *pieces)


def attention_kernel(terms, samples, first, *refs):
    kv_local, count = len(terms), sum(terms)
    cos_ref, sin_ref, lens_ref, k_ref, v_ref, out_ref = refs[count : count + 6]
    scores, k_held, v_held, held, tables, lens_held, k_sems, v_sems, sems = refs[count + 6 :]
    height = out_ref.shape[0]
    here = height // samples
    length = k_ref.shape[1]
    pieces = k_sems.shape[1]
    piece = length // pieces
    scale = HEAD_SIZE ** (-0.5) * LOG2_E
    group = HEAD_GROUP * samples
    tile = 1024

    chunk = pl.ds(first * samples, height)
    small = [
        pltpu.make_async_copy(ref.at[chunk], held.at[n], sems.at[n])
        for n, ref in enumerate(refs[:count])
    ]
    small += [
        pltpu.make_async_copy(ref.at[chunk], to, sems.at[count + n])
        for n, (ref, to) in enumerate(
            [(cos_ref, tables.at[0]), (sin_ref, tables.at[1]), (lens_ref, lens_held)]
        )
    ]

    def fetch(ref, buffer, buffer_sems, u):
        return [
            pltpu.make_async_copy(
                ref.at[first + u, pl.ds(c * piece, piece)],
                buffer.at[u % 2, pl.ds(c * piece, piece)],
                buffer_sems.at[u % 2, c],
            )
            for c in range(pieces)
        ]

    def start(copies):
        for copy in copies:
            copy.start()

    def wait(copies):
        for copy in copies:
            copy.wait()

    keys = [fetch(k_ref, k_held, k_sems, u) for u in range(here)]
    values = [fetch(v_ref, v_held, v_sems, u) for u in range(here)]
    start(small)
    for u in range(min(2, here)):
        start(keys[u] + values[u])
    wait(small)
    cosine, sine = tables[0], tables[1]
    lane = lax.broadcasted_iota(jnp.int32, (group, HEAD_SIZE), 1) % kv_local

    queries, owns, fresh = [], [], []
    for h in range(kv_local):
        at = sum(terms[:h])
        proj = sum(held[n].astype(jnp.float32) for n in range(at, at + terms[h]))

        def head(index):
            vec = proj[:, index * HEAD_SIZE : (index + 1) * HEAD_SIZE]
            vec = vec * lax.rsqrt(jnp.mean(vec * vec, axis=-1, keepdims=True) + EPS)
            vec = vec * cosine + pltpu.roll(vec, HEAD_SIZE // 2, 1) * sine
            return vec.astype(jnp.bfloat16).astype(jnp.float32)

        new_key = head(HEAD_GROUP)
        new_value = proj[:, (HEAD_GROUP + 1) * HEAD_SIZE : (HEAD_GROUP + 2) * HEAD_SIZE]
        fresh.append(new_value.astype(jnp.bfloat16).astype(jnp.float32))
        queries.append([head(j) for j in range(HEAD_GROUP)])
        owns.append([jnp.sum(q * new_key, axis=-1, keepdims=True) for q in queries[-1]])

    class Prompt:
        def __init__(self, u):
            self.u = u
            self.rows = slice(u * samples, (u + 1) * samples)
            self.query = jnp.concatenate(
                [q[self.rows] for head_queries in queries for q in head_queries], axis=0
            ).astype(jnp.bfloat16)
            self.own = [
                jnp.concatenate([o[self.rows] for o in head_owns], axis=0) for head_owns in owns
            ]
            self.lens = lens_held[self.rows, 0:1] * kv_local
            self.most = jnp.full((group, HEAD_SIZE), MASKED, jnp.float32)
            self.sums = jnp.zeros((group, HEAD_SIZE), jnp.float32)
            self.mixed = jnp.zeros((kv_local * group, HEAD_SIZE), jnp.float32)

        def score(self, c):
            part = lax.dot_general(
                self.query,
                k_held[self.u % 2, c : c + tile],
                (((1,), (1,)), ((), ())),
                preferred_element_type=jnp.float32,
            )
            for d in range(0, tile, HEAD_SIZE):
                dense = part[:group, d : d + HEAD_SIZE]
                for h in range(1, kv_local):
                    other = part[h * group : (h + 1) * group, d : d + HEAD_SIZE]
                    dense = jnp.where(lane == h, other, dense)
                slots = lax.broadcasted_iota(jnp.int32, (samples, HEAD_SIZE), 1) + (c + d)
                bias = jnp.where(slots < self.lens, 0.0, MASKED)
                dense = (dense.reshape(HEAD_GROUP, samples, HEAD_SIZE) + bias[None]).reshape(
                    group, HEAD_SIZE
                )
                scores[self.u % 2, :, c + d : c + d + HEAD_SIZE] = dense
                self.most = jnp.maximum(self.most, dense)

        def find_top(self):
            self.tops = [
                jnp.maximum(
                    jnp.max(jnp.where(lane == h, self.most, MASKED), axis=-1, keepdims=True),
                    self.own[h],
                )
                for h in range(kv_local)
            ]
            self.top = jnp.broadcast_to(self.tops[0], (group, HEAD_SIZE))
            for h in range(1, kv_local):
                self.top = jnp.where(lane == h, self.tops[h], self.top)

        def mix(self, c):
            weights = [[] for _ in range(kv_local)]
            for d in range(0, tile, HEAD_SIZE):
                score = scores[self.u % 2, :, c + d : c + d + HEAD_SIZE]
                expo = jnp.exp2((score - self.top) * scale)
                self.sums = self.sums + expo
                for h in range(kv_local):
                    kept = expo if kv_local == 1 else jnp.where(lane == h, expo, 0.0)
                    weights[h].append(kept.astype(jnp.bfloat16))
            weights = jnp.concatenate([jnp.concatenate(w, axis=1) for w in weights], axis=0)
            self.mixed = self.mixed + jnp.dot(
                weights, v_held[self.u % 2, c : c + tile], preferred_element_type=jnp.float32
            )

        def result(self):
            line = []
            for h in range(kv_local):
                own_expo = jnp.exp2((self.own[h] - self.tops[h]) * scale)
                kept = jnp.where(lane == h, self.sums, 0.0)
                inverse = 1.0 / (jnp.sum(kept, axis=-1, keepdims=True) + own_expo)
                own_weight = own_expo * inverse
                value = fresh[h][self.rows]
                for j in range(HEAD_GROUP):
                    at = slice(j * samples, (j + 1) * samples)
                    part = self.mixed[h * group + j * samples : h * group + (j + 1) * samples]
                    line.append(part * inverse[at] + own_weight[at] * value)
            return jnp.concatenate(line, axis=1)

    line_up = [Prompt(u) for u in range(here)]
    for u in range(here + 1):
        if u < here:
            wait(keys[u])
        if u > 0:
            wait(values[u - 1])
        for c in range(0, length, tile):
            if u < here:
                line_up[u].score(c)
            if u > 0:
                line_up[u - 1].mix(c)
        if u + 2 < here:
            start(keys[u + 2])
        if 0 < u and u + 1 < here:
            start(values[u + 1])
        if u < here:
            line_up[u].find_top()
    out_ref[...] = jnp.concatenate([prompt.result() for prompt in line_up], axis=0).astype(
        out_ref.dtype
    )


def attention(partials, cosine, sine, lens, k_cache, value_cache, chunk, chunks):
    rows, width = cosine.shape[0], partials[0][0].shape[1]
    kv_local, terms = len(partials), [len(head_terms) for head_terms in partials]
    prompts, length, _ = k_cache.shape
    samples = rows // prompts
    here = prompts // chunks
    height = here * samples
    heads = kv_local * HEAD_GROUP
    pieces = length // 2048
    return pl.pallas_call(
        functools.partial(attention_kernel, terms, samples, chunk * here),
        in_specs=[pl.BlockSpec(memory_space=pl.ANY)] * (sum(terms) + 5),
        out_specs=pl.BlockSpec(memory_space=pltpu.VMEM),
        out_shape=jax.ShapeDtypeStruct((height, heads * HEAD_SIZE), jnp.bfloat16),
        scratch_shapes=[
            pltpu.VMEM((2, HEAD_GROUP * samples, length), jnp.float32),
            pltpu.VMEM((2, length, HEAD_SIZE), jnp.bfloat16),
            pltpu.VMEM((2, length, HEAD_SIZE), jnp.bfloat16),
            pltpu.VMEM((sum(terms), height, width), jnp.bfloat16),
            pltpu.VMEM((2, height, HEAD_SIZE), jnp.float32),
            pltpu.VMEM((height, HEAD_SIZE), jnp.int32),
            pltpu.SemaphoreType.DMA((2, pieces)),
            pltpu.SemaphoreType.DMA((2, pieces)),
            pltpu.SemaphoreType.DMA((sum(terms) + 3,)),
        ],
        compiler_params=pltpu.CompilerParams(vmem_limit_bytes=48 * MIB),
        cost_estimate=pl.CostEstimate(
            flops=4 * here * heads * samples * length * HEAD_SIZE,
            bytes_accessed=4 * here * length * HEAD_SIZE,
            transcendentals=here * HEAD_GROUP * samples * length,
        ),
        name="attention",
    )(*[term for head_terms in partials for term in head_terms], cosine, sine, lens, k_cache, value_cache)


CHUNKS = 2


def after(value, *others):
    return lax.optimization_barrier((value, others))[0]


def local(hidden, query_key_value_weight, w_out, k_cache, value_cache, lengths, assign):
    tp_count = lax.axis_size("tp")
    grp_count = lax.axis_size("grp")
    ratio = grp_count // tp_count
    t = lax.axis_index("tp")
    plane = lax.axis_index("grp") // ratio
    core = lax.axis_index("grp") % ratio
    row_count, width = hidden.shape
    prompts, context, kv_local, _ = k_cache.shape
    shifts = range(tp_count)

    def to_rank(value, shift):
        if shift == 0:
            return value
        return lax.ppermute(value, "tp", [(i, i ^ shift) for i in range(tp_count)])

    def to_plane(value, shift):
        if shift == 0:
            return value
        pairs = [(i, ((i // ratio) ^ shift) * ratio + i % ratio) for i in range(grp_count)]
        return lax.ppermute(value, "grp", pairs)

    def to_core(value, turn):
        if turn == 0:
            return value
        pairs = [(i, i // ratio * ratio + (i + turn) % ratio) for i in range(grp_count)]
        return lax.ppermute(value, "grp", pairs)

    index = jnp.arange(row_count, dtype=jnp.int32)
    key = assign * row_count + index
    place = jnp.sum((key[None, :] < key[:, None]).astype(jnp.int32), axis=1)
    sort_rows = (place[None, :] == index[:, None]).astype(jnp.bfloat16)
    lens = jnp.sum(jnp.where(place[None, :] == index[:, None], lengths[None, :], 0), axis=1)
    cosine, sine = rotary_tables(lens)
    lens = jnp.broadcast_to(lens[:, None], (row_count, HEAD_SIZE))

    hidden = jnp.dot(sort_rows, hidden, preferred_element_type=jnp.float32).astype(jnp.bfloat16)
    full = [to_rank(hidden, shift) for shift in shifts]
    ranks = jnp.stack([t ^ shift for shift in shifts]).astype(jnp.int32)
    owners = jnp.stack([(core - turn) % ratio for turn in range(ratio)]).astype(jnp.int32)
    row_places = jnp.stack([plane ^ t ^ shift for shift in shifts]).astype(jnp.int32)
    head_width = query_key_value_weight.shape[1] // (tp_count * kv_local)
    slices, source = [], query_key_value_weight
    for h in range(kv_local):
        slices.append(
            [
                lax.dynamic_slice_in_dim(
                    source, ((t ^ shift) * kv_local + h) * head_width, head_width, 1
                )
                for shift in shifts
            ]
        )
        source = after(query_key_value_weight, slices[h])
    full = after(full, slices)
    normed = normalize(full, row_places)
    features = [to_plane(block, shift) for shift, block in zip(shifts, normed)]

    def exchanged(parts):
        return [to_rank(part, shift) for shift, part in zip(shifts, parts)]

    coming = exchanged(slices[0])
    features = lay(features, jnp.arange(tp_count, dtype=jnp.int32), 0, width)
    received = after(coming, features)
    partials = []
    for h in range(kv_local):
        laid = lay(received, ranks, 0, head_width)
        if h + 1 < kv_local:
            coming = exchanged(after(slices[h + 1], received))
        laid = [to_core(laid, turn) for turn in range(ratio)]
        blocks = project(features, laid, owners, [[n] for n in shifts])
        partials.append([to_plane(block, shift) for shift, block in zip(shifts, blocks)])
        if h + 1 < kv_local:
            received = after(coming, partials[h][1:3])

    depth = w_out.shape[0] // tp_count
    source = after(w_out, blocks)
    out_received = exchanged(
        [lax.dynamic_slice_in_dim(source, (t ^ shift) * depth, depth, 0).T for shift in shifts]
    )

    keys = k_cache.reshape(prompts, context * kv_local, HEAD_SIZE)
    values = value_cache.reshape(prompts, context * kv_local, HEAD_SIZE)
    plane_pairs = [
        (g * tp_count + r, (r * ratio + g % ratio) * tp_count + g // ratio)
        for g in range(grp_count)
        for r in range(tp_count)
    ]
    gathered = []
    for chunk in range(CHUNKS):
        if chunk > 0:
            lens = after(lens, mixed, out_received)
        mixed = attention(partials, cosine, sine, lens, keys, values, chunk, CHUNKS)
        gathered.append([to_plane(mixed, shift) for shift in shifts])
    laid = lay(after(out_received, mixed, gathered[:-1]), ranks, 0, depth)
    out_weights = [to_core(laid, turn) for turn in range(ratio)]
    results = []
    for mixed in gathered:
        if results:
            mixed = after(mixed, products)
        products = output(mixed, out_weights, owners, row_places)
        blocks = exchanged(products)
        summed = sum(block.astype(jnp.float32) for block in blocks).astype(jnp.bfloat16)
        results.append(lax.ppermute(summed, ("grp", "tp"), plane_pairs))
    result = jnp.concatenate(results, axis=0)
    return lax.dot_general(
        sort_rows, result, (((0,), (0,)), ((), ())), preferred_element_type=jnp.float32
    ).astype(jnp.bfloat16)


def solution(mesh):
    return jax.shard_map(
        local,
        mesh=mesh,
        in_specs=(
            P("grp", "tp"),
            P(("grp", "tp"), None),
            P(None, ("grp", "tp")),
            P("grp", None, "tp", None),
            P("grp", None, "tp", None),
            P("grp"),
            P("grp"),
        ),
        out_specs=P("grp", "tp"),
        check_vma=False,
    )
```
